128 devices in a mesh: dp: 16 (over y, z), row: 4 (over x_lo, core), col: 2 (over x_hi).
Axes of the slice: x: 4 (x_hi: 2, x_lo: 2; x = x_hi * 2 + x_lo), y: 4, z: 4, core: 2. Of those that a mesh axis runs over, the one named last changes fastest.
Arguments:
- block_input: bfloat16 [16384, 2048], P(('dp', 'col'), 'row'), may hold values from -6.2 to 6.2
- cotangent: bfloat16 [16384, 2048], P(('dp', 'col'), 'row'), may hold values from -6 to 6
- norm_gains: float32 [2, 2048], P(None, 'row'), may hold values from 0.2 to 2
- gains_first: float32 [2, 2048], P(None, 'row'), may hold values from -56 to 56
- gains_second: float32 [2, 2048], P(None, 'row'), may hold values from 180.224 to 2949.12
- heads_projection_weight: float32 [2048, 2560], P(('row', 'dp'), 'col'), may hold values from -0.125 to 0.125
- heads_first_moment: float32 [2048, 2560], P(('row', 'dp'), 'col'), may hold values from -64 to 64
- heads_second_moment: float32 [2048, 2560], P(('row', 'dp'), 'col'), may hold values from 212.992 to 3440.64
- merge_weight: float32 [2048, 2048], P(('col', 'dp'), 'row'), may hold values from -2 to 2
- merge_first: float32 [2048, 2048], P(('col', 'dp'), 'row'), may hold values from -6 to 6
- merge_second: float32 [2048, 2048], P(('col', 'dp'), 'row'), may hold values from 2.08 to 32
- gating_weight: float32 [2048, 2, 5632], P(('row', 'dp'), None, 'col'), may hold values from -0.125 to 0.125
- gating_first: float32 [2048, 2, 5632], P(('row', 'dp'), None, 'col'), may hold values from -32 to 32
- gating_second: float32 [2048, 2, 5632], P(('row', 'dp'), None, 'col'), may hold values from 52.4288 to 851.968
- down_weight: float32 [5632, 2048], P(('col', 'dp'), 'row'), may hold values from -0.078125 to 0.078125
- down_first: float32 [5632, 2048], P(('col', 'dp'), 'row'), may hold values from -48 to 48
- down_second: float32 [5632, 2048], P(('col', 'dp'), 'row'), may hold values from 155.648 to 2457.6
Outputs:
- block_output: bfloat16 [16384, 2048], P(('dp', 'col'), 'row')
- input_grad: float32 [16384, 2048], P(('dp', 'col'), 'row')
- gains_grad: float32 [2, 2048], P(None, 'row')
- gains_next: float32 [2, 2048], P(None, 'row')
- gains_mean: float32 [2, 2048], P(None, 'row')
- gains_square: float32 [2, 2048], P(None, 'row')
- heads_grad: float32 [2048, 2560], P(('row', 'dp'), 'col')
- heads_next: float32 [2048, 2560], P(('row', 'dp'), 'col')
- heads_mean: float32 [2048, 2560], P(('row', 'dp'), 'col')
- heads_square: float32 [2048, 2560], P(('row', 'dp'), 'col')
- merge_grad: float32 [2048, 2048], P(('col', 'dp'), 'row')
- merge_next: float32 [2048, 2048], P(('col', 'dp'), 'row')
- merge_mean: float32 [2048, 2048], P(('col', 'dp'), 'row')
- merge_square: float32 [2048, 2048], P(('col', 'dp'), 'row')
- gating_grad: float32 [2048, 2, 5632], P(('row', 'dp'), None, 'col')
- gating_next: float32 [2048, 2, 5632], P(('row', 'dp'), None, 'col')
- gating_mean: float32 [2048, 2, 5632], P(('row', 'dp'), None, 'col')
- gating_square: float32 [2048, 2, 5632], P(('row', 'dp'), None, 'col')
- down_grad: float32 [5632, 2048], P(('col', 'dp'), 'row')
- down_next: float32 [5632, 2048], P(('col', 'dp'), 'row')
- down_mean: float32 [5632, 2048], P(('col', 'dp'), 'row')
- down_square: float32 [5632, 2048], P(('col', 'dp'), 'row')
The draws below stay inside these ranges and needn't reach their ends.
All inputs are finite; a program needn't handle non-finite values.
Results may differ from the reference program's by a relative error of at most 0.025.
Values may be sent and summed in bfloat16 or wider, within the bound.
A program may use at most 192 MiB of HBM per device.

```python
import math
import jax
import jax.numpy as jnp
from jax import lax

MODEL_WIDTH = 2048
FF = 5632
HQ = 32
KEY_VALUE_HEADS = 4
HEAD_SIZE = 64
QUERY_PER_GROUP = 8
SEQUENCE_LENGTH = 1024
STEP = 10
TOKENS = 16384
N_DP = 16


def draw_block_input(key, part):
    key = jax.random.fold_in(key, 11)
    feature_pos = jnp.arange(MODEL_WIDTH, dtype=jnp.float32)[None, :] / MODEL_WIDTH
    noise = jnp.clip(jax.random.normal(key, (TOKENS, MODEL_WIDTH), jnp.float32), -5.0, 5.0)
    spread = jnp.sqrt(0.5 + feature_pos)
    return (noise * spread).astype(jnp.bfloat16)


def draw_norm_gains(key, part):
    key = jax.random.fold_in(key, 12)
    feature_pos = jnp.arange(MODEL_WIDTH, dtype=jnp.float32)[None, :] / MODEL_WIDTH
    jitter = jax.random.uniform(key, (2, MODEL_WIDTH), jnp.float32, 0.8, 1.2)
    result = (0.5 + feature_pos) * jitter
    return result.astype(jnp.float32)


def steps_of(rng, shape, cuts, low, largest):
    loudness = 1.0
    for axis_at, blocks in cuts:
        steps = jax.random.uniform(jax.random.fold_in(jax.random.fold_in(rng, 6), axis_at), (blocks,), jnp.float32, low / len(cuts), largest / len(cuts))
        loudness = loudness * jnp.repeat(jnp.exp(steps), shape[axis_at] // blocks).reshape((-1,) + (1,) * (len(shape) - 1 - axis_at))
    return loudness


def gaussian(own_key, extent, width, reach, shards=(), kind=jnp.bfloat16):
    gain = steps_of(own_key, extent, shards, -0.22, 0.18) if shards else 1.0
    values = jax.random.normal(own_key, extent, jnp.float32) * width * gain
    return jnp.minimum(jnp.maximum(values, -reach), reach).astype(kind)


def setup_inputs(seed: int = 0) -> dict:
    key_list = jax.random.split(jax.random.key(seed), 18)
    block_input = draw_block_input(jax.random.fold_in(key_list[17], 71), 0)
    cotangent = gaussian(key_list[1], (TOKENS, MODEL_WIDTH), 1.0, 6.0, ((0, 32), (1, 4)))
    norm_gains = draw_norm_gains(jax.random.fold_in(key_list[17], 71), 0)
    gains_first = gaussian(key_list[3], (2, MODEL_WIDTH), (0.072 * (SEQUENCE_LENGTH * N_DP) ** 0.5), 56.0, ((1, 4),), jnp.float32)
    gains_second = jnp.clip(jnp.exp(math.log(2949.12) - 2.7950616 * jax.random.uniform(key_list[4], (2, MODEL_WIDTH), jnp.float32) ** steps_of(key_list[4], (2, MODEL_WIDTH), ((1, 4),), -0.2, 0.2)), 180.224, 2949.12)
    heads_projection_weight = gaussian(key_list[5], (MODEL_WIDTH, KEY_VALUE_HEADS * (QUERY_PER_GROUP + 2) * HEAD_SIZE), MODEL_WIDTH ** -0.5, 0.125, ((0, 64), (1, 2)), jnp.float32)
    heads_first_moment = gaussian(key_list[6], (MODEL_WIDTH, KEY_VALUE_HEADS * (QUERY_PER_GROUP + 2) * HEAD_SIZE), (0.078 * (SEQUENCE_LENGTH * N_DP) ** 0.5), 64.0, ((0, 64), (1, 2)), jnp.float32)
    heads_second_moment = jnp.clip(jnp.exp(math.log(3440.64) - 2.7821581 * jax.random.uniform(key_list[7], (MODEL_WIDTH, KEY_VALUE_HEADS * (QUERY_PER_GROUP + 2) * HEAD_SIZE), jnp.float32) ** steps_of(key_list[7], (MODEL_WIDTH, KEY_VALUE_HEADS * (QUERY_PER_GROUP + 2) * HEAD_SIZE), ((0, 64), (1, 2)), -0.2, 0.2)), 212.992, 3440.64)
    merge_weight = gaussian(key_list[8], (HQ * HEAD_SIZE, MODEL_WIDTH), (max(1, HQ * HEAD_SIZE * 4 // SEQUENCE_LENGTH)) ** -0.5, 2.0, ((0, 32), (1, 4)), jnp.float32)
    merge_first = gaussian(key_list[9], (HQ * HEAD_SIZE, MODEL_WIDTH), (0.24 * N_DP ** 0.5), 6.0, ((0, 32), (1, 4)), jnp.float32)
    merge_second = jnp.clip(jnp.exp(math.log(32.0) - 2.73336805 * jax.random.uniform(key_list[10], (HQ * HEAD_SIZE, MODEL_WIDTH), jnp.float32) ** steps_of(key_list[10], (HQ * HEAD_SIZE, MODEL_WIDTH), ((0, 32), (1, 4)), -0.2, 0.2)), 2.08, 32.0)
    gating_weight = gaussian(key_list[11], (MODEL_WIDTH, 2, FF), MODEL_WIDTH ** -0.5, 0.125, ((0, 64), (2, 2)), jnp.float32)
    gating_first = gaussian(key_list[12], (MODEL_WIDTH, 2, FF), (0.039 * (SEQUENCE_LENGTH * N_DP) ** 0.5), 32.0, ((0, 64), (2, 2)), jnp.float32)
    gating_second = jnp.clip(jnp.exp(math.log(851.968) - 2.78809295 * jax.random.uniform(key_list[13], (MODEL_WIDTH, 2, FF), jnp.float32) ** steps_of(key_list[13], (MODEL_WIDTH, 2, FF), ((0, 64), (2, 2)), -0.2, 0.2)), 52.4288, 851.968)
    down_weight = gaussian(key_list[14], (FF, MODEL_WIDTH), FF ** -0.5, 0.078125, ((0, 32), (1, 4)), jnp.float32)
    down_first = gaussian(key_list[15], (FF, MODEL_WIDTH), (0.067 * (SEQUENCE_LENGTH * N_DP) ** 0.5), 48.0, ((0, 32), (1, 4)), jnp.float32)
    down_second = jnp.clip(jnp.exp(math.log(2457.6) - 2.7593436 * jax.random.uniform(key_list[16], (FF, MODEL_WIDTH), jnp.float32) ** steps_of(key_list[16], (FF, MODEL_WIDTH), ((0, 32), (1, 4)), -0.2, 0.2)), 155.648, 2457.6)
    return {"block_input": block_input, "cotangent": cotangent, "norm_gains": norm_gains, "gains_first": gains_first, "gains_second": gains_second, "heads_projection_weight": heads_projection_weight, "heads_first_moment": heads_first_moment, "heads_second_moment": heads_second_moment, "merge_weight": merge_weight, "merge_first": merge_first, "merge_second": merge_second, "gating_weight": gating_weight, "gating_first": gating_first, "gating_second": gating_second, "down_weight": down_weight, "down_first": down_first, "down_second": down_second}


EPS_NORM = 1e-05
PRECISE = lax.Precision.HIGHEST
BETA_ONE = 0.9
BETA_TWO = 0.95
EPS_ADAM = 1e-08
RATE_MATRIX = 0.05
RATE_MERGE = 0.5
RATE_GAIN = 1.0
WEIGHT_DECAY = 0.1
ROPE_BASE = 10000.0
MASK_FILL = -1e+30

@jax.custom_vjp
def low(v):
    return lax.optimization_barrier(v.astype(jnp.bfloat16)).astype(jnp.float32)

@jax.custom_vjp
def low_back(v):
    return v

def low_keep(v):
    return (low(v), None)

def low_pass(kept, grad):
    return (grad,)

def back_keep(v):
    return (v, None)

def back_low(kept, grad):
    return (low(grad),)
low.defvjp(low_keep, low_pass)
low_back.defvjp(back_keep, back_low)

def rope_tables(positions):
    half_width = HEAD_SIZE // 2
    frequency = ROPE_BASE ** (-jnp.arange(half_width, dtype=jnp.float32) * 2.0 / HEAD_SIZE)
    angles = positions.astype(jnp.float32)[:, None] * frequency[None, :]
    return (jnp.cos(angles), jnp.sin(angles))

def rotate(vector, cosine_rows, sine_rows):
    piece_one, piece_two = jnp.split(vector, 2, axis=-1)
    return jnp.concatenate([piece_one * cosine_rows - piece_two * sine_rows, piece_two * cosine_rows + piece_one * sine_rows], axis=-1)

def rms_norm(values, gain_row):
    scaled = lax.rsqrt(lax.optimization_barrier(jnp.mean(values * values, axis=-1, keepdims=True)) + EPS_NORM)
    return values * scaled * gain_row

def attend(group_block):
    query_rows, key_rows, value_rows = group_block
    token_length = key_rows.shape[0]
    scores = jnp.einsum('tqd,sd->qts', query_rows, key_rows, precision=PRECISE) * HEAD_SIZE ** (-0.5)
    causal = jnp.arange(token_length)[:, None] >= jnp.arange(token_length)[None, :]
    scores = low_back(jnp.where(causal[None], scores, MASK_FILL))
    row_max = lax.optimization_barrier(jnp.max(scores, axis=-1, keepdims=True))
    exponent = jnp.exp(scores - row_max)
    probs_low = low(exponent / lax.optimization_barrier(jnp.sum(exponent, axis=-1, keepdims=True)))
    return jnp.einsum('qts,sd->tqd', probs_low, value_rows, precision=PRECISE)

def block_forward(inputs, norm_gains, heads_projection_weight, merge_weight, gating_weight, down_weight):
    token_length = inputs.shape[0]
    cosine_rows, sine_rows = rope_tables(jnp.arange(token_length))
    normed_one = low(rms_norm(inputs, norm_gains[0]))
    mixed_token_rows = low_back(jnp.dot(normed_one, low(heads_projection_weight), precision=PRECISE))
    mixed_token_rows = mixed_token_rows.reshape(token_length, KEY_VALUE_HEADS, QUERY_PER_GROUP + 2, HEAD_SIZE)
    query_rows = low(rotate(mixed_token_rows[:, :, :QUERY_PER_GROUP], cosine_rows[:, None, None], sine_rows[:, None, None]))
    key_rows = low(rotate(mixed_token_rows[:, :, QUERY_PER_GROUP], cosine_rows[:, None], sine_rows[:, None]))
    value_rows = low(mixed_token_rows[:, :, QUERY_PER_GROUP + 1])
    attended = lax.map(jax.checkpoint(attend), (jnp.moveaxis(query_rows, 1, 0), jnp.moveaxis(key_rows, 1, 0), jnp.moveaxis(value_rows, 1, 0)))
    attended = jnp.moveaxis(attended, 0, 1).reshape(token_length, HQ * HEAD_SIZE)
    attended = low_back(low(attended))
    branch = low_back(jnp.dot(attended, low(merge_weight), precision=PRECISE))
    middle = inputs + branch
    normed_two = low(rms_norm(middle, norm_gains[1]))
    gated = low_back(jnp.einsum('td,dkf->tkf', normed_two, low(gating_weight), precision=PRECISE))
    hidden = low(jax.nn.silu(gated[:, 0]) * gated[:, 1])
    return middle + low_back(jnp.dot(hidden, low(down_weight), precision=PRECISE))

def adamw(current, gradient, first, second, step_rate, decay_rate):
    mean_new = BETA_ONE * first + (1.0 - BETA_ONE) * gradient
    square_new = BETA_TWO * second + (1.0 - BETA_TWO) * gradient * gradient
    mean_hat = mean_new / (1.0 - BETA_ONE ** STEP)
    square_hat = square_new / (1.0 - BETA_TWO ** STEP)
    updated = current - step_rate * (mean_hat / (jnp.sqrt(square_hat) + EPS_ADAM) + decay_rate * current)
    return (updated, mean_new, square_new)

def reference(block_input, cotangent, norm_gains, gains_first, gains_second, heads_projection_weight, heads_first_moment, heads_second_moment, merge_weight, merge_first, merge_second, gating_weight, gating_first, gating_second, down_weight, down_first, down_second):
    inputs = block_input.astype(jnp.float32).reshape(N_DP, SEQUENCE_LENGTH, MODEL_WIDTH)
    back_rows = cotangent.astype(jnp.float32).reshape(N_DP, SEQUENCE_LENGTH, MODEL_WIDTH)
    weights = (norm_gains, heads_projection_weight, merge_weight, gating_weight, down_weight)

    def per_sequence(summed, sequence_pair):
        sequence, sequence_back = sequence_pair
        result, pullback = jax.vjp(block_forward, sequence, *weights)
        gradients = pullback(sequence_back)
        summed = tuple((a + b for a, b in zip(summed, gradients[1:])))
        return (summed, (result, gradients[0]))
    zero_sums = tuple((jnp.zeros_like(w) for w in weights))
    summed, (outputs, input_rows) = lax.scan(per_sequence, zero_sums, (inputs, back_rows))
    gains_grad, heads_grad, merge_grad, gating_grad, down_grad = summed
    gains_next, gains_mean, gains_square = adamw(norm_gains, gains_grad, gains_first, gains_second, RATE_GAIN, 0.0)
    heads_next, heads_mean, heads_square = adamw(heads_projection_weight, heads_grad, heads_first_moment, heads_second_moment, RATE_MATRIX, WEIGHT_DECAY)
    merge_next, merge_mean, merge_square = adamw(merge_weight, merge_grad, merge_first, merge_second, RATE_MERGE, WEIGHT_DECAY)
    gating_next, gating_mean, gating_square = adamw(gating_weight, gating_grad, gating_first, gating_second, RATE_MATRIX, WEIGHT_DECAY)
    down_next, down_mean, down_square = adamw(down_weight, down_grad, down_first, down_second, RATE_MATRIX, WEIGHT_DECAY)
    block_output = outputs.reshape(TOKENS, MODEL_WIDTH).astype(jnp.bfloat16)
    input_grad = input_rows.reshape(TOKENS, MODEL_WIDTH)
    return (block_output, input_grad, gains_grad, gains_next, gains_mean, gains_square, heads_grad, heads_next, heads_mean, heads_square, merge_grad, merge_next, merge_mean, merge_square, gating_grad, gating_next, gating_mean, gating_square, down_grad, down_next, down_mean, down_square)
```

```python
import functools

import jax
import jax.numpy as jnp
from jax import lax
from jax.experimental import pallas as pl
from jax.experimental.pallas import tpu as pltpu
from jax.sharding import PartitionSpec as P

MODEL_WIDTH = 2048
KEY_VALUE_HEADS = 4
HEAD_SIZE = 64
QUERY_PER_GROUP = 8
STEP = 10


EPS_NORM = 1e-05
BETA_ONE = 0.9
BETA_TWO = 0.95
EPS_ADAM = 1e-08
RATE_MATRIX = 0.05
RATE_MERGE = 0.5
RATE_GAIN = 1.0
WEIGHT_DECAY = 0.1
ROPE_BASE = 10000.0
MASK_FILL = -1e30

MESH = pl.DeviceIdType.MESH
VMEM_BYTES = 60 * 2**20
BF16 = jnp.bfloat16
F32 = jnp.float32

SEQ = 1024
OWN = 128
HEADS_COLS = 384
HIDDEN = 768
PIECE = 48
PIECE_USED = 44


class Place:
    def __init__(self):
        self.dp = lax.axis_index("dp")
        self.row = lax.axis_index("row")
        self.col = lax.axis_index("col")
        self.y = lax.div(self.dp, 4)
        self.z = lax.rem(self.dp, 4)
        self.core = lax.rem(self.row, 2)
        self.x = self.col * 2 + lax.div(self.row, 2)

    def near(self, x=0, core=0, y=0, z=0):
        new_x = lax.rem(self.x + x + 4, 4)
        new_core = lax.rem(self.core + core, 2)
        new_y = lax.rem(self.y + y + 4, 4)
        new_z = lax.rem(self.z + z + 4, 4)
        return {
            "dp": new_y * 4 + new_z,
            "row": lax.rem(new_x, 2) * 2 + new_core,
            "col": lax.div(new_x, 2),
        }

    def slot(self, first_axis, first, second):
        y, z = (first, second) if first_axis == "y" else (second, first)
        return lax.rem(self.y + y + 4, 4) * 4 + lax.rem(self.z + z + 4, 4)

    def line(self, x, core):
        return lax.rem(self.x + x + 4, 4) * 2 + lax.rem(self.core + core, 2)

    def peer(self, step):
        other = lax.rem(self.row + step, 4)
        return other, {"dp": self.dp, "row": other, "col": self.col}


class Wires:
    def __init__(self, send, recv, local):
        self.send, self.recv, self.local = send, recv, local
        self.count = 0
        self.local_count = 0
        self.sent = []
        self.kept = []

    def push(self, source, target, device):
        index = self.count
        self.count += 1
        copy = pltpu.make_async_remote_copy(
            src_ref=source,
            dst_ref=target,
            send_sem=self.send.at[index],
            recv_sem=self.recv.at[index],
            device_id=device,
            device_id_type=MESH,
        )
        copy.start()
        self.sent.append(copy)
        return copy

    def keep(self, source, target):
        copy = pltpu.make_async_copy(source, target, self.local.at[self.local_count])
        self.local_count += 1
        copy.start()
        return copy

    def drain(self):
        for copy in self.sent:
            copy.wait_send()


def meet(devices, more=0):
    barrier = pltpu.get_barrier_semaphore()
    for device in devices:
        pl.semaphore_signal(barrier, inc=1, device_id=device, device_id_type=MESH)
    pl.semaphore_wait(barrier, len(devices))


def interleave(*plans):
    waiting = [[next(plan), order, plan] for order, plan in enumerate(plans)]
    while waiting:
        waiting.sort(key=lambda entry: (entry[0], entry[1]))
        entry = waiting[0]
        try:
            entry[0] = max(entry[0], next(entry[2]))
        except StopIteration:
            waiting.pop(0)


def ring_neighbours(place):
    return [place.near(y=1), place.near(y=-1), place.near(z=1), place.near(z=-1)]


def line_neighbours(place):
    return [place.near(x=1), place.near(x=-1), place.near(core=1)]


def line_gather(place, wires, own, out, block, half, start, cost):
    me = place.line(0, 0)
    yield start
    kept = wires.keep(own, block(out, me))
    right = wires.push(own, block(out, me), place.near(x=1))
    left = wires.push(own, block(out, me), place.near(x=-1))
    beside = [wires.push(own, block(out, me), place.near(core=1))]
    yield start + cost + 2
    right.wait_recv()
    came = place.line(-1, 0)
    far_right = wires.push(half(out, came, 0), half(out, came, 0), place.near(x=1))
    beside.append(wires.push(block(out, came), block(out, came), place.near(core=1)))
    left.wait_recv()
    came = place.line(1, 0)
    far_left = wires.push(half(out, came, 1), half(out, came, 1), place.near(x=-1))
    beside.append(wires.push(block(out, came), block(out, came), place.near(core=1)))
    yield start + 1.5 * cost + 4
    far_right.wait_recv()
    far_left.wait_recv()
    came = place.line(2, 0)
    beside.append(wires.push(block(out, came), block(out, came), place.near(core=1)))
    yield start + 1.5 * cost + 6
    kept.wait()
    for copy in beside:
        copy.wait_recv()


def token_block(ref, index):
    return ref.at[pl.ds(pl.multiple_of(index * OWN, OWN), OWN)]


def token_half(ref, index, side):
    return ref.at[pl.ds(pl.multiple_of(index * OWN + side * (OWN // 2), OWN // 2), OWN // 2)]


def tile_block(ref, index):
    x, core = lax.div(index, 2), lax.rem(index, 2)
    rows = pl.ds(pl.multiple_of(lax.div(x, 2) * 512, 512), 512)
    columns = pl.ds(pl.multiple_of((lax.rem(x, 2) * 2 + core) * 512, 512), 512)
    return ref.at[rows, columns]


def tile_half(ref, index, side):
    x, core = lax.div(index, 2), lax.rem(index, 2)
    rows = pl.ds(pl.multiple_of(lax.div(x, 2) * 512 + side * 256, 256), 256)
    columns = pl.ds(pl.multiple_of((lax.rem(x, 2) * 2 + core) * 512, 512), 512)
    return ref.at[rows, columns]


def add_rows(out, terms, rows, step=16):
    def chunk(index, carry):
        at = pl.ds(pl.multiple_of(index * step, step), step)
        out[at, :] = functools.reduce(
            lambda a, b: a + b, [term[at, :].astype(F32) for term in terms]
        ).astype(out.dtype)
        return carry

    lax.fori_loop(0, rows // step, chunk, 0)


LINE_SCATTER_SCRATCH = [
    pltpu.VMEM((4, OWN, MODEL_WIDTH), BF16),
    pltpu.VMEM((2, OWN // 2, MODEL_WIDTH), BF16),
    pltpu.VMEM((2, OWN, MODEL_WIDTH), BF16),
    pltpu.VMEM((3, OWN, MODEL_WIDTH), BF16),
]


def line_scatter(place, wires, part, scratch, start, cost):
    beside, halves, full, total = scratch
    yield start
    pairs = {}
    for offset in (2, 1, 3, 0):
        pairs[offset] = wires.push(
            token_block(part, place.line(offset, 1)), beside.at[offset], place.near(core=1)
        )
    yield start + 2
    pairs[2].wait_recv()
    add_rows(total.at[2], [token_block(part, place.line(2, 0)), beside.at[2]], OWN)
    far_right = wires.push(
        total.at[2, pl.ds(0, OWN // 2)], halves.at[0], place.near(x=1)
    )
    far_left = wires.push(
        total.at[2, pl.ds(OWN // 2, OWN // 2)], halves.at[1], place.near(x=-1)
    )
    yield start + 3
    pairs[1].wait_recv()
    add_rows(total.at[0], [token_block(part, place.line(1, 0)), beside.at[1]], OWN)
    right_late = wires.push(
        total.at[0, pl.ds(OWN // 2, OWN // 2)],
        full.at[0, pl.ds(OWN // 2, OWN // 2)],
        place.near(x=1),
    )
    pairs[3].wait_recv()
    add_rows(total.at[1], [token_block(part, place.line(3, 0)), beside.at[3]], OWN)
    left_late = wires.push(
        total.at[1, pl.ds(0, OWN // 2)], full.at[1, pl.ds(0, OWN // 2)], place.near(x=-1)
    )
    yield start + 5 + 0.5 * cost
    far_right.wait_recv()
    first = total.at[0, pl.ds(0, OWN // 2)]
    add_rows(first, [first, halves.at[0]], OWN // 2)
    right = wires.push(first, full.at[0, pl.ds(0, OWN // 2)], place.near(x=1))
    far_left.wait_recv()
    second = total.at[1, pl.ds(OWN // 2, OWN // 2)]
    add_rows(second, [second, halves.at[1]], OWN // 2)
    left = wires.push(second, full.at[1, pl.ds(OWN // 2, OWN // 2)], place.near(x=-1))
    yield start + 6 + 1.5 * cost
    pairs[0].wait_recv()
    right_late.wait_recv()
    left_late.wait_recv()
    right.wait_recv()
    left.wait_recv()


def scatter_terms(place, part, scratch):
    beside, halves, full, total = scratch
    return [token_block(part, place.line(0, 0)), beside.at[0], full.at[0], full.at[1]]


class Rows:
    def __init__(self, columns):
        self.item_shape = (2, 32, columns)
        self.half_shape = (1, 32, columns)

    def item(self, ref, side, slot):
        return ref.at[pl.ds(2 * side, 2), slot]

    def half(self, ref, side, part, slot):
        return ref.at[pl.ds(2 * side + part, 1), slot]

    def cut(self, item, part):
        return item.at[pl.ds(part, 1)]


class Flat:
    def __init__(self):
        self.item_shape = (PIECE, MODEL_WIDTH // 2)
        self.half_shape = (PIECE, MODEL_WIDTH // 4)

    def item(self, ref, side, slot):
        rows = pl.ds(pl.multiple_of(slot * PIECE, PIECE), PIECE)
        return ref.at[rows, pl.ds(side * (MODEL_WIDTH // 2), MODEL_WIDTH // 2)]

    def half(self, ref, side, part, slot):
        rows = pl.ds(pl.multiple_of(slot * PIECE, PIECE), PIECE)
        return ref.at[rows, pl.ds((2 * side + part) * (MODEL_WIDTH // 4), MODEL_WIDTH // 4)]

    def cut(self, item, part):
        return item.at[:, pl.ds(part * (MODEL_WIDTH // 4), MODEL_WIDTH // 4)]


def ring_move(place, axis, step):
    return place.near(y=step) if axis == "y" else place.near(z=step)


def ring_gather(place, wires, kind, out, side, start, cost):
    first, second = ("z", "y") if side == 0 else ("y", "z")
    slot = functools.partial(place.slot, first)
    spread = {}

    def send_on(offset):
        item = kind.item(out, side, slot(offset, 0))
        spread[offset] = [
            wires.push(item, item, ring_move(place, second, step)) for step in (1, -1)
        ]

    def pass_on(offset):
        right, left = spread[offset]
        right.wait_recv()
        piece = kind.half(out, side, 0, slot(offset, -1))
        one = wires.push(piece, piece, ring_move(place, second, 1))
        left.wait_recv()
        piece = kind.half(out, side, 1, slot(offset, 1))
        return [one, wires.push(piece, piece, ring_move(place, second, -1))]

    yield start
    own = kind.item(out, side, slot(0, 0))
    right = wires.push(own, own, ring_move(place, first, 1))
    left = wires.push(own, own, ring_move(place, first, -1))
    send_on(0)
    yield start + cost + 2
    right.wait_recv()
    piece = kind.half(out, side, 0, slot(-1, 0))
    far_right = wires.push(piece, piece, ring_move(place, first, 1))
    send_on(-1)
    left.wait_recv()
    piece = kind.half(out, side, 1, slot(1, 0))
    far_left = wires.push(piece, piece, ring_move(place, first, -1))
    send_on(1)
    last = []
    yield start + 2 * cost + 4
    last += pass_on(0)
    yield start + 2.5 * cost + 4
    far_right.wait_recv()
    far_left.wait_recv()
    send_on(2)
    yield start + 4 * cost + 4
    last += pass_on(-1)
    yield start + 5.5 * cost + 4
    last += pass_on(1)
    yield start + 6.5 * cost + 4
    last += pass_on(2)
    yield start + 7.5 * cost + 6
    for copy in last:
        copy.wait_recv()


def ring_scatter_scratch(kind):
    def stack(count, shape):
        return pltpu.VMEM((count, *shape), BF16)

    one_side = [
        stack(8, kind.half_shape),
        stack(8, kind.item_shape),
        stack(8, kind.item_shape),
        stack(4, kind.item_shape),
        stack(2, kind.half_shape),
        stack(2, kind.item_shape),
        stack(2, kind.item_shape),
    ]
    return one_side + one_side


def add_item(out, terms):
    out[...] = functools.reduce(lambda a, b: a + b, [t[...].astype(F32) for t in terms]).astype(
        out.dtype
    )


def ring_scatter(place, wires, kind, part, side, scratch, result, start, cost):
    far, sums, came, column, far_last, sums_last, came_last = scratch[7 * side : 7 * side + 7]
    first, second = ("z", "y") if side == 0 else ("y", "z")
    slot = functools.partial(place.slot, first)
    order = (2, 1, -1, 0)
    yield start
    right, left = {}, {}
    for n, offset in enumerate(order):
        target = slot(offset, 2)
        right[offset] = wires.push(
            kind.half(part, side, 0, target), far.at[2 * n], ring_move(place, second, 1)
        )
        left[offset] = wires.push(
            kind.half(part, side, 1, target), far.at[2 * n + 1], ring_move(place, second, -1)
        )

    def add_far(source, halves, out, way):
        keep = 1 - way
        add_item(kind.cut(out, way), [kind.cut(source, way), halves])
        held = kind.cut(out, keep)
        held[...] = kind.cut(source, keep)[...]

    moved = {}
    for n, offset in enumerate(order):
        yield start + 2.5 + (0.5 + n) * cost
        right[offset].wait_recv()
        add_far(kind.item(part, side, slot(offset, 1)), far.at[2 * n], sums.at[2 * n], 0)
        one = wires.push(sums.at[2 * n], came.at[2 * n], ring_move(place, second, 1))
        left[offset].wait_recv()
        add_far(kind.item(part, side, slot(offset, -1)), far.at[2 * n + 1], sums.at[2 * n + 1], 1)
        two = wires.push(sums.at[2 * n + 1], came.at[2 * n + 1], ring_move(place, second, -1))
        moved[offset] = (one, two)

    def finish(n, offset):
        for copy in moved[offset]:
            copy.wait_recv()
        add_item(
            column.at[n],
            [kind.item(part, side, slot(offset, 0)), came.at[2 * n], came.at[2 * n + 1]],
        )

    yield start + 4 + 3 * cost
    finish(0, 2)
    far_right = wires.push(kind.cut(column.at[0], 0), far_last.at[0], ring_move(place, first, 1))
    far_left = wires.push(kind.cut(column.at[0], 1), far_last.at[1], ring_move(place, first, -1))
    yield start + 4 + 4 * cost
    finish(1, 1)
    yield start + 4 + 5 * cost
    finish(2, -1)
    far_right.wait_recv()
    add_far(column.at[1], far_last.at[0], sums_last.at[0], 0)
    one = wires.push(sums_last.at[0], came_last.at[0], ring_move(place, first, 1))
    far_left.wait_recv()
    add_far(column.at[2], far_last.at[1], sums_last.at[1], 1)
    two = wires.push(sums_last.at[1], came_last.at[1], ring_move(place, first, -1))
    yield start + 5 + 6 * cost
    finish(3, 0)
    yield start + 8 + 7.5 * cost
    one.wait_recv()
    two.wait_recv()
    add_item(result, [column.at[3], came_last.at[0], came_last.at[1]])


def call(kernel, outs, ins, scratch, wires, name, cost):
    return pl.pallas_call(
        kernel,
        out_shape=[shape for shape, _ in outs],
        in_specs=[pl.BlockSpec(memory_space=space) for _, space in ins],
        out_specs=[pl.BlockSpec(memory_space=space) for _, space in outs],
        scratch_shapes=list(scratch)
        + [
            pltpu.SemaphoreType.DMA((wires,)),
            pltpu.SemaphoreType.DMA((wires,)),
            pltpu.SemaphoreType.DMA((16,)),
        ],
        compiler_params=pltpu.CompilerParams(
            collective_id=name, has_side_effects=True, vmem_limit_bytes=VMEM_BYTES
        ),
        cost_estimate=pl.CostEstimate(flops=0, bytes_accessed=cost, transcendentals=0),
    )(*[array for array, _ in ins])


def shape(*extent, dtype=BF16):
    return jax.ShapeDtypeStruct(extent, dtype)


def merge_devices(place):
    homes = [
        {"dp": place.row * 4 + z, "row": jnp.int32(row), "col": place.col}
        for z in range(4)
        for row in range(4)
    ]
    users = [{"dp": jnp.int32(dp), "row": place.y, "col": place.col} for dp in range(16)]
    return homes, users


def start_kernel(
    heads_own, gating_own, down_own, merge_own, input_own, gains_own,
    heads, gating, down, merge, inputs, gains,
    send, recv, local,
):
    place = Place()
    wires = Wires(send, recv, local)
    homes, users = merge_devices(place)
    peers = [place.peer(step) for step in (1, 2, 3)]
    same = place.row == place.y
    barrier = pltpu.get_barrier_semaphore()
    devices = ring_neighbours(place) + line_neighbours(place) + [p for _, p in peers]
    for device in devices:
        pl.semaphore_signal(barrier, inc=1, device_id=device, device_id_type=MESH)
    for index, device in enumerate(homes):
        alone = (device["dp"] == place.dp) & (device["row"] == place.row)

        @pl.when(jnp.logical_not(alone))
        def _():
            pl.semaphore_signal(barrier, inc=1, device_id=device, device_id_type=MESH)

    pl.semaphore_wait(barrier, len(devices) + 16 - same.astype(jnp.int32))

    def down_columns(ref, row):
        return ref.at[:, pl.ds(pl.multiple_of(row * 512, 512), 512)]

    def exchange():
        yield 0.0
        moved = []
        kept = wires.keep(heads_own.at[place.row], heads.at[place.row, place.dp])
        for other, device in peers:
            moved.append(
                wires.push(heads_own.at[other], heads.at[place.row, place.dp], device)
            )
        for other, device in peers:
            moved.append(wires.push(gains_own, gains.at[place.row], device))
        kept_gains = wires.keep(gains_own, gains.at[place.row])
        yield 0.2
        rest = [
            wires.keep(gating_own.at[place.row], gating.at[place.row]),
            wires.keep(down_own.at[place.row], down_columns(down, place.row)),
        ]
        later = []
        for other, device in peers:
            later.append(wires.push(gating_own.at[other], gating.at[place.row], device))
            later.append(
                wires.push(down_own.at[other], down_columns(down, place.row), device)
            )
        yield 4.0
        kept.wait()
        kept_gains.wait()
        for copy in moved:
            copy.wait_recv()
        sides = [
            ring_gather(place, wires, Rows(HEADS_COLS), heads, side, 4.1, 1.1) for side in (0, 1)
        ]
        pending = [(next(plan), plan) for plan in sides]
        while pending:
            pending.sort(key=lambda entry: entry[0])
            when, plan = pending[0]
            yield when
            try:
                pending[0] = (next(plan), plan)
            except StopIteration:
                pending.pop(0)
        yield 30.0
        for copy in rest:
            copy.wait()
        for copy in later:
            copy.wait_recv()

    def merge_rows():
        yield 0.15
        target = merge.at[
            pl.ds(pl.multiple_of(place.z * 64, 64), 64),
            pl.ds(pl.multiple_of(place.row * 512, 512), 512),
        ]
        base = wires.count
        wires.count += 16
        copies = []
        for index, device in enumerate(users):
            copy = pltpu.make_async_remote_copy(
                src_ref=merge_own,
                dst_ref=target,
                send_sem=wires.send.at[base + index],
                recv_sem=wires.recv.at[base + place.row * 4 + place.z],
                device_id=device,
                device_id_type=MESH,
            )
            here = pltpu.make_async_copy(
                merge_own, target, wires.recv.at[base + place.row * 4 + place.z]
            )
            alone = (device["dp"] == place.dp) & same
            copies.append((copy, alone))

            @pl.when(alone)
            def _():
                here.start()

            @pl.when(jnp.logical_not(alone))
            def _():
                copy.start()

        yield 28.0
        for index in range(16):
            pltpu.make_async_copy(merge_own, target, wires.recv.at[base + index]).wait()
        for copy, alone in copies:

            @pl.when(jnp.logical_not(alone))
            def _():
                copy.wait_send()

    interleave(
        exchange(),
        merge_rows(),
        line_gather(place, wires, input_own, inputs, tile_block, tile_half, 0.1, 11.4),
    )
    wires.drain()


def middle_kernel(
    part, input_rows, gains, gating_own, down_own, back_own,
    middle, normed, gating, down, back,
    *scratch,
):
    line_scratch, (normed_own, send, recv, local) = scratch[:4], scratch[4:]
    place = Place()
    wires = Wires(send, recv, local)
    meet(ring_neighbours(place) + line_neighbours(place))

    def main():
        yield from line_scatter(place, wires, part, line_scratch, 0.0, 11.4)
        terms = scatter_terms(place, part, line_scratch)

        def chunk(index, carry):
            at = pl.ds(pl.multiple_of(index * 16, 16), 16)
            total = functools.reduce(lambda a, b: a + b, [t[at, :].astype(F32) for t in terms])
            total = total + input_rows[at, :].astype(F32)
            middle[at, :] = total
            scale = lax.rsqrt(
                jnp.sum(total * total, axis=1, keepdims=True) / MODEL_WIDTH + EPS_NORM
            )
            normed_own[at, :] = (total * scale * gains[1:2, :]).astype(BF16)
            return carry

        lax.fori_loop(0, OWN // 16, chunk, 0)
        yield from line_gather(
            place, wires, normed_own, normed, token_block, token_half, 25.0, 11.4
        )

    def weights():
        yield 0.3
        kept = [
            wires.keep(gating_own.at[r], gating.at[r, place.dp]) for r in range(4)
        ]
        rows = pl.ds(pl.multiple_of(place.dp * PIECE, PIECE), PIECE)
        kept.append(wires.keep(down_own, down.at[rows]))
        for copy in kept:
            copy.wait()
        plans = [
            ring_gather(place, wires, Rows(2 * HIDDEN), gating, side, 0.5, 4.3) for side in (0, 1)
        ] + [ring_gather(place, wires, Flat(), down, side, 0.6, 4.3) for side in (0, 1)]
        pending = [(next(plan), order, plan) for order, plan in enumerate(plans)]
        while pending:
            pending.sort(key=lambda entry: entry[:2])
            when, order, plan = pending[0]
            yield when
            try:
                pending[0] = (max(when, next(plan)), order, plan)
            except StopIteration:
                pending.pop(0)

    interleave(
        main(),
        weights(),
        line_gather(place, wires, back_own, back, tile_block, tile_half, 25.5, 22.0),
    )
    wires.drain()


def branch_kernel(
    part, middle, back_rows, gains, gating_part, down_part,
    grad_middle, branch, gain_part, gating_sum, down_sum,
    *scratch,
):
    line_scratch, scratch = scratch[:4], scratch[4:]
    gating_scratch, scratch = scratch[:14], scratch[14:]
    down_scratch, scratch = scratch[:14], scratch[14:]
    branch_own, send, recv, local = scratch
    place = Place()
    wires = Wires(send, recv, local)
    meet(ring_neighbours(place) + line_neighbours(place))

    def main():
        yield from line_scatter(place, wires, part, line_scratch, 0.0, 11.4)
        terms = scatter_terms(place, part, line_scratch)
        gain_part[...] = jnp.zeros_like(gain_part)

        def chunk(index, carry):
            at = pl.ds(pl.multiple_of(index * 16, 16), 16)
            grad = functools.reduce(lambda a, b: a + b, [t[at, :].astype(F32) for t in terms])
            through, gain = norm_back(middle[at, :], gains[1:2, :], grad)
            total = back_rows[at, :].astype(F32) + through
            grad_middle[at, :] = total
            branch_own[at, :] = total.astype(BF16)
            gain_part[...] += gain.reshape(2, 8, MODEL_WIDTH).sum(axis=0)
            return carry

        lax.fori_loop(0, OWN // 16, chunk, 0)
        yield from line_gather(
            place, wires, branch_own, branch, token_block, token_half, 25.0, 11.4
        )

    rows = Rows(2 * HIDDEN)
    flat = Flat()
    interleave(
        main(),
        *[
            ring_scatter(
                place, wires, rows, gating_part, side, gating_scratch,
                gating_sum.at[pl.ds(2 * side, 2)], 0.5, 4.3,
            )
            for side in (0, 1)
        ],
        *[
            ring_scatter(
                place, wires, flat, down_part, side, down_scratch,
                down_sum.at[:, pl.ds(side * 1024, 1024)], 0.6, 4.3,
            )
            for side in (0, 1)
        ],
    )
    wires.drain()


def norm_back(values, gain_row, gradient):
    scale = lax.rsqrt(jnp.sum(values * values, axis=1, keepdims=True) / MODEL_WIDTH + EPS_NORM)
    weighted = gain_row * gradient
    inner = jnp.sum(weighted * values, axis=1, keepdims=True)
    through = scale * weighted - values * (scale * scale * scale * inner / MODEL_WIDTH)
    return through, gradient * values * scale


def finish_kernel(
    part, down_out, middle, grad_middle, input_rows, gains, gain_part,
    heads_part, merge_part, gating_sum, down_sum,
    output, input_grad, gains_grad, heads_pieces, merge_pieces, gating_pieces, down_pieces,
    *scratch,
):
    line_scratch, scratch = scratch[:4], scratch[4:]
    out_scratch, scratch = scratch[:4], scratch[4:]
    heads_scratch, scratch = scratch[:14], scratch[14:]
    (
        heads_sum, output_own, input_grad_own, gain_rows, gain_came, gain_all, send, recv, local,
    ) = scratch
    place = Place()
    wires = Wires(send, recv, local)
    homes, users = merge_devices(place)
    peers = [place.peer(step) for step in (1, 2, 3)]
    same = place.row == place.y
    barrier = pltpu.get_barrier_semaphore()
    devices = ring_neighbours(place) + line_neighbours(place) + [p for _, p in peers]
    for device in devices:
        pl.semaphore_signal(barrier, inc=1, device_id=device, device_id_type=MESH)
    for device in users:
        alone = (device["dp"] == place.dp) & same

        @pl.when(jnp.logical_not(alone))
        def _():
            pl.semaphore_signal(barrier, inc=1, device_id=device, device_id_type=MESH)

    def far(step):
        index = lax.rem(place.col * 16 + place.dp + step, 32)
        return {"dp": lax.rem(index, 16), "row": place.row, "col": lax.div(index, 16)}

    def greet(step, carry):
        pl.semaphore_signal(barrier, inc=1, device_id=far(step), device_id_type=MESH)
        return carry

    lax.fori_loop(1, 32, greet, 0)
    pl.semaphore_wait(barrier, len(devices) + 31 + 16 - same.astype(jnp.int32))

    def column_block(ref, row):
        return ref.at[:, pl.ds(pl.multiple_of(row * 512, 512), 512)]

    def own_rows(ref, row):
        return ref.at[pl.ds(pl.multiple_of(row * OWN, OWN), OWN)]

    def recut(own, out, when):
        kept = wires.keep(column_block(own, place.row), own_rows(out, place.row))
        moved = [
            wires.push(column_block(own, other), own_rows(out, place.row), device)
            for other, device in peers
        ]
        yield when
        kept.wait()
        for copy in moved:
            copy.wait_recv()

    def gradient():
        yield from line_scatter(place, wires, part, line_scratch, 0.0, 11.4)
        terms = scatter_terms(place, part, line_scratch)
        gain_rows[0] = jnp.zeros((8, MODEL_WIDTH), F32)
        gain_rows[1] = gain_part[...]

        def chunk(index, carry):
            at = pl.ds(pl.multiple_of(index * 16, 16), 16)
            grad = functools.reduce(lambda a, b: a + b, [t[at, :].astype(F32) for t in terms])
            through, gain = norm_back(input_rows[at, :].astype(F32), gains[0:1, :], grad)
            input_grad_own[at, :] = grad_middle[at, :] + through
            gain_rows[0] += gain.reshape(2, 8, MODEL_WIDTH).sum(axis=0)
            return carry

        lax.fori_loop(0, OWN // 16, chunk, 0)
        moved = []
        for other, device in peers:
            piece = gain_rows.at[:, :, pl.ds(pl.multiple_of(other * 512, 512), 512)]
            moved.append(wires.push(piece, gain_came.at[place.row], device))
        piece = gain_rows.at[:, :, pl.ds(pl.multiple_of(place.row * 512, 512), 512)]
        kept = wires.keep(piece, gain_came.at[place.row])
        waits = recut(input_grad_own, input_grad, 38.0)
        next(waits)
        yield 28.0
        kept.wait()
        for copy in moved:
            copy.wait_recv()
        local_sum = gain_came[0] + gain_came[1] + gain_came[2] + gain_came[3]
        me = place.col * 16 + place.dp
        gain_all[me] = jnp.concatenate(
            [jnp.sum(local_sum, axis=1), jnp.zeros((6, 512), F32)], axis=0
        )
        base = wires.count
        wires.count += 32

        def gain_copy(step):
            return pltpu.make_async_remote_copy(
                src_ref=gain_all.at[me],
                dst_ref=gain_all.at[me],
                send_sem=wires.send.at[base + step],
                recv_sem=wires.recv.at[base + step],
                device_id=far(step),
                device_id_type=MESH,
            )

        def start(step, carry):
            gain_copy(step).start()
            return carry

        def finish(step, carry):
            gain_copy(step).wait()
            return carry

        lax.fori_loop(1, 32, start, 0)
        yield 36.0
        lax.fori_loop(1, 32, finish, 0)
        gains_grad[...] = functools.reduce(lambda a, b: a + b, [gain_all[i] for i in range(32)])
        yield 38.0
        for _ in waits:
            pass

    def outputs():
        yield from line_scatter(place, wires, down_out, out_scratch, 0.3, 22.0)
        terms = scatter_terms(place, down_out, out_scratch)

        def chunk(index, carry):
            at = pl.ds(pl.multiple_of(index * 16, 16), 16)
            total = functools.reduce(lambda a, b: a + b, [t[at, :].astype(F32) for t in terms])
            output_own[at, :] = (total + middle[at, :]).astype(BF16)
            return carry

        lax.fori_loop(0, OWN // 16, chunk, 0)
        yield from recut(output_own, output, 45.0)

    def back_pieces(part_of, out, when):
        kept = wires.keep(part_of(place.row), out.at[place.row])
        moved = [
            wires.push(part_of(other), out.at[place.row], device) for other, device in peers
        ]
        yield when
        kept.wait()
        for copy in moved:
            copy.wait_recv()

    def heads():
        plans = [
            ring_scatter(
                place, wires, Rows(HEADS_COLS), heads_part, side, heads_scratch,
                heads_sum.at[pl.ds(2 * side, 2)], 0.2, 1.1,
            )
            for side in (0, 1)
        ]
        pending = [(next(plan), order, plan) for order, plan in enumerate(plans)]
        while pending:
            pending.sort(key=lambda entry: entry[:2])
            when, order, plan = pending[0]
            yield when
            try:
                pending[0] = (max(when, next(plan)), order, plan)
            except StopIteration:
                pending.pop(0)
        yield 18.0
        yield from back_pieces(lambda row: heads_sum.at[row], heads_pieces, 40.0)

    def gating():
        yield 0.4
        yield from back_pieces(lambda row: gating_sum.at[row], gating_pieces, 41.0)

    def down():
        yield 0.5
        yield from back_pieces(lambda row: column_block(down_sum, row), down_pieces, 41.0)

    def merge():
        yield 0.1
        base = wires.count
        wires.count += 32
        copies = []
        for index, device in enumerate(homes):
            z, row = index // 4, index % 4
            source = merge_part.at[pl.ds(z * 64, 64), pl.ds(row * 512, 512)]
            copy = pltpu.make_async_remote_copy(
                src_ref=source,
                dst_ref=merge_pieces.at[place.dp],
                send_sem=wires.send.at[base + index],
                recv_sem=wires.recv.at[base + 16 + place.dp],
                device_id=device,
                device_id_type=MESH,
            )
            here = pltpu.make_async_copy(
                source, merge_pieces.at[place.dp], wires.recv.at[base + 16 + place.dp]
            )
            alone = (device["dp"] == place.dp) & (device["row"] == place.row)
            copies.append((copy, alone))

            @pl.when(alone)
            def _():
                here.start()

            @pl.when(jnp.logical_not(alone))
            def _():
                copy.start()

        yield 42.0
        for index in range(16):
            pltpu.make_async_copy(
                merge_part.at[pl.ds(0, 64), pl.ds(0, 512)],
                merge_pieces.at[index],
                wires.recv.at[base + 16 + index],
            ).wait()
        for copy, alone in copies:

            @pl.when(jnp.logical_not(alone))
            def _():
                copy.wait_send()

    interleave(gradient(), outputs(), heads(), gating(), down(), merge())
    wires.drain()


def rope_tables(positions):
    half_width = HEAD_SIZE // 2
    frequency = ROPE_BASE ** (-jnp.arange(half_width, dtype=jnp.float32) * 2.0 / HEAD_SIZE)
    angles = positions.astype(jnp.float32)[:, None] * frequency[None, :]
    return (jnp.cos(angles), jnp.sin(angles))


def rotate(vector, cosine_rows, sine_rows):
    piece_one, piece_two = jnp.split(vector, 2, axis=-1)
    return jnp.concatenate(
        [
            piece_one * cosine_rows - piece_two * sine_rows,
            piece_two * cosine_rows + piece_one * sine_rows,
        ],
        axis=-1,
    )


def product(left, right):
    return jnp.dot(left, right, preferred_element_type=F32)


def contract_last(left, right):
    return lax.dot_general(left, right, (((1,), (1,)), ((), ())), preferred_element_type=F32)


def token_product(left, right):
    return lax.dot_general(left, right, (((0,), (0,)), ((), ())), preferred_element_type=F32)


def adamw(current, gradient, first, second, step_rate, decay_rate):
    mean_new = BETA_ONE * first + (1.0 - BETA_ONE) * gradient
    square_new = BETA_TWO * second + (1.0 - BETA_TWO) * gradient * gradient
    mean_hat = mean_new / (1.0 - BETA_ONE**STEP)
    square_hat = square_new / (1.0 - BETA_TWO**STEP)
    updated = current - step_rate * (
        mean_hat / (jnp.sqrt(square_hat) + EPS_ADAM) + decay_rate * current
    )
    return (updated, mean_new, square_new)


def pack_heads(weight):
    groups = weight.astype(BF16).reshape(32, 2, 640)
    query = groups[:, :, :512].reshape(32, 2, 2, 256).transpose(1, 2, 0, 3)
    pair = groups[:, :, 512:].transpose(1, 0, 2)[:, None]
    pair = jnp.broadcast_to(pair, (2, 2, 32, 128))
    return jnp.concatenate([query, pair], axis=3).reshape(4, 32, HEADS_COLS)


def unpack_heads(pieces):
    pieces = pieces.astype(F32).reshape(2, 2, 32, HEADS_COLS)
    query = pieces[..., :256].transpose(2, 0, 1, 3).reshape(32, 2, 512)
    pair = (pieces[:, 0, :, 256:] + pieces[:, 1, :, 256:]).transpose(1, 0, 2)
    return jnp.concatenate([query, pair], axis=2).reshape(32, 1280)


def pack_gating(weight):
    cut = weight.astype(BF16).reshape(32, 2, 16, 4, PIECE_USED).transpose(3, 0, 1, 2, 4)
    cut = jnp.pad(cut, ((0, 0),) * 4 + ((0, PIECE - PIECE_USED),))
    return cut.reshape(4, 32, 2 * HIDDEN)


def unpack_gating(pieces):
    cut = pieces.reshape(4, 32, 2, 16, PIECE)[..., :PIECE_USED]
    return cut.transpose(1, 2, 3, 0, 4).reshape(32, 2, 2816).astype(F32)


def pack_down(weight):
    cut = weight.astype(BF16).reshape(4, PIECE_USED, 512)
    return jnp.pad(cut, ((0, 0), (0, PIECE - PIECE_USED), (0, 0)))


def unpack_down(pieces):
    return pieces[:, :PIECE_USED].reshape(4 * PIECE_USED, 512).astype(F32)


def body(
    block_input,
    cotangent,
    norm_gains,
    gains_first,
    gains_second,
    heads_projection_weight,
    heads_first_moment,
    heads_second_moment,
    merge_weight,
    merge_first,
    merge_second,
    gating_weight,
    gating_first,
    gating_second,
    down_weight,
    down_first,
    down_second,
):
    ANY, VMEM = pl.ANY, pltpu.VMEM
    head_scale = HEAD_SIZE ** (-0.5)
    row, col = lax.axis_index("row"), lax.axis_index("col")
    line = col * 4 + row

    def own_rows(values):
        return lax.dynamic_slice_in_dim(values, line * OWN, OWN, axis=0)

    w_heads, gating_own, down_own, w_merge, inputs, gains = call(
        start_kernel,
        [
            (shape(4, 16, 32, HEADS_COLS), ANY),
            (shape(4, 32, 2 * HIDDEN), ANY),
            (shape(PIECE, MODEL_WIDTH), ANY),
            (shape(256, MODEL_WIDTH), ANY),
            (shape(SEQ, MODEL_WIDTH), ANY),
            (shape(4, 8, 128, dtype=F32), ANY),
        ],
        [
            (pack_heads(heads_projection_weight), ANY),
            (pack_gating(gating_weight), ANY),
            (pack_down(down_weight), ANY),
            (merge_weight.astype(BF16), ANY),
            (block_input, ANY),
            (norm_gains.reshape(8, 128), ANY),
        ],
        [],
        100,
        0,
        2**24,
    )
    w_heads = w_heads.reshape(MODEL_WIDTH, HEADS_COLS)
    gains = gains.reshape(4, 2, 512).transpose(1, 0, 2).reshape(2, MODEL_WIDTH)
    input_rows = own_rows(inputs)
    wide = inputs.astype(F32)
    scale_one = lax.rsqrt(jnp.mean(wide * wide, axis=1, keepdims=True) + EPS_NORM)
    normed_one = (wide * scale_one * gains[0]).astype(BF16)

    mixed = product(normed_one, w_heads)
    cosine_rows, sine_rows = rope_tables(jnp.arange(SEQ, dtype=jnp.int32))
    query = rotate(
        mixed[:, :256].reshape(SEQ, 4, HEAD_SIZE), cosine_rows[:, None], sine_rows[:, None]
    ).astype(BF16)
    key = rotate(mixed[:, 256:320], cosine_rows, sine_rows).astype(BF16)
    value = mixed[:, 320:].astype(BF16)
    causal = jnp.arange(SEQ)[:, None] >= jnp.arange(SEQ)[None, :]

    def scores_of():
        raw = jnp.einsum("tqd,sd->qts", query, key, preferred_element_type=F32) * head_scale
        return jnp.where(causal, raw, MASK_FILL)

    scores = scores_of()
    row_max = jnp.max(scores, axis=-1, keepdims=True)
    exponent = jnp.exp(scores - row_max)
    exp_total = jnp.sum(exponent, axis=-1, keepdims=True)
    probs_low = (exponent / exp_total).astype(BF16)
    log_total = row_max + jnp.log(exp_total)
    attended = jnp.einsum("qts,sd->tqd", probs_low, value, preferred_element_type=F32)
    attended = attended.reshape(SEQ, 256).astype(BF16)
    merged = product(attended, w_merge).astype(BF16)

    middle, normed_two, w_gating, w_down, back = call(
        middle_kernel,
        [
            (shape(OWN, MODEL_WIDTH, dtype=F32), VMEM),
            (shape(SEQ, MODEL_WIDTH), ANY),
            (shape(4, 16, 32, 2 * HIDDEN), ANY),
            (shape(16 * PIECE, MODEL_WIDTH), ANY),
            (shape(SEQ, MODEL_WIDTH), ANY),
        ],
        [
            (merged, VMEM),
            (input_rows, VMEM),
            (gains, VMEM),
            (gating_own, ANY),
            (down_own, ANY),
            (cotangent, ANY),
        ],
        LINE_SCATTER_SCRATCH + [pltpu.VMEM((OWN, MODEL_WIDTH), BF16)],
        130,
        1,
        2**25,
    )
    w_gating = w_gating.reshape(MODEL_WIDTH, 2 * HIDDEN)

    gated = product(normed_two, w_gating)
    gate_value, up_value = gated[:, :HIDDEN], gated[:, HIDDEN:]
    gate_sigmoid = jax.nn.sigmoid(gate_value)
    silu_gate = gate_value * gate_sigmoid
    hidden = (silu_gate * up_value).astype(BF16)
    grad_hidden = contract_last(back, w_down)
    grad_gate = grad_hidden * up_value * gate_sigmoid * (1.0 + gate_value * (1.0 - gate_sigmoid))
    grad_up = grad_hidden * silu_gate
    grad_gated = jnp.concatenate([grad_gate, grad_up], axis=1).astype(BF16)
    down_out = product(hidden, w_down).astype(BF16)
    down_part = token_product(hidden, back).astype(BF16)
    gating_part = token_product(normed_two, grad_gated).astype(BF16)
    normed_two_part = contract_last(grad_gated, w_gating).astype(BF16)

    grad_middle, branch, gain_part, gating_sum, down_sum = call(
        branch_kernel,
        [
            (shape(OWN, MODEL_WIDTH, dtype=F32), VMEM),
            (shape(SEQ, MODEL_WIDTH), ANY),
            (shape(8, MODEL_WIDTH, dtype=F32), VMEM),
            (shape(4, 32, 2 * HIDDEN), VMEM),
            (shape(PIECE, MODEL_WIDTH), VMEM),
        ],
        [
            (normed_two_part, VMEM),
            (middle, VMEM),
            (own_rows(back), VMEM),
            (gains, VMEM),
            (gating_part.reshape(4, 16, 32, 2 * HIDDEN), VMEM),
            (down_part, VMEM),
        ],
        LINE_SCATTER_SCRATCH
        + ring_scatter_scratch(Rows(2 * HIDDEN))
        + ring_scatter_scratch(Flat())
        + [pltpu.VMEM((OWN, MODEL_WIDTH), BF16)],
        130,
        2,
        2**25,
    )

    merge_part = token_product(attended, branch).astype(BF16)
    grad_attended = contract_last(branch, w_merge).astype(BF16).reshape(SEQ, 4, HEAD_SIZE)
    soft = jnp.exp(scores_of() - log_total)
    grad_probs = jnp.einsum("tqd,sd->qts", grad_attended, value, preferred_element_type=F32)
    inner_sum = jnp.sum(soft * grad_probs, axis=-1, keepdims=True)
    grad_scores = (soft * (grad_probs - inner_sum)).astype(BF16)
    grad_query = (
        jnp.einsum("qts,sd->tqd", grad_scores, key, preferred_element_type=F32) * head_scale
    )
    grad_key = (
        jnp.einsum("qts,tqd->sd", grad_scores, query, preferred_element_type=F32) * head_scale
    )
    grad_value = jnp.einsum(
        "qts,tqd->sd", soft.astype(BF16), grad_attended, preferred_element_type=F32
    )
    grad_query = rotate(grad_query, cosine_rows[:, None], -sine_rows[:, None]).reshape(SEQ, 256)
    grad_key = rotate(grad_key, cosine_rows, -sine_rows)
    grad_mixed = jnp.concatenate([grad_query, grad_key, grad_value], axis=1).astype(BF16)
    heads_part = token_product(normed_one, grad_mixed).astype(BF16)
    normed_one_part = contract_last(grad_mixed, w_heads).astype(BF16)

    (
        block_output, input_grad, gains_grad,
        heads_pieces, merge_pieces, gating_pieces, down_pieces,
    ) = call(
        finish_kernel,
        [
            (shape(512, 512), ANY),
            (shape(512, 512, dtype=F32), ANY),
            (shape(8, 512, dtype=F32), VMEM),
            (shape(4, 32, HEADS_COLS), ANY),
            (shape(16, 64, 512), ANY),
            (shape(4, 32, 2 * HIDDEN), ANY),
            (shape(4, PIECE, 512), ANY),
        ],
        [
            (normed_one_part, VMEM),
            (down_out, VMEM),
            (middle, VMEM),
            (grad_middle, VMEM),
            (input_rows, VMEM),
            (gains, VMEM),
            (gain_part, VMEM),
            (heads_part.reshape(4, 16, 32, HEADS_COLS), VMEM),
            (merge_part, ANY),
            (gating_sum, ANY),
            (down_sum, ANY),
        ],
        LINE_SCATTER_SCRATCH
        + LINE_SCATTER_SCRATCH
        + ring_scatter_scratch(Rows(HEADS_COLS))
        + [
            pltpu.VMEM((4, 32, HEADS_COLS), BF16),
            pltpu.VMEM((OWN, MODEL_WIDTH), BF16),
            pltpu.VMEM((OWN, MODEL_WIDTH), F32),
            pltpu.VMEM((2, 8, MODEL_WIDTH), F32),
            pltpu.VMEM((4, 2, 8, 512), F32),
            pltpu.VMEM((32, 8, 512), F32),
        ],
        180,
        3,
        2**25,
    )
    gains_grad = gains_grad[:2]
    heads_grad = unpack_heads(heads_pieces)
    merge_grad = jnp.sum(merge_pieces.astype(F32), axis=0)
    gating_grad = unpack_gating(gating_pieces)
    down_grad = unpack_down(down_pieces)
    gains_next, gains_mean, gains_square = adamw(
        norm_gains, gains_grad, gains_first, gains_second, RATE_GAIN, 0.0
    )
    heads_next, heads_mean, heads_square = adamw(
        heads_projection_weight,
        heads_grad,
        heads_first_moment,
        heads_second_moment,
        RATE_MATRIX,
        WEIGHT_DECAY,
    )
    merge_next, merge_mean, merge_square = adamw(
        merge_weight, merge_grad, merge_first, merge_second, RATE_MERGE, WEIGHT_DECAY
    )
    gating_next, gating_mean, gating_square = adamw(
        gating_weight, gating_grad, gating_first, gating_second, RATE_MATRIX, WEIGHT_DECAY
    )
    down_next, down_mean, down_square = adamw(
        down_weight, down_grad, down_first, down_second, RATE_MATRIX, WEIGHT_DECAY
    )
    return (
        block_output,
        input_grad,
        gains_grad,
        gains_next,
        gains_mean,
        gains_square,
        heads_grad,
        heads_next,
        heads_mean,
        heads_square,
        merge_grad,
        merge_next,
        merge_mean,
        merge_square,
        gating_grad,
        gating_next,
        gating_mean,
        gating_square,
        down_grad,
        down_next,
        down_mean,
        down_square,
    )


def solution(mesh):
    in_specs = (
        P(("dp", "col"), "row"),
        P(("dp", "col"), "row"),
        P(None, "row"),
        P(None, "row"),
        P(None, "row"),
        P(("row", "dp"), "col"),
        P(("row", "dp"), "col"),
        P(("row", "dp"), "col"),
        P(("col", "dp"), "row"),
        P(("col", "dp"), "row"),
        P(("col", "dp"), "row"),
        P(("row", "dp"), None, "col"),
        P(("row", "dp"), None, "col"),
        P(("row", "dp"), None, "col"),
        P(("col", "dp"), "row"),
        P(("col", "dp"), "row"),
        P(("col", "dp"), "row"),
    )
    out_specs = (
        P(("dp", "col"), "row"),
        P(("dp", "col"), "row"),
        P(None, "row"),
        P(None, "row"),
        P(None, "row"),
        P(None, "row"),
        P(("row", "dp"), "col"),
        P(("row", "dp"), "col"),
        P(("row", "dp"), "col"),
        P(("row", "dp"), "col"),
        P(("col", "dp"), "row"),
        P(("col", "dp"), "row"),
        P(("col", "dp"), "row"),
        P(("col", "dp"), "row"),
        P(("row", "dp"), None, "col"),
        P(("row", "dp"), None, "col"),
        P(("row", "dp"), None, "col"),
        P(("row", "dp"), None, "col"),
        P(("col", "dp"), "row"),
        P(("col", "dp"), "row"),
        P(("col", "dp"), "row"),
        P(("col", "dp"), "row"),
    )
    return jax.shard_map(body, mesh=mesh, in_specs=in_specs, out_specs=out_specs, check_vma=False)
```

```python
import functools

import jax
import jax.numpy as jnp
from jax import lax
from jax.experimental import pallas as pl
from jax.experimental.pallas import tpu as pltpu
from jax.sharding import PartitionSpec as P

MODEL_WIDTH = 2048
KEY_VALUE_HEADS = 4
HEAD_SIZE = 64
QUERY_PER_GROUP = 8
STEP = 10


EPS_NORM = 1e-05
BETA_ONE = 0.9
BETA_TWO = 0.95
EPS_ADAM = 1e-08
RATE_MATRIX = 0.05
RATE_MERGE = 0.5
RATE_GAIN = 1.0
WEIGHT_DECAY = 0.1
ROPE_BASE = 10000.0
MASK_FILL = -1e30

MESH = pl.DeviceIdType.MESH
VMEM_BYTES = 60 * 2**20
BF16 = jnp.bfloat16
F32 = jnp.float32

SEQ = 1024
OWN = 128
HEADS_COLS = 384
HIDDEN = 768
PIECE = 48
PIECE_USED = 44


class Place:
    def __init__(self):
        self.dp = lax.axis_index("dp")
        self.row = lax.axis_index("row")
        self.col = lax.axis_index("col")
        self.y = lax.div(self.dp, 4)
        self.z = lax.rem(self.dp, 4)
        self.core = lax.rem(self.row, 2)
        self.x = self.col * 2 + lax.div(self.row, 2)

    def near(self, x=0, core=0, y=0, z=0):
        new_x = lax.rem(self.x + x + 4, 4)
        new_core = lax.rem(self.core + core, 2)
        new_y = lax.rem(self.y + y + 4, 4)
        new_z = lax.rem(self.z + z + 4, 4)
        return {
            "dp": new_y * 4 + new_z,
            "row": lax.rem(new_x, 2) * 2 + new_core,
            "col": lax.div(new_x, 2),
        }

    def slot(self, first_axis, first, second):
        y, z = (first, second) if first_axis == "y" else (second, first)
        return lax.rem(self.y + y + 4, 4) * 4 + lax.rem(self.z + z + 4, 4)

    def line(self, x, core):
        return lax.rem(self.x + x + 4, 4) * 2 + lax.rem(self.core + core, 2)

    def peer(self, step):
        other = lax.rem(self.row + step, 4)
        return other, {"dp": self.dp, "row": other, "col": self.col}


class Wires:
    def __init__(self, send, recv, local):
        self.send, self.recv, self.local = send, recv, local
        self.count = 0
        self.local_count = 0
        self.sent = []
        self.kept = []

    def push(self, source, target, device):
        index = self.count
        self.count += 1
        copy = pltpu.make_async_remote_copy(
            src_ref=source,
            dst_ref=target,
            send_sem=self.send.at[index],
            recv_sem=self.recv.at[index],
            device_id=device,
            device_id_type=MESH,
        )
        copy.start()
        self.sent.append(copy)
        return copy

    def keep(self, source, target):
        copy = pltpu.make_async_copy(source, target, self.local.at[self.local_count])
        self.local_count += 1
        copy.start()
        return copy

    def drain(self):
        for copy in self.sent:
            copy.wait_send()


def meet(devices, more=0):
    barrier = pltpu.get_barrier_semaphore()
    for device in devices:
        pl.semaphore_signal(barrier, inc=1, device_id=device, device_id_type=MESH)
    pl.semaphore_wait(barrier, len(devices))


def interleave(*plans):
    waiting = [[next(plan), order, plan] for order, plan in enumerate(plans)]
    while waiting:
        waiting.sort(key=lambda entry: (entry[0], entry[1]))
        entry = waiting[0]
        try:
            entry[0] = max(entry[0], next(entry[2]))
        except StopIteration:
            waiting.pop(0)


def ring_neighbours(place):
    return [place.near(y=1), place.near(y=-1), place.near(z=1), place.near(z=-1)]


def line_neighbours(place):
    return [place.near(x=1), place.near(x=-1), place.near(core=1)]


def line_gather(place, wires, own, out, block, half, start, cost):
    me = place.line(0, 0)
    yield start
    kept = wires.keep(own, block(out, me))
    right = wires.push(own, block(out, me), place.near(x=1))
    left = wires.push(own, block(out, me), place.near(x=-1))
    beside = [wires.push(own, block(out, me), place.near(core=1))]
    yield start + cost + 2
    right.wait_recv()
    came = place.line(-1, 0)
    far_right = wires.push(half(out, came, 0), half(out, came, 0), place.near(x=1))
    beside.append(wires.push(block(out, came), block(out, came), place.near(core=1)))
    left.wait_recv()
    came = place.line(1, 0)
    far_left = wires.push(half(out, came, 1), half(out, came, 1), place.near(x=-1))
    beside.append(wires.push(block(out, came), block(out, came), place.near(core=1)))
    yield start + 1.5 * cost + 4
    far_right.wait_recv()
    far_left.wait_recv()
    came = place.line(2, 0)
    beside.append(wires.push(block(out, came), block(out, came), place.near(core=1)))
    yield start + 1.5 * cost + 6
    kept.wait()
    for copy in beside:
        copy.wait_recv()


def token_block(ref, index):
    return ref.at[pl.ds(pl.multiple_of(index * OWN, OWN), OWN)]


def token_half(ref, index, side):
    return ref.at[pl.ds(pl.multiple_of(index * OWN + side * (OWN // 2), OWN // 2), OWN // 2)]


def tile_block(ref, index):
    x, core = lax.div(index, 2), lax.rem(index, 2)
    rows = pl.ds(pl.multiple_of(lax.div(x, 2) * 512, 512), 512)
    columns = pl.ds(pl.multiple_of((lax.rem(x, 2) * 2 + core) * 512, 512), 512)
    return ref.at[rows, columns]


def tile_half(ref, index, side):
    x, core = lax.div(index, 2), lax.rem(index, 2)
    rows = pl.ds(pl.multiple_of(lax.div(x, 2) * 512 + side * 256, 256), 256)
    columns = pl.ds(pl.multiple_of((lax.rem(x, 2) * 2 + core) * 512, 512), 512)
    return ref.at[rows, columns]


def add_rows(out, terms, rows, step=16):
    def chunk(index, carry):
        at = pl.ds(pl.multiple_of(index * step, step), step)
        out[at, :] = functools.reduce(
            lambda a, b: a + b, [term[at, :].astype(F32) for term in terms]
        ).astype(out.dtype)
        return carry

    lax.fori_loop(0, rows // step, chunk, 0)


LINE_SCATTER_SCRATCH = [
    pltpu.VMEM((4, OWN, MODEL_WIDTH), BF16),
    pltpu.VMEM((2, OWN // 2, MODEL_WIDTH), BF16),
    pltpu.VMEM((2, OWN, MODEL_WIDTH), BF16),
    pltpu.VMEM((3, OWN, MODEL_WIDTH), BF16),
]


def line_scatter(place, wires, part, scratch, start, cost):
    beside, halves, full, total = scratch
    yield start
    pairs = {}
    for offset in (2, 1, 3, 0):
        pairs[offset] = wires.push(
            token_block(part, place.line(offset, 1)), beside.at[offset], place.near(core=1)
        )
    yield start + 2
    pairs[2].wait_recv()
    add_rows(total.at[2], [token_block(part, place.line(2, 0)), beside.at[2]], OWN)
    far_right = wires.push(
        total.at[2, pl.ds(0, OWN // 2)], halves.at[0], place.near(x=1)
    )
    far_left = wires.push(
        total.at[2, pl.ds(OWN // 2, OWN // 2)], halves.at[1], place.near(x=-1)
    )
    yield start + 3
    pairs[1].wait_recv()
    add_rows(total.at[0], [token_block(part, place.line(1, 0)), beside.at[1]], OWN)
    right_late = wires.push(
        total.at[0, pl.ds(OWN // 2, OWN // 2)],
        full.at[0, pl.ds(OWN // 2, OWN // 2)],
        place.near(x=1),
    )
    pairs[3].wait_recv()
    add_rows(total.at[1], [token_block(part, place.line(3, 0)), beside.at[3]], OWN)
    left_late = wires.push(
        total.at[1, pl.ds(0, OWN // 2)], full.at[1, pl.ds(0, OWN // 2)], place.near(x=-1)
    )
    yield start + 5 + 0.5 * cost
    far_right.wait_recv()
    first = total.at[0, pl.ds(0, OWN // 2)]
    add_rows(first, [first, halves.at[0]], OWN // 2)
    right = wires.push(first, full.at[0, pl.ds(0, OWN // 2)], place.near(x=1))
    far_left.wait_recv()
    second = total.at[1, pl.ds(OWN // 2, OWN // 2)]
    add_rows(second, [second, halves.at[1]], OWN // 2)
    left = wires.push(second, full.at[1, pl.ds(OWN // 2, OWN // 2)], place.near(x=-1))
    yield start + 6 + 1.5 * cost
    pairs[0].wait_recv()
    right_late.wait_recv()
    left_late.wait_recv()
    right.wait_recv()
    left.wait_recv()


def scatter_terms(place, part, scratch):
    beside, halves, full, total = scratch
    return [token_block(part, place.line(0, 0)), beside.at[0], full.at[0], full.at[1]]


class Rows:
    def __init__(self, columns):
        self.item_shape = (2, 32, columns)
        self.half_shape = (1, 32, columns)

    def item(self, ref, side, slot):
        return ref.at[pl.ds(2 * side, 2), slot]

    def half(self, ref, side, part, slot):
        return ref.at[pl.ds(2 * side + part, 1), slot]

    def cut(self, item, part):
        return item.at[pl.ds(part, 1)]


class Flat:
    def __init__(self):
        self.item_shape = (PIECE, MODEL_WIDTH // 2)
        self.half_shape = (PIECE, MODEL_WIDTH // 4)

    def item(self, ref, side, slot):
        rows = pl.ds(pl.multiple_of(slot * PIECE, PIECE), PIECE)
        return ref.at[rows, pl.ds(side * (MODEL_WIDTH // 2), MODEL_WIDTH // 2)]

    def half(self, ref, side, part, slot):
        rows = pl.ds(pl.multiple_of(slot * PIECE, PIECE), PIECE)
        return ref.at[rows, pl.ds((2 * side + part) * (MODEL_WIDTH // 4), MODEL_WIDTH // 4)]

    def cut(self, item, part):
        return item.at[:, pl.ds(part * (MODEL_WIDTH // 4), MODEL_WIDTH // 4)]


def ring_move(place, axis, step):
    return place.near(y=step) if axis == "y" else place.near(z=step)


def ring_gather(place, wires, kind, out, side, start, cost):
    first, second = ("z", "y") if side == 0 else ("y", "z")
    slot = functools.partial(place.slot, first)
    spread = {}

    def send_on(offset):
        item = kind.item(out, side, slot(offset, 0))
        spread[offset] = [
            wires.push(item, item, ring_move(place, second, step)) for step in (1, -1)
        ]

    def pass_on(offset):
        right, left = spread[offset]
        right.wait_recv()
        piece = kind.half(out, side, 0, slot(offset, -1))
        one = wires.push(piece, piece, ring_move(place, second, 1))
        left.wait_recv()
        piece = kind.half(out, side, 1, slot(offset, 1))
        return [one, wires.push(piece, piece, ring_move(place, second, -1))]

    yield start
    own = kind.item(out, side, slot(0, 0))
    right = wires.push(own, own, ring_move(place, first, 1))
    left = wires.push(own, own, ring_move(place, first, -1))
    send_on(0)
    yield start + cost + 2
    right.wait_recv()
    piece = kind.half(out, side, 0, slot(-1, 0))
    far_right = wires.push(piece, piece, ring_move(place, first, 1))
    send_on(-1)
    left.wait_recv()
    piece = kind.half(out, side, 1, slot(1, 0))
    far_left = wires.push(piece, piece, ring_move(place, first, -1))
    send_on(1)
    last = []
    yield start + 2 * cost + 4
    last += pass_on(0)
    yield start + 2.5 * cost + 4
    far_right.wait_recv()
    far_left.wait_recv()
    send_on(2)
    yield start + 4 * cost + 4
    last += pass_on(-1)
    yield start + 5.5 * cost + 4
    last += pass_on(1)
    yield start + 6.5 * cost + 4
    last += pass_on(2)
    yield start + 7.5 * cost + 6
    for copy in last:
        copy.wait_recv()


def ring_scatter_scratch(kind):
    def stack(count, shape):
        return pltpu.VMEM((count, *shape), BF16)

    one_side = [
        stack(8, kind.half_shape),
        stack(8, kind.item_shape),
        stack(8, kind.item_shape),
        stack(4, kind.item_shape),
        stack(2, kind.half_shape),
        stack(2, kind.item_shape),
        stack(2, kind.item_shape),
    ]
    return one_side + one_side


def add_item(out, terms):
    out[...] = functools.reduce(lambda a, b: a + b, [t[...].astype(F32) for t in terms]).astype(
        out.dtype
    )


def ring_scatter(place, wires, kind, part, side, scratch, result, start, cost):
    far, sums, came, column, far_last, sums_last, came_last = scratch[7 * side : 7 * side + 7]
    first, second = ("z", "y") if side == 0 else ("y", "z")
    slot = functools.partial(place.slot, first)
    order = (2, 1, -1, 0)
    yield start
    right, left = {}, {}
    for n, offset in enumerate(order):
        target = slot(offset, 2)
        right[offset] = wires.push(
            kind.half(part, side, 0, target), far.at[2 * n], ring_move(place, second, 1)
        )
        left[offset] = wires.push(
            kind.half(part, side, 1, target), far.at[2 * n + 1], ring_move(place, second, -1)
        )

    def add_far(source, halves, out, way):
        keep = 1 - way
        add_item(kind.cut(out, way), [kind.cut(source, way), halves])
        held = kind.cut(out, keep)
        held[...] = kind.cut(source, keep)[...]

    moved = {}
    for n, offset in enumerate(order):
        yield start + 2.5 + (0.5 + n) * cost
        right[offset].wait_recv()
        add_far(kind.item(part, side, slot(offset, 1)), far.at[2 * n], sums.at[2 * n], 0)
        one = wires.push(sums.at[2 * n], came.at[2 * n], ring_move(place, second, 1))
        left[offset].wait_recv()
        add_far(kind.item(part, side, slot(offset, -1)), far.at[2 * n + 1], sums.at[2 * n + 1], 1)
        two = wires.push(sums.at[2 * n + 1], came.at[2 * n + 1], ring_move(place, second, -1))
        moved[offset] = (one, two)

    def finish(n, offset):
        for copy in moved[offset]:
            copy.wait_recv()
        add_item(
            column.at[n],
            [kind.item(part, side, slot(offset, 0)), came.at[2 * n], came.at[2 * n + 1]],
        )

    yield start + 4 + 3 * cost
    finish(0, 2)
    far_right = wires.push(kind.cut(column.at[0], 0), far_last.at[0], ring_move(place, first, 1))
    far_left = wires.push(kind.cut(column.at[0], 1), far_last.at[1], ring_move(place, first, -1))
    yield start + 4 + 4 * cost
    finish(1, 1)
    yield start + 4 + 5 * cost
    finish(2, -1)
    far_right.wait_recv()
    add_far(column.at[1], far_last.at[0], sums_last.at[0], 0)
    one = wires.push(sums_last.at[0], came_last.at[0], ring_move(place, first, 1))
    far_left.wait_recv()
    add_far(column.at[2], far_last.at[1], sums_last.at[1], 1)
    two = wires.push(sums_last.at[1], came_last.at[1], ring_move(place, first, -1))
    yield start + 5 + 6 * cost
    finish(3, 0)
    yield start + 8 + 7.5 * cost
    one.wait_recv()
    two.wait_recv()
    add_item(result, [column.at[3], came_last.at[0], came_last.at[1]])


def call(kernel, outs, ins, scratch, wires, name, cost):
    return pl.pallas_call(
        kernel,
        out_shape=[shape for shape, _ in outs],
        in_specs=[pl.BlockSpec(memory_space=space) for _, space in ins],
        out_specs=[pl.BlockSpec(memory_space=space) for _, space in outs],
        scratch_shapes=list(scratch)
        + [
            pltpu.SemaphoreType.DMA((wires,)),
            pltpu.SemaphoreType.DMA((wires,)),
            pltpu.SemaphoreType.DMA((16,)),
        ],
        compiler_params=pltpu.CompilerParams(
            collective_id=name, has_side_effects=True, vmem_limit_bytes=VMEM_BYTES
        ),
        cost_estimate=pl.CostEstimate(flops=0, bytes_accessed=cost, transcendentals=0),
    )(*[array for array, _ in ins])


def shape(*extent, dtype=BF16):
    return jax.ShapeDtypeStruct(extent, dtype)


def merge_devices(place):
    users = [{"dp": j * 4 + place.z, "row": place.y, "col": place.col} for j in range(4)]
    homes = [
        {"dp": place.row * 4 + place.z, "row": jnp.int32(row), "col": place.col} for row in range(4)
    ]
    return users, homes


def signal_others(place, devices):
    barrier = pltpu.get_barrier_semaphore()
    for device in devices:
        alone = (device["dp"] == place.dp) & (device["row"] == place.row)

        @pl.when(jnp.logical_not(alone))
        def _():
            pl.semaphore_signal(barrier, inc=1, device_id=device, device_id_type=MESH)


def merge_exchange(place, wires, devices, source, target, mine):
    base = wires.count
    wires.count += 4
    copies = []
    for index, device in enumerate(devices):
        copy = pltpu.make_async_remote_copy(
            src_ref=source(index),
            dst_ref=target(index),
            send_sem=wires.send.at[base + index],
            recv_sem=wires.recv.at[base + mine],
            device_id=device,
            device_id_type=MESH,
        )
        here = pltpu.make_async_copy(source(index), target(index), wires.recv.at[base + mine])
        alone = (device["dp"] == place.dp) & (device["row"] == place.row)
        copies.append((copy, alone))
        pl.when(alone)(here.start)
        pl.when(jnp.logical_not(alone))(copy.start)

    def wait():
        for index in range(4):
            pltpu.make_async_copy(source(0), target(0), wires.recv.at[base + index]).wait()
        for copy, alone in copies:
            pl.when(jnp.logical_not(alone))(copy.wait_send)

    return wait


def nested(plans):
    pending = [[next(plan), order, plan] for order, plan in enumerate(plans)]
    while pending:
        pending.sort(key=lambda entry: entry[:2])
        entry = pending[0]
        yield entry[0]
        try:
            entry[0] = max(entry[0], next(entry[2]))
        except StopIteration:
            pending.pop(0)


def column_block(ref, row):
    return ref.at[:, pl.ds(pl.multiple_of(row * 512, 512), 512)]


def down_slot(ref, slot, row):
    rows = pl.ds(pl.multiple_of(slot * PIECE, PIECE), PIECE)
    return ref.at[rows, pl.ds(pl.multiple_of(row * 512, 512), 512)]


def start_kernel(
    heads_weight, merge_weight, gating_weight, down_weight, input_own, back_own, gains_own,
    heads, gating, down, inputs, back, gains,
    heads_cut, merge_cut, gating_cut, down_cut, send, recv, local,
):
    place = Place()
    wires = Wires(send, recv, local)
    users, homes = merge_devices(place)
    peers = [place.peer(step) for step in (1, 2, 3)]
    same = place.row == place.y
    devices = ring_neighbours(place) + line_neighbours(place) + [p for _, p in peers]
    signal_others(place, devices + homes)
    pl.semaphore_wait(
        pltpu.get_barrier_semaphore(), len(devices) + 4 - same.astype(jnp.int32)
    )

    def exchange():
        yield 0.2
        for row in range(4):
            group, half = divmod(row, 2)
            query = heads_weight[:, pl.ds(group * 640 + half * 256, 256)]
            heads_cut[row, :, pl.ds(0, 256)] = query.astype(BF16)
            pair = heads_weight[:, pl.ds(group * 640 + 512, 128)]
            heads_cut[row, :, pl.ds(256, 128)] = pair.astype(BF16)
            for side in range(2):
                piece = merge_weight[pl.ds(16 * row, 16), pl.ds(256 * side, 256)]
                merge_cut[row, pl.ds(16 * side, 16)] = piece.astype(BF16)

        def heads_columns(row, slot):
            return heads.at[row, slot, :, pl.ds(0, HEADS_COLS)]

        moved = [
            wires.push(heads_cut.at[other], heads_columns(place.row, place.dp), device)
            for other, device in peers
        ]
        kept = [wires.keep(heads_cut.at[place.row], heads_columns(place.row, place.dp))]
        merge_wait = merge_exchange(
            place, wires, users,
            lambda j: merge_cut.at[j],
            lambda j: heads.at[place.row, j * 4 + place.z, :, pl.ds(HEADS_COLS, 256)],
            place.row,
        )
        for other, device in peers:
            moved.append(wires.push(gains_own, gains.at[place.row], device))
        kept.append(wires.keep(gains_own, gains.at[place.row]))
        for row in range(4):
            piece = down_weight[pl.ds(PIECE_USED * row, PIECE_USED), :]
            down_cut[row] = jnp.concatenate(
                [piece, jnp.zeros((PIECE - PIECE_USED, 512), F32)], axis=0
            ).astype(BF16)
        later = [
            wires.push(down_cut.at[other], down_slot(down, place.dp, place.row), device)
            for other, device in peers
        ]
        kept.append(wires.keep(down_cut.at[place.row], down_slot(down, place.dp, place.row)))
        yield 5.0
        for copy in kept:
            copy.wait()
        for copy in moved:
            copy.wait_recv()
        merge_wait()
        plans = [
            ring_gather(place, wires, Rows(HEADS_COLS + 256), heads, side, 5.0, 1.8)
            for side in (0, 1)
        ]
        for copy in later:
            copy.wait_recv()
        plans += [ring_gather(place, wires, Flat(), down, side, 7.0, 4.0) for side in (0, 1)]
        yield from nested(plans)

    def gating_exchange():
        yield 5.5
        zeros = jnp.zeros((32, PIECE - PIECE_USED), F32)
        for kind in range(2):
            for row in range(4):
                pieces = []
                for slot in range(16):
                    first = slot * 4 * PIECE_USED + row * PIECE_USED
                    pieces += [gating_weight[:, kind, pl.ds(first, PIECE_USED)], zeros]
                gating_cut[row, :, pl.ds(kind * HIDDEN, HIDDEN)] = jnp.concatenate(
                    pieces, axis=1
                ).astype(BF16)
        kept = wires.keep(gating_cut.at[place.row], gating.at[place.row])
        moved = [
            wires.push(gating_cut.at[other], gating.at[place.row], device)
            for other, device in peers
        ]
        yield 40.0
        kept.wait()
        for copy in moved:
            copy.wait_recv()

    interleave(
        line_gather(place, wires, input_own, inputs, tile_block, tile_half, 0.1, 11.4),
        exchange(),
        gating_exchange(),
        line_gather(place, wires, back_own, back, tile_block, tile_half, 6.0, 22.0),
    )
    wires.drain()


def middle_kernel(
    part, input_rows, gains, gating_own,
    middle, normed, gating,
    *scratch,
):
    line_scratch, (normed_own, send, recv, local) = scratch[:4], scratch[4:]
    place = Place()
    wires = Wires(send, recv, local)
    meet(ring_neighbours(place) + line_neighbours(place))

    def main():
        yield from line_scatter(place, wires, part, line_scratch, 0.0, 11.4)
        terms = scatter_terms(place, part, line_scratch)

        def chunk(index, carry):
            at = pl.ds(pl.multiple_of(index * 16, 16), 16)
            total = functools.reduce(lambda a, b: a + b, [t[at, :].astype(F32) for t in terms])
            total = total + input_rows[at, :].astype(F32)
            middle[at, :] = total
            scale = lax.rsqrt(
                jnp.sum(total * total, axis=1, keepdims=True) / MODEL_WIDTH + EPS_NORM
            )
            normed_own[at, :] = (total * scale * gains[1:2, :]).astype(BF16)
            return carry

        lax.fori_loop(0, OWN // 16, chunk, 0)
        yield from line_gather(
            place, wires, normed_own, normed, token_block, token_half, 25.0, 11.4
        )

    def weights():
        yield 0.3
        kept = [
            wires.keep(gating_own.at[r], gating.at[r, place.dp]) for r in range(4)
        ]
        for copy in kept:
            copy.wait()
        yield from nested(
            ring_gather(place, wires, Rows(2 * HIDDEN), gating, side, 0.5, 4.3) for side in (0, 1)
        )

    interleave(main(), weights())
    wires.drain()


def branch_kernel(
    part, middle, back_rows, gains, gating_part,
    grad_middle, branch, gain_part, gating_sum,
    *scratch,
):
    line_scratch, scratch = scratch[:4], scratch[4:]
    gating_scratch, scratch = scratch[:14], scratch[14:]
    branch_own, send, recv, local = scratch
    place = Place()
    wires = Wires(send, recv, local)
    meet(ring_neighbours(place) + line_neighbours(place))

    def main():
        yield from line_scatter(place, wires, part, line_scratch, 0.0, 11.4)
        terms = scatter_terms(place, part, line_scratch)
        gain_part[...] = jnp.zeros_like(gain_part)

        def chunk(index, carry):
            at = pl.ds(pl.multiple_of(index * 16, 16), 16)
            grad = functools.reduce(lambda a, b: a + b, [t[at, :].astype(F32) for t in terms])
            through, gain = norm_back(middle[at, :], gains[1:2, :], grad)
            total = back_rows[at, :].astype(F32) + through
            grad_middle[at, :] = total
            branch_own[at, :] = total.astype(BF16)
            gain_part[...] += gain.reshape(2, 8, MODEL_WIDTH).sum(axis=0)
            return carry

        lax.fori_loop(0, OWN // 16, chunk, 0)
        yield from line_gather(
            place, wires, branch_own, branch, token_block, token_half, 25.0, 11.4
        )

    rows = Rows(2 * HIDDEN)
    interleave(
        main(),
        *[
            ring_scatter(
                place, wires, rows, gating_part, side, gating_scratch,
                gating_sum.at[pl.ds(2 * side, 2)], 0.5, 4.3,
            )
            for side in (0, 1)
        ],
    )
    wires.drain()


def norm_back(values, gain_row, gradient):
    scale = lax.rsqrt(jnp.sum(values * values, axis=1, keepdims=True) / MODEL_WIDTH + EPS_NORM)
    weighted = gain_row * gradient
    inner = jnp.sum(weighted * values, axis=1, keepdims=True)
    through = scale * weighted - values * (scale * scale * scale * inner / MODEL_WIDTH)
    return through, gradient * values * scale


def finish_kernel(
    part, down_out, middle, grad_middle, input_rows, gains, gain_part,
    heads_part, merge_part, gating_sum, down_part,
    output, input_grad, gains_grad, heads_pieces, merge_pieces, gating_pieces, down_pieces,
    *scratch,
):
    line_scratch, scratch = scratch[:4], scratch[4:]
    out_scratch, scratch = scratch[:4], scratch[4:]
    heads_scratch, scratch = scratch[:14], scratch[14:]
    down_scratch, scratch = scratch[:14], scratch[14:]
    (
        heads_all, heads_sum, down_sum, output_own, input_grad_own, gain_rows, gain_came, gain_all,
        send, recv, local,
    ) = scratch
    place = Place()
    wires = Wires(send, recv, local)
    users, homes = merge_devices(place)
    peers = [place.peer(step) for step in (1, 2, 3)]
    same = place.row == place.y
    barrier = pltpu.get_barrier_semaphore()
    devices = ring_neighbours(place) + line_neighbours(place) + [p for _, p in peers]
    signal_others(place, devices + users)

    def far(step):
        index = lax.rem(place.col * 16 + place.dp + step, 32)
        return {"dp": lax.rem(index, 16), "row": place.row, "col": lax.div(index, 16)}

    def greet(step, carry):
        pl.semaphore_signal(barrier, inc=1, device_id=far(step), device_id_type=MESH)
        return carry

    lax.fori_loop(1, 32, greet, 0)
    pl.semaphore_wait(barrier, len(devices) + 31 + 4 - same.astype(jnp.int32))

    def own_rows(ref, row):
        return ref.at[pl.ds(pl.multiple_of(row * OWN, OWN), OWN)]

    def recut(own, out, when):
        kept = wires.keep(column_block(own, place.row), own_rows(out, place.row))
        moved = [
            wires.push(column_block(own, other), own_rows(out, place.row), device)
            for other, device in peers
        ]
        yield when
        kept.wait()
        for copy in moved:
            copy.wait_recv()

    def gradient():
        yield from line_scatter(place, wires, part, line_scratch, 0.0, 11.4)
        terms = scatter_terms(place, part, line_scratch)
        gain_rows[0] = jnp.zeros((8, MODEL_WIDTH), F32)
        gain_rows[1] = gain_part[...]

        def chunk(index, carry):
            at = pl.ds(pl.multiple_of(index * 16, 16), 16)
            grad = functools.reduce(lambda a, b: a + b, [t[at, :].astype(F32) for t in terms])
            through, gain = norm_back(input_rows[at, :].astype(F32), gains[0:1, :], grad)
            input_grad_own[at, :] = grad_middle[at, :] + through
            gain_rows[0] += gain.reshape(2, 8, MODEL_WIDTH).sum(axis=0)
            return carry

        lax.fori_loop(0, OWN // 16, chunk, 0)
        moved = []
        for other, device in peers:
            piece = gain_rows.at[:, :, pl.ds(pl.multiple_of(other * 512, 512), 512)]
            moved.append(wires.push(piece, gain_came.at[place.row], device))
        piece = gain_rows.at[:, :, pl.ds(pl.multiple_of(place.row * 512, 512), 512)]
        kept = wires.keep(piece, gain_came.at[place.row])
        waits = recut(input_grad_own, input_grad, 38.0)
        next(waits)
        yield 28.0
        kept.wait()
        for copy in moved:
            copy.wait_recv()
        local_sum = gain_came[0] + gain_came[1] + gain_came[2] + gain_came[3]
        me = place.col * 16 + place.dp
        gain_all[me] = jnp.concatenate(
            [jnp.sum(local_sum, axis=1), jnp.zeros((6, 512), F32)], axis=0
        )
        base = wires.count
        wires.count += 32

        def gain_copy(step):
            return pltpu.make_async_remote_copy(
                src_ref=gain_all.at[me],
                dst_ref=gain_all.at[me],
                send_sem=wires.send.at[base + step],
                recv_sem=wires.recv.at[base + step],
                device_id=far(step),
                device_id_type=MESH,
            )

        def start(step, carry):
            gain_copy(step).start()
            return carry

        def finish(step, carry):
            gain_copy(step).wait()
            return carry

        lax.fori_loop(1, 32, start, 0)
        yield 36.0
        lax.fori_loop(1, 32, finish, 0)
        gains_grad[...] = functools.reduce(lambda a, b: a + b, [gain_all[i] for i in range(32)])
        yield 38.0
        for _ in waits:
            pass

    def outputs():
        yield from line_scatter(place, wires, down_out, out_scratch, 0.3, 22.0)
        terms = scatter_terms(place, down_out, out_scratch)

        def chunk(index, carry):
            at = pl.ds(pl.multiple_of(index * 16, 16), 16)
            total = functools.reduce(lambda a, b: a + b, [t[at, :].astype(F32) for t in terms])
            output_own[at, :] = (total + middle[at, :]).astype(BF16)
            return carry

        lax.fori_loop(0, OWN // 16, chunk, 0)
        yield from recut(output_own, output, 45.0)

    def back_pieces(part_of, out, when):
        kept = wires.keep(part_of(place.row), out.at[place.row])
        moved = [
            wires.push(part_of(other), out.at[place.row], device) for other, device in peers
        ]
        yield when
        kept.wait()
        for copy in moved:
            copy.wait_recv()

    def weights():
        yield 0.1
        for row in range(4):
            for slot in range(16):
                rows = pl.ds((row * 16 + slot) * 32, 32)
                heads_all[row, slot, :, pl.ds(0, HEADS_COLS)] = heads_part[rows, :]
                y, z = divmod(slot, 4)
                for half in range(2):
                    piece = merge_part[
                        pl.ds(z * 64 + y * 16, 16), pl.ds(row * 512 + half * 256, 256)
                    ]
                    heads_all[row, slot, pl.ds(16 * half, 16), pl.ds(HEADS_COLS, 256)] = piece
        plans = [
            ring_scatter(
                place, wires, Rows(HEADS_COLS + 256), heads_all, side, heads_scratch,
                heads_sum.at[pl.ds(2 * side, 2)], 0.2, 1.8,
            )
            for side in (0, 1)
        ] + [
            ring_scatter(
                place, wires, Flat(), down_part, side, down_scratch,
                down_sum.at[:, pl.ds(side * 1024, 1024)], 0.3, 4.0,
            )
            for side in (0, 1)
        ]
        yield from nested(plans)
        merge_wait = merge_exchange(
            place, wires, homes,
            lambda row: heads_sum.at[row, :, pl.ds(HEADS_COLS, 256)],
            lambda row: merge_pieces.at[place.y],
            place.y,
        )
        heads_back = back_pieces(
            lambda row: heads_sum.at[row, :, pl.ds(0, HEADS_COLS)], heads_pieces, 50.0
        )
        next(heads_back)
        down_back = back_pieces(lambda row: column_block(down_sum, row), down_pieces, 50.0)
        next(down_back)
        yield 50.0
        for _ in heads_back:
            pass
        for _ in down_back:
            pass
        merge_wait()

    def gating():
        yield 0.4
        yield from back_pieces(lambda row: gating_sum.at[row], gating_pieces, 41.0)

    interleave(gradient(), outputs(), weights(), gating())
    wires.drain()


def turn(tile, cosine, sine):
    lane = lax.broadcasted_iota(jnp.int32, tile.shape, 1)
    first = lax.rem(lane, HEAD_SIZE) < HEAD_SIZE // 2
    swapped = jnp.where(first, pltpu.roll(tile, 96, axis=1), pltpu.roll(tile, 32, axis=1))
    return tile * cosine + swapped * sine


def keys_only(cosine, sine):
    key = lax.broadcasted_iota(jnp.int32, cosine.shape, 1) < HEAD_SIZE
    return jnp.where(key, cosine, 1.0), jnp.where(key, sine, 0.0)


def heads_weight_of(heads):
    return heads[:, :, :, pl.ds(0, HEADS_COLS)].reshape(MODEL_WIDTH, HEADS_COLS)


QUERY_BLOCK = 256


def forward_kernel(
    inputs, gains, heads, cosine, sine,
    normed, query, pair, sums, attended, merge, part,
):
    for row in range(4):
        for slot in range(16):
            y, z = divmod(slot, 4)
            for half in range(2):
                merge[pl.ds(z * 64 + y * 16, 16), pl.ds(row * 512 + half * 256, 256)] = heads[
                    row, slot, pl.ds(16 * half, 16), pl.ds(HEADS_COLS, 256)
                ]

    def project(index, carry):
        at = pl.ds(pl.multiple_of(index * 128, 128), 128)
        wide = inputs[at, :].astype(F32)
        scale = lax.rsqrt(jnp.sum(wide * wide, axis=1, keepdims=True) / MODEL_WIDTH + EPS_NORM)
        low = (wide * scale * gains[0:1, :]).astype(BF16)
        normed[at, :] = low
        mixed = product(low, heads_weight_of(heads))
        cos, sin = cosine[at, :], sine[at, :]
        query[at, pl.ds(0, 128)] = turn(mixed[:, :128], cos, sin).astype(BF16)
        query[at, pl.ds(128, 128)] = turn(mixed[:, 128:256], cos, sin).astype(BF16)
        pair[at, :] = turn(mixed[:, 256:], *keys_only(cos, sin)).astype(BF16)
        return carry

    lax.fori_loop(0, SEQ // 128, project, 0)
    scale = HEAD_SIZE ** (-0.5)
    rows_at = lax.broadcasted_iota(jnp.int32, (QUERY_BLOCK, QUERY_BLOCK), 0)
    keys_at = lax.broadcasted_iota(jnp.int32, (QUERY_BLOCK, QUERY_BLOCK), 1)
    for block in range(SEQ // QUERY_BLOCK):
        at = pl.ds(block * QUERY_BLOCK, QUERY_BLOCK)
        before = block * QUERY_BLOCK
        out = []
        for head in range(4):
            rows = query[at, pl.ds(head * HEAD_SIZE, HEAD_SIZE)]
            scores = [
                jnp.where(
                    rows_at >= keys_at,
                    contract_last(rows, pair[at, pl.ds(0, HEAD_SIZE)]) * scale,
                    MASK_FILL,
                )
            ]
            if before:
                scores.append(
                    contract_last(rows, pair[pl.ds(0, before), pl.ds(0, HEAD_SIZE)]) * scale
                )
            top = functools.reduce(
                jnp.maximum, [jnp.max(part_, axis=1, keepdims=True) for part_ in scores]
            )
            powers = [jnp.exp(part_ - top) for part_ in scores]
            total = functools.reduce(
                lambda a, b: a + b, [jnp.sum(part_, axis=1, keepdims=True) for part_ in powers]
            )
            low = [(part_ * (1.0 / total)).astype(BF16) for part_ in powers]
            result = product(low[0], pair[at, pl.ds(HEAD_SIZE, HEAD_SIZE)])
            if before:
                result += product(low[1], pair[pl.ds(0, before), pl.ds(HEAD_SIZE, HEAD_SIZE)])
            sums[at, pl.ds(head, 1)] = top + jnp.log(total)
            out.append(result.astype(BF16))
        attended[at, :] = jnp.concatenate(out, axis=1)

    def merge_rows(index, carry):
        at = pl.ds(pl.multiple_of(index * 128, 128), 128)
        part[at, :] = product(attended[at, :], merge[...]).astype(BF16)
        return carry

    lax.fori_loop(0, SEQ // 128, merge_rows, 0)


def backward_kernel(
    branch, merge, heads, query, pair, sums, cosine, sine,
    grad_mixed, part,
    grad_attended, grad_key, grad_value, key_columns,
):
    def attended_rows(index, carry):
        at = pl.ds(pl.multiple_of(index * 128, 128), 128)
        grad_attended[at, :] = contract_last(branch[at, :], merge[...]).astype(BF16)
        return carry

    lax.fori_loop(0, SEQ // 128, attended_rows, 0)
    key_columns[...] = jnp.transpose(pair[...].astype(F32))[:HEAD_SIZE].astype(BF16)
    grad_key[...] = jnp.zeros_like(grad_key)
    grad_value[...] = jnp.zeros_like(grad_value)
    scale = HEAD_SIZE ** (-0.5)
    keys_at = lax.broadcasted_iota(jnp.int32, (QUERY_BLOCK, QUERY_BLOCK), 0)
    rows_at = lax.broadcasted_iota(jnp.int32, (QUERY_BLOCK, QUERY_BLOCK), 1)
    for block in range(SEQ // QUERY_BLOCK):
        at = pl.ds(block * QUERY_BLOCK, QUERY_BLOCK)
        before = block * QUERY_BLOCK
        for two in range(2):
            turned = []
            for head in (2 * two, 2 * two + 1):
                columns = pl.ds(head * HEAD_SIZE, HEAD_SIZE)
                rows, back = query[at, columns], grad_attended[at, columns]
                log_total = sums[pl.ds(head, 1), at]
                spans = [at] + ([pl.ds(0, before)] if before else [])
                softs, grads = [], []
                for span in spans:
                    scores = contract_last(pair[span, pl.ds(0, HEAD_SIZE)], rows) * scale
                    soft = jnp.exp(scores - log_total)
                    if span is at:
                        soft = jnp.where(rows_at >= keys_at, soft, 0.0)
                    softs.append(soft)
                    grads.append(contract_last(pair[span, pl.ds(HEAD_SIZE, HEAD_SIZE)], back))
                inner = functools.reduce(
                    lambda a, b: a + b,
                    [jnp.sum(s * g, axis=0, keepdims=True) for s, g in zip(softs, grads)],
                )
                result = 0.0
                for span, soft, grad in zip(spans, softs, grads):
                    low = (soft * (grad - inner)).astype(BF16)
                    grad_key[span, :] += product(low, rows)
                    grad_value[span, :] += product(soft.astype(BF16), back)
                    result += product(key_columns[:, span], low)
                turned.append(result)
            tile = jnp.transpose(jnp.concatenate(turned, axis=0)) * scale
            grad_mixed[at, pl.ds(two * 128, 128)] = turn(
                tile, cosine[at, :], -sine[at, :]
            ).astype(BF16)

    def finish_rows(index, carry):
        at = pl.ds(pl.multiple_of(index * 128, 128), 128)
        cos, sin = keys_only(cosine[at, :], sine[at, :])
        tile = jnp.concatenate([grad_key[at, :] * scale, grad_value[at, :]], axis=1)
        grad_mixed[at, pl.ds(256, 128)] = turn(tile, cos, -sin).astype(BF16)
        part[at, :] = contract_last(grad_mixed[at, :], heads_weight_of(heads)).astype(BF16)
        return carry

    lax.fori_loop(0, SEQ // 128, finish_rows, 0)


def local_call(kernel, outs, ins, scratch, flops):
    return pl.pallas_call(
        kernel,
        out_shape=outs,
        in_specs=[pl.BlockSpec(memory_space=pltpu.VMEM)] * len(ins),
        out_specs=[pl.BlockSpec(memory_space=pltpu.VMEM)] * len(outs),
        scratch_shapes=scratch,
        compiler_params=pltpu.CompilerParams(vmem_limit_bytes=VMEM_BYTES),
        cost_estimate=pl.CostEstimate(flops=flops, bytes_accessed=2**24, transcendentals=2**22),
    )(*ins)


def rope_tables():
    half_width = HEAD_SIZE // 2
    frequency = ROPE_BASE ** (-jnp.arange(half_width, dtype=F32) * 2.0 / HEAD_SIZE)
    angles = jnp.arange(SEQ, dtype=F32)[:, None] * frequency[None, :]
    cosine, sine = jnp.cos(angles), jnp.sin(angles)
    return jnp.tile(cosine, (1, 4)), jnp.concatenate([-sine, sine, -sine, sine], axis=1)


def product(left, right):
    return jnp.dot(left, right, preferred_element_type=F32)


def contract_last(left, right):
    return lax.dot_general(left, right, (((1,), (1,)), ((), ())), preferred_element_type=F32)


def token_product(left, right):
    return lax.dot_general(left, right, (((0,), (0,)), ((), ())), preferred_element_type=F32)


def adamw(current, gradient, first, second, step_rate, decay_rate):
    mean_new = BETA_ONE * first + (1.0 - BETA_ONE) * gradient
    square_new = BETA_TWO * second + (1.0 - BETA_TWO) * gradient * gradient
    mean_hat = mean_new / (1.0 - BETA_ONE**STEP)
    square_hat = square_new / (1.0 - BETA_TWO**STEP)
    updated = current - step_rate * (
        mean_hat / (jnp.sqrt(square_hat) + EPS_ADAM) + decay_rate * current
    )
    return (updated, mean_new, square_new)


def unpack_heads(pieces):
    pieces = pieces.astype(F32).reshape(2, 2, 32, HEADS_COLS)
    query = pieces[..., :256].transpose(2, 0, 1, 3).reshape(32, 2, 512)
    pair = (pieces[:, 0, :, 256:] + pieces[:, 1, :, 256:]).transpose(1, 0, 2)
    return jnp.concatenate([query, pair], axis=2).reshape(32, 1280)


def unpack_gating(pieces):
    cut = pieces.reshape(4, 32, 2, 16, PIECE)[..., :PIECE_USED]
    return cut.transpose(1, 2, 3, 0, 4).reshape(32, 2, 2816).astype(F32)


def unpack_merge(pieces):
    return pieces.reshape(4, 2, 16, 256).transpose(0, 2, 1, 3).reshape(64, 512).astype(F32)


def unpack_down(pieces):
    return pieces[:, :PIECE_USED].reshape(4 * PIECE_USED, 512).astype(F32)


def body(
    block_input,
    cotangent,
    norm_gains,
    gains_first,
    gains_second,
    heads_projection_weight,
    heads_first_moment,
    heads_second_moment,
    merge_weight,
    merge_first,
    merge_second,
    gating_weight,
    gating_first,
    gating_second,
    down_weight,
    down_first,
    down_second,
):
    ANY, VMEM = pl.ANY, pltpu.VMEM
    row, col = lax.axis_index("row"), lax.axis_index("col")
    line = col * 4 + row

    def own_rows(values):
        return lax.dynamic_slice_in_dim(values, line * OWN, OWN, axis=0)

    w_heads, gating_own, w_down, inputs, back, gains = call(
        start_kernel,
        [
            (shape(4, 16, 32, HEADS_COLS + 256), VMEM),
            (shape(4, 32, 2 * HIDDEN), VMEM),
            (shape(16 * PIECE, MODEL_WIDTH), VMEM),
            (shape(SEQ, MODEL_WIDTH), VMEM),
            (shape(SEQ, MODEL_WIDTH), VMEM),
            (shape(4, 8, 128, dtype=F32), VMEM),
        ],
        [
            (heads_projection_weight, VMEM),
            (merge_weight, VMEM),
            (gating_weight, VMEM),
            (down_weight, VMEM),
            (block_input, VMEM),
            (cotangent, VMEM),
            (norm_gains.reshape(8, 128), VMEM),
        ],
        [
            pltpu.VMEM((4, 32, HEADS_COLS), BF16),
            pltpu.VMEM((4, 32, 256), BF16),
            pltpu.VMEM((4, 32, 2 * HIDDEN), BF16),
            pltpu.VMEM((4, PIECE, 512), BF16),
        ],
        140,
        0,
        2**24,
    )
    gains = gains.reshape(4, 2, 512).transpose(1, 0, 2).reshape(2, MODEL_WIDTH)
    input_rows = own_rows(inputs)
    cosine, sine = rope_tables()
    normed_one, query, pair, sums, attended, w_merge, merged = local_call(
        forward_kernel,
        [
            shape(SEQ, MODEL_WIDTH),
            shape(SEQ, 256),
            shape(SEQ, 128),
            shape(SEQ, 128, dtype=F32),
            shape(SEQ, 256),
            shape(256, MODEL_WIDTH),
            shape(SEQ, MODEL_WIDTH),
        ],
        [inputs, gains, w_heads, cosine, sine],
        [],
        2**32,
    )

    middle, normed_two, w_gating = call(
        middle_kernel,
        [
            (shape(OWN, MODEL_WIDTH, dtype=F32), VMEM),
            (shape(SEQ, MODEL_WIDTH), VMEM),
            (shape(4, 16, 32, 2 * HIDDEN), VMEM),
        ],
        [
            (merged, VMEM),
            (input_rows, VMEM),
            (gains, VMEM),
            (gating_own, VMEM),
        ],
        LINE_SCATTER_SCRATCH + [pltpu.VMEM((OWN, MODEL_WIDTH), BF16)],
        100,
        1,
        2**25,
    )
    w_gating = w_gating.reshape(MODEL_WIDTH, 2 * HIDDEN)

    gated = product(normed_two, w_gating)
    gate_value, up_value = gated[:, :HIDDEN], gated[:, HIDDEN:]
    gate_sigmoid = jax.nn.sigmoid(gate_value)
    silu_gate = gate_value * gate_sigmoid
    hidden = (silu_gate * up_value).astype(BF16)
    grad_hidden = contract_last(back, w_down)
    grad_gate = grad_hidden * up_value * gate_sigmoid * (1.0 + gate_value * (1.0 - gate_sigmoid))
    grad_up = grad_hidden * silu_gate
    grad_gated = jnp.concatenate([grad_gate, grad_up], axis=1).astype(BF16)
    down_out = product(hidden, w_down).astype(BF16)
    down_part = token_product(hidden, back).astype(BF16)
    gating_part = token_product(normed_two, grad_gated).astype(BF16)
    normed_two_part = contract_last(grad_gated, w_gating).astype(BF16)

    grad_middle, branch, gain_part, gating_sum = call(
        branch_kernel,
        [
            (shape(OWN, MODEL_WIDTH, dtype=F32), VMEM),
            (shape(SEQ, MODEL_WIDTH), VMEM),
            (shape(8, MODEL_WIDTH, dtype=F32), VMEM),
            (shape(4, 32, 2 * HIDDEN), VMEM),
        ],
        [
            (normed_two_part, VMEM),
            (middle, VMEM),
            (own_rows(back), VMEM),
            (gains, VMEM),
            (gating_part.reshape(4, 16, 32, 2 * HIDDEN), VMEM),
        ],
        LINE_SCATTER_SCRATCH
        + ring_scatter_scratch(Rows(2 * HIDDEN))
        + [pltpu.VMEM((OWN, MODEL_WIDTH), BF16)],
        100,
        2,
        2**25,
    )

    merge_part = token_product(attended, branch).astype(BF16)
    grad_mixed, normed_one_part = local_call(
        backward_kernel,
        [shape(SEQ, HEADS_COLS), shape(SEQ, MODEL_WIDTH)],
        [branch, w_merge, w_heads, query, pair, sums[:, :8].T, cosine, sine],
        [
            pltpu.VMEM((SEQ, 256), BF16),
            pltpu.VMEM((SEQ, HEAD_SIZE), F32),
            pltpu.VMEM((SEQ, HEAD_SIZE), F32),
            pltpu.VMEM((HEAD_SIZE, SEQ), BF16),
        ],
        2**33,
    )
    heads_part = token_product(normed_one, grad_mixed).astype(BF16)

    (
        block_output, input_grad, gains_grad,
        heads_pieces, merge_pieces, gating_pieces, down_pieces,
    ) = call(
        finish_kernel,
        [
            (shape(512, 512), VMEM),
            (shape(512, 512, dtype=F32), VMEM),
            (shape(8, 512, dtype=F32), VMEM),
            (shape(4, 32, HEADS_COLS), VMEM),
            (shape(4, 32, 256), VMEM),
            (shape(4, 32, 2 * HIDDEN), VMEM),
            (shape(4, PIECE, 512), VMEM),
        ],
        [
            (normed_one_part, VMEM),
            (down_out, VMEM),
            (middle, VMEM),
            (grad_middle, VMEM),
            (input_rows, VMEM),
            (gains, VMEM),
            (gain_part, VMEM),
            (heads_part, VMEM),
            (merge_part, VMEM),
            (gating_sum, VMEM),
            (down_part, VMEM),
        ],
        LINE_SCATTER_SCRATCH
        + LINE_SCATTER_SCRATCH
        + ring_scatter_scratch(Rows(HEADS_COLS + 256))
        + ring_scatter_scratch(Flat())
        + [
            pltpu.VMEM((4, 16, 32, HEADS_COLS + 256), BF16),
            pltpu.VMEM((4, 32, HEADS_COLS + 256), BF16),
            pltpu.VMEM((PIECE, MODEL_WIDTH), BF16),
            pltpu.VMEM((OWN, MODEL_WIDTH), BF16),
            pltpu.VMEM((OWN, MODEL_WIDTH), F32),
            pltpu.VMEM((2, 8, MODEL_WIDTH), F32),
            pltpu.VMEM((4, 2, 8, 512), F32),
            pltpu.VMEM((32, 8, 512), F32),
        ],
        180,
        3,
        2**25,
    )
    gains_grad = gains_grad[:2]
    heads_grad = unpack_heads(heads_pieces)
    merge_grad = unpack_merge(merge_pieces)
    gating_grad = unpack_gating(gating_pieces)
    down_grad = unpack_down(down_pieces)
    gains_next, gains_mean, gains_square = adamw(
        norm_gains, gains_grad, gains_first, gains_second, RATE_GAIN, 0.0
    )
    heads_next, heads_mean, heads_square = adamw(
        heads_projection_weight,
        heads_grad,
        heads_first_moment,
        heads_second_moment,
        RATE_MATRIX,
        WEIGHT_DECAY,
    )
    merge_next, merge_mean, merge_square = adamw(
        merge_weight, merge_grad, merge_first, merge_second, RATE_MERGE, WEIGHT_DECAY
    )
    gating_next, gating_mean, gating_square = adamw(
        gating_weight, gating_grad, gating_first, gating_second, RATE_MATRIX, WEIGHT_DECAY
    )
    down_next, down_mean, down_square = adamw(
        down_weight, down_grad, down_first, down_second, RATE_MATRIX, WEIGHT_DECAY
    )
    return (
        block_output,
        input_grad,
        gains_grad,
        gains_next,
        gains_mean,
        gains_square,
        heads_grad,
        heads_next,
        heads_mean,
        heads_square,
        merge_grad,
        merge_next,
        merge_mean,
        merge_square,
        gating_grad,
        gating_next,
        gating_mean,
        gating_square,
        down_grad,
        down_next,
        down_mean,
        down_square,
    )


def solution(mesh):
    in_specs = (
        P(("dp", "col"), "row"),
        P(("dp", "col"), "row"),
        P(None, "row"),
        P(None, "row"),
        P(None, "row"),
        P(("row", "dp"), "col"),
        P(("row", "dp"), "col"),
        P(("row", "dp"), "col"),
        P(("col", "dp"), "row"),
        P(("col", "dp"), "row"),
        P(("col", "dp"), "row"),
        P(("row", "dp"), None, "col"),
        P(("row", "dp"), None, "col"),
        P(("row", "dp"), None, "col"),
        P(("col", "dp"), "row"),
        P(("col", "dp"), "row"),
        P(("col", "dp"), "row"),
    )
    out_specs = (
        P(("dp", "col"), "row"),
        P(("dp", "col"), "row"),
        P(None, "row"),
        P(None, "row"),
        P(None, "row"),
        P(None, "row"),
        P(("row", "dp"), "col"),
        P(("row", "dp"), "col"),
        P(("row", "dp"), "col"),
        P(("row", "dp"), "col"),
        P(("col", "dp"), "row"),
        P(("col", "dp"), "row"),
        P(("col", "dp"), "row"),
        P(("col", "dp"), "row"),
        P(("row", "dp"), None, "col"),
        P(("row", "dp"), None, "col"),
        P(("row", "dp"), None, "col"),
        P(("row", "dp"), None, "col"),
        P(("col", "dp"), "row"),
        P(("col", "dp"), "row"),
        P(("col", "dp"), "row"),
        P(("col", "dp"), "row"),
    )
    return jax.shard_map(body, mesh=mesh, in_specs=in_specs, out_specs=out_specs, check_vma=False)
```

```python
import functools

import jax
import jax.numpy as jnp
from jax import lax
from jax.experimental import pallas as pl
from jax.experimental.pallas import tpu as pltpu
from jax.sharding import PartitionSpec as P

MODEL_WIDTH = 2048
KEY_VALUE_HEADS = 4
HEAD_SIZE = 64
QUERY_PER_GROUP = 8
STEP = 10


EPS_NORM = 1e-05
BETA_ONE = 0.9
BETA_TWO = 0.95
EPS_ADAM = 1e-08
RATE_MATRIX = 0.05
RATE_MERGE = 0.5
RATE_GAIN = 1.0
WEIGHT_DECAY = 0.1
ROPE_BASE = 10000.0
MASK_FILL = -1e30

MESH = pl.DeviceIdType.MESH
VMEM_BYTES = 60 * 2**20
BF16 = jnp.bfloat16
F32 = jnp.float32

SEQ = 1024
OWN = 128
HEADS_COLS = 384
HIDDEN = 768
PIECE = 48
PIECE_USED = 44


class Place:
    def __init__(self):
        self.dp = lax.axis_index("dp")
        self.row = lax.axis_index("row")
        self.col = lax.axis_index("col")
        self.y = lax.div(self.dp, 4)
        self.z = lax.rem(self.dp, 4)
        self.core = lax.rem(self.row, 2)
        self.x = self.col * 2 + lax.div(self.row, 2)

    def near(self, x=0, core=0, y=0, z=0):
        new_x = lax.rem(self.x + x + 4, 4)
        new_core = lax.rem(self.core + core, 2)
        new_y = lax.rem(self.y + y + 4, 4)
        new_z = lax.rem(self.z + z + 4, 4)
        return {
            "dp": new_y * 4 + new_z,
            "row": lax.rem(new_x, 2) * 2 + new_core,
            "col": lax.div(new_x, 2),
        }

    def slot(self, first_axis, first, second):
        y, z = (first, second) if first_axis == "y" else (second, first)
        return lax.rem(self.y + y + 4, 4) * 4 + lax.rem(self.z + z + 4, 4)

    def line(self, x, core):
        return lax.rem(self.x + x + 4, 4) * 2 + lax.rem(self.core + core, 2)

    def peer(self, step):
        other = lax.rem(self.row + step, 4)
        return other, {"dp": self.dp, "row": other, "col": self.col}


class Wires:
    def __init__(self, send, recv, local, parent=None):
        self.send, self.recv, self.local = send, recv, local
        self.root = parent or self
        self.count = 0
        self.local_count = 0
        self.sent = []

    def part(self):
        return Wires(self.send, self.recv, self.local, self.root)

    def push(self, source, target, device):
        index = self.root.count
        self.root.count += 1
        copy = pltpu.make_async_remote_copy(
            src_ref=source,
            dst_ref=target,
            send_sem=self.send.at[index],
            recv_sem=self.recv.at[index],
            device_id=device,
            device_id_type=MESH,
        )
        copy.start()
        self.sent.append(copy)
        return copy

    def keep(self, source, target):
        copy = pltpu.make_async_copy(source, target, self.local.at[self.root.local_count])
        self.root.local_count += 1
        copy.start()
        return copy

    def settle(self, copies):
        for copy in copies:
            copy.wait_send()
        self.sent = [copy for copy in self.sent if all(copy is not other for other in copies)]

    def drain(self):
        self.settle(list(self.sent))


def meet(devices, more=0):
    barrier = pltpu.get_barrier_semaphore()
    for device in devices:
        pl.semaphore_signal(barrier, inc=1, device_id=device, device_id_type=MESH)
    pl.semaphore_wait(barrier, len(devices))


def interleave(*plans):
    waiting = [[next(plan), order, plan] for order, plan in enumerate(plans)]
    while waiting:
        waiting.sort(key=lambda entry: (entry[0], entry[1]))
        entry = waiting[0]
        try:
            entry[0] = max(entry[0], next(entry[2]))
        except StopIteration:
            waiting.pop(0)


def ring_neighbours(place):
    return [place.near(y=1), place.near(y=-1), place.near(z=1), place.near(z=-1)]


def line_neighbours(place):
    return [place.near(x=1), place.near(x=-1), place.near(core=1)]


def line_gather(place, wires, own, out, block, half, start, cost):
    me = place.line(0, 0)
    yield start
    kept = wires.keep(own, block(out, me))
    right = wires.push(own, block(out, me), place.near(x=1))
    left = wires.push(own, block(out, me), place.near(x=-1))
    beside = [wires.push(own, block(out, me), place.near(core=1))]
    yield start + cost + 2
    right.wait_recv()
    came = place.line(-1, 0)
    far_right = wires.push(half(out, came, 0), half(out, came, 0), place.near(x=1))
    beside.append(wires.push(block(out, came), block(out, came), place.near(core=1)))
    left.wait_recv()
    came = place.line(1, 0)
    far_left = wires.push(half(out, came, 1), half(out, came, 1), place.near(x=-1))
    beside.append(wires.push(block(out, came), block(out, came), place.near(core=1)))
    yield start + 1.5 * cost + 4
    far_right.wait_recv()
    far_left.wait_recv()
    came = place.line(2, 0)
    beside.append(wires.push(block(out, came), block(out, came), place.near(core=1)))
    yield start + 1.5 * cost + 6
    kept.wait()
    for copy in beside:
        copy.wait_recv()


def token_block(ref, index):
    return ref.at[pl.ds(pl.multiple_of(index * OWN, OWN), OWN)]


def token_half(ref, index, side):
    return ref.at[pl.ds(pl.multiple_of(index * OWN + side * (OWN // 2), OWN // 2), OWN // 2)]


def tile_block(ref, index):
    x, core = lax.div(index, 2), lax.rem(index, 2)
    rows = pl.ds(pl.multiple_of(lax.div(x, 2) * 512, 512), 512)
    columns = pl.ds(pl.multiple_of((lax.rem(x, 2) * 2 + core) * 512, 512), 512)
    return ref.at[rows, columns]


def tile_half(ref, index, side):
    x, core = lax.div(index, 2), lax.rem(index, 2)
    rows = pl.ds(pl.multiple_of(lax.div(x, 2) * 512 + side * 256, 256), 256)
    columns = pl.ds(pl.multiple_of((lax.rem(x, 2) * 2 + core) * 512, 512), 512)
    return ref.at[rows, columns]


def add_rows(out, terms, rows, step=16):
    def chunk(index, carry):
        at = pl.ds(pl.multiple_of(index * step, step), step)
        out[at, :] = functools.reduce(
            lambda a, b: a + b, [term[at, :].astype(F32) for term in terms]
        ).astype(out.dtype)
        return carry

    lax.fori_loop(0, rows // step, chunk, 0)


LINE_SCATTER_SCRATCH = [
    pltpu.VMEM((4, OWN, MODEL_WIDTH), BF16),
    pltpu.VMEM((2, OWN // 2, MODEL_WIDTH), BF16),
    pltpu.VMEM((2, OWN, MODEL_WIDTH), BF16),
    pltpu.VMEM((3, OWN, MODEL_WIDTH), BF16),
]


def line_scatter(place, wires, part, scratch, start, cost, sent=None, pairs=None):
    beside, halves, full, total = scratch
    yield start
    if pairs is None:
        pairs = {}
        for offset in (2, 1, 3, 0):
            pairs[offset] = wires.push(
                token_block(part, place.line(offset, 1)), beside.at[offset], place.near(core=1)
            )
        yield start + 2
    if sent is not None:
        sent.extend(pairs.values())
    pairs[2].wait_recv()
    add_rows(total.at[2], [token_block(part, place.line(2, 0)), beside.at[2]], OWN)
    far_right = wires.push(
        total.at[2, pl.ds(0, OWN // 2)], halves.at[0], place.near(x=1)
    )
    far_left = wires.push(
        total.at[2, pl.ds(OWN // 2, OWN // 2)], halves.at[1], place.near(x=-1)
    )
    yield start + 3
    pairs[1].wait_recv()
    add_rows(total.at[0], [token_block(part, place.line(1, 0)), beside.at[1]], OWN)
    right_late = wires.push(
        total.at[0, pl.ds(OWN // 2, OWN // 2)],
        full.at[0, pl.ds(OWN // 2, OWN // 2)],
        place.near(x=1),
    )
    pairs[3].wait_recv()
    add_rows(total.at[1], [token_block(part, place.line(3, 0)), beside.at[3]], OWN)
    left_late = wires.push(
        total.at[1, pl.ds(0, OWN // 2)], full.at[1, pl.ds(0, OWN // 2)], place.near(x=-1)
    )
    yield start + 5 + 0.5 * cost
    far_right.wait_recv()
    first = total.at[0, pl.ds(0, OWN // 2)]
    add_rows(first, [first, halves.at[0]], OWN // 2)
    right = wires.push(first, full.at[0, pl.ds(0, OWN // 2)], place.near(x=1))
    far_left.wait_recv()
    second = total.at[1, pl.ds(OWN // 2, OWN // 2)]
    add_rows(second, [second, halves.at[1]], OWN // 2)
    left = wires.push(second, full.at[1, pl.ds(OWN // 2, OWN // 2)], place.near(x=-1))
    yield start + 6 + 1.5 * cost
    pairs[0].wait_recv()
    right_late.wait_recv()
    left_late.wait_recv()
    right.wait_recv()
    left.wait_recv()


def scatter_terms(place, part, scratch):
    beside, halves, full, total = scratch
    return [token_block(part, place.line(0, 0)), beside.at[0], full.at[0], full.at[1]]


class Rows:
    def __init__(self, columns):
        self.item_shape = (2, 32, columns)
        self.half_shape = (1, 32, columns)

    def item(self, ref, side, slot):
        return ref.at[pl.ds(2 * side, 2), slot]

    def half(self, ref, side, part, slot):
        return ref.at[pl.ds(2 * side + part, 1), slot]

    def cut(self, item, part):
        return item.at[pl.ds(part, 1)]


class Flat:
    def __init__(self):
        self.item_shape = (PIECE, MODEL_WIDTH // 2)
        self.half_shape = (PIECE, MODEL_WIDTH // 4)

    def item(self, ref, side, slot):
        rows = pl.ds(pl.multiple_of(slot * PIECE, PIECE), PIECE)
        return ref.at[rows, pl.ds(side * (MODEL_WIDTH // 2), MODEL_WIDTH // 2)]

    def half(self, ref, side, part, slot):
        rows = pl.ds(pl.multiple_of(slot * PIECE, PIECE), PIECE)
        return ref.at[rows, pl.ds((2 * side + part) * (MODEL_WIDTH // 4), MODEL_WIDTH // 4)]

    def cut(self, item, part):
        return item.at[:, pl.ds(part * (MODEL_WIDTH // 4), MODEL_WIDTH // 4)]


def ring_move(place, axis, step):
    return place.near(y=step) if axis == "y" else place.near(z=step)


def ring_gather(place, wires, kind, out, side, start, cost):
    first, second = ("z", "y") if side == 0 else ("y", "z")
    slot = functools.partial(place.slot, first)
    spread = {}

    def send_on(offset):
        item = kind.item(out, side, slot(offset, 0))
        spread[offset] = [
            wires.push(item, item, ring_move(place, second, step)) for step in (1, -1)
        ]

    def pass_on(offset):
        right, left = spread[offset]
        right.wait_recv()
        piece = kind.half(out, side, 0, slot(offset, -1))
        one = wires.push(piece, piece, ring_move(place, second, 1))
        left.wait_recv()
        piece = kind.half(out, side, 1, slot(offset, 1))
        return [one, wires.push(piece, piece, ring_move(place, second, -1))]

    yield start
    own = kind.item(out, side, slot(0, 0))
    right = wires.push(own, own, ring_move(place, first, 1))
    left = wires.push(own, own, ring_move(place, first, -1))
    send_on(0)
    yield start + cost + 2
    right.wait_recv()
    piece = kind.half(out, side, 0, slot(-1, 0))
    far_right = wires.push(piece, piece, ring_move(place, first, 1))
    send_on(-1)
    left.wait_recv()
    piece = kind.half(out, side, 1, slot(1, 0))
    far_left = wires.push(piece, piece, ring_move(place, first, -1))
    send_on(1)
    last = []
    yield start + 2 * cost + 4
    last += pass_on(0)
    yield start + 2.5 * cost + 4
    far_right.wait_recv()
    far_left.wait_recv()
    send_on(2)
    yield start + 4 * cost + 4
    last += pass_on(-1)
    yield start + 5.5 * cost + 4
    last += pass_on(1)
    yield start + 6.5 * cost + 4
    last += pass_on(2)
    yield start + 7.5 * cost + 6
    for copy in last:
        copy.wait_recv()


RING_SCATTER_SCRATCH = 8


def ring_scatter_scratch(kind):
    def stack(count, shape):
        return pltpu.VMEM((count, *shape), BF16)

    one_side = [
        stack(8, kind.half_shape),
        stack(8, kind.item_shape),
        stack(2, kind.half_shape),
        stack(2, kind.item_shape),
    ]
    return one_side + one_side


def add_to(out, *terms):
    out[...] = functools.reduce(
        lambda a, b: a + b, [t[...].astype(F32) for t in (out, *terms)]
    ).astype(out.dtype)


def ring_scatter(place, wires, kind, part, side, scratch, result, start, cost):
    far, came, far_last, came_last = scratch[4 * side : 4 * side + 4]
    first, second = ("z", "y") if side == 0 else ("y", "z")
    slot = functools.partial(place.slot, first)
    order = (2, 1, -1, 0)
    yield start
    right, left = {}, {}
    for n, offset in enumerate(order):
        target = slot(offset, 2)
        right[offset] = wires.push(
            kind.half(part, side, 0, target), far.at[2 * n], ring_move(place, second, 1)
        )
        left[offset] = wires.push(
            kind.half(part, side, 1, target), far.at[2 * n + 1], ring_move(place, second, -1)
        )

    moved = {}
    for n, offset in enumerate(order):
        yield start + 2.5 + (0.5 + n) * cost
        right[offset].wait_recv()
        add_to(kind.half(part, side, 0, slot(offset, 1)), far.at[2 * n])
        item = kind.item(part, side, slot(offset, 1))
        one = wires.push(item, came.at[2 * n], ring_move(place, second, 1))
        left[offset].wait_recv()
        add_to(kind.half(part, side, 1, slot(offset, -1)), far.at[2 * n + 1])
        item = kind.item(part, side, slot(offset, -1))
        two = wires.push(item, came.at[2 * n + 1], ring_move(place, second, -1))
        moved[offset] = (one, two)

    def finish(n, offset):
        for copy in moved[offset]:
            copy.wait_recv()
        add_to(kind.item(part, side, slot(offset, 0)), came.at[2 * n], came.at[2 * n + 1])

    yield start + 4 + 3 * cost
    finish(0, 2)
    far_right = wires.push(
        kind.half(part, side, 0, slot(2, 0)), far_last.at[0], ring_move(place, first, 1)
    )
    far_left = wires.push(
        kind.half(part, side, 1, slot(2, 0)), far_last.at[1], ring_move(place, first, -1)
    )
    yield start + 4 + 4 * cost
    finish(1, 1)
    yield start + 4 + 5 * cost
    finish(2, -1)
    far_right.wait_recv()
    add_to(kind.half(part, side, 0, slot(1, 0)), far_last.at[0])
    item = kind.item(part, side, slot(1, 0))
    one = wires.push(item, came_last.at[0], ring_move(place, first, 1))
    far_left.wait_recv()
    add_to(kind.half(part, side, 1, slot(-1, 0)), far_last.at[1])
    item = kind.item(part, side, slot(-1, 0))
    two = wires.push(item, came_last.at[1], ring_move(place, first, -1))
    yield start + 5 + 6 * cost
    finish(3, 0)
    yield start + 8 + 7.5 * cost
    one.wait_recv()
    two.wait_recv()
    own = kind.item(part, side, slot(0, 0))
    add_to(own, came_last.at[0], came_last.at[1])
    result[...] = own[...]


def call(kernel, outs, ins, scratch, wires, name, cost):
    return pl.pallas_call(
        kernel,
        out_shape=[shape for shape, _ in outs],
        in_specs=[pl.BlockSpec(memory_space=space) for _, space in ins],
        out_specs=[pl.BlockSpec(memory_space=space) for _, space in outs],
        scratch_shapes=list(scratch)
        + [
            pltpu.SemaphoreType.DMA((wires,)),
            pltpu.SemaphoreType.DMA((wires,)),
            pltpu.SemaphoreType.DMA((16,)),
        ],
        compiler_params=pltpu.CompilerParams(
            collective_id=name, has_side_effects=True, vmem_limit_bytes=VMEM_BYTES
        ),
        cost_estimate=pl.CostEstimate(flops=0, bytes_accessed=cost, transcendentals=0),
    )(*[array for array, _ in ins])


def shape(*extent, dtype=BF16):
    return jax.ShapeDtypeStruct(extent, dtype)


def merge_devices(place):
    users = [{"dp": j * 4 + place.z, "row": place.y, "col": place.col} for j in range(4)]
    homes = [
        {"dp": place.row * 4 + place.z, "row": jnp.int32(row), "col": place.col} for row in range(4)
    ]
    return users, homes


def signal_others(place, devices):
    barrier = pltpu.get_barrier_semaphore()
    for device in devices:
        alone = (device["dp"] == place.dp) & (device["row"] == place.row)

        @pl.when(jnp.logical_not(alone))
        def _():
            pl.semaphore_signal(barrier, inc=1, device_id=device, device_id_type=MESH)


def merge_exchange(place, wires, devices, source, target, mine):
    base = wires.count
    wires.count += 4
    copies = []
    for index, device in enumerate(devices):
        copy = pltpu.make_async_remote_copy(
            src_ref=source(index),
            dst_ref=target(index),
            send_sem=wires.send.at[base + index],
            recv_sem=wires.recv.at[base + mine],
            device_id=device,
            device_id_type=MESH,
        )
        here = pltpu.make_async_copy(source(index), target(index), wires.recv.at[base + mine])
        alone = (device["dp"] == place.dp) & (device["row"] == place.row)
        copies.append((copy, alone))
        pl.when(alone)(here.start)
        pl.when(jnp.logical_not(alone))(copy.start)

    def wait():
        for index in range(4):
            pltpu.make_async_copy(source(0), target(0), wires.recv.at[base + index]).wait()
        for copy, alone in copies:
            pl.when(jnp.logical_not(alone))(copy.wait_send)

    return wait


def nested(plans):
    pending = [[next(plan), order, plan] for order, plan in enumerate(plans)]
    while pending:
        pending.sort(key=lambda entry: entry[:2])
        entry = pending[0]
        yield entry[0]
        try:
            entry[0] = max(entry[0], next(entry[2]))
        except StopIteration:
            pending.pop(0)


def column_block(ref, row):
    return ref.at[:, pl.ds(pl.multiple_of(row * 512, 512), 512)]


def down_slot(ref, slot, row):
    rows = pl.ds(pl.multiple_of(slot * PIECE, PIECE), PIECE)
    return ref.at[rows, pl.ds(pl.multiple_of(row * 512, 512), 512)]


def own_token_rows(ref, row):
    return ref.at[pl.ds(pl.multiple_of(row * OWN, OWN), OWN)]


def recut(place, wires, own, out, when):
    peers = [place.peer(step) for step in (1, 2, 3)]
    kept = wires.keep(column_block(own, place.row), own_token_rows(out, place.row))
    moved = [
        wires.push(column_block(own, other), own_token_rows(out, place.row), device)
        for other, device in peers
    ]
    yield when
    kept.wait()
    for copy in moved:
        copy.wait_recv()


def back_pieces(place, wires, part_of, out, when):
    peers = [place.peer(step) for step in (1, 2, 3)]
    kept = wires.keep(part_of(place.row), out.at[place.row])
    moved = [wires.push(part_of(other), out.at[place.row], device) for other, device in peers]
    yield when
    kept.wait()
    for copy in moved:
        copy.wait_recv()


def start_kernel(
    heads_weight, merge_weight, gating_weight, down_weight, input_own, gains_own,
    heads, gating, down, inputs, gains,
    heads_cut, merge_cut, gating_cut, down_cut, send, recv, local,
):
    place = Place()
    wires = Wires(send, recv, local)
    users, homes = merge_devices(place)
    peers = [place.peer(step) for step in (1, 2, 3)]
    same = place.row == place.y
    devices = ring_neighbours(place) + line_neighbours(place) + [p for _, p in peers]
    signal_others(place, devices + homes)
    for row in range(4):
        group, half = divmod(row, 2)
        query = heads_weight[:, pl.ds(group * 640 + half * 256, 256)]
        heads_cut[row, :, pl.ds(0, 256)] = query.astype(BF16)
        pair = heads_weight[:, pl.ds(group * 640 + 512, 128)]
        heads_cut[row, :, pl.ds(256, 128)] = pair.astype(BF16)
        for side in range(2):
            piece = merge_weight[pl.ds(16 * row, 16), pl.ds(256 * side, 256)]
            merge_cut[row, pl.ds(16 * side, 16)] = piece.astype(BF16)
    pl.semaphore_wait(
        pltpu.get_barrier_semaphore(), len(devices) + 4 - same.astype(jnp.int32)
    )

    def exchange():
        def heads_columns(row, slot):
            return heads.at[row, slot, :, pl.ds(0, HEADS_COLS)]

        yield 0.0
        kept = [wires.keep(heads_cut.at[place.row], heads_columns(place.row, place.dp))]
        moved = [
            wires.push(heads_cut.at[other], heads_columns(place.row, place.dp), device)
            for other, device in peers
        ]
        merge_wait = merge_exchange(
            place, wires, users,
            lambda j: merge_cut.at[j],
            lambda j: heads.at[place.row, j * 4 + place.z, :, pl.ds(HEADS_COLS, 256)],
            place.row,
        )
        yield 0.2
        rest = [
            wires.keep(gains_own, gains.at[place.row]),
        ]
        later = [wires.push(gains_own, gains.at[place.row], device) for _, device in peers]
        for row in range(4):
            piece = down_weight[pl.ds(PIECE_USED * row, PIECE_USED), :]
            down_cut[row] = jnp.concatenate(
                [piece, jnp.zeros((PIECE - PIECE_USED, 512), F32)], axis=0
            ).astype(BF16)
        later += [
            wires.push(down_cut.at[other], column_block(down, place.row), device)
            for other, device in peers
        ]
        rest.append(wires.keep(down_cut.at[place.row], column_block(down, place.row)))
        zeros = jnp.zeros((32, PIECE - PIECE_USED), F32)
        for kind in range(2):
            for row in range(4):
                pieces = []
                for slot in range(16):
                    first = slot * 4 * PIECE_USED + row * PIECE_USED
                    pieces += [gating_weight[:, kind, pl.ds(first, PIECE_USED)], zeros]
                gating_cut[row, :, pl.ds(kind * HIDDEN, HIDDEN)] = jnp.concatenate(
                    pieces, axis=1
                ).astype(BF16)
        rest.append(wires.keep(gating_cut.at[place.row], gating.at[place.row]))
        later += [
            wires.push(gating_cut.at[other], gating.at[place.row], device)
            for other, device in peers
        ]
        yield 5.0
        for copy in kept:
            copy.wait()
        for copy in moved:
            copy.wait_recv()
        merge_wait()
        yield from nested(
            ring_gather(place, wires, Rows(HEADS_COLS + 256), heads, side, 5.0, 1.8)
            for side in (0, 1)
        )
        yield 30.0
        for copy in rest:
            copy.wait()
        for copy in later:
            copy.wait_recv()

    interleave(
        line_gather(place, wires, input_own, inputs, tile_block, tile_half, 0.1, 11.4),
        exchange(),
    )
    wires.drain()


def feedforward_kernel(
    merged, input_rows, gains, gating_own, w_down, back,
    middle, grad_middle, branch, gain_part, gating_sum, down_out, down_part,
    *scratch,
):
    first_scratch, scratch = scratch[:4], scratch[4:]
    second_scratch, scratch = scratch[:4], scratch[4:]
    ring_scratch, scratch = scratch[:RING_SCATTER_SCRATCH], scratch[RING_SCATTER_SCRATCH:]
    part, normed, gating, grad_hidden, hidden, grad_gated, rows_own, send, recv, local = scratch
    place = Place()
    wires = Wires(send, recv, local)
    gating_wires = wires.part()
    kept = [wires.keep(gating_own.at[r], gating.at[r, place.dp]) for r in range(4)]
    loaded = wires.keep(merged, part)
    meet(ring_neighbours(place) + line_neighbours(place))
    for copy in kept:
        copy.wait()

    def weights():
        yield 0.0
        yield from nested(
            ring_gather(place, gating_wires, Rows(2 * HIDDEN), gating, side, 0.1, 4.3)
            for side in (0, 1)
        )

    def chip_rows(offset):
        start = pl.multiple_of(lax.rem(place.x + offset + 4, 4) * 256, 256)
        return pl.ds(start, 256)

    def grad_hidden_rows():
        for index in range(4):
            yield 3.0 + 4.0 * index
            at = pl.ds(index * 256, 256)
            grad_hidden[at, :] = contract_last(back[at, :], w_down[...])

    def forward(offset, when):
        at = chip_rows(offset)
        for tile in range(3):
            gate_at, up_at = pl.ds(tile * 256, 256), pl.ds(HIDDEN + tile * 256, 256)
            rows = normed[at, :]
            gate = product(rows, gating[:, :, :, gate_at].reshape(MODEL_WIDTH, 256))
            up = product(rows, gating[:, :, :, up_at].reshape(MODEL_WIDTH, 256))
            grad = grad_hidden[at, gate_at]
            sigmoid = jax.nn.sigmoid(gate)
            silu = gate * sigmoid
            hidden[at, gate_at] = (silu * up).astype(BF16)
            grad_gated[at, gate_at] = (grad * up * sigmoid * (1.0 + gate * (1.0 - sigmoid))).astype(
                BF16
            )
            grad_gated[at, up_at] = (grad * silu).astype(BF16)
            yield when + 0.6 * tile
        for row in range(4):
            part[at, pl.ds(row * 512, 512)] = contract_last(
                grad_gated[at, :], gating[row].reshape(512, 2 * HIDDEN)
            ).astype(BF16)
            if row % 2:
                yield when + 2.0 + 0.7 * row

    done = {}

    def main():
        yield 0.2
        loaded.wait()
        pairs = []
        yield from line_scatter(place, wires, part, first_scratch, 0.2, 11.4, pairs)
        terms = scatter_terms(place, part, first_scratch)

        def chunk(index, carry):
            at = pl.ds(pl.multiple_of(index * 16, 16), 16)
            total = functools.reduce(lambda a, b: a + b, [t[at, :].astype(F32) for t in terms])
            total = total + input_rows[at, :].astype(F32)
            middle[at, :] = total
            scale = lax.rsqrt(
                jnp.sum(total * total, axis=1, keepdims=True) / MODEL_WIDTH + EPS_NORM
            )
            rows_own[at, :] = (total * scale * gains[1:2, :]).astype(BF16)
            return carry

        lax.fori_loop(0, OWN // 16, chunk, 0)
        wires.settle(pairs)
        me, block, half = place.line(0, 0), token_block, token_half
        mine = wires.keep(rows_own, block(normed, me))
        right = wires.push(rows_own, block(normed, me), place.near(x=1))
        left = wires.push(rows_own, block(normed, me), place.near(x=-1))
        beside = wires.push(rows_own, block(normed, me), place.near(core=1))

        def pass_beside(offset):
            came = block(normed, place.line(offset, 0))
            return wires.push(came, came, place.near(core=1))

        yield 38.0
        mine.wait()
        beside.wait_recv()
        right.wait_recv()
        piece = half(normed, place.line(-1, 0), 0)
        far_right = wires.push(piece, piece, place.near(x=1))
        beside_left = pass_beside(-1)
        left.wait_recv()
        piece = half(normed, place.line(1, 0), 1)
        far_left = wires.push(piece, piece, place.near(x=-1))
        beside_right = pass_beside(1)
        yield 42.0
        yield from forward(0, 43.0)
        far_right.wait_recv()
        far_left.wait_recv()
        beside_far = pass_beside(2)
        beside_left.wait_recv()
        beside_right.wait_recv()
        beside_far.wait_recv()
        pairs = {}

        def pair(offset):
            pairs[offset] = wires.push(
                token_block(part, place.line(offset, 1)),
                second_scratch[0].at[offset],
                place.near(core=1),
            )

        pair(0)
        yield 48.0
        yield from forward(2, 48.0)
        pair(2)
        yield 52.0
        yield from forward(1, 52.0)
        pair(1)
        yield 56.0
        yield from forward(-1, 56.0)
        pair(3)
        done["forward"] = True
        yield 60.0
        yield from line_scatter(place, wires, part, second_scratch, 60.0, 11.4, [], pairs)
        terms = scatter_terms(place, part, second_scratch)
        gain_part[...] = jnp.zeros_like(gain_part)
        back_own = token_block(back, place.line(0, 0))

        def chunk_back(index, carry):
            at = pl.ds(pl.multiple_of(index * 16, 16), 16)
            grad = functools.reduce(lambda a, b: a + b, [t[at, :].astype(F32) for t in terms])
            through, gain = norm_back(middle[at, :], gains[1:2, :], grad)
            total = back_own[at, :].astype(F32) + through
            grad_middle[at, :] = total
            rows_own[at, :] = total.astype(BF16)
            gain_part[...] += gain.reshape(2, 8, MODEL_WIDTH).sum(axis=0)
            return carry

        wires.settle([right, left, beside])
        lax.fori_loop(0, OWN // 16, chunk_back, 0)
        yield from line_gather(
            place, wires, rows_own, branch, token_block, token_half, 82.0, 11.4
        )

    def gradients():
        yield 60.5
        assert done["forward"]
        gating_wires.drain()
        sides = []
        for side in range(2):
            for row in (2 * side, 2 * side + 1):
                for piece in range(2):
                    columns = pl.ds(row * 512 + piece * 256, 256)
                    gating[row, pl.ds(8 * piece, 8)] = (
                        token_product(normed[:, columns], grad_gated[...])
                        .astype(BF16)
                        .reshape(8, 32, 2 * HIDDEN)
                    )
                    yield 61.0 + 1.2 * (2 * row + piece)
            sides.append(
                ring_scatter(
                    place, wires, Rows(2 * HIDDEN), gating, side, ring_scratch,
                    gating_sum.at[pl.ds(2 * side, 2)], 65.0 + 5 * side, 4.3,
                )
            )
        yield from nested(sides)

    def down_products():
        yield 72.0
        for tile in range(3):
            columns = pl.ds(tile * 256, 256)
            down_part[columns, :] = token_product(hidden[:, columns], back[...]).astype(BF16)
            yield 74.0 + 2 * tile
        for index in range(4):
            at = pl.ds(index * 256, 256)
            down_out[at, :] = product(hidden[at, :], w_down[...]).astype(BF16)
            yield 82.0 + 2 * index

    interleave(main(), weights(), grad_hidden_rows(), gradients(), down_products())
    wires.drain()


def norm_back(values, gain_row, gradient):
    scale = lax.rsqrt(jnp.sum(values * values, axis=1, keepdims=True) / MODEL_WIDTH + EPS_NORM)
    weighted = gain_row * gradient
    inner = jnp.sum(weighted * values, axis=1, keepdims=True)
    through = scale * weighted - values * (scale * scale * scale * inner / MODEL_WIDTH)
    return through, gradient * values * scale


def finish_kernel(
    part, grad_middle, input_rows, gains, gain_part, heads_part, merge_part, down_sum,
    input_grad, gains_grad, heads_pieces, merge_pieces, down_pieces,
    *scratch,
):
    line_scratch, scratch = scratch[:4], scratch[4:]
    heads_scratch, scratch = scratch[:8], scratch[8:]
    (
        heads_all, heads_sum, input_grad_own, gain_rows, gain_came, gain_all,
        send, recv, local,
    ) = scratch
    place = Place()
    wires = Wires(send, recv, local)
    users, homes = merge_devices(place)
    peers = [place.peer(step) for step in (1, 2, 3)]
    same = place.row == place.y
    barrier = pltpu.get_barrier_semaphore()
    devices = ring_neighbours(place) + line_neighbours(place) + [p for _, p in peers]
    signal_others(place, devices + users)

    def far(step):
        index = lax.rem(place.col * 16 + place.dp + step, 32)
        return {"dp": lax.rem(index, 16), "row": place.row, "col": lax.div(index, 16)}

    def greet(step, carry):
        pl.semaphore_signal(barrier, inc=1, device_id=far(step), device_id_type=MESH)
        return carry

    lax.fori_loop(1, 32, greet, 0)
    pl.semaphore_wait(barrier, len(devices) + 31 + 4 - same.astype(jnp.int32))

    def gradient():
        yield from line_scatter(place, wires, part, line_scratch, 0.0, 11.4)
        terms = scatter_terms(place, part, line_scratch)
        gain_rows[0] = jnp.zeros((8, MODEL_WIDTH), F32)
        gain_rows[1] = gain_part[...]

        def chunk(index, carry):
            at = pl.ds(pl.multiple_of(index * 16, 16), 16)
            grad = functools.reduce(lambda a, b: a + b, [t[at, :].astype(F32) for t in terms])
            through, gain = norm_back(input_rows[at, :].astype(F32), gains[0:1, :], grad)
            input_grad_own[at, :] = (grad_middle[at, :] + through).astype(BF16)
            gain_rows[0] += gain.reshape(2, 8, MODEL_WIDTH).sum(axis=0)
            return carry

        lax.fori_loop(0, OWN // 16, chunk, 0)
        moved = []
        for other, device in peers:
            piece = gain_rows.at[:, :, pl.ds(pl.multiple_of(other * 512, 512), 512)]
            moved.append(wires.push(piece, gain_came.at[place.row], device))
        piece = gain_rows.at[:, :, pl.ds(pl.multiple_of(place.row * 512, 512), 512)]
        kept = wires.keep(piece, gain_came.at[place.row])
        waits = recut(place, wires, input_grad_own, input_grad, 38.0)
        next(waits)
        yield 28.0
        kept.wait()
        for copy in moved:
            copy.wait_recv()
        local_sum = gain_came[0] + gain_came[1] + gain_came[2] + gain_came[3]
        me = place.col * 16 + place.dp
        gain_all[me] = jnp.concatenate(
            [jnp.sum(local_sum, axis=1), jnp.zeros((6, 512), F32)], axis=0
        )
        base = wires.count
        wires.count += 32

        def gain_copy(step):
            return pltpu.make_async_remote_copy(
                src_ref=gain_all.at[me],
                dst_ref=gain_all.at[me],
                send_sem=wires.send.at[base + step],
                recv_sem=wires.recv.at[base + step],
                device_id=far(step),
                device_id_type=MESH,
            )

        def start(step, carry):
            gain_copy(step).start()
            return carry

        def finish(step, carry):
            gain_copy(step).wait()
            return carry

        lax.fori_loop(1, 32, start, 0)
        yield 36.0
        lax.fori_loop(1, 32, finish, 0)
        gains_grad[...] = functools.reduce(lambda a, b: a + b, [gain_all[i] for i in range(32)])
        yield 38.0
        for _ in waits:
            pass

    def down_back():
        yield 0.4
        yield from back_pieces(
            place, wires, lambda row: column_block(down_sum, row), down_pieces, 35.0
        )

    def weights():
        yield 0.1
        for row in range(4):
            for slot in range(16):
                rows = pl.ds((row * 16 + slot) * 32, 32)
                heads_all[row, slot, :, pl.ds(0, HEADS_COLS)] = heads_part[rows, :]
                y, z = divmod(slot, 4)
                for half in range(2):
                    piece = merge_part[
                        pl.ds(z * 64 + y * 16, 16), pl.ds(row * 512 + half * 256, 256)
                    ]
                    heads_all[row, slot, pl.ds(16 * half, 16), pl.ds(HEADS_COLS, 256)] = piece
        yield from nested(
            ring_scatter(
                place, wires, Rows(HEADS_COLS + 256), heads_all, side, heads_scratch,
                heads_sum.at[pl.ds(2 * side, 2)], 0.2, 1.8,
            )
            for side in (0, 1)
        )
        merge_wait = merge_exchange(
            place, wires, homes,
            lambda row: heads_sum.at[row, :, pl.ds(HEADS_COLS, 256)],
            lambda row: merge_pieces.at[place.y],
            place.y,
        )
        yield from back_pieces(
            place, wires,
            lambda row: heads_sum.at[row, :, pl.ds(0, HEADS_COLS)], heads_pieces, 37.0,
        )
        merge_wait()

    interleave(gradient(), weights(), down_back())
    wires.drain()


def turn(tile, cosine, sine):
    lane = lax.broadcasted_iota(jnp.int32, tile.shape, 1)
    first = lax.rem(lane, HEAD_SIZE) < HEAD_SIZE // 2
    swapped = jnp.where(first, pltpu.roll(tile, 96, axis=1), pltpu.roll(tile, 32, axis=1))
    return tile * cosine + swapped * sine


def keys_only(cosine, sine):
    key = lax.broadcasted_iota(jnp.int32, cosine.shape, 1) < HEAD_SIZE
    return jnp.where(key, cosine, 1.0), jnp.where(key, sine, 0.0)


def heads_weight_of(heads):
    return heads[:, :, :, pl.ds(0, HEADS_COLS)].reshape(MODEL_WIDTH, HEADS_COLS)


QUERY_BLOCK = 256


def forward_kernel(
    inputs, gains, heads, cosine, sine, back_own, down_own,
    normed, query, pair, sums, attended, merge, part, back, down,
    send, recv, local,
):
    place = Place()
    wires = Wires(send, recv, local)
    meet(ring_neighbours(place) + line_neighbours(place))

    def down_rows():
        yield 0.1
        rows = pl.ds(pl.multiple_of(place.dp * PIECE, PIECE), PIECE)
        wires.keep(down_own, down.at[rows]).wait()
        yield from nested(
            ring_gather(place, wires, Flat(), down, side, 0.2, 2.1) for side in (0, 1)
        )

    interleave(
        line_gather(place, wires, back_own, back, tile_block, tile_half, 0.0, 11.4),
        down_rows(),
        attention(
            inputs, gains, heads, cosine, sine,
            normed, query, pair, sums, attended, merge, part,
        ),
    )
    wires.drain()


def attention(
    inputs, gains, heads, cosine, sine,
    normed, query, pair, sums, attended, merge, part,
):
    yield 0.3
    for row in range(4):
        for slot in range(16):
            y, z = divmod(slot, 4)
            for half in range(2):
                merge[pl.ds(z * 64 + y * 16, 16), pl.ds(row * 512 + half * 256, 256)] = heads[
                    row, slot, pl.ds(16 * half, 16), pl.ds(HEADS_COLS, 256)
                ]

    def project(index, carry):
        at = pl.ds(pl.multiple_of(index * 128, 128), 128)
        wide = inputs[at, :].astype(F32)
        scale = lax.rsqrt(jnp.sum(wide * wide, axis=1, keepdims=True) / MODEL_WIDTH + EPS_NORM)
        low = (wide * scale * gains[0:1, :]).astype(BF16)
        normed[at, :] = low
        mixed = product(low, heads_weight_of(heads))
        cos, sin = cosine[at, :], sine[at, :]
        query[at, pl.ds(0, 128)] = turn(mixed[:, :128], cos, sin).astype(BF16)
        query[at, pl.ds(128, 128)] = turn(mixed[:, 128:256], cos, sin).astype(BF16)
        pair[at, :] = turn(mixed[:, 256:], *keys_only(cos, sin)).astype(BF16)
        return carry

    for index in range(4):
        lax.fori_loop(2 * index, 2 * index + 2, project, 0)
        yield 2.0 * (index + 1)
    scale = HEAD_SIZE ** (-0.5)
    rows_at = lax.broadcasted_iota(jnp.int32, (QUERY_BLOCK, QUERY_BLOCK), 0)
    keys_at = lax.broadcasted_iota(jnp.int32, (QUERY_BLOCK, QUERY_BLOCK), 1)
    for block in range(SEQ // QUERY_BLOCK):
        at = pl.ds(block * QUERY_BLOCK, QUERY_BLOCK)
        before = block * QUERY_BLOCK
        out = []
        for head in range(4):
            rows = query[at, pl.ds(head * HEAD_SIZE, HEAD_SIZE)]
            scores = [
                jnp.where(
                    rows_at >= keys_at,
                    contract_last(rows, pair[at, pl.ds(0, HEAD_SIZE)]) * scale,
                    MASK_FILL,
                )
            ]
            if before:
                scores.append(
                    contract_last(rows, pair[pl.ds(0, before), pl.ds(0, HEAD_SIZE)]) * scale
                )
            top = functools.reduce(
                jnp.maximum, [jnp.max(part_, axis=1, keepdims=True) for part_ in scores]
            )
            powers = [jnp.exp(part_ - top) for part_ in scores]
            total = functools.reduce(
                lambda a, b: a + b, [jnp.sum(part_, axis=1, keepdims=True) for part_ in powers]
            )
            low = [(part_ * (1.0 / total)).astype(BF16) for part_ in powers]
            result = product(low[0], pair[at, pl.ds(HEAD_SIZE, HEAD_SIZE)])
            if before:
                result += product(low[1], pair[pl.ds(0, before), pl.ds(HEAD_SIZE, HEAD_SIZE)])
            sums[at, pl.ds(head, 1)] = top + jnp.log(total)
            out.append(result.astype(BF16))
            yield 8.5 + 3.0 * block + 0.7 * head
        attended[at, :] = jnp.concatenate(out, axis=1)

    def merge_rows(index, carry):
        at = pl.ds(pl.multiple_of(index * 128, 128), 128)
        part[at, :] = product(attended[at, :], merge[...]).astype(BF16)
        return carry

    lax.fori_loop(0, SEQ // 256, merge_rows, 0)
    yield 22.0
    lax.fori_loop(SEQ // 256, SEQ // 128, merge_rows, 0)


def backward_kernel(
    branch, merge, heads, query, pair, sums, cosine, sine, down_out, middle, down_given, gating_sum,
    grad_mixed, part, output, down_sum, gating_pieces,
    *scratch,
):
    line_scratch, scratch = scratch[:4], scratch[4:]
    down_scratch, scratch = scratch[:8], scratch[8:]
    grad_attended, grad_key, grad_value, key_columns, output_own, down_part, send, recv, local = (
        scratch
    )
    place = Place()
    wires = Wires(send, recv, local)
    loaded = wires.keep(down_given, down_part)
    peers = [place.peer(step) for step in (1, 2, 3)]
    meet(ring_neighbours(place) + line_neighbours(place) + [p for _, p in peers])
    loaded.wait()

    def outputs():
        yield from line_scatter(place, wires, down_out, line_scratch, 0.0, 11.4)
        terms = scatter_terms(place, down_out, line_scratch)

        def chunk(index, carry):
            at = pl.ds(pl.multiple_of(index * 16, 16), 16)
            total = functools.reduce(lambda a, b: a + b, [t[at, :].astype(F32) for t in terms])
            output_own[at, :] = (total + middle[at, :]).astype(BF16)
            return carry

        lax.fori_loop(0, OWN // 16, chunk, 0)
        yield from recut(place, wires, output_own, output, 32.0)

    def gating():
        yield 0.4
        yield from back_pieces(
            place, wires, lambda row: gating_sum.at[row], gating_pieces, 30.0
        )

    interleave(
        outputs(),
        *[
            ring_scatter(
                place, wires, Flat(), down_part, side, down_scratch,
                down_sum.at[:, pl.ds(side * 1024, 1024)], 0.3, 2.1,
            )
            for side in (0, 1)
        ],
        gating(),
        attention_back(
            branch, merge, heads, query, pair, sums, cosine, sine, grad_mixed, part,
            grad_attended, grad_key, grad_value, key_columns,
        ),
    )
    wires.drain()


def attention_back(
    branch, merge, heads, query, pair, sums, cosine, sine, grad_mixed, part,
    grad_attended, grad_key, grad_value, key_columns,
):
    yield 0.5
    def attended_rows(index, carry):
        at = pl.ds(pl.multiple_of(index * 128, 128), 128)
        grad_attended[at, :] = contract_last(branch[at, :], merge[...]).astype(BF16)
        return carry

    lax.fori_loop(0, SEQ // 256, attended_rows, 0)
    yield 1.0
    lax.fori_loop(SEQ // 256, SEQ // 128, attended_rows, 0)
    key_columns[...] = jnp.transpose(pair[...].astype(F32))[:HEAD_SIZE].astype(BF16)
    grad_key[...] = jnp.zeros_like(grad_key)
    grad_value[...] = jnp.zeros_like(grad_value)
    scale = HEAD_SIZE ** (-0.5)
    keys_at = lax.broadcasted_iota(jnp.int32, (QUERY_BLOCK, QUERY_BLOCK), 0)
    rows_at = lax.broadcasted_iota(jnp.int32, (QUERY_BLOCK, QUERY_BLOCK), 1)
    for block in range(SEQ // QUERY_BLOCK):
        at = pl.ds(block * QUERY_BLOCK, QUERY_BLOCK)
        before = block * QUERY_BLOCK
        for two in range(2):
            turned = []
            for head in (2 * two, 2 * two + 1):
                columns = pl.ds(head * HEAD_SIZE, HEAD_SIZE)
                rows, back = query[at, columns], grad_attended[at, columns]
                log_total = sums[pl.ds(head, 1), at]
                spans = [at] + ([pl.ds(0, before)] if before else [])
                softs, grads = [], []
                for span in spans:
                    scores = contract_last(pair[span, pl.ds(0, HEAD_SIZE)], rows) * scale
                    soft = jnp.exp(scores - log_total)
                    if span is at:
                        soft = jnp.where(rows_at >= keys_at, soft, 0.0)
                    softs.append(soft)
                    grads.append(contract_last(pair[span, pl.ds(HEAD_SIZE, HEAD_SIZE)], back))
                inner = functools.reduce(
                    lambda a, b: a + b,
                    [jnp.sum(s * g, axis=0, keepdims=True) for s, g in zip(softs, grads)],
                )
                result = 0.0
                for span, soft, grad in zip(spans, softs, grads):
                    low = (soft * (grad - inner)).astype(BF16)
                    grad_key[span, :] += product(low, rows)
                    grad_value[span, :] += product(soft.astype(BF16), back)
                    result += product(key_columns[:, span], low)
                turned.append(result)
                yield 3.0 + 4.5 * block + 1.1 * head
            tile = jnp.transpose(jnp.concatenate(turned, axis=0)) * scale
            grad_mixed[at, pl.ds(two * 128, 128)] = turn(
                tile, cosine[at, :], -sine[at, :]
            ).astype(BF16)

    def finish_rows(index, carry):
        at = pl.ds(pl.multiple_of(index * 128, 128), 128)
        cos, sin = keys_only(cosine[at, :], sine[at, :])
        tile = jnp.concatenate([grad_key[at, :] * scale, grad_value[at, :]], axis=1)
        grad_mixed[at, pl.ds(256, 128)] = turn(tile, cos, -sin).astype(BF16)
        part[at, :] = contract_last(grad_mixed[at, :], heads_weight_of(heads)).astype(BF16)
        return carry

    lax.fori_loop(0, SEQ // 256, finish_rows, 0)
    yield 24.0
    lax.fori_loop(SEQ // 256, SEQ // 128, finish_rows, 0)


def rope_tables():
    half_width = HEAD_SIZE // 2
    frequency = ROPE_BASE ** (-jnp.arange(half_width, dtype=F32) * 2.0 / HEAD_SIZE)
    angles = jnp.arange(SEQ, dtype=F32)[:, None] * frequency[None, :]
    cosine, sine = jnp.cos(angles), jnp.sin(angles)
    return jnp.tile(cosine, (1, 4)), jnp.concatenate([-sine, sine, -sine, sine], axis=1)


def product(left, right):
    return jnp.dot(left, right, preferred_element_type=F32)


def contract_last(left, right):
    return lax.dot_general(left, right, (((1,), (1,)), ((), ())), preferred_element_type=F32)


def token_product(left, right):
    return lax.dot_general(left, right, (((0,), (0,)), ((), ())), preferred_element_type=F32)


def adamw(current, gradient, first, second, step_rate, decay_rate):
    mean_new = BETA_ONE * first + (1.0 - BETA_ONE) * gradient
    square_new = BETA_TWO * second + (1.0 - BETA_TWO) * gradient * gradient
    mean_hat = mean_new / (1.0 - BETA_ONE**STEP)
    square_hat = square_new / (1.0 - BETA_TWO**STEP)
    updated = current - step_rate * (
        mean_hat / (jnp.sqrt(square_hat) + EPS_ADAM) + decay_rate * current
    )
    return (updated, mean_new, square_new)


def unpack_heads(pieces):
    pieces = pieces.astype(F32).reshape(2, 2, 32, HEADS_COLS)
    query = pieces[..., :256].transpose(2, 0, 1, 3).reshape(32, 2, 512)
    pair = (pieces[:, 0, :, 256:] + pieces[:, 1, :, 256:]).transpose(1, 0, 2)
    return jnp.concatenate([query, pair], axis=2).reshape(32, 1280)


def unpack_gating(pieces):
    cut = pieces.reshape(4, 32, 2, 16, PIECE)[..., :PIECE_USED]
    return cut.transpose(1, 2, 3, 0, 4).reshape(32, 2, 2816).astype(F32)


def unpack_merge(pieces):
    return pieces.reshape(4, 2, 16, 256).transpose(0, 2, 1, 3).reshape(64, 512).astype(F32)


def unpack_down(pieces):
    return pieces[:, :PIECE_USED].reshape(4 * PIECE_USED, 512).astype(F32)


def body(
    block_input,
    cotangent,
    norm_gains,
    gains_first,
    gains_second,
    heads_projection_weight,
    heads_first_moment,
    heads_second_moment,
    merge_weight,
    merge_first,
    merge_second,
    gating_weight,
    gating_first,
    gating_second,
    down_weight,
    down_first,
    down_second,
):
    ANY, VMEM = pl.ANY, pltpu.VMEM
    row, col = lax.axis_index("row"), lax.axis_index("col")
    line = col * 4 + row

    def own_rows(values):
        return lax.dynamic_slice_in_dim(values, line * OWN, OWN, axis=0)

    w_heads, gating_own, down_own, inputs, gains = call(
        start_kernel,
        [
            (shape(4, 16, 32, HEADS_COLS + 256), VMEM),
            (shape(4, 32, 2 * HIDDEN), VMEM),
            (shape(PIECE, MODEL_WIDTH), VMEM),
            (shape(SEQ, MODEL_WIDTH), VMEM),
            (shape(4, 8, 128, dtype=F32), VMEM),
        ],
        [
            (heads_projection_weight, VMEM),
            (merge_weight, VMEM),
            (gating_weight, VMEM),
            (down_weight, VMEM),
            (block_input, VMEM),
            (norm_gains.reshape(8, 128), VMEM),
        ],
        [
            pltpu.VMEM((4, 32, HEADS_COLS), BF16),
            pltpu.VMEM((4, 32, 256), BF16),
            pltpu.VMEM((4, 32, 2 * HIDDEN), BF16),
            pltpu.VMEM((4, PIECE, 512), BF16),
        ],
        100,
        0,
        2**24,
    )
    gains = gains.reshape(4, 2, 512).transpose(1, 0, 2).reshape(2, MODEL_WIDTH)
    input_rows = own_rows(inputs)
    cosine, sine = rope_tables()
    normed_one, query, pair, sums, attended, w_merge, merged, back, w_down = call(
        forward_kernel,
        [
            (shape(SEQ, MODEL_WIDTH), VMEM),
            (shape(SEQ, 256), VMEM),
            (shape(SEQ, 128), VMEM),
            (shape(SEQ, 128, dtype=F32), VMEM),
            (shape(SEQ, 256), VMEM),
            (shape(256, MODEL_WIDTH), VMEM),
            (shape(SEQ, MODEL_WIDTH), VMEM),
            (shape(SEQ, MODEL_WIDTH), VMEM),
            (shape(16 * PIECE, MODEL_WIDTH), VMEM),
        ],
        [
            (inputs, VMEM),
            (gains, VMEM),
            (w_heads, VMEM),
            (cosine, VMEM),
            (sine, VMEM),
            (cotangent, VMEM),
            (down_own, VMEM),
        ],
        [],
        60,
        4,
        2**25,
    )

    middle, grad_middle, branch, gain_part, gating_sum, down_out, down_part = call(
        feedforward_kernel,
        [
            (shape(OWN, MODEL_WIDTH, dtype=F32), VMEM),
            (shape(OWN, MODEL_WIDTH, dtype=F32), VMEM),
            (shape(SEQ, MODEL_WIDTH), VMEM),
            (shape(8, MODEL_WIDTH, dtype=F32), VMEM),
            (shape(4, 32, 2 * HIDDEN), VMEM),
            (shape(SEQ, MODEL_WIDTH), VMEM),
            (shape(16 * PIECE, MODEL_WIDTH), VMEM),
        ],
        [
            (merged, ANY),
            (input_rows, VMEM),
            (gains, VMEM),
            (gating_own, ANY),
            (w_down, VMEM),
            (back, VMEM),
        ],
        LINE_SCATTER_SCRATCH
        + LINE_SCATTER_SCRATCH
        + ring_scatter_scratch(Rows(2 * HIDDEN))
        + [
            pltpu.VMEM((SEQ, MODEL_WIDTH), BF16),
            pltpu.VMEM((SEQ, MODEL_WIDTH), BF16),
            pltpu.VMEM((4, 16, 32, 2 * HIDDEN), BF16),
            pltpu.VMEM((SEQ, HIDDEN), F32),
            pltpu.VMEM((SEQ, HIDDEN), BF16),
            pltpu.VMEM((SEQ, 2 * HIDDEN), BF16),
            pltpu.VMEM((OWN, MODEL_WIDTH), BF16),
        ],
        160,
        1,
        2**25,
    )

    merge_part = token_product(attended, branch).astype(BF16)
    grad_mixed, normed_one_part, block_output, down_sum, gating_pieces = call(
        backward_kernel,
        [
            (shape(SEQ, HEADS_COLS), VMEM),
            (shape(SEQ, MODEL_WIDTH), VMEM),
            (shape(512, 512), VMEM),
            (shape(PIECE, MODEL_WIDTH), VMEM),
            (shape(4, 32, 2 * HIDDEN), VMEM),
        ],
        [
            (branch, VMEM),
            (w_merge, VMEM),
            (w_heads, VMEM),
            (query, VMEM),
            (pair, VMEM),
            (sums[:, :8].T, VMEM),
            (cosine, VMEM),
            (sine, VMEM),
            (down_out, VMEM),
            (middle, VMEM),
            (down_part, ANY),
            (gating_sum, VMEM),
        ],
        LINE_SCATTER_SCRATCH
        + ring_scatter_scratch(Flat())
        + [
            pltpu.VMEM((SEQ, 256), BF16),
            pltpu.VMEM((SEQ, HEAD_SIZE), F32),
            pltpu.VMEM((SEQ, HEAD_SIZE), F32),
            pltpu.VMEM((HEAD_SIZE, SEQ), BF16),
            pltpu.VMEM((OWN, MODEL_WIDTH), BF16),
            pltpu.VMEM((16 * PIECE, MODEL_WIDTH), BF16),
        ],
        100,
        5,
        2**25,
    )
    heads_part = token_product(normed_one, grad_mixed).astype(BF16)

    input_grad, gains_grad, heads_pieces, merge_pieces, down_pieces = call(
        finish_kernel,
        [
            (shape(512, 512), VMEM),
            (shape(8, 512, dtype=F32), VMEM),
            (shape(4, 32, HEADS_COLS), VMEM),
            (shape(4, 32, 256), VMEM),
            (shape(4, PIECE, 512), VMEM),
        ],
        [
            (normed_one_part, VMEM),
            (grad_middle, VMEM),
            (input_rows, VMEM),
            (gains, VMEM),
            (gain_part, VMEM),
            (heads_part, VMEM),
            (merge_part, VMEM),
            (down_sum, VMEM),
        ],
        LINE_SCATTER_SCRATCH
        + ring_scatter_scratch(Rows(HEADS_COLS + 256))
        + [
            pltpu.VMEM((4, 16, 32, HEADS_COLS + 256), BF16),
            pltpu.VMEM((4, 32, HEADS_COLS + 256), BF16),
            pltpu.VMEM((OWN, MODEL_WIDTH), BF16),
            pltpu.VMEM((2, 8, MODEL_WIDTH), F32),
            pltpu.VMEM((4, 2, 8, 512), F32),
            pltpu.VMEM((32, 8, 512), F32),
        ],
        140,
        3,
        2**25,
    )
    input_grad = input_grad.astype(F32)
    gains_grad = gains_grad[:2]
    heads_grad = unpack_heads(heads_pieces)
    merge_grad = unpack_merge(merge_pieces)
    gating_grad = unpack_gating(gating_pieces)
    down_grad = unpack_down(down_pieces)
    gains_next, gains_mean, gains_square = adamw(
        norm_gains, gains_grad, gains_first, gains_second, RATE_GAIN, 0.0
    )
    heads_next, heads_mean, heads_square = adamw(
        heads_projection_weight,
        heads_grad,
        heads_first_moment,
        heads_second_moment,
        RATE_MATRIX,
        WEIGHT_DECAY,
    )
    merge_next, merge_mean, merge_square = adamw(
        merge_weight, merge_grad, merge_first, merge_second, RATE_MERGE, WEIGHT_DECAY
    )
    gating_next, gating_mean, gating_square = adamw(
        gating_weight, gating_grad, gating_first, gating_second, RATE_MATRIX, WEIGHT_DECAY
    )
    down_next, down_mean, down_square = adamw(
        down_weight, down_grad, down_first, down_second, RATE_MATRIX, WEIGHT_DECAY
    )
    return (
        block_output,
        input_grad,
        gains_grad,
        gains_next,
        gains_mean,
        gains_square,
        heads_grad,
        heads_next,
        heads_mean,
        heads_square,
        merge_grad,
        merge_next,
        merge_mean,
        merge_square,
        gating_grad,
        gating_next,
        gating_mean,
        gating_square,
        down_grad,
        down_next,
        down_mean,
        down_square,
    )


def solution(mesh):
    in_specs = (
        P(("dp", "col"), "row"),
        P(("dp", "col"), "row"),
        P(None, "row"),
        P(None, "row"),
        P(None, "row"),
        P(("row", "dp"), "col"),
        P(("row", "dp"), "col"),
        P(("row", "dp"), "col"),
        P(("col", "dp"), "row"),
        P(("col", "dp"), "row"),
        P(("col", "dp"), "row"),
        P(("row", "dp"), None, "col"),
        P(("row", "dp"), None, "col"),
        P(("row", "dp"), None, "col"),
        P(("col", "dp"), "row"),
        P(("col", "dp"), "row"),
        P(("col", "dp"), "row"),
    )
    out_specs = (
        P(("dp", "col"), "row"),
        P(("dp", "col"), "row"),
        P(None, "row"),
        P(None, "row"),
        P(None, "row"),
        P(None, "row"),
        P(("row", "dp"), "col"),
        P(("row", "dp"), "col"),
        P(("row", "dp"), "col"),
        P(("row", "dp"), "col"),
        P(("col", "dp"), "row"),
        P(("col", "dp"), "row"),
        P(("col", "dp"), "row"),
        P(("col", "dp"), "row"),
        P(("row", "dp"), None, "col"),
        P(("row", "dp"), None, "col"),
        P(("row", "dp"), None, "col"),
        P(("row", "dp"), None, "col"),
        P(("col", "dp"), "row"),
        P(("col", "dp"), "row"),
        P(("col", "dp"), "row"),
        P(("col", "dp"), "row"),
    )
    return jax.shard_map(body, mesh=mesh, in_specs=in_specs, out_specs=out_specs, check_vma=False)
```

```python
import functools
import math

import jax
import jax.numpy as jnp
from jax import lax
from jax.experimental import pallas as pl
from jax.experimental.pallas import tpu as pltpu
from jax.sharding import PartitionSpec as P

MODEL_WIDTH = 2048
KEY_VALUE_HEADS = 4
HEAD_SIZE = 64
QUERY_PER_GROUP = 8
STEP = 10


EPS_NORM = 1e-05
BETA_ONE = 0.9
BETA_TWO = 0.95
EPS_ADAM = 1e-08
RATE_MATRIX = 0.05
RATE_MERGE = 0.5
RATE_GAIN = 1.0
WEIGHT_DECAY = 0.1
ROPE_BASE = 10000.0
MASK_FILL = -1e30

MESH = pl.DeviceIdType.MESH
VMEM_BYTES = 63 * 2**20
BF16 = jnp.bfloat16
F32 = jnp.float32

SEQ = 1024
OWN = 128
HEADS_COLS = 384
HIDDEN = 768
PIECE = 48
PIECE_USED = 44


class Place:
    def __init__(self):
        self.dp = lax.axis_index("dp")
        self.row = lax.axis_index("row")
        self.col = lax.axis_index("col")
        self.y = lax.div(self.dp, 4)
        self.z = lax.rem(self.dp, 4)
        self.core = lax.rem(self.row, 2)
        self.x = self.col * 2 + lax.div(self.row, 2)

    def near(self, x=0, core=0, y=0, z=0):
        new_x = lax.rem(self.x + x + 4, 4)
        new_core = lax.rem(self.core + core, 2)
        new_y = lax.rem(self.y + y + 4, 4)
        new_z = lax.rem(self.z + z + 4, 4)
        return {
            "dp": new_y * 4 + new_z,
            "row": lax.rem(new_x, 2) * 2 + new_core,
            "col": lax.div(new_x, 2),
        }

    def slot(self, first_axis, first, second):
        y, z = (first, second) if first_axis == "y" else (second, first)
        return lax.rem(self.y + y + 4, 4) * 4 + lax.rem(self.z + z + 4, 4)

    def line(self, x, core):
        return lax.rem(self.x + x + 4, 4) * 2 + lax.rem(self.core + core, 2)

    def peer(self, step):
        other = lax.rem(self.row + step, 4)
        return other, {"dp": self.dp, "row": other, "col": self.col}


class Wires:
    def __init__(self, send, recv, local, parent=None):
        self.send, self.recv, self.local = send, recv, local
        self.root = parent or self
        self.count = 0
        self.local_count = 0
        self.sent = []

    def part(self):
        return Wires(self.send, self.recv, self.local, self.root)

    def push(self, source, target, device):
        index = self.root.count
        self.root.count += 1
        copy = pltpu.make_async_remote_copy(
            src_ref=source,
            dst_ref=target,
            send_sem=self.send.at[index],
            recv_sem=self.recv.at[index],
            device_id=device,
            device_id_type=MESH,
        )
        copy.start()
        self.sent.append(copy)
        return copy

    def keep(self, source, target):
        copy = pltpu.make_async_copy(source, target, self.local.at[self.root.local_count])
        self.root.local_count += 1
        copy.start()
        return copy

    def settle(self, copies):
        for copy in copies:
            copy.wait_send()
        self.sent = [copy for copy in self.sent if all(copy is not other for other in copies)]

    def drain(self):
        self.settle(list(self.sent))


def meet(devices, more=0):
    barrier = pltpu.get_barrier_semaphore()
    for device in devices:
        pl.semaphore_signal(barrier, inc=1, device_id=device, device_id_type=MESH)
    pl.semaphore_wait(barrier, len(devices))


def interleave(*plans):
    waiting = [[next(plan), order, plan] for order, plan in enumerate(plans)]
    while waiting:
        waiting.sort(key=lambda entry: (entry[0], entry[1]))
        entry = waiting[0]
        try:
            entry[0] = max(entry[0], next(entry[2]))
        except StopIteration:
            waiting.pop(0)


def sweep(wires, since, until):
    yield since
    sent = [copy for account in wires for copy in account.sent]
    yield until
    for account in wires:
        account.settle([copy for copy in sent if any(copy is other for other in account.sent)])


def ring_neighbours(place):
    return [place.near(y=1), place.near(y=-1), place.near(z=1), place.near(z=-1)]


def line_neighbours(place):
    return [place.near(x=1), place.near(x=-1), place.near(core=1)]


def line_gather(place, wires, own, out, block, half, times, ready=None):
    me = place.line(0, 0)
    yield times[0]
    kept = wires.keep(own, block(out, me))
    right = wires.push(own, block(out, me), place.near(x=1))
    left = wires.push(own, block(out, me), place.near(x=-1))
    beside = [wires.push(own, block(out, me), place.near(core=1))]
    yield times[1]
    right.wait_recv()
    came = place.line(-1, 0)
    far_right = wires.push(half(out, came, 0), half(out, came, 0), place.near(x=1))
    beside.append(wires.push(block(out, came), block(out, came), place.near(core=1)))
    left.wait_recv()
    came = place.line(1, 0)
    far_left = wires.push(half(out, came, 1), half(out, came, 1), place.near(x=-1))
    beside.append(wires.push(block(out, came), block(out, came), place.near(core=1)))
    yield times[2]
    kept.wait()
    for copy in beside:
        copy.wait_recv()
    if ready:
        ready((0, 1, -1))
    far_right.wait_recv()
    far_left.wait_recv()
    came = place.line(2, 0)
    last = wires.push(block(out, came), block(out, came), place.near(core=1))
    yield times[3]
    last.wait_recv()
    if ready:
        ready((2,))


def token_block(ref, index):
    return ref.at[pl.ds(pl.multiple_of(index * OWN, OWN), OWN)]


def token_half(ref, index, side):
    return ref.at[pl.ds(pl.multiple_of(index * OWN + side * (OWN // 2), OWN // 2), OWN // 2)]


def tile_block(ref, index):
    x, core = lax.div(index, 2), lax.rem(index, 2)
    rows = pl.ds(pl.multiple_of(lax.div(x, 2) * 512, 512), 512)
    columns = pl.ds(pl.multiple_of((lax.rem(x, 2) * 2 + core) * 512, 512), 512)
    return ref.at[rows, columns]


def tile_half(ref, index, side):
    x, core = lax.div(index, 2), lax.rem(index, 2)
    rows = pl.ds(pl.multiple_of(lax.div(x, 2) * 512 + side * 256, 256), 256)
    columns = pl.ds(pl.multiple_of((lax.rem(x, 2) * 2 + core) * 512, 512), 512)
    return ref.at[rows, columns]


def add_rows(out, terms, rows, step=16):
    def chunk(index, carry):
        at = pl.ds(pl.multiple_of(index * step, step), step)
        out[at, :] = functools.reduce(
            lambda a, b: a + b, [term[at, :].astype(F32) for term in terms]
        ).astype(out.dtype)
        return carry

    lax.fori_loop(0, rows // step, chunk, 0)


LINE_SCATTER_SCRATCH = [
    pltpu.VMEM((4, OWN, MODEL_WIDTH), BF16),
    pltpu.VMEM((2, OWN // 2, MODEL_WIDTH), BF16),
    pltpu.VMEM((2, OWN, MODEL_WIDTH), BF16),
    pltpu.VMEM((3, OWN, MODEL_WIDTH), BF16),
]


class LineScatter:
    def __init__(self, place, wires, part, scratch):
        self.place, self.wires, self.part = place, wires, part
        self.beside, self.halves, self.full, self.total = scratch
        self.pairs, self.late = {}, []

    def pair(self, offset):
        self.pairs[offset] = self.wires.push(
            token_block(self.part, self.place.line(offset, 1)),
            self.beside.at[offset],
            self.place.near(core=1),
        )

    def own(self, offset):
        return token_block(self.part, self.place.line(offset, 0))

    def far(self):
        self.pairs[2].wait_recv()
        total = self.total.at[2]
        add_rows(total, [self.own(2), self.beside.at[2]], OWN)
        self.far_right = self.wires.push(
            total.at[pl.ds(0, OWN // 2)], self.halves.at[0], self.place.near(x=1)
        )
        self.far_left = self.wires.push(
            total.at[pl.ds(OWN // 2, OWN // 2)], self.halves.at[1], self.place.near(x=-1)
        )

    def near(self, offset):
        way, step, first = (0, 1, OWN // 2) if offset == 1 else (1, -1, 0)
        self.pairs[offset].wait_recv()
        add_rows(self.total.at[way], [self.own(offset), self.beside.at[offset]], OWN)
        self.send(way, step, first)

    def send(self, way, step, first):
        rows = pl.ds(first, OWN // 2)
        self.late.append(
            self.wires.push(
                self.total.at[way, rows], self.full.at[way, rows], self.place.near(x=step)
            )
        )

    def join(self):
        for copy, way, step, first in (
            (self.far_right, 0, 1, 0),
            (self.far_left, 1, -1, OWN // 2),
        ):
            copy.wait_recv()
            rows = self.total.at[way, pl.ds(first, OWN // 2)]
            add_rows(rows, [rows, self.halves.at[way]], OWN // 2)
            self.send(way, step, first)

    def finish(self):
        self.pairs[0].wait_recv()
        for copy in self.late:
            copy.wait_recv()

    def terms(self):
        return [self.own(0), self.beside.at[0], self.full.at[0], self.full.at[1]]

    def total_of(self, at):
        return functools.reduce(lambda a, b: a + b, [t[at, :].astype(F32) for t in self.terms()])

    def run(self, start, cost):
        yield start
        for offset in (2, 1, 3, 0):
            self.pair(offset)
        yield start + 2
        self.far()
        yield start + 3
        self.near(1)
        self.near(3)
        yield from self.rest(start, cost)

    def rest(self, start, cost):
        yield start + 5 + 0.5 * cost
        self.join()
        yield start + 3.5 + 1.4 * cost
        self.finish()


class Rows:
    def __init__(self, columns):
        self.item_shape = (2, 32, columns)
        self.half_shape = (1, 32, columns)

    def item(self, ref, side, slot):
        return ref.at[pl.ds(2 * side, 2), slot]

    def half(self, ref, side, part, slot):
        return ref.at[pl.ds(2 * side + part, 1), slot]

    def cut(self, item, part):
        return item.at[pl.ds(part, 1)]


class Flat:
    def __init__(self):
        self.item_shape = (PIECE, MODEL_WIDTH // 2)
        self.half_shape = (PIECE, MODEL_WIDTH // 4)

    def item(self, ref, side, slot):
        rows = pl.ds(pl.multiple_of(slot * PIECE, PIECE), PIECE)
        return ref.at[rows, pl.ds(side * (MODEL_WIDTH // 2), MODEL_WIDTH // 2)]

    def half(self, ref, side, part, slot):
        rows = pl.ds(pl.multiple_of(slot * PIECE, PIECE), PIECE)
        return ref.at[rows, pl.ds((2 * side + part) * (MODEL_WIDTH // 4), MODEL_WIDTH // 4)]

    def cut(self, item, part):
        return item.at[:, pl.ds(part * (MODEL_WIDTH // 4), MODEL_WIDTH // 4)]


def ring_move(place, axis, step):
    return place.near(y=step) if axis == "y" else place.near(z=step)


def ring_gather(place, wires, kind, out, side, times):
    first, second = ("z", "y") if side == 0 else ("y", "z")
    slot = functools.partial(place.slot, first)
    spread = {}

    def send_on(offset):
        item = kind.item(out, side, slot(offset, 0))
        spread[offset] = [
            wires.push(item, item, ring_move(place, second, step)) for step in (1, -1)
        ]

    def pass_on(offset):
        right, left = spread[offset]
        right.wait_recv()
        piece = kind.half(out, side, 0, slot(offset, -1))
        one = wires.push(piece, piece, ring_move(place, second, 1))
        left.wait_recv()
        piece = kind.half(out, side, 1, slot(offset, 1))
        return [one, wires.push(piece, piece, ring_move(place, second, -1))]

    yield times[0]
    own = kind.item(out, side, slot(0, 0))
    right = wires.push(own, own, ring_move(place, first, 1))
    left = wires.push(own, own, ring_move(place, first, -1))
    send_on(0)
    yield times[1]
    right.wait_recv()
    piece = kind.half(out, side, 0, slot(-1, 0))
    far_right = wires.push(piece, piece, ring_move(place, first, 1))
    send_on(-1)
    left.wait_recv()
    piece = kind.half(out, side, 1, slot(1, 0))
    far_left = wires.push(piece, piece, ring_move(place, first, -1))
    send_on(1)
    last = []
    yield times[2]
    last += pass_on(0)
    yield times[3]
    far_right.wait_recv()
    far_left.wait_recv()
    send_on(2)
    yield times[4]
    last += pass_on(-1)
    yield times[5]
    last += pass_on(1)
    yield times[6]
    last += pass_on(2)
    yield times[7]
    for copy in last:
        copy.wait_recv()


RING_SCATTER_SCRATCH = 8


def ring_scatter_scratch(kind):
    def stack(count, shape):
        return pltpu.VMEM((count, *shape), BF16)

    one_side = [
        stack(8, kind.half_shape),
        stack(8, kind.item_shape),
        stack(2, kind.half_shape),
        stack(2, kind.item_shape),
    ]
    return one_side + one_side


def add_to(out, *terms):
    out[...] = functools.reduce(
        lambda a, b: a + b, [t[...].astype(F32) for t in (out, *terms)]
    ).astype(out.dtype)


def ring_scatter(place, wires, kind, part, side, scratch, result, start, cost):
    far, came, far_last, came_last = scratch[4 * side : 4 * side + 4]
    first, second = ("z", "y") if side == 0 else ("y", "z")
    slot = functools.partial(place.slot, first)
    order = (2, 1, -1, 0)
    yield start
    right, left = {}, {}
    for n, offset in enumerate(order):
        target = slot(offset, 2)
        right[offset] = wires.push(
            kind.half(part, side, 0, target), far.at[2 * n], ring_move(place, second, 1)
        )
        left[offset] = wires.push(
            kind.half(part, side, 1, target), far.at[2 * n + 1], ring_move(place, second, -1)
        )

    moved = {}
    for n, offset in enumerate(order):
        yield start + 2.5 + (0.5 + n) * cost
        right[offset].wait_recv()
        add_to(kind.half(part, side, 0, slot(offset, 1)), far.at[2 * n])
        item = kind.item(part, side, slot(offset, 1))
        one = wires.push(item, came.at[2 * n], ring_move(place, second, 1))
        left[offset].wait_recv()
        add_to(kind.half(part, side, 1, slot(offset, -1)), far.at[2 * n + 1])
        item = kind.item(part, side, slot(offset, -1))
        two = wires.push(item, came.at[2 * n + 1], ring_move(place, second, -1))
        moved[offset] = (one, two)

    def finish(n, offset):
        for copy in moved[offset]:
            copy.wait_recv()
        add_to(kind.item(part, side, slot(offset, 0)), came.at[2 * n], came.at[2 * n + 1])

    yield start + 4 + 3 * cost
    finish(0, 2)
    far_right = wires.push(
        kind.half(part, side, 0, slot(2, 0)), far_last.at[0], ring_move(place, first, 1)
    )
    far_left = wires.push(
        kind.half(part, side, 1, slot(2, 0)), far_last.at[1], ring_move(place, first, -1)
    )
    yield start + 4 + 4 * cost
    finish(1, 1)
    yield start + 4 + 5 * cost
    finish(2, -1)
    far_right.wait_recv()
    add_to(kind.half(part, side, 0, slot(1, 0)), far_last.at[0])
    item = kind.item(part, side, slot(1, 0))
    one = wires.push(item, came_last.at[0], ring_move(place, first, 1))
    far_left.wait_recv()
    add_to(kind.half(part, side, 1, slot(-1, 0)), far_last.at[1])
    item = kind.item(part, side, slot(-1, 0))
    two = wires.push(item, came_last.at[1], ring_move(place, first, -1))
    yield start + 5 + 6 * cost
    finish(3, 0)
    yield start + 8 + 7.5 * cost
    one.wait_recv()
    two.wait_recv()
    own = kind.item(part, side, slot(0, 0))
    add_to(own, came_last.at[0], came_last.at[1])
    result[...] = own[...]


def call(kernel, outs, ins, scratch, wires, name, cost):
    return pl.pallas_call(
        kernel,
        out_shape=[shape for shape, _ in outs],
        in_specs=[pl.BlockSpec(memory_space=space) for _, space in ins],
        out_specs=[pl.BlockSpec(memory_space=space) for _, space in outs],
        scratch_shapes=list(scratch)
        + [
            pltpu.SemaphoreType.DMA((wires,)),
            pltpu.SemaphoreType.DMA((wires,)),
            pltpu.SemaphoreType.DMA((48,)),
        ],
        compiler_params=pltpu.CompilerParams(
            collective_id=name, has_side_effects=True, vmem_limit_bytes=VMEM_BYTES
        ),
        cost_estimate=pl.CostEstimate(flops=0, bytes_accessed=cost, transcendentals=0),
    )(*[array for array, _ in ins])


def shape(*extent, dtype=BF16):
    return jax.ShapeDtypeStruct(extent, dtype)


def merge_devices(place):
    users = [{"dp": j * 4 + place.z, "row": place.y, "col": place.col} for j in range(4)]
    homes = [
        {"dp": place.row * 4 + place.z, "row": jnp.int32(row), "col": place.col} for row in range(4)
    ]
    return users, homes


def signal_others(place, devices):
    barrier = pltpu.get_barrier_semaphore()
    for device in devices:
        alone = (device["dp"] == place.dp) & (device["row"] == place.row)

        @pl.when(jnp.logical_not(alone))
        def _():
            pl.semaphore_signal(barrier, inc=1, device_id=device, device_id_type=MESH)


def merge_exchange(place, wires, devices, source, target, mine):
    base = wires.count
    wires.count += 4
    copies = []
    for index, device in enumerate(devices):
        copy = pltpu.make_async_remote_copy(
            src_ref=source(index),
            dst_ref=target(index),
            send_sem=wires.send.at[base + index],
            recv_sem=wires.recv.at[base + mine],
            device_id=device,
            device_id_type=MESH,
        )
        here = pltpu.make_async_copy(source(index), target(index), wires.recv.at[base + mine])
        alone = (device["dp"] == place.dp) & (device["row"] == place.row)
        copies.append((copy, alone))
        pl.when(alone)(here.start)
        pl.when(jnp.logical_not(alone))(copy.start)

    def wait():
        for index in range(4):
            pltpu.make_async_copy(source(0), target(0), wires.recv.at[base + index]).wait()
        for copy, alone in copies:
            pl.when(jnp.logical_not(alone))(copy.wait_send)

    return wait


def nested(plans):
    pending = [[next(plan), order, plan] for order, plan in enumerate(plans)]
    while pending:
        pending.sort(key=lambda entry: entry[:2])
        entry = pending[0]
        yield entry[0]
        try:
            entry[0] = max(entry[0], next(entry[2]))
        except StopIteration:
            pending.pop(0)


def column_block(ref, row):
    return ref.at[:, pl.ds(pl.multiple_of(row * 512, 512), 512)]


def down_slot(ref, slot, row):
    rows = pl.ds(pl.multiple_of(slot * PIECE, PIECE), PIECE)
    return ref.at[rows, pl.ds(pl.multiple_of(row * 512, 512), 512)]


def own_token_rows(ref, row):
    return ref.at[pl.ds(pl.multiple_of(row * OWN, OWN), OWN)]


def recut(place, wires, own, out, when):
    peers = [place.peer(step) for step in (1, 2, 3)]
    kept = wires.keep(column_block(own, place.row), own_token_rows(out, place.row))
    moved = [
        wires.push(column_block(own, other), own_token_rows(out, place.row), device)
        for other, device in peers
    ]
    yield when
    kept.wait()
    for copy in moved:
        copy.wait_recv()


def back_pieces(place, wires, part_of, out, when):
    peers = [place.peer(step) for step in (1, 2, 3)]
    kept = wires.keep(part_of(place.row), out.at[place.row])
    moved = [wires.push(part_of(other), out.at[place.row], device) for other, device in peers]
    yield when
    kept.wait()
    for copy in moved:
        copy.wait_recv()


HEADS_TIMES = (2.6, 10.6, 11.5, 18.0, 19.8, 20.7, 24.5, 29.0)
DOWN_TIMES = (3.2, 12.1, 13.0, 20.8, 24.6, 25.5, 30.0, 35.0)
GATING_TIMES = (24.7, 38.0, 41.0, 49.0, 53.5, 57.0, 62.0, 68.0)


def opening_kernel(
    heads_weight, merge_weight, gating_weight, down_weight, input_own, back_own, gains_own,
    *refs,
):
    (
        normed_out, query_out, pair_out, sums_out, cosine_out, sine_out, attended_out, merge_out,
        heads_out, middle_out, grad_middle_out, branch_out, gain_part_out, gating_sum_out,
        down_part_out, down_out, gains_out, input_rows_out,
    ) = refs[:18]
    line_scratch, scratch = refs[18:22], refs[22:]
    ring_scratch, scratch = scratch[:RING_SCATTER_SCRATCH], scratch[RING_SCATTER_SCRATCH:]
    (
        tokens, part, back, gating, grad_hidden, hidden, grad_gated, rows_own,
        heads_cut, merge_cut, gating_cut, down_cut,
        query, pair, sums, cosine, sine, attended, merge, heads, middle, grad_middle, branch,
        gain_part, gating_sum, down, gains, input_rows,
        send, recv, local,
    ) = scratch
    handed = []

    def hand(*pairs):
        handed.extend(wires.keep(source, target) for source, target in pairs)

    place = Place()
    wires = Wires(send, recv, local)
    first_wires, token_wires, gating_wires, down_wires = [wires.part() for _ in range(4)]
    users, homes = merge_devices(place)
    peers = [place.peer(step) for step in (1, 2, 3)]
    same = place.row == place.y
    devices = ring_neighbours(place) + line_neighbours(place) + [p for _, p in peers]
    signal_others(place, devices + homes)
    for row in range(4):
        group, half = divmod(row, 2)
        rows = heads_weight[:, pl.ds(group * 640 + half * 256, 256)]
        heads_cut[row, :, pl.ds(0, 256)] = rows.astype(BF16)
        rows = heads_weight[:, pl.ds(group * 640 + 512, 128)]
        heads_cut[row, :, pl.ds(256, 128)] = rows.astype(BF16)
        for side in range(2):
            piece = merge_weight[pl.ds(16 * row, 16), pl.ds(256 * side, 256)]
            merge_cut[row, pl.ds(16 * side, 16)] = piece.astype(BF16)
    pl.semaphore_wait(
        pltpu.get_barrier_semaphore(), len(devices) + 4 - same.astype(jnp.int32)
    )
    down_came, gating_came = [], []

    def exchange():
        def heads_columns(row, slot):
            return heads.at[row, slot, :, pl.ds(0, HEADS_COLS)]

        yield 0.0
        came = [wires.keep(heads_cut.at[place.row], heads_columns(place.row, place.dp)).wait]
        came.append(wires.keep(gains_own, column_block(gains, place.row)).wait)
        came += [
            wires.push(heads_cut.at[other], heads_columns(place.row, place.dp), device).wait_recv
            for other, device in peers
        ]
        came.append(
            merge_exchange(
                place, wires, users,
                lambda j: merge_cut.at[j],
                lambda j: heads.at[place.row, j * 4 + place.z, :, pl.ds(HEADS_COLS, 256)],
                place.row,
            )
        )
        came += [
            wires.push(gains_own, column_block(gains, place.row), device).wait_recv
            for _, device in peers
        ]
        for row in range(4):
            piece = down_weight[pl.ds(PIECE_USED * row, PIECE_USED), :]
            down_cut[row] = jnp.concatenate(
                [piece, jnp.zeros((PIECE - PIECE_USED, 512), F32)], axis=0
            ).astype(BF16)
        target = down_slot(down, place.dp, place.row)
        down_came.append(wires.keep(down_cut.at[place.row], target).wait)
        down_came.extend(
            wires.push(down_cut.at[other], target, device).wait_recv for other, device in peers
        )
        yield 2.6
        for wait in came:
            wait()
        yield from nested(
            ring_gather(place, wires, Rows(HEADS_COLS + 256), heads, side, HEADS_TIMES)
            for side in (0, 1)
        )

    def gating_exchange():
        yield 3.0
        zeros = jnp.zeros((32, PIECE - PIECE_USED), F32)
        for kind in range(2):
            for row in range(4):
                pieces = []
                for slot in range(16):
                    first = slot * 4 * PIECE_USED + row * PIECE_USED
                    pieces += [gating_weight[:, kind, pl.ds(first, PIECE_USED)], zeros]
                gating_cut[row, :, pl.ds(kind * HIDDEN, HIDDEN)] = jnp.concatenate(
                    pieces, axis=1
                ).astype(BF16)
        target = gating.at[place.row, place.dp]
        gating_came.append(wires.keep(gating_cut.at[place.row], target).wait)
        gating_came.extend(
            wires.push(gating_cut.at[other], target, device).wait_recv for other, device in peers
        )

    def tables():
        yield 3.4
        rope_tables(cosine, sine)

    def down_rows():
        yield 3.2
        for wait in down_came:
            wait()
        yield from nested(
            ring_gather(place, down_wires, Flat(), down, side, DOWN_TIMES) for side in (0, 1)
        )

    def gating_rows():
        yield 24.7
        for wait in gating_came:
            wait()
        yield from nested(
            ring_gather(place, gating_wires, Rows(2 * HIDDEN), gating, side, GATING_TIMES)
            for side in (0, 1)
        )

    def chip_rows(offset):
        start = pl.multiple_of(lax.rem(place.x + offset + 4, 4) * 256, 256)
        return pl.ds(start, 256)

    def grad_hidden_rows():
        for index in range(4):
            yield 58.0 + 1.4 * index
            at = pl.ds(index * 256, 256)
            grad_hidden[at, :] = contract_last(back[at, :], down[...])

    def forward(offset, when):
        at = chip_rows(offset)
        for tile in range(3):
            gate_at, up_at = pl.ds(tile * 256, 256), pl.ds(HIDDEN + tile * 256, 256)
            rows = tokens[at, :]
            gate = product(rows, gating[:, :, :, gate_at].reshape(MODEL_WIDTH, 256))
            up = product(rows, gating[:, :, :, up_at].reshape(MODEL_WIDTH, 256))
            grad = grad_hidden[at, gate_at]
            sigmoid = jax.nn.sigmoid(gate)
            silu = gate * sigmoid
            hidden[at, gate_at] = (silu * up).astype(BF16)
            grad_gated[at, gate_at] = (grad * up * sigmoid * (1.0 + gate * (1.0 - sigmoid))).astype(
                BF16
            )
            grad_gated[at, up_at] = (grad * silu).astype(BF16)
            yield when + 0.6 * (tile + 1)
        for row in range(4):
            part[at, pl.ds(row * 512, 512)] = contract_last(
                grad_gated[at, :], gating[row].reshape(512, 2 * HIDDEN)
            ).astype(BF16)
            if row % 2:
                yield when + 2.0 + 0.6 * row

    def main():
        yield 0.1
        yield from line_gather(
            place, token_wires, input_own, tokens, tile_block, tile_half, (0.1, 15.0, 26.5, 28.5)
        )
        input_rows[...] = token_block(tokens, place.line(0, 0))[...]
        yield 29.2
        normed = branch
        first = LineScatter(place, first_wires, part, line_scratch)
        yield from projections(
            tokens, gains, heads, cosine, sine, normed, query, pair, merge,
        )
        normed_copy = wires.keep(normed, normed_out)
        token_wires.drain()
        for order, offset in enumerate((2, 1, -1, 0)):
            at = chip_rows(offset)
            attention(at, lax.rem(place.x + offset + 4, 4), query, pair, sums, attended)
            part[at, :] = product(attended[at, :], merge[...]).astype(BF16)
            first.pair(offset % 4)
            if order == 1:
                first.far()
            elif order == 2:
                first.near(1)
            yield 34.3 + 3.8 * (order + 1)
        first.near(3)
        hand(
            (query, query_out), (pair, pair_out), (sums, sums_out), (cosine, cosine_out),
            (sine, sine_out), (attended, attended_out), (merge, merge_out), (heads, heads_out),
            (gains, gains_out), (input_rows, input_rows_out),
        )
        yield 52.0
        first.join()
        yield 63.0
        first.finish()

        def chunk(index, carry):
            at = pl.ds(pl.multiple_of(index * 16, 16), 16)
            total = first.total_of(at) + input_rows[at, :].astype(F32)
            middle[at, :] = total
            scale = lax.rsqrt(
                jnp.sum(total * total, axis=1, keepdims=True) / MODEL_WIDTH + EPS_NORM
            )
            rows_own[at, :] = (total * scale * gains[1:2, :]).astype(BF16)
            return carry

        lax.fori_loop(0, OWN // 16, chunk, 0)
        first_wires.drain()
        normed_copy.wait()
        hand((middle, middle_out))
        me, block, half = place.line(0, 0), token_block, token_half
        mine = wires.keep(rows_own, block(tokens, me))
        right = token_wires.push(rows_own, block(tokens, me), place.near(x=1))
        left = token_wires.push(rows_own, block(tokens, me), place.near(x=-1))
        beside = token_wires.push(rows_own, block(tokens, me), place.near(core=1))

        def pass_beside(offset):
            came = block(tokens, place.line(offset, 0))
            return token_wires.push(came, came, place.near(core=1))

        second = LineScatter(place, wires, part, line_scratch)
        yield 70.0
        mine.wait()
        beside.wait_recv()
        yield from forward(0, 70.0)
        second.pair(0)
        yield 78.5
        right.wait_recv()
        piece = half(tokens, place.line(-1, 0), 0)
        far_right = token_wires.push(piece, piece, place.near(x=1))
        beside_left = pass_beside(-1)
        left.wait_recv()
        piece = half(tokens, place.line(1, 0), 1)
        far_left = token_wires.push(piece, piece, place.near(x=-1))
        beside_right = pass_beside(1)
        yield 80.5
        beside_left.wait_recv()
        beside_right.wait_recv()
        yield from forward(1, 80.5)
        second.pair(1)
        yield 84.1
        yield from forward(-1, 84.1)
        second.pair(3)
        second.near(1)
        yield 87.8
        far_right.wait_recv()
        far_left.wait_recv()
        beside_far = pass_beside(2)
        yield 89.5
        beside_far.wait_recv()
        yield from forward(2, 89.5)
        second.pair(2)
        second.near(3)
        yield 94.5
        second.far()
        yield from second.rest(96.0, 11.4)
        gain_part[...] = jnp.zeros_like(gain_part)
        back_own_rows = token_block(back, place.line(0, 0))

        def chunk_back(index, carry):
            at = pl.ds(pl.multiple_of(index * 16, 16), 16)
            through, gain = norm_back(middle[at, :], gains[1:2, :], second.total_of(at))
            total = back_own_rows[at, :].astype(F32) + through
            grad_middle[at, :] = total
            rows_own[at, :] = total.astype(BF16)
            gain_part[...] += gain.reshape(2, 8, MODEL_WIDTH).sum(axis=0)
            return carry

        token_wires.drain()
        lax.fori_loop(0, OWN // 16, chunk_back, 0)

        def ready(offsets):
            hand(*[(branch.at[chip_rows(o)], branch_out.at[chip_rows(o)]) for o in offsets])

        yield from line_gather(
            place, wires, rows_own, branch, token_block, token_half, (117.2, 131.0, 138.8, 141.0), ready
        )
        hand((grad_middle, grad_middle_out), (gain_part, gain_part_out))

    computed = []

    def gradients():
        yield 94.6
        gating_wires.drain()
        for row in range(4):
            for piece in range(2):
                columns = pl.ds(row * 512 + piece * 256, 256)
                gating[row, pl.ds(8 * piece, 8)] = (
                    token_product(tokens[:, columns], grad_gated[...])
                    .astype(BF16)
                    .reshape(8, 32, 2 * HIDDEN)
                )
                computed.append(row)
                yield 96.0 + 1.05 * (2 * row + piece + 1)

    def gradient_side(side):
        yield 100.3 + 4.2 * side
        assert len(computed) >= 4 + 4 * side
        yield from ring_scatter(
            place, wires, Rows(2 * HIDDEN), gating, side, ring_scratch,
            gating_sum.at[pl.ds(2 * side, 2)], 100.3 + 4.2 * side, 4.3,
        )
        hand((gating_sum.at[pl.ds(2 * side, 2)], gating_sum_out.at[pl.ds(2 * side, 2)]))

    def down_products():
        yield 106.9
        token_wires.drain()
        for index in range(4):
            at = pl.ds(index * 256, 256)
            tokens[at, :] = product(hidden[at, :], down[...]).astype(BF16)
            hand((tokens.at[at], down_out.at[at]))
            yield 107.9 + 1.0 * index
        down_wires.drain()
        for tile in range(3):
            columns = pl.ds(tile * 256, 256)
            down[columns, :] = token_product(hidden[:, columns], back[...]).astype(BF16)
            hand((down.at[columns], down_part_out.at[columns]))
            yield 112.3 + 1.2 * tile

    interleave(
        main(),
        exchange(),
        gating_exchange(),
        tables(),
        down_rows(),
        gating_rows(),
        line_gather(
            place, wires, back_own, back, tile_block, tile_half, (24.0, 38.0, 45.8, 47.8)
        ),
        grad_hidden_rows(),
        gradients(),
        gradient_side(0),
        gradient_side(1),
        down_products(),
        sweep([wires, gating_wires, down_wires], 66.0, 76.5),
        sweep([wires, token_wires], 117.5, 126.0),
    )
    wires.drain()
    for copy in handed:
        copy.wait()


def norm_back(values, gain_row, gradient):
    scale = lax.rsqrt(jnp.sum(values * values, axis=1, keepdims=True) / MODEL_WIDTH + EPS_NORM)
    weighted = gain_row * gradient
    inner = jnp.sum(weighted * values, axis=1, keepdims=True)
    through = scale * weighted - values * (scale * scale * scale * inner / MODEL_WIDTH)
    return through, gradient * values * scale


def turn(tile, cosine, sine):
    lane = lax.broadcasted_iota(jnp.int32, tile.shape, 1)
    first = lax.rem(lane, HEAD_SIZE) < HEAD_SIZE // 2
    swapped = jnp.where(first, pltpu.roll(tile, 96, axis=1), pltpu.roll(tile, 32, axis=1))
    return tile * cosine + swapped * sine


def rope_tables(cosine, sine):
    half_width = HEAD_SIZE // 2

    def chunk(index, carry):
        at = pl.ds(pl.multiple_of(index * 128, 128), 128)
        lane = lax.broadcasted_iota(jnp.int32, (128, 128), 1)
        row = lax.broadcasted_iota(jnp.int32, (128, 128), 0) + index * 128
        frequency = jnp.exp(
            lax.rem(lane, half_width).astype(F32) * (-2.0 / HEAD_SIZE * math.log(ROPE_BASE))
        )
        angles = row.astype(F32) * frequency
        cosine[at, :] = jnp.cos(angles)
        first = lax.rem(lane, HEAD_SIZE) < half_width
        sine[at, :] = jnp.where(first, -jnp.sin(angles), jnp.sin(angles))
        return carry

    lax.fori_loop(0, SEQ // 128, chunk, 0)


def keys_only(cosine, sine):
    key = lax.broadcasted_iota(jnp.int32, cosine.shape, 1) < HEAD_SIZE
    return jnp.where(key, cosine, 1.0), jnp.where(key, sine, 0.0)


def heads_weight_of(heads):
    return heads[:, :, :, pl.ds(0, HEADS_COLS)].reshape(MODEL_WIDTH, HEADS_COLS)


QUERY_BLOCK = 256


def projections(
    inputs, gains, heads, cosine, sine,
    normed, query, pair, merge,
):
    for row in range(4):
        for slot in range(16):
            y, z = divmod(slot, 4)
            for half in range(2):
                merge[pl.ds(z * 64 + y * 16, 16), pl.ds(row * 512 + half * 256, 256)] = heads[
                    row, slot, pl.ds(16 * half, 16), pl.ds(HEADS_COLS, 256)
                ]
    for index in range(4):
        at = pl.ds(index * 256, 256)
        wide = inputs[at, :].astype(F32)
        scale = lax.rsqrt(jnp.sum(wide * wide, axis=1, keepdims=True) / MODEL_WIDTH + EPS_NORM)
        low = (wide * scale * gains[0:1, :]).astype(BF16)
        normed[at, :] = low
        mixed = product(low, heads_weight_of(heads))
        cos, sin = cosine[at, :], sine[at, :]
        query[at, pl.ds(0, 128)] = turn(mixed[:, :128], cos, sin).astype(BF16)
        query[at, pl.ds(128, 128)] = turn(mixed[:, 128:256], cos, sin).astype(BF16)
        pair[at, :] = turn(mixed[:, 256:], *keys_only(cos, sin)).astype(BF16)
        yield 29.2 + 1.25 * (index + 1)


def attention(at, block, query, pair, sums, attended):
    scale = HEAD_SIZE ** (-0.5)
    rows_at = lax.broadcasted_iota(jnp.int32, (QUERY_BLOCK, QUERY_BLOCK), 0)
    keys_at = lax.broadcasted_iota(jnp.int32, (QUERY_BLOCK, QUERY_BLOCK), 1)
    out, logs = [], []
    for two in range(2):
        queries = [
            query[at, pl.ds(head * HEAD_SIZE, HEAD_SIZE)] for head in (2 * two, 2 * two + 1)
        ]

        def weigh(rows, keys):
            return contract_last(rows, pair[keys, pl.ds(0, HEAD_SIZE)]) * scale

        def values(keys):
            return pair[keys, pl.ds(HEAD_SIZE, HEAD_SIZE)]

        state = []
        for rows in queries:
            scores = jnp.where(rows_at >= keys_at, weigh(rows, at), MASK_FILL)
            top = jnp.max(scores, axis=1, keepdims=True)
            powers = jnp.exp(scores - top)
            total = jnp.sum(powers, axis=1, keepdims=True)
            state.append((top, total, product(powers.astype(BF16), values(at))))

        def step(index, state):
            keys = pl.ds(pl.multiple_of(index * QUERY_BLOCK, QUERY_BLOCK), QUERY_BLOCK)
            result = []
            for rows, (top, total, mean) in zip(queries, state):
                scores = weigh(rows, keys)
                higher = jnp.maximum(top, jnp.max(scores, axis=1, keepdims=True))
                shrink = jnp.exp(top - higher)
                powers = jnp.exp(scores - higher)
                total = total * shrink + jnp.sum(powers, axis=1, keepdims=True)
                mean = mean * shrink + product(powers.astype(BF16), values(keys))
                result.append((higher, total, mean))
            return tuple(result)

        for top, total, mean in lax.fori_loop(0, block, step, tuple(state)):
            out.append((mean * (1.0 / total)).astype(BF16))
            logs.append(top + jnp.log(total))
    logs.append(jnp.zeros((QUERY_BLOCK, 124), F32))
    sums[:, at] = jnp.transpose(jnp.concatenate(logs, axis=1))[:8]
    attended[at, :] = jnp.concatenate(out, axis=1)


def backward_kernel(*refs):
    given, refs = refs[:18], refs[18:]
    (
        output, input_grad, gains_grad, heads_pieces, merge_pieces, gating_pieces, down_pieces,
    ) = refs[:7]
    out_scratch, scratch = refs[7:11], refs[11:]
    line_scratch, scratch = scratch[:4], scratch[4:]
    down_scratch, scratch = scratch[:8], scratch[8:]
    heads_scratch, scratch = scratch[:8], scratch[8:]
    held, scratch = scratch[:18], scratch[18:]
    (
        branch, merge, query, pair, sums, cosine, sine, down_out, down_part, gating_sum,
        middle, heads, attended, normed, grad_middle, input_rows, gains, gain_part,
    ) = held
    (
        part, grad_mixed, grad_attended, grad_key, grad_value, key_columns, rows_own,
        down_sum, heads_all, heads_sum, input_grad_own, gain_rows, gain_came, gain_all,
        send, recv, local,
    ) = scratch
    place = Place()
    wires = Wires(send, recv, local)
    loads = [wires.keep(source, target) for source, target in zip(given, held)]

    def need(*names):
        for index in names:
            if loads[index] is not None:
                loads[index].wait()
                loads[index] = None

    users, homes = merge_devices(place)
    peers = [place.peer(step) for step in (1, 2, 3)]
    same = place.row == place.y
    barrier = pltpu.get_barrier_semaphore()
    devices = ring_neighbours(place) + line_neighbours(place) + [p for _, p in peers]
    signal_others(place, devices + users)

    def far(step):
        index = lax.rem(place.col * 16 + place.dp + step, 32)
        return {"dp": lax.rem(index, 16), "row": place.row, "col": lax.div(index, 16)}

    def greet(step, carry):
        pl.semaphore_signal(barrier, inc=1, device_id=far(step), device_id_type=MESH)
        return carry

    lax.fori_loop(1, 32, greet, 0)
    need(0, 1)
    attend = attention_back(
        branch, merge, query, pair, sums, cosine, sine, grad_mixed,
        grad_attended, grad_key, grad_value, key_columns,
    )
    next(attend)
    next(attend)
    pl.semaphore_wait(barrier, len(devices) + 31 + 4 - same.astype(jnp.int32))

    def outputs():
        yield 0.1
        need(7)
        scatter = LineScatter(place, wires, down_out, out_scratch)
        yield from scatter.run(0.1, 11.4)
        need(10)

        def chunk(index, carry):
            at = pl.ds(pl.multiple_of(index * 16, 16), 16)
            rows_own[at, :] = (scatter.total_of(at) + middle[at, :]).astype(BF16)
            return carry

        lax.fori_loop(0, OWN // 16, chunk, 0)
        yield 31.5
        yield from recut(place, wires, rows_own, output, 46.0)

    def down_rows():
        yield 0.3
        need(8)
        yield from nested(
            ring_scatter(
                place, wires, Flat(), down_part, side, down_scratch,
                down_sum.at[:, pl.ds(side * 1024, 1024)], 0.3, 2.1,
            )
            for side in (0, 1)
        )
        yield from back_pieces(
            place, wires, lambda row: column_block(down_sum, row), down_pieces, 45.0
        )

    def gating():
        yield 0.4
        need(9)
        yield from back_pieces(
            place, wires, lambda row: gating_sum.at[row], gating_pieces, 35.0
        )

    def compute():
        yield 0.2
        need(2, 3, 4, 5, 6)
        yield from attend
        need(11)
        scatter = LineScatter(place, wires, part, line_scratch)
        for row in range(4):
            part[:, pl.ds(row * 512, 512)] = contract_last(
                grad_mixed[...],
                heads[row, :, :, pl.ds(0, HEADS_COLS)].reshape(512, HEADS_COLS),
            ).astype(BF16)
        for offset in (2, 1, 3, 0):
            scatter.pair(offset)
        yield 19.6
        yield from gradient(scatter)

    computed = []

    def weights():
        yield 21.5
        need(12, 13, 16, 17)
        gain_rows[...] = jnp.zeros_like(gain_rows)
        gain_rows[1:2, :] = jnp.sum(gain_part[...], axis=0, keepdims=True)
        ones = jnp.ones((8, HEADS_COLS), BF16)
        for row in range(4):
            columns = pl.ds(row * 512, 512)
            merge_part = token_product(attended[...], branch[:, columns]).astype(BF16)
            for slot in range(16):
                y, z = divmod(slot, 4)
                for half in range(2):
                    heads_all[row, slot, pl.ds(16 * half, 16), pl.ds(HEADS_COLS, 256)] = (
                        merge_part[
                            z * 64 + y * 16 : z * 64 + y * 16 + 16,
                            half * 256 : half * 256 + 256,
                        ]
                    )
            for piece in range(2):
                columns = pl.ds(row * 512 + piece * 256, 256)
                grad = token_product(normed[:, columns], grad_mixed[...])
                slots = pl.ds(8 * piece, 8)
                heads_all[row, slots, :, pl.ds(0, HEADS_COLS)] = grad.astype(BF16).reshape(
                    8, 32, HEADS_COLS
                )
                weight = heads[row, slots, :, pl.ds(0, HEADS_COLS)].reshape(256, HEADS_COLS)
                terms = grad * weight.astype(F32)
                high = terms.astype(BF16)
                low = (terms - high.astype(F32)).astype(BF16)
                sums_ = contract_last(ones, high) + contract_last(ones, low)
                gain_rows[0:1, columns] = sums_[0:1] / gains[0:1, columns]
            computed.append(row)
            yield 21.5 + 1.55 * (row + 1)
        yield from gain_sums()

    def heads_side(side):
        yield 24.7 + 3.1 * side
        assert len(computed) >= 2 + 2 * side
        yield from ring_scatter(
            place, wires, Rows(HEADS_COLS + 256), heads_all, side, heads_scratch,
            heads_sum.at[pl.ds(2 * side, 2)], 24.7 + 3.1 * side, 1.8,
        )
        computed.append("side")

    def heads_back():
        yield 49.4
        assert computed.count("side") == 2
        merge_wait = merge_exchange(
            place, wires, homes,
            lambda row: heads_sum.at[row, :, pl.ds(HEADS_COLS, 256)],
            lambda row: merge_pieces.at[place.y],
            place.y,
        )
        yield from back_pieces(
            place, wires,
            lambda row: heads_sum.at[row, :, pl.ds(0, HEADS_COLS)], heads_pieces, 55.0,
        )
        merge_wait()

    def gain_sums():
        moved = [
            wires.push(column_block(gain_rows, other), gain_came.at[place.row], device)
            for other, device in peers
        ]
        kept = wires.keep(column_block(gain_rows, place.row), gain_came.at[place.row])
        yield 35.0
        kept.wait()
        for copy in moved:
            copy.wait_recv()
        local_sum = gain_came[0] + gain_came[1] + gain_came[2] + gain_came[3]
        me = place.col * 16 + place.dp
        for kind in range(2):
            for tile in range(4):
                gain_all[me, pl.ds(4 * kind + tile, 1), :] = local_sum[
                    kind : kind + 1, tile * 128 : tile * 128 + 128
                ]
        base = wires.count
        wires.count += 32

        def gain_copy(step):
            return pltpu.make_async_remote_copy(
                src_ref=gain_all.at[me],
                dst_ref=gain_all.at[me],
                send_sem=wires.send.at[base + step],
                recv_sem=wires.recv.at[base + step],
                device_id=far(step),
                device_id_type=MESH,
            )

        def start(step, carry):
            gain_copy(step).start()
            return carry

        def finish(step, carry):
            gain_copy(step).wait()
            return carry

        lax.fori_loop(1, 32, start, 0)
        yield 47.0
        lax.fori_loop(1, 32, finish, 0)
        gains_grad[...] = functools.reduce(lambda a, b: a + b, [gain_all[i] for i in range(32)])

    def gradient(scatter):
        scatter.far()
        scatter.near(1)
        scatter.near(3)
        yield from scatter.rest(20.0, 11.4)
        need(14, 15)

        def chunk(index, carry):
            at = pl.ds(pl.multiple_of(index * 16, 16), 16)
            grad = scatter.total_of(at)
            through, _ = norm_back(input_rows[at, :].astype(F32), gains[0:1, :], grad)
            input_grad_own[at, :] = (grad_middle[at, :] + through).astype(BF16)
            return carry

        lax.fori_loop(0, OWN // 16, chunk, 0)
        yield from recut(place, wires, input_grad_own, input_grad, 52.0)

    interleave(
        compute(),
        outputs(),
        down_rows(),
        gating(),
        weights(),
        heads_side(0),
        heads_side(1),
        heads_back(),
        sweep([wires], 30.0, 40.0),
    )
    wires.drain()


def attention_back(
    branch, merge, query, pair, sums, cosine, sine, grad_mixed,
    grad_attended, grad_key, grad_value, key_columns,
):
    yield 0.3
    def attended_rows(index, carry):
        at = pl.ds(pl.multiple_of(index * 512, 512), 512)
        grad_attended[at, :] = contract_last(branch[at, :], merge[...]).astype(BF16)
        return carry

    attended_rows(0, 0)
    yield 2.0
    attended_rows(1, 0)
    key_columns[...] = jnp.transpose(pair[...].astype(F32))[:HEAD_SIZE].astype(BF16)
    grad_key[...] = jnp.zeros_like(grad_key)
    grad_value[...] = jnp.zeros_like(grad_value)
    scale = HEAD_SIZE ** (-0.5)
    keys_at = lax.broadcasted_iota(jnp.int32, (QUERY_BLOCK, QUERY_BLOCK), 0)
    rows_at = lax.broadcasted_iota(jnp.int32, (QUERY_BLOCK, QUERY_BLOCK), 1)
    for block in range(SEQ // QUERY_BLOCK):
        at = pl.ds(block * QUERY_BLOCK, QUERY_BLOCK)
        before = block * QUERY_BLOCK
        for two in range(2):
            turned = []
            for head in (2 * two, 2 * two + 1):
                columns = pl.ds(head * HEAD_SIZE, HEAD_SIZE)
                rows, back = query[at, columns], grad_attended[at, columns]
                log_total = sums[pl.ds(head, 1), at]
                spans = [at] + ([pl.ds(0, before)] if before else [])
                softs, grads = [], []
                for span in spans:
                    scores = contract_last(pair[span, pl.ds(0, HEAD_SIZE)], rows) * scale
                    soft = jnp.exp(scores - log_total)
                    if span is at:
                        soft = jnp.where(rows_at >= keys_at, soft, 0.0)
                    softs.append(soft)
                    grads.append(contract_last(pair[span, pl.ds(HEAD_SIZE, HEAD_SIZE)], back))
                inner = functools.reduce(
                    lambda a, b: a + b,
                    [jnp.sum(s * g, axis=0, keepdims=True) for s, g in zip(softs, grads)],
                )
                result = 0.0
                for span, soft, grad in zip(spans, softs, grads):
                    low = (soft * (grad - inner)).astype(BF16)
                    grad_key[span, :] += product(low, rows)
                    grad_value[span, :] += product(soft.astype(BF16), back)
                    result += product(key_columns[:, span], low)
                turned.append(result)
                yield 1.9 + (2.1, 5.0, 8.7, 13.2)[block] - (0.52, 0.72, 0.92, 1.15)[block] * (3 - head)
            tile = jnp.transpose(jnp.concatenate(turned, axis=0)) * scale
            grad_mixed[at, pl.ds(two * 128, 128)] = turn(
                tile, cosine[at, :], -sine[at, :]
            ).astype(BF16)

    def finish_rows(index, carry):
        at = pl.ds(pl.multiple_of(index * 128, 128), 128)
        cos, sin = keys_only(cosine[at, :], sine[at, :])
        tile = jnp.concatenate([grad_key[at, :] * scale, grad_value[at, :]], axis=1)
        grad_mixed[at, pl.ds(256, 128)] = turn(tile, cos, -sin).astype(BF16)
        return carry

    lax.fori_loop(0, SEQ // 128, finish_rows, 0)


def product(left, right):
    return jnp.dot(left, right, preferred_element_type=F32)


def contract_last(left, right):
    return lax.dot_general(left, right, (((1,), (1,)), ((), ())), preferred_element_type=F32)


def token_product(left, right):
    return lax.dot_general(left, right, (((0,), (0,)), ((), ())), preferred_element_type=F32)


def adamw(current, gradient, first, second, step_rate, decay_rate):
    mean_new = BETA_ONE * first + (1.0 - BETA_ONE) * gradient
    square_new = BETA_TWO * second + (1.0 - BETA_TWO) * gradient * gradient
    mean_hat = mean_new / (1.0 - BETA_ONE**STEP)
    square_hat = square_new / (1.0 - BETA_TWO**STEP)
    updated = current - step_rate * (
        mean_hat / (jnp.sqrt(square_hat) + EPS_ADAM) + decay_rate * current
    )
    return (updated, mean_new, square_new)


def update_kernel(*refs):
    output_given, input_grad_given, gains, heads, merge, gating, down = refs[:7]
    states = [refs[7 + 3 * n : 10 + 3 * n] for n in range(5)]
    output, input_grad = refs[22:24]
    results = [refs[24 + 4 * n : 28 + 4 * n] for n in range(5)]
    output[...] = output_given[...]
    input_grad[...] = input_grad_given[...].astype(F32)
    gains_grad, heads_grad, merge_grad, gating_grad, down_grad = [r[0] for r in results]
    for kind in range(2):
        for tile in range(4):
            gains_grad[pl.ds(kind, 1), pl.ds(tile * 128, 128)] = gains[
                pl.ds(4 * kind + tile, 1), :
            ]
    for row in range(4):
        group, half = divmod(row, 2)
        heads_grad[:, pl.ds(group * 640 + half * 256, 256)] = heads[
            row, :, pl.ds(0, 256)
        ].astype(F32)
        for side in range(2):
            merge_grad[pl.ds(16 * row, 16), pl.ds(256 * side, 256)] = merge[
                row, pl.ds(16 * side, 16)
            ].astype(F32)
        down_grad[pl.ds(PIECE_USED * row, PIECE_USED), :] = down[row].astype(F32)[:PIECE_USED]
    for group in range(2):
        pair = pl.ds(256, 128)
        heads_grad[:, pl.ds(group * 640 + 512, 128)] = heads[2 * group, :, pair].astype(
            F32
        ) + heads[2 * group + 1, :, pair].astype(F32)
    for kind in range(2):
        rows = [gating[row, :, pl.ds(kind * HIDDEN, HIDDEN)].astype(F32) for row in range(4)]
        whole = jnp.concatenate(
            [
                rows[row][:, slot * PIECE : slot * PIECE + PIECE_USED]
                for slot in range(16)
                for row in range(4)
            ],
            axis=1,
        )
        gating_grad[:, kind, :] = whole
    rates = [RATE_GAIN, RATE_MATRIX, RATE_MERGE, RATE_MATRIX, RATE_MATRIX]
    decays = [0.0] + [WEIGHT_DECAY] * 4
    for state, result, rate, decay in zip(states, results, rates, decays):
        rows = state[0].shape[0]
        step = 16 if rows % 16 == 0 else rows

        def chunk(index, carry):
            at = pl.ds(pl.multiple_of(index * step, step), step)
            new = adamw(state[0][at], result[0][at], state[1][at], state[2][at], rate, decay)
            for ref, value in zip(result[1:], new):
                ref[at] = value
            return carry

        lax.fori_loop(0, rows // step, chunk, 0)


def update(given, states):
    ins = list(given) + [array for state in states for array in state]
    outs = [shape(512, 512), shape(512, 512, dtype=F32)]
    for state in states:
        outs += [shape(*state[0].shape, dtype=F32)] * 4
    return pl.pallas_call(
        update_kernel,
        out_shape=outs,
        in_specs=[pl.BlockSpec(memory_space=pltpu.VMEM)] * len(ins),
        out_specs=[pl.BlockSpec(memory_space=pltpu.VMEM)] * len(outs),
        compiler_params=pltpu.CompilerParams(vmem_limit_bytes=VMEM_BYTES),
        cost_estimate=pl.CostEstimate(flops=2**24, bytes_accessed=2**24, transcendentals=2**20),
    )(*ins)


def body(
    block_input,
    cotangent,
    norm_gains,
    gains_first,
    gains_second,
    heads_projection_weight,
    heads_first_moment,
    heads_second_moment,
    merge_weight,
    merge_first,
    merge_second,
    gating_weight,
    gating_first,
    gating_second,
    down_weight,
    down_first,
    down_second,
):
    ANY, VMEM = pl.ANY, pltpu.VMEM
    saved = [
        shape(SEQ, 256),
        shape(SEQ, 128),
        shape(8, SEQ, dtype=F32),
        shape(SEQ, 128, dtype=F32),
        shape(SEQ, 128, dtype=F32),
        shape(SEQ, 256),
        shape(256, MODEL_WIDTH),
        shape(4, 16, 32, HEADS_COLS + 256),
        shape(OWN, MODEL_WIDTH, dtype=F32),
        shape(OWN, MODEL_WIDTH, dtype=F32),
        shape(SEQ, MODEL_WIDTH),
        shape(8, MODEL_WIDTH, dtype=F32),
        shape(4, 32, 2 * HIDDEN),
        shape(16 * PIECE, MODEL_WIDTH),
        shape(2, MODEL_WIDTH, dtype=F32),
        shape(OWN, MODEL_WIDTH),
    ]

    def held(array):
        return pltpu.VMEM(array.shape, array.dtype)

    (
        normed_one, query, pair, sums, cosine, sine, attended, w_merge, w_heads,
        middle, grad_middle, branch, gain_part, gating_sum, down_part, down_out, gains, input_rows,
    ) = call(
        opening_kernel,
        [(shape(SEQ, MODEL_WIDTH), ANY)]
        + [(array, ANY) for array in saved[:14]]
        + [(shape(SEQ, MODEL_WIDTH), ANY)]
        + [(array, ANY) for array in saved[14:]],
        [
            (heads_projection_weight, VMEM),
            (merge_weight, VMEM),
            (gating_weight, VMEM),
            (down_weight, VMEM),
            (block_input, VMEM),
            (cotangent, VMEM),
            (norm_gains, VMEM),
        ],
        LINE_SCATTER_SCRATCH
        + ring_scatter_scratch(Rows(2 * HIDDEN))
        + [
            pltpu.VMEM((SEQ, MODEL_WIDTH), BF16),
            pltpu.VMEM((SEQ, MODEL_WIDTH), BF16),
            pltpu.VMEM((SEQ, MODEL_WIDTH), BF16),
            pltpu.VMEM((4, 16, 32, 2 * HIDDEN), BF16),
            pltpu.VMEM((SEQ, HIDDEN), F32),
            pltpu.VMEM((SEQ, HIDDEN), BF16),
            pltpu.VMEM((SEQ, 2 * HIDDEN), BF16),
            pltpu.VMEM((OWN, MODEL_WIDTH), BF16),
            pltpu.VMEM((4, 32, HEADS_COLS), BF16),
            pltpu.VMEM((4, 32, 256), BF16),
            pltpu.VMEM((4, 32, 2 * HIDDEN), BF16),
            pltpu.VMEM((4, PIECE, 512), BF16),
        ]
        + [held(array) for array in saved],
        228,
        0,
        2**25,
    )
    given = [
        branch, w_merge, query, pair, sums, cosine, sine, down_out, down_part, gating_sum,
        middle, w_heads, attended, normed_one, grad_middle, input_rows, gains, gain_part,
    ]
    (
        block_output, input_grad, gains_grad,
        heads_pieces, merge_pieces, gating_pieces, down_pieces,
    ) = call(
        backward_kernel,
        [
            (shape(512, 512), VMEM),
            (shape(512, 512), VMEM),
            (shape(8, 128, dtype=F32), VMEM),
            (shape(4, 32, HEADS_COLS), VMEM),
            (shape(4, 32, 256), VMEM),
            (shape(4, 32, 2 * HIDDEN), VMEM),
            (shape(4, PIECE, 512), VMEM),
        ],
        [(array, ANY) for array in given],
        LINE_SCATTER_SCRATCH
        + LINE_SCATTER_SCRATCH
        + ring_scatter_scratch(Flat())
        + ring_scatter_scratch(Rows(HEADS_COLS + 256))
        + [held(array) for array in given]
        + [
            pltpu.VMEM((SEQ, MODEL_WIDTH), BF16),
            pltpu.VMEM((SEQ, HEADS_COLS), BF16),
            pltpu.VMEM((SEQ, 256), BF16),
            pltpu.VMEM((SEQ, HEAD_SIZE), F32),
            pltpu.VMEM((SEQ, HEAD_SIZE), F32),
            pltpu.VMEM((HEAD_SIZE, SEQ), BF16),
            pltpu.VMEM((OWN, MODEL_WIDTH), BF16),
            pltpu.VMEM((PIECE, MODEL_WIDTH), BF16),
            pltpu.VMEM((4, 16, 32, HEADS_COLS + 256), BF16),
            pltpu.VMEM((4, 32, HEADS_COLS + 256), BF16),
            pltpu.VMEM((OWN, MODEL_WIDTH), BF16),
            pltpu.VMEM((8, MODEL_WIDTH), F32),
            pltpu.VMEM((4, 8, 512), F32),
            pltpu.VMEM((32, 8, 128), F32),
        ],
        180,
        3,
        2**25,
    )
    (
        block_output, input_grad,
        gains_grad, gains_next, gains_mean, gains_square,
        heads_grad, heads_next, heads_mean, heads_square,
        merge_grad, merge_next, merge_mean, merge_square,
        gating_grad, gating_next, gating_mean, gating_square,
        down_grad, down_next, down_mean, down_square,
    ) = update(
        (
            block_output, input_grad, gains_grad,
            heads_pieces, merge_pieces, gating_pieces, down_pieces,
        ),
        (
            (norm_gains, gains_first, gains_second),
            (heads_projection_weight, heads_first_moment, heads_second_moment),
            (merge_weight, merge_first, merge_second),
            (gating_weight, gating_first, gating_second),
            (down_weight, down_first, down_second),
        ),
    )
    return (
        block_output,
        input_grad,
        gains_grad,
        gains_next,
        gains_mean,
        gains_square,
        heads_grad,
        heads_next,
        heads_mean,
        heads_square,
        merge_grad,
        merge_next,
        merge_mean,
        merge_square,
        gating_grad,
        gating_next,
        gating_mean,
        gating_square,
        down_grad,
        down_next,
        down_mean,
        down_square,
    )


def solution(mesh):
    in_specs = (
        P(("dp", "col"), "row"),
        P(("dp", "col"), "row"),
        P(None, "row"),
        P(None, "row"),
        P(None, "row"),
        P(("row", "dp"), "col"),
        P(("row", "dp"), "col"),
        P(("row", "dp"), "col"),
        P(("col", "dp"), "row"),
        P(("col", "dp"), "row"),
        P(("col", "dp"), "row"),
        P(("row", "dp"), None, "col"),
        P(("row", "dp"), None, "col"),
        P(("row", "dp"), None, "col"),
        P(("col", "dp"), "row"),
        P(("col", "dp"), "row"),
        P(("col", "dp"), "row"),
    )
    out_specs = (
        P(("dp", "col"), "row"),
        P(("dp", "col"), "row"),
        P(None, "row"),
        P(None, "row"),
        P(None, "row"),
        P(None, "row"),
        P(("row", "dp"), "col"),
        P(("row", "dp"), "col"),
        P(("row", "dp"), "col"),
        P(("row", "dp"), "col"),
        P(("col", "dp"), "row"),
        P(("col", "dp"), "row"),
        P(("col", "dp"), "row"),
        P(("col", "dp"), "row"),
        P(("row", "dp"), None, "col"),
        P(("row", "dp"), None, "col"),
        P(("row", "dp"), None, "col"),
        P(("row", "dp"), None, "col"),
        P(("col", "dp"), "row"),
        P(("col", "dp"), "row"),
        P(("col", "dp"), "row"),
        P(("col", "dp"), "row"),
    )
    return jax.shard_map(body, mesh=mesh, in_specs=in_specs, out_specs=out_specs, check_vma=False)
```

```python
import functools
import math

import jax
import jax.numpy as jnp
from jax import lax
from jax.experimental import pallas as pl
from jax.experimental.pallas import tpu as pltpu
from jax.sharding import PartitionSpec as P

MODEL_WIDTH = 2048
KEY_VALUE_HEADS = 4
HEAD_SIZE = 64
QUERY_PER_GROUP = 8
STEP = 10


EPS_NORM = 1e-05
BETA_ONE = 0.9
BETA_TWO = 0.95
EPS_ADAM = 1e-08
RATE_MATRIX = 0.05
RATE_MERGE = 0.5
RATE_GAIN = 1.0
WEIGHT_DECAY = 0.1
ROPE_BASE = 10000.0
MASK_FILL = -1e30

MESH = pl.DeviceIdType.MESH
VMEM_BYTES = 63 * 2**20
BF16 = jnp.bfloat16
F32 = jnp.float32

SEQ = 1024
OWN = 128
HEADS_COLS = 384
HIDDEN = 768
PIECE = 48
PIECE_USED = 44


class Place:
    def __init__(self):
        self.dp = lax.axis_index("dp")
        self.row = lax.axis_index("row")
        self.col = lax.axis_index("col")
        self.y = lax.div(self.dp, 4)
        self.z = lax.rem(self.dp, 4)
        self.core = lax.rem(self.row, 2)
        self.x = self.col * 2 + lax.div(self.row, 2)

    def near(self, x=0, core=0, y=0, z=0):
        new_x = lax.rem(self.x + x + 4, 4)
        new_core = lax.rem(self.core + core, 2)
        new_y = lax.rem(self.y + y + 4, 4)
        new_z = lax.rem(self.z + z + 4, 4)
        return {
            "dp": new_y * 4 + new_z,
            "row": lax.rem(new_x, 2) * 2 + new_core,
            "col": lax.div(new_x, 2),
        }

    def slot(self, first_axis, first, second):
        y, z = (first, second) if first_axis == "y" else (second, first)
        return lax.rem(self.y + y + 4, 4) * 4 + lax.rem(self.z + z + 4, 4)

    def line(self, x, core):
        return lax.rem(self.x + x + 4, 4) * 2 + lax.rem(self.core + core, 2)

    def peer(self, step):
        other = lax.rem(self.row + step, 4)
        return other, {"dp": self.dp, "row": other, "col": self.col}


class Wires:
    def __init__(self, send, recv, local, parent=None):
        self.send, self.recv, self.local = send, recv, local
        self.root = parent or self
        self.used = {"send": 0, "recv": 0, "local": 0}
        self.debts = []

    def part(self):
        return Wires(self.send, self.recv, self.local, self.root)

    def reserve(self, kind, count=1):
        first = self.root.used[kind]
        self.root.used[kind] += count
        return first

    def start(self, source, target, device, send, recv):
        pltpu.make_async_remote_copy(
            src_ref=source,
            dst_ref=target,
            send_sem=self.send.at[send],
            recv_sem=self.recv.at[recv],
            device_id=device,
            device_id_type=MESH,
        ).start()

    def batch(self, copies, size, send=None):
        recv = self.reserve("recv")
        if send is None:
            send = self.reserve("send")
            self.owe(send, size)
        for source, target, device in copies:
            self.start(source, target, device, send, recv)
        return lambda: self.take(self.recv.at[recv], size)

    def push(self, source, target, device, send=None):
        return self.batch([(source, target, device)], target, send)

    def take(self, semaphore, size):
        pltpu.make_async_copy(size, size, semaphore).wait()

    def owe(self, send, size):
        self.debts.append((send, size))

    def keep(self, source, target):
        copy = pltpu.make_async_copy(source, target, self.local.at[self.reserve("local")])
        copy.start()
        return copy

    def settle(self, debts):
        for send, size in debts:
            self.take(self.send.at[send], size)
        self.debts = [debt for debt in self.debts if all(debt is not other for other in debts)]

    def drain(self):
        self.settle(list(self.debts))


def meet(devices, more=0):
    barrier = pltpu.get_barrier_semaphore()
    for device in devices:
        pl.semaphore_signal(barrier, inc=1, device_id=device, device_id_type=MESH)
    pl.semaphore_wait(barrier, len(devices))


def interleave(*plans):
    waiting = [[next(plan), order, plan] for order, plan in enumerate(plans)]
    while waiting:
        waiting.sort(key=lambda entry: (entry[0], entry[1]))
        entry = waiting[0]
        try:
            entry[0] = max(entry[0], next(entry[2]))
        except StopIteration:
            waiting.pop(0)


def sweep(accounts, since, until):
    yield since
    debts = [(account, debt) for account in accounts for debt in account.debts]
    yield until
    for account, debt in debts:
        if any(debt is other for other in account.debts):
            account.settle([debt])


def ring_neighbours(place):
    return [place.near(y=1), place.near(y=-1), place.near(z=1), place.near(z=-1)]


def line_neighbours(place):
    return [place.near(x=1), place.near(x=-1), place.near(core=1)]


def line_gather(place, wires, own, out, block, half, times, ready=None):
    def size(blocks):
        return out.at[pl.ds(0, blocks * OWN)]

    me = place.line(0, 0)
    send = wires.reserve("send")
    yield times[0]
    kept = wires.keep(own, block(out, me))
    near = wires.batch(
        [(own, block(out, me), place.near(x=1)), (own, block(out, me), place.near(x=-1))],
        size(2),
        send,
    )
    beside = [wires.push(own, block(out, me), place.near(core=1), send)]
    yield times[1]
    near()
    left, right = place.line(-1, 0), place.line(1, 0)
    far = wires.batch(
        [
            (half(out, left, 0), half(out, left, 0), place.near(x=1)),
            (half(out, right, 1), half(out, right, 1), place.near(x=-1)),
        ],
        size(1),
        send,
    )
    beside.append(
        wires.batch(
            [(block(out, came), block(out, came), place.near(core=1)) for came in (left, right)],
            size(2),
            send,
        )
    )
    yield times[2]
    kept.wait()
    for wait in beside:
        wait()
    if ready:
        ready((0, 1, -1))
    far()
    came = block(out, place.line(2, 0))
    last = wires.push(came, came, place.near(core=1), send)
    wires.owe(send, size(7))
    yield times[3]
    last()
    if ready:
        ready((2,))


def token_block(ref, index):
    return ref.at[pl.ds(pl.multiple_of(index * OWN, OWN), OWN)]


def token_half(ref, index, side):
    return ref.at[pl.ds(pl.multiple_of(index * OWN + side * (OWN // 2), OWN // 2), OWN // 2)]


def tile_block(ref, index):
    x, core = lax.div(index, 2), lax.rem(index, 2)
    rows = pl.ds(pl.multiple_of(lax.div(x, 2) * 512, 512), 512)
    columns = pl.ds(pl.multiple_of((lax.rem(x, 2) * 2 + core) * 512, 512), 512)
    return ref.at[rows, columns]


def tile_half(ref, index, side):
    x, core = lax.div(index, 2), lax.rem(index, 2)
    rows = pl.ds(pl.multiple_of(lax.div(x, 2) * 512 + side * 256, 256), 256)
    columns = pl.ds(pl.multiple_of((lax.rem(x, 2) * 2 + core) * 512, 512), 512)
    return ref.at[rows, columns]


def add_rows(out, terms, rows, step=16):
    def chunk(index, carry):
        at = pl.ds(pl.multiple_of(index * step, step), step)
        out[at, :] = functools.reduce(
            lambda a, b: a + b, [term[at, :].astype(F32) for term in terms]
        ).astype(out.dtype)
        return carry

    lax.fori_loop(0, rows // step, chunk, 0)


LINE_SCATTER_SCRATCH = [
    pltpu.VMEM((4, OWN, MODEL_WIDTH), BF16),
    pltpu.VMEM((2, OWN // 2, MODEL_WIDTH), BF16),
    pltpu.VMEM((2, OWN, MODEL_WIDTH), BF16),
]


class LineScatter:
    def __init__(self, place, wires, part, scratch):
        self.place, self.wires, self.part = place, wires, part
        self.beside, self.halves, self.full = scratch
        self.out = wires.reserve("send")
        self.late = wires.reserve("recv")
        self.pairs = {}

    def pair(self, offset):
        self.pairs[offset] = self.wires.push(
            token_block(self.part, self.place.line(offset, 1)),
            self.beside.at[offset],
            self.place.near(core=1),
            self.out,
        )

    def own(self, offset):
        return token_block(self.part, self.place.line(offset, 0))

    def far(self):
        self.pairs[2]()
        total = self.beside.at[2]
        add_rows(total, [self.own(2), total], OWN)
        self.beyond = self.wires.batch(
            [
                (total.at[pl.ds(0, OWN // 2)], self.halves.at[0], self.place.near(x=1)),
                (total.at[pl.ds(OWN // 2, OWN // 2)], self.halves.at[1], self.place.near(x=-1)),
            ],
            self.halves,
            self.out,
        )

    def near(self, offset):
        self.pairs[offset]()
        total = self.beside.at[offset]
        add_rows(total, [self.own(offset), total], OWN)
        self.send(offset, OWN // 2 if offset == 1 else 0)

    def send(self, offset, first):
        rows = pl.ds(first, OWN // 2)
        self.wires.start(
            self.beside.at[offset, rows],
            self.full.at[0 if offset == 1 else 1, rows],
            self.place.near(x=1 if offset == 1 else -1),
            self.out,
            self.late,
        )

    def join(self):
        self.beyond()
        for way, offset, first in ((0, 1, 0), (1, 3, OWN // 2)):
            rows = self.beside.at[offset, pl.ds(first, OWN // 2)]
            add_rows(rows, [rows, self.halves.at[way]], OWN // 2)
            self.send(offset, first)
        self.wires.owe(self.out, self.part.at[pl.ds(0, 7 * OWN)])

    def finish(self):
        self.pairs[0]()
        self.wires.take(self.wires.recv.at[self.late], self.full)

    def terms(self):
        return [self.own(0), self.beside.at[0], self.full.at[0], self.full.at[1]]

    def total_of(self, at):
        return functools.reduce(lambda a, b: a + b, [t[at, :].astype(F32) for t in self.terms()])

    def run(self, start, cost):
        yield start
        for offset in (2, 1, 3, 0):
            self.pair(offset)
        yield start + 2
        self.far()
        yield start + 3
        self.near(1)
        self.near(3)
        yield from self.rest(start, cost)

    def rest(self, start, cost):
        yield start + 5 + 0.5 * cost
        self.join()
        yield start + 4.5 + 1.4 * cost
        self.finish()


class Rows:
    def __init__(self, columns):
        self.item_shape = (2, 32, columns)
        self.half_shape = (1, 32, columns)

    def item(self, ref, side, slot):
        return ref.at[pl.ds(2 * side, 2), slot]

    def half(self, ref, side, part, slot):
        return ref.at[pl.ds(2 * side + part, 1), slot]

    def cut(self, item, part):
        return item.at[pl.ds(part, 1)]

    def span(self, ref, side, items):
        return ref.at[pl.ds(2 * side, 2), pl.ds(0, items)]


class Flat:
    def __init__(self):
        self.item_shape = (PIECE, MODEL_WIDTH // 2)
        self.half_shape = (PIECE, MODEL_WIDTH // 4)

    def item(self, ref, side, slot):
        rows = pl.ds(pl.multiple_of(slot * PIECE, PIECE), PIECE)
        return ref.at[rows, pl.ds(side * (MODEL_WIDTH // 2), MODEL_WIDTH // 2)]

    def half(self, ref, side, part, slot):
        rows = pl.ds(pl.multiple_of(slot * PIECE, PIECE), PIECE)
        return ref.at[rows, pl.ds((2 * side + part) * (MODEL_WIDTH // 4), MODEL_WIDTH // 4)]

    def cut(self, item, part):
        return item.at[:, pl.ds(part * (MODEL_WIDTH // 4), MODEL_WIDTH // 4)]

    def span(self, ref, side, items):
        return ref.at[pl.ds(0, items * PIECE), pl.ds(side * (MODEL_WIDTH // 2), MODEL_WIDTH // 2)]


def ring_move(place, axis, step):
    return place.near(y=step) if axis == "y" else place.near(z=step)


def ring_gather(place, wires, kind, out, side, times):
    first, second = ("z", "y") if side == 0 else ("y", "z")
    slot = functools.partial(place.slot, first)
    size = functools.partial(kind.span, out, side)
    send = wires.reserve("send")
    spread = {}

    def both(axis, items, count):
        return wires.batch(
            [(item, item, ring_move(place, axis, step)) for item, step in zip(items, (1, -1))],
            size(count),
            send,
        )

    def halves(axis, before, after):
        return both(
            axis,
            [kind.half(out, side, 0, before), kind.half(out, side, 1, after)],
            1,
        )

    def send_on(offset):
        spread[offset] = both(second, [kind.item(out, side, slot(offset, 0))] * 2, 2)

    last = wires.reserve("recv")

    def pass_on(offset):
        spread[offset]()
        for part, way, step in ((0, -1, 1), (1, 1, -1)):
            piece = kind.half(out, side, part, slot(offset, way))
            wires.start(piece, piece, ring_move(place, second, step), send, last)

    yield times[0]
    near = both(first, [kind.item(out, side, slot(0, 0))] * 2, 2)
    send_on(0)
    yield times[1]
    near()
    far = halves(first, slot(-1, 0), slot(1, 0))
    send_on(-1)
    send_on(1)
    yield times[2]
    pass_on(0)
    yield times[3]
    far()
    send_on(2)
    yield times[4]
    pass_on(-1)
    yield times[5]
    pass_on(1)
    yield times[6]
    pass_on(2)
    wires.owe(send, size(15))
    yield times[7]
    wires.take(wires.recv.at[last], size(4))


RING_SCATTER_SCRATCH = 8


def ring_scatter_scratch(kind):
    def stack(count, shape):
        return pltpu.VMEM((count, *shape), BF16)

    one_side = [
        stack(8, kind.half_shape),
        stack(8, kind.item_shape),
        stack(2, kind.half_shape),
        stack(2, kind.item_shape),
    ]
    return one_side + one_side


def add_to(out, *terms):
    out[...] = functools.reduce(
        lambda a, b: a + b, [t[...].astype(F32) for t in (out, *terms)]
    ).astype(out.dtype)


def ring_scatter(place, wires, kind, part, side, scratch, result, start, cost, then=None):
    far, came, far_last, came_last = scratch[4 * side : 4 * side + 4]
    first, second = ("z", "y") if side == 0 else ("y", "z")
    slot = functools.partial(place.slot, first)
    size = functools.partial(kind.span, part, side)
    send = wires.reserve("send")
    order = (2, 1, -1, 0)

    def both(axis, sources, targets, count):
        return wires.batch(
            [
                (source, target, ring_move(place, axis, step))
                for source, target, step in zip(sources, targets, (1, -1))
            ],
            size(count),
            send,
        )

    def halves(axis, target, into):
        return both(axis, [kind.half(part, side, n, target) for n in (0, 1)], into, 1)

    def add_halves(came_halves, after, before):
        add_to(kind.half(part, side, 0, after), came_halves[0])
        add_to(kind.half(part, side, 1, before), came_halves[1])

    yield start
    start = start if then is None else then
    beyond = [
        halves(second, slot(offset, 2), [far.at[2 * n], far.at[2 * n + 1]])
        for n, offset in enumerate(order)
    ]
    moved = []
    for n, offset in enumerate(order):
        yield start + 2.5 + (0.5 + n) * cost
        beyond[n]()
        after, before = slot(offset, 1), slot(offset, -1)
        add_halves([far.at[2 * n], far.at[2 * n + 1]], after, before)
        items = [kind.item(part, side, after), kind.item(part, side, before)]
        moved.append(both(second, items, [came.at[2 * n], came.at[2 * n + 1]], 2))

    def finish(n, offset):
        moved[n]()
        add_to(kind.item(part, side, slot(offset, 0)), came.at[2 * n], came.at[2 * n + 1])

    yield start + 4 + 3 * cost
    finish(0, 2)
    beyond_last = halves(first, slot(2, 0), [far_last.at[0], far_last.at[1]])
    yield start + 4 + 4 * cost
    finish(1, 1)
    yield start + 4 + 5 * cost
    finish(2, -1)
    beyond_last()
    after, before = slot(1, 0), slot(-1, 0)
    add_halves([far_last.at[0], far_last.at[1]], after, before)
    items = [kind.item(part, side, after), kind.item(part, side, before)]
    last = both(first, items, [came_last.at[0], came_last.at[1]], 2)
    wires.owe(send, size(15))
    yield start + 5 + 6 * cost
    finish(3, 0)
    yield start + 8 + 7.5 * cost
    last()
    own = kind.item(part, side, slot(0, 0))
    add_to(own, came_last.at[0], came_last.at[1])
    result[...] = own[...]


def call(kernel, outs, ins, scratch, wires, name, cost):
    return pl.pallas_call(
        kernel,
        out_shape=[shape for shape, _ in outs],
        in_specs=[pl.BlockSpec(memory_space=space) for _, space in ins],
        out_specs=[pl.BlockSpec(memory_space=space) for _, space in outs],
        scratch_shapes=list(scratch)
        + [pltpu.SemaphoreType.DMA((count,)) for count in wires],
        compiler_params=pltpu.CompilerParams(
            collective_id=name, has_side_effects=True, vmem_limit_bytes=VMEM_BYTES
        ),
        cost_estimate=pl.CostEstimate(flops=0, bytes_accessed=cost, transcendentals=0),
    )(*[array for array, _ in ins])


def shape(*extent, dtype=BF16):
    return jax.ShapeDtypeStruct(extent, dtype)


def merge_devices(place):
    users = [{"dp": j * 4 + place.z, "row": place.y, "col": place.col} for j in range(4)]
    homes = [
        {"dp": place.row * 4 + place.z, "row": jnp.int32(row), "col": place.col} for row in range(4)
    ]
    return users, homes


def signal_others(place, devices):
    barrier = pltpu.get_barrier_semaphore()
    for device in devices:
        alone = (device["dp"] == place.dp) & (device["row"] == place.row)

        @pl.when(jnp.logical_not(alone))
        def _():
            pl.semaphore_signal(barrier, inc=1, device_id=device, device_id_type=MESH)


def merge_exchange(place, wires, devices, source, target, mine):
    send, recv = wires.reserve("send", 4), wires.reserve("recv", 4)
    copies = []
    for index, device in enumerate(devices):
        copy = pltpu.make_async_remote_copy(
            src_ref=source(index),
            dst_ref=target(index),
            send_sem=wires.send.at[send + index],
            recv_sem=wires.recv.at[recv + mine],
            device_id=device,
            device_id_type=MESH,
        )
        here = pltpu.make_async_copy(source(index), target(index), wires.recv.at[recv + mine])
        alone = (device["dp"] == place.dp) & (device["row"] == place.row)
        copies.append((copy, alone))
        pl.when(alone)(here.start)
        pl.when(jnp.logical_not(alone))(copy.start)

    def wait():
        for index in range(4):
            wires.take(wires.recv.at[recv + index], target(0))
        for copy, alone in copies:
            pl.when(jnp.logical_not(alone))(copy.wait_send)

    return wait


def nested(plans):
    pending = [[next(plan), order, plan] for order, plan in enumerate(plans)]
    while pending:
        pending.sort(key=lambda entry: entry[:2])
        entry = pending[0]
        yield entry[0]
        try:
            entry[0] = max(entry[0], next(entry[2]))
        except StopIteration:
            pending.pop(0)


def column_block(ref, row):
    return ref.at[:, pl.ds(pl.multiple_of(row * 512, 512), 512)]


def down_slot(ref, slot, row):
    rows = pl.ds(pl.multiple_of(slot * PIECE, PIECE), PIECE)
    return ref.at[rows, pl.ds(pl.multiple_of(row * 512, 512), 512)]


def own_token_rows(ref, row):
    return ref.at[pl.ds(pl.multiple_of(row * OWN, OWN), OWN)]


def recut(place, wires, own, out, when):
    peers = [place.peer(step) for step in (1, 2, 3)]
    kept = wires.keep(column_block(own, place.row), own_token_rows(out, place.row))
    moved = wires.batch(
        [
            (column_block(own, other), own_token_rows(out, place.row), device)
            for other, device in peers
        ],
        out.at[pl.ds(0, 3 * OWN)],
    )
    yield when
    kept.wait()
    moved()


def back_pieces(place, wires, part_of, out, when):
    peers = [place.peer(step) for step in (1, 2, 3)]
    kept = wires.keep(part_of(place.row), out.at[place.row])
    moved = wires.batch(
        [(part_of(other), out.at[place.row], device) for other, device in peers],
        out.at[pl.ds(0, 3)],
    )
    yield when
    kept.wait()
    moved()


HEADS_TIMES = (2.6, 9.4, 10.0, 15.0, 15.5, 16.0, 20.0, 23.5)
MERGE_TIMES = (3.2, 11.2, 12.0, 16.5, 18.0, 18.5, 22.0, 26.0)
DOWN_TIMES = (16.2, 23.6, 24.2, 31.0, 34.0, 34.5, 39.0, 49.0)
GATING_TIMES = (24.5, 38.0, 40.0, 49.5, 53.0, 55.0, 60.0, 66.0)


def opening_kernel(
    heads_weight, merge_weight, gating_weight, down_weight, input_own, back_own, gains_own,
    *refs,
):
    (
        normed_out, query_out, pair_out, sums_out, cosine_out, sine_out, attended_out, merge_out,
        heads_out, middle_out, grad_middle_out, branch_out, gain_part_out, gating_sum_out,
        down_part_out, down_out, gains_out, input_rows_out,
    ) = refs[:18]
    line_scratch, scratch = refs[18:21], refs[21:]
    ring_scratch, scratch = scratch[:RING_SCATTER_SCRATCH], scratch[RING_SCATTER_SCRATCH:]
    (
        tokens, part, back, gating, grad_hidden, hidden, grad_gated, rows_own,
        heads_cut, merge_cut, gating_cut, down_cut,
        query, pair, sums, cosine, sine, attended, merge, heads, middle, grad_middle, branch,
        gain_part, gating_sum, down, gains, input_rows, merge_all,
        send, recv, local,
    ) = scratch
    handed = []

    def hand(*pairs):
        handed.extend(wires.keep(source, target) for source, target in pairs)

    place = Place()
    wires = Wires(send, recv, local)
    first_wires, token_wires, gating_wires, down_wires = [wires.part() for _ in range(4)]
    users, homes = merge_devices(place)
    peers = [place.peer(step) for step in (1, 2, 3)]
    same = place.row == place.y
    devices = ring_neighbours(place) + line_neighbours(place) + [p for _, p in peers]
    signal_others(place, devices + homes)
    for row in range(4):
        group, half = divmod(row, 2)
        rows = heads_weight[:, pl.ds(group * 640 + half * 256, 256)]
        heads_cut[row, :, pl.ds(0, 256)] = rows.astype(BF16)
        rows = heads_weight[:, pl.ds(group * 640 + 512, 128)]
        heads_cut[row, :, pl.ds(256, 128)] = rows.astype(BF16)
        for side in range(2):
            piece = merge_weight[pl.ds(16 * row, 16), pl.ds(256 * side, 256)]
            merge_cut[row, pl.ds(16 * side, 16)] = piece.astype(BF16)
    pl.semaphore_wait(
        pltpu.get_barrier_semaphore(), len(devices) + 4 - same.astype(jnp.int32)
    )
    merge_came, down_came, gating_came = [], [], []

    def exchange():
        yield 0.0
        came = [wires.keep(heads_cut.at[place.row], heads.at[place.row, place.dp]).wait]
        came.append(wires.keep(gains_own, column_block(gains, place.row)).wait)
        came.append(
            wires.batch(
                [
                    (heads_cut.at[other], heads.at[place.row, place.dp], device)
                    for other, device in peers
                ],
                heads_cut.at[pl.ds(0, 3)],
            )
        )
        merge_came.append(
            merge_exchange(
                place, wires, users,
                lambda j: merge_cut.at[j],
                lambda j: merge_all.at[place.row, j * 4 + place.z],
                place.row,
            )
        )
        came.append(
            wires.batch(
                [(gains_own, column_block(gains, place.row), device) for _, device in peers],
                gains.at[:, pl.ds(0, 1536)],
            )
        )
        for row in range(4):
            piece = down_weight[pl.ds(PIECE_USED * row, PIECE_USED), :]
            down_cut[row] = jnp.concatenate(
                [piece, jnp.zeros((PIECE - PIECE_USED, 512), F32)], axis=0
            ).astype(BF16)
        target = down_slot(down, place.dp, place.row)
        down_came.append(wires.keep(down_cut.at[place.row], target).wait)
        down_came.append(
            wires.batch(
                [(down_cut.at[other], target, device) for other, device in peers],
                down_cut.at[pl.ds(0, 3)],
            )
        )
        yield 2.6
        for wait in came:
            wait()
        yield from nested(
            ring_gather(place, wires, Rows(HEADS_COLS), heads, side, HEADS_TIMES)
            for side in (0, 1)
        )

    def gating_exchange():
        yield 3.0
        zeros = jnp.zeros((32, PIECE - PIECE_USED), F32)
        for kind in range(2):
            for row in range(4):
                pieces = []
                for slot in range(16):
                    first = slot * 4 * PIECE_USED + row * PIECE_USED
                    pieces += [gating_weight[:, kind, pl.ds(first, PIECE_USED)], zeros]
                gating_cut[row, :, pl.ds(kind * HIDDEN, HIDDEN)] = jnp.concatenate(
                    pieces, axis=1
                ).astype(BF16)
        yield 17.6
        target = gating.at[place.row, place.dp]
        gating_came.append(wires.keep(gating_cut.at[place.row], target).wait)
        gating_came.append(
            wires.batch(
                [(gating_cut.at[other], target, device) for other, device in peers],
                gating_cut.at[pl.ds(0, 3)],
            )
        )

    def tables():
        yield 3.4
        rope_tables(cosine, sine)

    def merge_rows():
        yield 3.2
        for wait in merge_came:
            wait()
        yield from nested(
            ring_gather(place, wires, Rows(256), merge_all, side, MERGE_TIMES) for side in (0, 1)
        )

    def down_rows():
        yield 16.2
        for wait in down_came:
            wait()
        yield from nested(
            ring_gather(place, down_wires, Flat(), down, side, DOWN_TIMES) for side in (0, 1)
        )

    def gating_rows():
        yield 24.5
        for wait in gating_came:
            wait()
        yield from nested(
            ring_gather(place, gating_wires, Rows(2 * HIDDEN), gating, side, GATING_TIMES)
            for side in (0, 1)
        )

    def chip_rows(offset):
        start = pl.multiple_of(lax.rem(place.x + offset + 4, 4) * 256, 256)
        return pl.ds(start, 256)

    def grad_hidden_rows():
        for index in range(4):
            yield 60.5 + 1.3 * index
            at = pl.ds(index * 256, 256)
            grad_hidden[at, :] = contract_last(back[at, :], down[...])

    def forward(offset, when):
        at = chip_rows(offset)
        for tile in range(3):
            gate_at, up_at = pl.ds(tile * 256, 256), pl.ds(HIDDEN + tile * 256, 256)
            rows = tokens[at, :]
            gate = product(rows, gating[:, :, :, gate_at].reshape(MODEL_WIDTH, 256))
            up = product(rows, gating[:, :, :, up_at].reshape(MODEL_WIDTH, 256))
            grad = grad_hidden[at, gate_at]
            sigmoid = jax.nn.sigmoid(gate)
            silu = gate * sigmoid
            hidden[at, gate_at] = (silu * up).astype(BF16)
            grad_gated[at, gate_at] = (grad * up * sigmoid * (1.0 + gate * (1.0 - sigmoid))).astype(
                BF16
            )
            grad_gated[at, up_at] = (grad * silu).astype(BF16)
            yield when + 0.6 * (tile + 1)
        for row in range(4):
            part[at, pl.ds(row * 512, 512)] = contract_last(
                grad_gated[at, :], gating[row].reshape(512, 2 * HIDDEN)
            ).astype(BF16)
            if row % 2:
                yield when + 2.0 + 0.6 * row

    def main():
        yield 0.1
        yield from line_gather(
            place, token_wires, input_own, tokens, tile_block, tile_half, (0.1, 17.5, 24.6, 26.4)
        )
        input_rows[...] = token_block(tokens, place.line(0, 0))[...]
        yield 26.6
        normed = branch
        first = LineScatter(place, first_wires, part, line_scratch)
        yield from projections(
            tokens, gains, heads, cosine, sine, normed, query, pair,
        )
        normed_copy = wires.keep(normed, normed_out)
        token_wires.drain()
        yield 31.7
        for row in range(4):
            for slot in range(16):
                y, z = divmod(slot, 4)
                for half in range(2):
                    merge[pl.ds(z * 64 + y * 16, 16), pl.ds(row * 512 + half * 256, 256)] = (
                        merge_all[row, slot, pl.ds(16 * half, 16), :]
                    )
        then = [None, first.far, lambda: first.near(1), lambda: first.near(3)]
        for order, offset in enumerate((2, 1, -1, 0)):
            at = chip_rows(offset)
            when = 32.2 + 3.8 * order
            for _ in attention(
                at, lax.rem(place.x + offset + 4, 4), query, pair, sums, attended
            ):
                yield when + 1.5
                if order:
                    then[order]()
            part[at, :] = product(attended[at, :], merge[...]).astype(BF16)
            first.pair(offset % 4)
            yield when + 3.8
        hand(
            (query, query_out), (pair, pair_out), (sums, sums_out), (cosine, cosine_out),
            (sine, sine_out), (attended, attended_out), (merge, merge_out), (heads, heads_out),
            (gains, gains_out), (input_rows, input_rows_out),
        )
        yield 48.0
        first.join()
        yield 58.0
        first.finish()

        def chunk(index, carry):
            at = pl.ds(pl.multiple_of(index * 16, 16), 16)
            total = first.total_of(at) + input_rows[at, :].astype(F32)
            middle[at, :] = total
            scale = lax.rsqrt(
                jnp.sum(total * total, axis=1, keepdims=True) / MODEL_WIDTH + EPS_NORM
            )
            rows_own[at, :] = (total * scale * gains[1:2, :]).astype(BF16)
            return carry

        lax.fori_loop(0, OWN // 16, chunk, 0)
        first_wires.drain()
        normed_copy.wait()
        hand((middle, middle_out))
        me, block, half = place.line(0, 0), token_block, token_half
        mine = wires.keep(rows_own, block(tokens, me))
        near = token_wires.batch(
            [(rows_own, block(tokens, me), place.near(x=step)) for step in (1, -1)],
            tokens.at[pl.ds(0, 2 * OWN)],
        )
        beside = token_wires.push(rows_own, block(tokens, me), place.near(core=1))

        def pass_beside(offset):
            came = block(tokens, place.line(offset, 0))
            return token_wires.push(came, came, place.near(core=1))

        second = LineScatter(place, wires, part, line_scratch)
        yield 70.0
        mine.wait()
        beside()
        yield from forward(0, 70.0)
        second.pair(0)
        yield 78.5
        near()
        pieces = [half(tokens, place.line(-1, 0), 0), half(tokens, place.line(1, 0), 1)]
        far = token_wires.batch(
            [(piece, piece, place.near(x=step)) for piece, step in zip(pieces, (1, -1))],
            tokens.at[pl.ds(0, OWN)],
        )
        beside_left, beside_right = pass_beside(-1), pass_beside(1)
        yield 80.5
        beside_left()
        beside_right()
        yield from forward(1, 80.5)
        second.pair(1)
        yield 84.1
        yield from forward(-1, 84.1)
        second.pair(3)
        second.near(1)
        yield 87.8
        far()
        beside_far = pass_beside(2)
        yield 89.5
        beside_far()
        yield from forward(2, 89.5)
        second.pair(2)
        second.near(3)
        yield 94.5
        second.far()
        yield from second.rest(94.0, 11.4)
        gain_part[...] = jnp.zeros_like(gain_part)
        back_own_rows = token_block(back, place.line(0, 0))

        def chunk_back(index, carry):
            at = pl.ds(pl.multiple_of(index * 16, 16), 16)
            through, gain = norm_back(middle[at, :], gains[1:2, :], second.total_of(at))
            total = back_own_rows[at, :].astype(F32) + through
            grad_middle[at, :] = total
            rows_own[at, :] = total.astype(BF16)
            gain_part[...] += gain.reshape(2, 8, MODEL_WIDTH).sum(axis=0)
            return carry

        token_wires.drain()
        lax.fori_loop(0, OWN // 16, chunk_back, 0)

        def ready(offsets):
            hand(*[(branch.at[chip_rows(o)], branch_out.at[chip_rows(o)]) for o in offsets])

        yield from line_gather(
            place, wires, rows_own, branch, token_block, token_half, (117.2, 131.0, 138.8, 141.0), ready
        )
        hand((grad_middle, grad_middle_out), (gain_part, gain_part_out))

    computed = []

    def gradients():
        yield 94.6
        gating_wires.drain()
        for row in range(4):
            for piece in range(2):
                columns = pl.ds(row * 512 + piece * 256, 256)
                gating[row, pl.ds(8 * piece, 8)] = (
                    token_product(tokens[:, columns], grad_gated[...])
                    .astype(BF16)
                    .reshape(8, 32, 2 * HIDDEN)
                )
                computed.append(row)
                yield 96.0 + 1.05 * (2 * row + piece + 1)

    def gradient_side(side):
        yield 100.3 + 4.2 * side
        assert len(computed) >= 4 + 4 * side
        yield from ring_scatter(
            place, wires, Rows(2 * HIDDEN), gating, side, ring_scratch,
            gating_sum.at[pl.ds(2 * side, 2)], 100.3 + 4.2 * side, 4.3,
        )
        hand((gating_sum.at[pl.ds(2 * side, 2)], gating_sum_out.at[pl.ds(2 * side, 2)]))

    def down_products():
        yield 106.9
        token_wires.drain()
        for index in range(4):
            at = pl.ds(index * 256, 256)
            tokens[at, :] = product(hidden[at, :], down[...]).astype(BF16)
            hand((tokens.at[at], down_out.at[at]))
            yield 107.9 + 1.0 * index
        down_wires.drain()
        for tile in range(3):
            columns = pl.ds(tile * 256, 256)
            down[columns, :] = token_product(hidden[:, columns], back[...]).astype(BF16)
            hand((down.at[columns], down_part_out.at[columns]))
            yield 112.3 + 1.2 * tile

    interleave(
        main(),
        exchange(),
        gating_exchange(),
        merge_rows(),
        tables(),
        down_rows(),
        gating_rows(),
        line_gather(
            place, wires, back_own, back, tile_block, tile_half, (26.5, 38.0, 50.5, 52.0)
        ),
        grad_hidden_rows(),
        gradients(),
        gradient_side(0),
        gradient_side(1),
        down_products(),
        sweep([wires, gating_wires, down_wires], 66.0, 76.5),
        sweep([wires, token_wires], 117.5, 126.0),
    )
    wires.drain()
    for copy in handed:
        copy.wait()


def norm_back(values, gain_row, gradient):
    scale = lax.rsqrt(jnp.sum(values * values, axis=1, keepdims=True) / MODEL_WIDTH + EPS_NORM)
    weighted = gain_row * gradient
    inner = jnp.sum(weighted * values, axis=1, keepdims=True)
    through = scale * weighted - values * (scale * scale * scale * inner / MODEL_WIDTH)
    return through, gradient * values * scale


def turn(tile, cosine, sine):
    lane = lax.broadcasted_iota(jnp.int32, tile.shape, 1)
    first = lax.rem(lane, HEAD_SIZE) < HEAD_SIZE // 2
    swapped = jnp.where(first, pltpu.roll(tile, 96, axis=1), pltpu.roll(tile, 32, axis=1))
    return tile * cosine + swapped * sine


def rope_tables(cosine, sine):
    half_width = HEAD_SIZE // 2

    def chunk(index, carry):
        at = pl.ds(pl.multiple_of(index * 128, 128), 128)
        lane = lax.broadcasted_iota(jnp.int32, (128, 128), 1)
        row = lax.broadcasted_iota(jnp.int32, (128, 128), 0) + index * 128
        frequency = jnp.exp(
            lax.rem(lane, half_width).astype(F32) * (-2.0 / HEAD_SIZE * math.log(ROPE_BASE))
        )
        angles = row.astype(F32) * frequency
        cosine[at, :] = jnp.cos(angles)
        first = lax.rem(lane, HEAD_SIZE) < half_width
        sine[at, :] = jnp.where(first, -jnp.sin(angles), jnp.sin(angles))
        return carry

    lax.fori_loop(0, SEQ // 128, chunk, 0)


def keys_only(cosine, sine):
    key = lax.broadcasted_iota(jnp.int32, cosine.shape, 1) < HEAD_SIZE
    return jnp.where(key, cosine, 1.0), jnp.where(key, sine, 0.0)


def heads_weight_of(heads):
    return heads[...].reshape(MODEL_WIDTH, HEADS_COLS)


QUERY_BLOCK = 256


def projections(
    inputs, gains, heads, cosine, sine,
    normed, query, pair,
):
    for index in range(4):
        at = pl.ds(index * 256, 256)
        wide = inputs[at, :].astype(F32)
        scale = lax.rsqrt(jnp.sum(wide * wide, axis=1, keepdims=True) / MODEL_WIDTH + EPS_NORM)
        low = (wide * scale * gains[0:1, :]).astype(BF16)
        normed[at, :] = low
        mixed = product(low, heads_weight_of(heads))
        cos, sin = cosine[at, :], sine[at, :]
        query[at, pl.ds(0, 128)] = turn(mixed[:, :128], cos, sin).astype(BF16)
        query[at, pl.ds(128, 128)] = turn(mixed[:, 128:256], cos, sin).astype(BF16)
        pair[at, :] = turn(mixed[:, 256:], *keys_only(cos, sin)).astype(BF16)
        yield 26.6 + 1.25 * (index + 1)


def attention(at, block, query, pair, sums, attended):
    scale = HEAD_SIZE ** (-0.5)
    rows_at = lax.broadcasted_iota(jnp.int32, (QUERY_BLOCK, QUERY_BLOCK), 0)
    keys_at = lax.broadcasted_iota(jnp.int32, (QUERY_BLOCK, QUERY_BLOCK), 1)
    out, logs = [], []
    for two in range(2):
        if two:
            yield
        queries = [
            query[at, pl.ds(head * HEAD_SIZE, HEAD_SIZE)] for head in (2 * two, 2 * two + 1)
        ]

        def weigh(rows, keys):
            return contract_last(rows, pair[keys, pl.ds(0, HEAD_SIZE)]) * scale

        def values(keys):
            return pair[keys, pl.ds(HEAD_SIZE, HEAD_SIZE)]

        state = []
        for rows in queries:
            scores = jnp.where(rows_at >= keys_at, weigh(rows, at), MASK_FILL)
            top = jnp.max(scores, axis=1, keepdims=True)
            powers = jnp.exp(scores - top)
            total = jnp.sum(powers, axis=1, keepdims=True)
            state.append((top, total, product(powers.astype(BF16), values(at))))

        def step(index, state):
            keys = pl.ds(pl.multiple_of(index * QUERY_BLOCK, QUERY_BLOCK), QUERY_BLOCK)
            result = []
            for rows, (top, total, mean) in zip(queries, state):
                scores = weigh(rows, keys)
                higher = jnp.maximum(top, jnp.max(scores, axis=1, keepdims=True))
                shrink = jnp.exp(top - higher)
                powers = jnp.exp(scores - higher)
                total = total * shrink + jnp.sum(powers, axis=1, keepdims=True)
                mean = mean * shrink + product(powers.astype(BF16), values(keys))
                result.append((higher, total, mean))
            return tuple(result)

        for top, total, mean in lax.fori_loop(0, block, step, tuple(state)):
            out.append((mean * (1.0 / total)).astype(BF16))
            logs.append(top + jnp.log(total))
    logs.append(jnp.zeros((QUERY_BLOCK, 124), F32))
    sums[:, at] = jnp.transpose(jnp.concatenate(logs, axis=1))[:8]
    attended[at, :] = jnp.concatenate(out, axis=1)


def backward_kernel(*refs):
    given, refs = refs[:18], refs[18:]
    (
        output, input_grad, gains_grad, heads_pieces, merge_pieces, gating_pieces, down_pieces,
    ) = refs[:7]
    out_scratch, scratch = refs[7:10], refs[10:]
    line_scratch, scratch = scratch[:3], scratch[3:]
    down_scratch, scratch = scratch[:8], scratch[8:]
    heads_scratch, scratch = scratch[:8], scratch[8:]
    held, scratch = scratch[:18], scratch[18:]
    (
        branch, merge, query, pair, sums, cosine, sine, down_out, down_part, gating_sum,
        middle, heads, attended, normed, grad_middle, input_rows, gains, gain_part,
    ) = held
    (
        part, grad_mixed, grad_attended, grad_key, grad_value, key_columns, rows_own,
        down_sum, heads_all, heads_sum, input_grad_own, gain_rows, gain_came, gain_all,
        send, recv, local,
    ) = scratch
    place = Place()
    wires = Wires(send, recv, local)
    loads = [wires.keep(source, target) for source, target in zip(given, held)]

    def need(*names):
        for index in names:
            if loads[index] is not None:
                loads[index].wait()
                loads[index] = None

    users, homes = merge_devices(place)
    peers = [place.peer(step) for step in (1, 2, 3)]
    same = place.row == place.y
    barrier = pltpu.get_barrier_semaphore()
    devices = ring_neighbours(place) + line_neighbours(place) + [p for _, p in peers]
    signal_others(place, devices + users)

    def far(step):
        index = lax.rem(place.col * 16 + place.dp + step, 32)
        return {"dp": lax.rem(index, 16), "row": place.row, "col": lax.div(index, 16)}

    def greet(step, carry):
        pl.semaphore_signal(barrier, inc=1, device_id=far(step), device_id_type=MESH)
        return carry

    lax.fori_loop(1, 32, greet, 0)
    need(0, 1)
    attend = attention_back(
        branch, merge, query, pair, sums, cosine, sine, grad_mixed,
        grad_attended, grad_key, grad_value, key_columns,
    )
    next(attend)
    next(attend)
    pl.semaphore_wait(barrier, len(devices) + 31 + 4 - same.astype(jnp.int32))

    def outputs():
        yield 0.1
        need(7)
        scatter = LineScatter(place, wires, down_out, out_scratch)
        yield from scatter.run(0.1, 11.4)
        yield 21.2
        need(10)

        def chunk(index, carry):
            at = pl.ds(pl.multiple_of(index * 16, 16), 16)
            rows_own[at, :] = (scatter.total_of(at) + middle[at, :]).astype(BF16)
            return carry

        lax.fori_loop(0, OWN // 16, chunk, 0)
        yield 26.3
        yield from recut(place, wires, rows_own, output, 46.0)

    def down_rows():
        yield 0.3
        need(8)
        yield from nested(
            ring_scatter(
                place, wires, Flat(), down_part, side, down_scratch,
                down_sum.at[:, pl.ds(side * 1024, 1024)], 0.3, 2.1,
            )
            for side in (0, 1)
        )
        yield from back_pieces(
            place, wires, lambda row: column_block(down_sum, row), down_pieces, 46.0
        )

    def gating():
        yield 0.4
        need(9)
        yield from back_pieces(
            place, wires, lambda row: gating_sum.at[row], gating_pieces, 36.0
        )

    def compute():
        yield 0.2
        need(2, 3, 4, 5, 6)
        yield from attend
        need(11)
        scatter = LineScatter(place, wires, part, line_scratch)
        then = [None, scatter.far, lambda: scatter.near(1), None]
        for order, offset in enumerate((2, 1, -1, 0)):
            start = pl.multiple_of(lax.rem(place.x + offset + 4, 4) * 256, 256)
            at = pl.ds(start, 256)
            for row in range(4):
                part[at, pl.ds(row * 512, 512)] = contract_last(
                    grad_mixed[at, :],
                    heads[row].reshape(512, HEADS_COLS),
                ).astype(BF16)
            scatter.pair(offset % 4)
            if then[order]:
                then[order]()
        yield 19.6
        yield from gradient(scatter)

    computed = []

    def weights():
        yield 21.5
        need(12, 13, 16, 17)
        gain_rows[...] = jnp.zeros_like(gain_rows)
        gain_rows[1:2, :] = jnp.sum(gain_part[...], axis=0, keepdims=True)
        ones = jnp.ones((8, HEADS_COLS), BF16)
        for row in range(4):
            columns = pl.ds(row * 512, 512)
            merge_part = token_product(attended[...], branch[:, columns]).astype(BF16)
            for slot in range(16):
                y, z = divmod(slot, 4)
                for half in range(2):
                    heads_all[row, slot, pl.ds(16 * half, 16), pl.ds(HEADS_COLS, 256)] = (
                        merge_part[
                            z * 64 + y * 16 : z * 64 + y * 16 + 16,
                            half * 256 : half * 256 + 256,
                        ]
                    )
            for piece in range(2):
                columns = pl.ds(row * 512 + piece * 256, 256)
                grad = token_product(normed[:, columns], grad_mixed[...])
                slots = pl.ds(8 * piece, 8)
                heads_all[row, slots, :, pl.ds(0, HEADS_COLS)] = grad.astype(BF16).reshape(
                    8, 32, HEADS_COLS
                )
                weight = heads[row, slots].reshape(256, HEADS_COLS)
                terms = grad * weight.astype(F32)
                high = terms.astype(BF16)
                low = (terms - high.astype(F32)).astype(BF16)
                sums_ = contract_last(ones, high) + contract_last(ones, low)
                gain_rows[0:1, columns] = sums_[0:1] / gains[0:1, columns]
            computed.append(row)
            yield 21.5 + 1.55 * (row + 1)
        yield from gain_sums()

    def heads_side(side):
        yield 24.7 + 3.1 * side
        assert len(computed) >= 2 + 2 * side
        yield from ring_scatter(
            place, wires, Rows(HEADS_COLS + 256), heads_all, side, heads_scratch,
            heads_sum.at[pl.ds(2 * side, 2)], 24.7 + 3.1 * side, 1.8,
        )
        computed.append("side")

    def heads_back():
        yield 49.4
        assert computed.count("side") == 2
        merge_wait = merge_exchange(
            place, wires, homes,
            lambda row: heads_sum.at[row, :, pl.ds(HEADS_COLS, 256)],
            lambda row: merge_pieces.at[place.y],
            place.y,
        )
        yield from back_pieces(
            place, wires,
            lambda row: heads_sum.at[row, :, pl.ds(0, HEADS_COLS)], heads_pieces, 55.0,
        )
        merge_wait()

    def gain_sums():
        moved = wires.batch(
            [
                (column_block(gain_rows, other), gain_came.at[place.row], device)
                for other, device in peers
            ],
            gain_came.at[pl.ds(0, 3)],
        )
        kept = wires.keep(column_block(gain_rows, place.row), gain_came.at[place.row])
        yield 36.5
        kept.wait()
        moved()
        local_sum = gain_came[0] + gain_came[1] + gain_came[2] + gain_came[3]
        me = place.col * 16 + place.dp
        for kind in range(2):
            for tile in range(4):
                gain_all[me, pl.ds(4 * kind + tile, 1), :] = local_sum[
                    kind : kind + 1, tile * 128 : tile * 128 + 128
                ]
        send, recv = wires.reserve("send"), wires.reserve("recv")

        def start(step, carry):
            wires.start(gain_all.at[me], gain_all.at[me], far(step), send, recv)
            return carry

        lax.fori_loop(1, 32, start, 0)
        wires.owe(send, gain_all.at[pl.ds(0, 31)])
        yield 50.0
        wires.take(wires.recv.at[recv], gain_all.at[pl.ds(0, 31)])
        gains_grad[...] = functools.reduce(lambda a, b: a + b, [gain_all[i] for i in range(32)])

    def gradient(scatter):
        scatter.near(3)
        yield 26.2
        scatter.join()
        yield 36.0
        scatter.finish()
        need(14, 15)

        def chunk(index, carry):
            at = pl.ds(pl.multiple_of(index * 16, 16), 16)
            grad = scatter.total_of(at)
            through, _ = norm_back(input_rows[at, :].astype(F32), gains[0:1, :], grad)
            input_grad_own[at, :] = (grad_middle[at, :] + through).astype(BF16)
            return carry

        lax.fori_loop(0, OWN // 16, chunk, 0)
        yield from recut(place, wires, input_grad_own, input_grad, 52.0)

    interleave(
        compute(),
        outputs(),
        down_rows(),
        gating(),
        weights(),
        heads_side(0),
        heads_side(1),
        heads_back(),
        sweep([wires], 30.0, 35.9),
    )
    wires.drain()


def attention_back(
    branch, merge, query, pair, sums, cosine, sine, grad_mixed,
    grad_attended, grad_key, grad_value, key_columns,
):
    yield 0.3
    def attended_rows(index, carry):
        at = pl.ds(pl.multiple_of(index * 512, 512), 512)
        grad_attended[at, :] = contract_last(branch[at, :], merge[...]).astype(BF16)
        return carry

    attended_rows(0, 0)
    yield 2.0
    attended_rows(1, 0)
    key_columns[...] = jnp.transpose(pair[...].astype(F32))[:HEAD_SIZE].astype(BF16)
    grad_key[...] = jnp.zeros_like(grad_key)
    grad_value[...] = jnp.zeros_like(grad_value)
    scale = HEAD_SIZE ** (-0.5)
    keys_at = lax.broadcasted_iota(jnp.int32, (QUERY_BLOCK, QUERY_BLOCK), 0)
    rows_at = lax.broadcasted_iota(jnp.int32, (QUERY_BLOCK, QUERY_BLOCK), 1)
    for block in range(SEQ // QUERY_BLOCK):
        at = pl.ds(block * QUERY_BLOCK, QUERY_BLOCK)
        before = block * QUERY_BLOCK
        for two in range(2):
            turned = []
            for head in (2 * two, 2 * two + 1):
                columns = pl.ds(head * HEAD_SIZE, HEAD_SIZE)
                rows, back = query[at, columns], grad_attended[at, columns]
                log_total = sums[pl.ds(head, 1), at]
                spans = [at] + ([pl.ds(0, before)] if before else [])
                softs, grads = [], []
                for span in spans:
                    scores = contract_last(pair[span, pl.ds(0, HEAD_SIZE)], rows) * scale
                    soft = jnp.exp(scores - log_total)
                    if span is at:
                        soft = jnp.where(rows_at >= keys_at, soft, 0.0)
                    softs.append(soft)
                    grads.append(contract_last(pair[span, pl.ds(HEAD_SIZE, HEAD_SIZE)], back))
                inner = functools.reduce(
                    lambda a, b: a + b,
                    [jnp.sum(s * g, axis=0, keepdims=True) for s, g in zip(softs, grads)],
                )
                result = 0.0
                for span, soft, grad in zip(spans, softs, grads):
                    low = (soft * (grad - inner)).astype(BF16)
                    grad_key[span, :] += product(low, rows)
                    grad_value[span, :] += product(soft.astype(BF16), back)
                    result += product(key_columns[:, span], low)
                turned.append(result)
                yield 1.9 + (2.1, 5.0, 8.7, 13.2)[block] - (0.52, 0.72, 0.92, 1.15)[block] * (3 - head)
            tile = jnp.transpose(jnp.concatenate(turned, axis=0)) * scale
            grad_mixed[at, pl.ds(two * 128, 128)] = turn(
                tile, cosine[at, :], -sine[at, :]
            ).astype(BF16)

    def finish_rows(index, carry):
        at = pl.ds(pl.multiple_of(index * 128, 128), 128)
        cos, sin = keys_only(cosine[at, :], sine[at, :])
        tile = jnp.concatenate([grad_key[at, :] * scale, grad_value[at, :]], axis=1)
        grad_mixed[at, pl.ds(256, 128)] = turn(tile, cos, -sin).astype(BF16)
        return carry

    lax.fori_loop(0, SEQ // 128, finish_rows, 0)


def product(left, right):
    return jnp.dot(left, right, preferred_element_type=F32)


def contract_last(left, right):
    return lax.dot_general(left, right, (((1,), (1,)), ((), ())), preferred_element_type=F32)


def token_product(left, right):
    return lax.dot_general(left, right, (((0,), (0,)), ((), ())), preferred_element_type=F32)


def adamw(current, gradient, first, second, step_rate, decay_rate):
    mean_new = BETA_ONE * first + (1.0 - BETA_ONE) * gradient
    square_new = BETA_TWO * second + (1.0 - BETA_TWO) * gradient * gradient
    mean_hat = mean_new / (1.0 - BETA_ONE**STEP)
    square_hat = square_new / (1.0 - BETA_TWO**STEP)
    updated = current - step_rate * (
        mean_hat / (jnp.sqrt(square_hat) + EPS_ADAM) + decay_rate * current
    )
    return (updated, mean_new, square_new)


def update_kernel(*refs):
    output_given, input_grad_given, gains, heads, merge, gating, down = refs[:7]
    states = [refs[7 + 3 * n : 10 + 3 * n] for n in range(5)]
    output, input_grad = refs[22:24]
    results = [refs[24 + 4 * n : 28 + 4 * n] for n in range(5)]
    output[...] = output_given[...]
    input_grad[...] = input_grad_given[...].astype(F32)
    gains_grad, heads_grad, merge_grad, gating_grad, down_grad = [r[0] for r in results]
    for kind in range(2):
        for tile in range(4):
            gains_grad[pl.ds(kind, 1), pl.ds(tile * 128, 128)] = gains[
                pl.ds(4 * kind + tile, 1), :
            ]
    for row in range(4):
        group, half = divmod(row, 2)
        heads_grad[:, pl.ds(group * 640 + half * 256, 256)] = heads[
            row, :, pl.ds(0, 256)
        ].astype(F32)
        for side in range(2):
            merge_grad[pl.ds(16 * row, 16), pl.ds(256 * side, 256)] = merge[
                row, pl.ds(16 * side, 16)
            ].astype(F32)
        down_grad[pl.ds(PIECE_USED * row, PIECE_USED), :] = down[row].astype(F32)[:PIECE_USED]
    for group in range(2):
        pair = pl.ds(256, 128)
        heads_grad[:, pl.ds(group * 640 + 512, 128)] = heads[2 * group, :, pair].astype(
            F32
        ) + heads[2 * group + 1, :, pair].astype(F32)
    for kind in range(2):
        rows = [gating[row, :, pl.ds(kind * HIDDEN, HIDDEN)].astype(F32) for row in range(4)]
        whole = jnp.concatenate(
            [
                rows[row][:, slot * PIECE : slot * PIECE + PIECE_USED]
                for slot in range(16)
                for row in range(4)
            ],
            axis=1,
        )
        gating_grad[:, kind, :] = whole
    rates = [RATE_GAIN, RATE_MATRIX, RATE_MERGE, RATE_MATRIX, RATE_MATRIX]
    decays = [0.0] + [WEIGHT_DECAY] * 4
    for state, result, rate, decay in zip(states, results, rates, decays):
        rows = state[0].shape[0]
        step = 16 if rows % 16 == 0 else rows

        def chunk(index, carry):
            at = pl.ds(pl.multiple_of(index * step, step), step)
            new = adamw(state[0][at], result[0][at], state[1][at], state[2][at], rate, decay)
            for ref, value in zip(result[1:], new):
                ref[at] = value
            return carry

        lax.fori_loop(0, rows // step, chunk, 0)


def update(given, states):
    ins = list(given) + [array for state in states for array in state]
    outs = [shape(512, 512), shape(512, 512, dtype=F32)]
    for state in states:
        outs += [shape(*state[0].shape, dtype=F32)] * 4
    return pl.pallas_call(
        update_kernel,
        out_shape=outs,
        in_specs=[pl.BlockSpec(memory_space=pltpu.VMEM)] * len(ins),
        out_specs=[pl.BlockSpec(memory_space=pltpu.VMEM)] * len(outs),
        compiler_params=pltpu.CompilerParams(vmem_limit_bytes=VMEM_BYTES),
        cost_estimate=pl.CostEstimate(flops=2**24, bytes_accessed=2**24, transcendentals=2**20),
    )(*ins)


def body(
    block_input,
    cotangent,
    norm_gains,
    gains_first,
    gains_second,
    heads_projection_weight,
    heads_first_moment,
    heads_second_moment,
    merge_weight,
    merge_first,
    merge_second,
    gating_weight,
    gating_first,
    gating_second,
    down_weight,
    down_first,
    down_second,
):
    ANY, VMEM = pl.ANY, pltpu.VMEM
    saved = [
        shape(SEQ, 256),
        shape(SEQ, 128),
        shape(8, SEQ, dtype=F32),
        shape(SEQ, 128, dtype=F32),
        shape(SEQ, 128, dtype=F32),
        shape(SEQ, 256),
        shape(256, MODEL_WIDTH),
        shape(4, 16, 32, HEADS_COLS),
        shape(OWN, MODEL_WIDTH, dtype=F32),
        shape(OWN, MODEL_WIDTH, dtype=F32),
        shape(SEQ, MODEL_WIDTH),
        shape(8, MODEL_WIDTH, dtype=F32),
        shape(4, 32, 2 * HIDDEN),
        shape(16 * PIECE, MODEL_WIDTH),
        shape(2, MODEL_WIDTH, dtype=F32),
        shape(OWN, MODEL_WIDTH),
    ]

    def held(array):
        return pltpu.VMEM(array.shape, array.dtype)

    (
        normed_one, query, pair, sums, cosine, sine, attended, w_merge, w_heads,
        middle, grad_middle, branch, gain_part, gating_sum, down_part, down_out, gains, input_rows,
    ) = call(
        opening_kernel,
        [(shape(SEQ, MODEL_WIDTH), ANY)]
        + [(array, ANY) for array in saved[:14]]
        + [(shape(SEQ, MODEL_WIDTH), ANY)]
        + [(array, ANY) for array in saved[14:]],
        [
            (heads_projection_weight, VMEM),
            (merge_weight, VMEM),
            (gating_weight, VMEM),
            (down_weight, VMEM),
            (block_input, VMEM),
            (cotangent, VMEM),
            (norm_gains, VMEM),
        ],
        LINE_SCATTER_SCRATCH
        + ring_scatter_scratch(Rows(2 * HIDDEN))
        + [
            pltpu.VMEM((SEQ, MODEL_WIDTH), BF16),
            pltpu.VMEM((SEQ, MODEL_WIDTH), BF16),
            pltpu.VMEM((SEQ, MODEL_WIDTH), BF16),
            pltpu.VMEM((4, 16, 32, 2 * HIDDEN), BF16),
            pltpu.VMEM((SEQ, HIDDEN), F32),
            pltpu.VMEM((SEQ, HIDDEN), BF16),
            pltpu.VMEM((SEQ, 2 * HIDDEN), BF16),
            pltpu.VMEM((OWN, MODEL_WIDTH), BF16),
            pltpu.VMEM((4, 32, HEADS_COLS), BF16),
            pltpu.VMEM((4, 32, 256), BF16),
            pltpu.VMEM((4, 32, 2 * HIDDEN), BF16),
            pltpu.VMEM((4, PIECE, 512), BF16),
        ]
        + [held(array) for array in saved]
        + [pltpu.VMEM((4, 16, 32, 256), BF16)],
        (29, 117, 35),
        0,
        2**25,
    )
    given = [
        branch, w_merge, query, pair, sums, cosine, sine, down_out, down_part, gating_sum,
        middle, w_heads, attended, normed_one, grad_middle, input_rows, gains, gain_part,
    ]
    (
        block_output, input_grad, gains_grad,
        heads_pieces, merge_pieces, gating_pieces, down_pieces,
    ) = call(
        backward_kernel,
        [
            (shape(512, 512), VMEM),
            (shape(512, 512), VMEM),
            (shape(8, 128, dtype=F32), VMEM),
            (shape(4, 32, HEADS_COLS), VMEM),
            (shape(4, 32, 256), VMEM),
            (shape(4, 32, 2 * HIDDEN), VMEM),
            (shape(4, PIECE, 512), VMEM),
        ],
        [(array, ANY) for array in given],
        LINE_SCATTER_SCRATCH
        + LINE_SCATTER_SCRATCH
        + ring_scatter_scratch(Flat())
        + ring_scatter_scratch(Rows(HEADS_COLS + 256))
        + [held(array) for array in given]
        + [
            pltpu.VMEM((SEQ, MODEL_WIDTH), BF16),
            pltpu.VMEM((SEQ, HEADS_COLS), BF16),
            pltpu.VMEM((SEQ, 256), BF16),
            pltpu.VMEM((SEQ, HEAD_SIZE), F32),
            pltpu.VMEM((SEQ, HEAD_SIZE), F32),
            pltpu.VMEM((HEAD_SIZE, SEQ), BF16),
            pltpu.VMEM((OWN, MODEL_WIDTH), BF16),
            pltpu.VMEM((PIECE, MODEL_WIDTH), BF16),
            pltpu.VMEM((4, 16, 32, HEADS_COLS + 256), BF16),
            pltpu.VMEM((4, 32, HEADS_COLS + 256), BF16),
            pltpu.VMEM((OWN, MODEL_WIDTH), BF16),
            pltpu.VMEM((8, MODEL_WIDTH), F32),
            pltpu.VMEM((4, 8, 512), F32),
            pltpu.VMEM((32, 8, 128), F32),
        ],
        (17, 63, 24),
        3,
        2**25,
    )
    (
        block_output, input_grad,
        gains_grad, gains_next, gains_mean, gains_square,
        heads_grad, heads_next, heads_mean, heads_square,
        merge_grad, merge_next, merge_mean, merge_square,
        gating_grad, gating_next, gating_mean, gating_square,
        down_grad, down_next, down_mean, down_square,
    ) = update(
        (
            block_output, input_grad, gains_grad,
            heads_pieces, merge_pieces, gating_pieces, down_pieces,
        ),
        (
            (norm_gains, gains_first, gains_second),
            (heads_projection_weight, heads_first_moment, heads_second_moment),
            (merge_weight, merge_first, merge_second),
            (gating_weight, gating_first, gating_second),
            (down_weight, down_first, down_second),
        ),
    )
    return (
        block_output,
        input_grad,
        gains_grad,
        gains_next,
        gains_mean,
        gains_square,
        heads_grad,
        heads_next,
        heads_mean,
        heads_square,
        merge_grad,
        merge_next,
        merge_mean,
        merge_square,
        gating_grad,
        gating_next,
        gating_mean,
        gating_square,
        down_grad,
        down_next,
        down_mean,
        down_square,
    )


def solution(mesh):
    in_specs = (
        P(("dp", "col"), "row"),
        P(("dp", "col"), "row"),
        P(None, "row"),
        P(None, "row"),
        P(None, "row"),
        P(("row", "dp"), "col"),
        P(("row", "dp"), "col"),
        P(("row", "dp"), "col"),
        P(("col", "dp"), "row"),
        P(("col", "dp"), "row"),
        P(("col", "dp"), "row"),
        P(("row", "dp"), None, "col"),
        P(("row", "dp"), None, "col"),
        P(("row", "dp"), None, "col"),
        P(("col", "dp"), "row"),
        P(("col", "dp"), "row"),
        P(("col", "dp"), "row"),
    )
    out_specs = (
        P(("dp", "col"), "row"),
        P(("dp", "col"), "row"),
        P(None, "row"),
        P(None, "row"),
        P(None, "row"),
        P(None, "row"),
        P(("row", "dp"), "col"),
        P(("row", "dp"), "col"),
        P(("row", "dp"), "col"),
        P(("row", "dp"), "col"),
        P(("col", "dp"), "row"),
        P(("col", "dp"), "row"),
        P(("col", "dp"), "row"),
        P(("col", "dp"), "row"),
        P(("row", "dp"), None, "col"),
        P(("row", "dp"), None, "col"),
        P(("row", "dp"), None, "col"),
        P(("row", "dp"), None, "col"),
        P(("col", "dp"), "row"),
        P(("col", "dp"), "row"),
        P(("col", "dp"), "row"),
        P(("col", "dp"), "row"),
    )
    return jax.shard_map(body, mesh=mesh, in_specs=in_specs, out_specs=out_specs, check_vma=False)
```

```python
import functools
import math

import jax
import jax.numpy as jnp
from jax import lax
from jax.experimental import pallas as pl
from jax.experimental.pallas import tpu as pltpu
from jax.sharding import PartitionSpec as P

MODEL_WIDTH = 2048
KEY_VALUE_HEADS = 4
HEAD_SIZE = 64
QUERY_PER_GROUP = 8
STEP = 10


EPS_NORM = 1e-05
BETA_ONE = 0.9
BETA_TWO = 0.95
EPS_ADAM = 1e-08
RATE_MATRIX = 0.05
RATE_MERGE = 0.5
RATE_GAIN = 1.0
WEIGHT_DECAY = 0.1
ROPE_BASE = 10000.0
MASK_FILL = -1e30

MESH = pl.DeviceIdType.MESH
VMEM_BYTES = 63 * 2**20
BF16 = jnp.bfloat16
F32 = jnp.float32

SEQ = 1024
OWN = 128
HEADS_COLS = 384
HIDDEN = 768
PIECE = 48
PIECE_USED = 44


class Place:
    def __init__(self):
        self.dp = lax.axis_index("dp")
        self.row = lax.axis_index("row")
        self.col = lax.axis_index("col")
        self.y = lax.div(self.dp, 4)
        self.z = lax.rem(self.dp, 4)
        self.core = lax.rem(self.row, 2)
        self.x = self.col * 2 + lax.div(self.row, 2)

    def near(self, x=0, core=0, y=0, z=0):
        new_x = lax.rem(self.x + x + 4, 4)
        new_core = lax.rem(self.core + core, 2)
        new_y = lax.rem(self.y + y + 4, 4)
        new_z = lax.rem(self.z + z + 4, 4)
        return {
            "dp": new_y * 4 + new_z,
            "row": lax.rem(new_x, 2) * 2 + new_core,
            "col": lax.div(new_x, 2),
        }

    def slot(self, first_axis, first, second):
        y, z = (first, second) if first_axis == "y" else (second, first)
        return lax.rem(self.y + y + 4, 4) * 4 + lax.rem(self.z + z + 4, 4)

    def line(self, x, core):
        return lax.rem(self.x + x + 4, 4) * 2 + lax.rem(self.core + core, 2)

    def peer(self, step):
        other = lax.rem(self.row + step, 4)
        return other, {"dp": self.dp, "row": other, "col": self.col}


class Wires:
    def __init__(self, send, recv, local, parent=None):
        self.send, self.recv, self.local = send, recv, local
        self.root = parent or self
        self.used = {"send": 0, "recv": 0, "local": 0}
        self.debts = []

    def part(self):
        return Wires(self.send, self.recv, self.local, self.root)

    def reserve(self, kind, count=1):
        first = self.root.used[kind]
        self.root.used[kind] += count
        return first

    def start(self, source, target, device, send, recv):
        pltpu.make_async_remote_copy(
            src_ref=source,
            dst_ref=target,
            send_sem=self.send.at[send],
            recv_sem=self.recv.at[recv],
            device_id=device,
            device_id_type=MESH,
        ).start()

    def batch(self, copies, size, send=None):
        recv = self.reserve("recv")
        if send is None:
            send = self.reserve("send")
            self.owe(send, size)
        for source, target, device in copies:
            self.start(source, target, device, send, recv)
        return lambda: self.take(self.recv.at[recv], size)

    def push(self, source, target, device, send=None):
        return self.batch([(source, target, device)], target, send)

    def take(self, semaphore, size):
        pltpu.make_async_copy(size, size, semaphore).wait()

    def owe(self, send, size):
        self.debts.append((send, size))

    def keep(self, source, target):
        copy = pltpu.make_async_copy(source, target, self.local.at[self.reserve("local")])
        copy.start()
        return copy

    def settle(self, debts):
        for send, size in debts:
            self.take(self.send.at[send], size)
        self.debts = [debt for debt in self.debts if all(debt is not other for other in debts)]

    def drain(self):
        self.settle(list(self.debts))


def meet(devices, more=0):
    barrier = pltpu.get_barrier_semaphore()
    for device in devices:
        pl.semaphore_signal(barrier, inc=1, device_id=device, device_id_type=MESH)
    pl.semaphore_wait(barrier, len(devices))


def interleave(*plans):
    waiting = [[next(plan), order, plan] for order, plan in enumerate(plans)]
    while waiting:
        waiting.sort(key=lambda entry: (entry[0], entry[1]))
        entry = waiting[0]
        try:
            entry[0] = max(entry[0], next(entry[2]))
        except StopIteration:
            waiting.pop(0)


def sweep(accounts, since, until):
    yield since
    debts = [(account, debt) for account in accounts for debt in account.debts]
    yield until
    for account, debt in debts:
        if any(debt is other for other in account.debts):
            account.settle([debt])


def ring_neighbours(place):
    return [place.near(y=1), place.near(y=-1), place.near(z=1), place.near(z=-1)]


def line_neighbours(place):
    return [place.near(x=1), place.near(x=-1), place.near(core=1)]


def line_gather(place, wires, own, out, block, half, times, ready=None):
    def size(blocks):
        return out.at[pl.ds(0, blocks * OWN)]

    me = place.line(0, 0)
    send = wires.reserve("send")
    yield times[0]
    kept = wires.keep(own, block(out, me))
    near = wires.batch(
        [(own, block(out, me), place.near(x=1)), (own, block(out, me), place.near(x=-1))],
        size(2),
        send,
    )
    beside = [wires.push(own, block(out, me), place.near(core=1), send)]
    yield times[1]
    near()
    left, right = place.line(-1, 0), place.line(1, 0)
    far = wires.batch(
        [
            (half(out, left, 0), half(out, left, 0), place.near(x=1)),
            (half(out, right, 1), half(out, right, 1), place.near(x=-1)),
        ],
        size(1),
        send,
    )
    beside.append(
        wires.batch(
            [(block(out, came), block(out, came), place.near(core=1)) for came in (left, right)],
            size(2),
            send,
        )
    )
    yield times[2]
    kept.wait()
    for wait in beside:
        wait()
    if ready:
        ready((0, 1, -1))
    far()
    came = block(out, place.line(2, 0))
    last = wires.push(came, came, place.near(core=1), send)
    wires.owe(send, size(7))
    yield times[3]
    last()
    if ready:
        ready((2,))


def token_block(ref, index):
    return ref.at[pl.ds(pl.multiple_of(index * OWN, OWN), OWN)]


def token_half(ref, index, side):
    return ref.at[pl.ds(pl.multiple_of(index * OWN + side * (OWN // 2), OWN // 2), OWN // 2)]


def tile_block(ref, index):
    x, core = lax.div(index, 2), lax.rem(index, 2)
    rows = pl.ds(pl.multiple_of(lax.div(x, 2) * 512, 512), 512)
    columns = pl.ds(pl.multiple_of((lax.rem(x, 2) * 2 + core) * 512, 512), 512)
    return ref.at[rows, columns]


def tile_half(ref, index, side):
    x, core = lax.div(index, 2), lax.rem(index, 2)
    rows = pl.ds(pl.multiple_of(lax.div(x, 2) * 512 + side * 256, 256), 256)
    columns = pl.ds(pl.multiple_of((lax.rem(x, 2) * 2 + core) * 512, 512), 512)
    return ref.at[rows, columns]


def add_rows(out, terms, rows, step=16):
    def chunk(index, carry):
        at = pl.ds(pl.multiple_of(index * step, step), step)
        out[at, :] = functools.reduce(
            lambda a, b: a + b, [term[at, :].astype(F32) for term in terms]
        ).astype(out.dtype)
        return carry

    lax.fori_loop(0, rows // step, chunk, 0)


LINE_SCATTER_SCRATCH = [
    pltpu.VMEM((4, OWN, MODEL_WIDTH), BF16),
    pltpu.VMEM((2, OWN // 2, MODEL_WIDTH), BF16),
    pltpu.VMEM((2, OWN, MODEL_WIDTH), BF16),
]


class LineScatter:
    def __init__(self, place, wires, part, scratch):
        self.place, self.wires, self.part = place, wires, part
        self.beside, self.halves, self.full = scratch
        self.out = wires.reserve("send")
        self.late = wires.reserve("recv")
        self.pairs = {}

    def pair(self, offset):
        self.pairs[offset] = self.wires.push(
            token_block(self.part, self.place.line(offset, 1)),
            self.beside.at[offset],
            self.place.near(core=1),
            self.out,
        )

    def own(self, offset):
        return token_block(self.part, self.place.line(offset, 0))

    def far(self):
        self.pairs[2]()
        total = self.beside.at[2]
        add_rows(total, [self.own(2), total], OWN)
        self.beyond = self.wires.batch(
            [
                (total.at[pl.ds(0, OWN // 2)], self.halves.at[0], self.place.near(x=1)),
                (total.at[pl.ds(OWN // 2, OWN // 2)], self.halves.at[1], self.place.near(x=-1)),
            ],
            self.halves,
            self.out,
        )

    def near(self, offset):
        self.pairs[offset]()
        total = self.beside.at[offset]
        add_rows(total, [self.own(offset), total], OWN)
        self.send(offset, OWN // 2 if offset == 1 else 0)

    def send(self, offset, first):
        rows = pl.ds(first, OWN // 2)
        self.wires.start(
            self.beside.at[offset, rows],
            self.full.at[0 if offset == 1 else 1, rows],
            self.place.near(x=1 if offset == 1 else -1),
            self.out,
            self.late,
        )

    def join(self):
        self.beyond()
        for way, offset, first in ((0, 1, 0), (1, 3, OWN // 2)):
            rows = self.beside.at[offset, pl.ds(first, OWN // 2)]
            add_rows(rows, [rows, self.halves.at[way]], OWN // 2)
            self.send(offset, first)
        self.wires.owe(self.out, self.part.at[pl.ds(0, 7 * OWN)])

    def finish(self):
        self.pairs[0]()
        self.wires.take(self.wires.recv.at[self.late], self.full)

    def terms(self):
        return [self.own(0), self.beside.at[0], self.full.at[0], self.full.at[1]]

    def total_of(self, at):
        return functools.reduce(lambda a, b: a + b, [t[at, :].astype(F32) for t in self.terms()])

    def run(self, start, cost):
        yield start
        for offset in (2, 1, 3, 0):
            self.pair(offset)
        yield start + 2
        self.far()
        yield start + 3
        self.near(1)
        self.near(3)
        yield from self.rest(start, cost)

    def rest(self, start, cost):
        yield start + 5 + 0.5 * cost
        self.join()
        yield start + 4.5 + 1.4 * cost
        self.finish()


class Rows:
    def __init__(self, columns):
        self.item_shape = (2, 32, columns)
        self.half_shape = (1, 32, columns)

    def item(self, ref, side, slot):
        return ref.at[pl.ds(2 * side, 2), slot]

    def half(self, ref, side, part, slot):
        return ref.at[pl.ds(2 * side + part, 1), slot]

    def cut(self, item, part):
        return item.at[pl.ds(part, 1)]

    def span(self, ref, side, items):
        return ref.at[pl.ds(2 * side, 2), pl.ds(0, items)]


class Flat:
    def __init__(self):
        self.item_shape = (PIECE, MODEL_WIDTH // 2)
        self.half_shape = (PIECE, MODEL_WIDTH // 4)

    def item(self, ref, side, slot):
        rows = pl.ds(pl.multiple_of(slot * PIECE, PIECE), PIECE)
        return ref.at[rows, pl.ds(side * (MODEL_WIDTH // 2), MODEL_WIDTH // 2)]

    def half(self, ref, side, part, slot):
        rows = pl.ds(pl.multiple_of(slot * PIECE, PIECE), PIECE)
        return ref.at[rows, pl.ds((2 * side + part) * (MODEL_WIDTH // 4), MODEL_WIDTH // 4)]

    def cut(self, item, part):
        return item.at[:, pl.ds(part * (MODEL_WIDTH // 4), MODEL_WIDTH // 4)]

    def span(self, ref, side, items):
        return ref.at[pl.ds(0, items * PIECE), pl.ds(side * (MODEL_WIDTH // 2), MODEL_WIDTH // 2)]


def ring_move(place, axis, step):
    return place.near(y=step) if axis == "y" else place.near(z=step)


def ring_gather(place, wires, kind, out, side, times):
    first, second = ("z", "y") if side == 0 else ("y", "z")
    slot = functools.partial(place.slot, first)
    size = functools.partial(kind.span, out, side)
    send = wires.reserve("send")
    spread = {}

    def both(axis, items, count):
        return wires.batch(
            [(item, item, ring_move(place, axis, step)) for item, step in zip(items, (1, -1))],
            size(count),
            send,
        )

    def halves(axis, before, after):
        return both(
            axis,
            [kind.half(out, side, 0, before), kind.half(out, side, 1, after)],
            1,
        )

    def send_on(offset):
        spread[offset] = both(second, [kind.item(out, side, slot(offset, 0))] * 2, 2)

    last = wires.reserve("recv")

    def pass_on(offset):
        spread[offset]()
        for part, way, step in ((0, -1, 1), (1, 1, -1)):
            piece = kind.half(out, side, part, slot(offset, way))
            wires.start(piece, piece, ring_move(place, second, step), send, last)

    yield times[0]
    near = both(first, [kind.item(out, side, slot(0, 0))] * 2, 2)
    send_on(0)
    yield times[1]
    near()
    far = halves(first, slot(-1, 0), slot(1, 0))
    send_on(-1)
    send_on(1)
    yield times[2]
    pass_on(0)
    yield times[3]
    far()
    send_on(2)
    yield times[4]
    pass_on(-1)
    yield times[5]
    pass_on(1)
    yield times[6]
    pass_on(2)
    wires.owe(send, size(15))
    yield times[7]
    wires.take(wires.recv.at[last], size(4))


RING_SCATTER_SCRATCH = 8


def ring_scatter_scratch(kind):
    def stack(count, shape):
        return pltpu.VMEM((count, *shape), BF16)

    one_side = [
        stack(8, kind.half_shape),
        stack(8, kind.item_shape),
        stack(2, kind.half_shape),
        stack(2, kind.item_shape),
    ]
    return one_side + one_side


def add_to(out, *terms):
    out[...] = functools.reduce(
        lambda a, b: a + b, [t[...].astype(F32) for t in (out, *terms)]
    ).astype(out.dtype)


def ring_scatter(place, wires, kind, part, side, scratch, result, start, cost, then=None):
    far, came, far_last, came_last = scratch[4 * side : 4 * side + 4]
    first, second = ("z", "y") if side == 0 else ("y", "z")
    slot = functools.partial(place.slot, first)
    size = functools.partial(kind.span, part, side)
    send = wires.reserve("send")
    order = (2, 1, -1, 0)

    def both(axis, sources, targets, count):
        return wires.batch(
            [
                (source, target, ring_move(place, axis, step))
                for source, target, step in zip(sources, targets, (1, -1))
            ],
            size(count),
            send,
        )

    def halves(axis, target, into):
        return both(axis, [kind.half(part, side, n, target) for n in (0, 1)], into, 1)

    def add_halves(came_halves, after, before):
        add_to(kind.half(part, side, 0, after), came_halves[0])
        add_to(kind.half(part, side, 1, before), came_halves[1])

    yield start
    start = start if then is None else then
    beyond = [
        halves(second, slot(offset, 2), [far.at[2 * n], far.at[2 * n + 1]])
        for n, offset in enumerate(order)
    ]
    moved = []
    for n, offset in enumerate(order):
        yield start + 2.5 + (0.5 + n) * cost
        beyond[n]()
        after, before = slot(offset, 1), slot(offset, -1)
        add_halves([far.at[2 * n], far.at[2 * n + 1]], after, before)
        items = [kind.item(part, side, after), kind.item(part, side, before)]
        moved.append(both(second, items, [came.at[2 * n], came.at[2 * n + 1]], 2))

    def finish(n, offset):
        moved[n]()
        add_to(kind.item(part, side, slot(offset, 0)), came.at[2 * n], came.at[2 * n + 1])

    yield start + 4 + 3 * cost
    finish(0, 2)
    beyond_last = halves(first, slot(2, 0), [far_last.at[0], far_last.at[1]])
    yield start + 4 + 4 * cost
    finish(1, 1)
    yield start + 4 + 5 * cost
    finish(2, -1)
    beyond_last()
    after, before = slot(1, 0), slot(-1, 0)
    add_halves([far_last.at[0], far_last.at[1]], after, before)
    items = [kind.item(part, side, after), kind.item(part, side, before)]
    last = both(first, items, [came_last.at[0], came_last.at[1]], 2)
    wires.owe(send, size(15))
    yield start + 5 + 6 * cost
    finish(3, 0)
    yield start + 8 + 7.5 * cost
    last()
    own = kind.item(part, side, slot(0, 0))
    add_to(own, came_last.at[0], came_last.at[1])
    result[...] = own[...]


def call(kernel, outs, ins, scratch, wires, name, cost):
    return pl.pallas_call(
        kernel,
        out_shape=[shape for shape, _ in outs],
        in_specs=[pl.BlockSpec(memory_space=space) for _, space in ins],
        out_specs=[pl.BlockSpec(memory_space=space) for _, space in outs],
        scratch_shapes=list(scratch)
        + [pltpu.SemaphoreType.DMA((count,)) for count in wires],
        compiler_params=pltpu.CompilerParams(
            collective_id=name, has_side_effects=True, vmem_limit_bytes=VMEM_BYTES
        ),
        cost_estimate=pl.CostEstimate(flops=0, bytes_accessed=cost, transcendentals=0),
    )(*[array for array, _ in ins])


def shape(*extent, dtype=BF16):
    return jax.ShapeDtypeStruct(extent, dtype)


def merge_devices(place):
    users = [{"dp": j * 4 + place.z, "row": place.y, "col": place.col} for j in range(4)]
    homes = [
        {"dp": place.row * 4 + place.z, "row": jnp.int32(row), "col": place.col} for row in range(4)
    ]
    return users, homes


def signal_others(place, devices):
    barrier = pltpu.get_barrier_semaphore()
    for device in devices:
        alone = (device["dp"] == place.dp) & (device["row"] == place.row)

        @pl.when(jnp.logical_not(alone))
        def _():
            pl.semaphore_signal(barrier, inc=1, device_id=device, device_id_type=MESH)


def merge_exchange(place, wires, devices, source, target, mine):
    send, recv = wires.reserve("send", 4), wires.reserve("recv", 4)
    copies = []
    for index, device in enumerate(devices):
        copy = pltpu.make_async_remote_copy(
            src_ref=source(index),
            dst_ref=target(index),
            send_sem=wires.send.at[send + index],
            recv_sem=wires.recv.at[recv + mine],
            device_id=device,
            device_id_type=MESH,
        )
        here = pltpu.make_async_copy(source(index), target(index), wires.recv.at[recv + mine])
        alone = (device["dp"] == place.dp) & (device["row"] == place.row)
        copies.append((copy, alone))
        pl.when(alone)(here.start)
        pl.when(jnp.logical_not(alone))(copy.start)

    def wait():
        for index in range(4):
            wires.take(wires.recv.at[recv + index], target(0))
        for copy, alone in copies:
            pl.when(jnp.logical_not(alone))(copy.wait_send)

    return wait


def nested(plans):
    pending = [[next(plan), order, plan] for order, plan in enumerate(plans)]
    while pending:
        pending.sort(key=lambda entry: entry[:2])
        entry = pending[0]
        yield entry[0]
        try:
            entry[0] = max(entry[0], next(entry[2]))
        except StopIteration:
            pending.pop(0)


def column_block(ref, row):
    return ref.at[:, pl.ds(pl.multiple_of(row * 512, 512), 512)]


def down_slot(ref, slot, row):
    rows = pl.ds(pl.multiple_of(slot * PIECE, PIECE), PIECE)
    return ref.at[rows, pl.ds(pl.multiple_of(row * 512, 512), 512)]


def own_token_rows(ref, row):
    return ref.at[pl.ds(pl.multiple_of(row * OWN, OWN), OWN)]


def recut(place, wires, own, out, when):
    peers = [place.peer(step) for step in (1, 2, 3)]
    kept = wires.keep(column_block(own, place.row), own_token_rows(out, place.row))
    moved = wires.batch(
        [
            (column_block(own, other), own_token_rows(out, place.row), device)
            for other, device in peers
        ],
        out.at[pl.ds(0, 3 * OWN)],
    )
    yield when
    kept.wait()
    moved()


def back_pieces(place, wires, part_of, out, when):
    peers = [place.peer(step) for step in (1, 2, 3)]
    kept = wires.keep(part_of(place.row), out.at[place.row])
    moved = wires.batch(
        [(part_of(other), out.at[place.row], device) for other, device in peers],
        out.at[pl.ds(0, 3)],
    )
    yield when
    kept.wait()
    moved()


HEADS_TIMES = (2.6, 9.4, 10.0, 15.0, 15.5, 16.0, 20.0, 23.5)
MERGE_TIMES = (3.2, 11.2, 12.0, 16.5, 18.0, 18.5, 24.7, 28.0)
DOWN_TIMES = (20.1, 26.1, 26.2, 31.0, 34.0, 34.5, 39.0, 49.0)
GATING_TIMES = (26.3, 38.0, 40.0, 49.5, 53.0, 55.0, 60.0, 66.0)


def opening_kernel(
    heads_weight, merge_weight, gating_weight, down_weight, input_own, back_own, gains_own,
    *refs,
):
    (
        normed_out, query_out, pair_out, sums_out, cosine_out, sine_out, attended_out, merge_out,
        heads_out, middle_out, grad_middle_out, branch_out, gain_part_out, gating_sum_out,
        down_part_out, down_out, gains_out, input_rows_out,
    ) = refs[:18]
    line_scratch, scratch = refs[18:21], refs[21:]
    ring_scratch, scratch = scratch[:RING_SCATTER_SCRATCH], scratch[RING_SCATTER_SCRATCH:]
    (
        tokens, part, back, gating, grad_hidden, hidden, grad_gated, rows_own,
        heads_cut, merge_cut, gating_cut, down_cut,
        query, pair, sums, cosine, sine, attended, merge, heads, middle, grad_middle, branch,
        gain_part, gating_sum, down, gains, input_rows, merge_all,
        send, recv, local,
    ) = scratch
    handed = []

    def hand(*pairs):
        handed.extend(wires.keep(source, target) for source, target in pairs)

    place = Place()
    wires = Wires(send, recv, local)
    first_wires, token_wires, gating_wires, down_wires = [wires.part() for _ in range(4)]
    users, homes = merge_devices(place)
    peers = [place.peer(step) for step in (1, 2, 3)]
    same = place.row == place.y
    devices = ring_neighbours(place) + line_neighbours(place) + [p for _, p in peers]
    signal_others(place, devices + homes)
    for row in range(4):
        group, half = divmod(row, 2)
        rows = heads_weight[:, pl.ds(group * 640 + half * 256, 256)]
        heads_cut[row, :, pl.ds(0, 256)] = rows.astype(BF16)
        rows = heads_weight[:, pl.ds(group * 640 + 512, 128)]
        heads_cut[row, :, pl.ds(256, 128)] = rows.astype(BF16)
        for side in range(2):
            piece = merge_weight[pl.ds(16 * row, 16), pl.ds(256 * side, 256)]
            merge_cut[row, pl.ds(16 * side, 16)] = piece.astype(BF16)
    pl.semaphore_wait(
        pltpu.get_barrier_semaphore(), len(devices) + 4 - same.astype(jnp.int32)
    )
    merge_came, down_came, gating_came = [], [], []

    def exchange():
        yield 0.0
        came = [wires.keep(heads_cut.at[place.row], heads.at[place.row, place.dp]).wait]
        came.append(wires.keep(gains_own, column_block(gains, place.row)).wait)
        came.append(
            wires.batch(
                [
                    (heads_cut.at[other], heads.at[place.row, place.dp], device)
                    for other, device in peers
                ],
                heads_cut.at[pl.ds(0, 3)],
            )
        )
        merge_came.append(
            merge_exchange(
                place, wires, users,
                lambda j: merge_cut.at[j],
                lambda j: merge_all.at[place.row, j * 4 + place.z],
                place.row,
            )
        )
        came.append(
            wires.batch(
                [(gains_own, column_block(gains, place.row), device) for _, device in peers],
                gains.at[:, pl.ds(0, 1536)],
            )
        )
        yield 2.6
        for wait in came:
            wait()
        yield from nested(
            ring_gather(place, wires, Rows(HEADS_COLS), heads, side, HEADS_TIMES)
            for side in (0, 1)
        )

    def gating_exchange():
        yield 3.0
        for row in range(4):
            piece = down_weight[pl.ds(PIECE_USED * row, PIECE_USED), :]
            down_cut[row] = jnp.concatenate(
                [piece, jnp.zeros((PIECE - PIECE_USED, 512), F32)], axis=0
            ).astype(BF16)
        target = down_slot(down, place.dp, place.row)
        down_came.append(wires.keep(down_cut.at[place.row], target).wait)
        down_came.append(
            wires.batch(
                [(down_cut.at[other], target, device) for other, device in peers],
                down_cut.at[pl.ds(0, 3)],
            )
        )
        zeros = jnp.zeros((32, PIECE - PIECE_USED), F32)
        for kind in range(2):
            for row in range(4):
                pieces = []
                for slot in range(16):
                    first = slot * 4 * PIECE_USED + row * PIECE_USED
                    pieces += [gating_weight[:, kind, pl.ds(first, PIECE_USED)], zeros]
                gating_cut[row, :, pl.ds(kind * HIDDEN, HIDDEN)] = jnp.concatenate(
                    pieces, axis=1
                ).astype(BF16)
        yield 17.6
        target = gating.at[place.row, place.dp]
        gating_came.append(wires.keep(gating_cut.at[place.row], target).wait)
        gating_came.append(
            wires.batch(
                [(gating_cut.at[other], target, device) for other, device in peers],
                gating_cut.at[pl.ds(0, 3)],
            )
        )

    def tables():
        yield 3.4
        rope_tables(cosine, sine)

    def merge_rows():
        yield 3.2
        for wait in merge_came:
            wait()
        yield from nested(
            ring_gather(place, wires, Rows(256), merge_all, side, MERGE_TIMES) for side in (0, 1)
        )

    def down_rows():
        yield 20.1
        for wait in down_came:
            wait()
        yield from nested(
            ring_gather(place, down_wires, Flat(), down, side, DOWN_TIMES) for side in (0, 1)
        )

    def gating_rows():
        yield 26.3
        for wait in gating_came:
            wait()
        yield from nested(
            ring_gather(place, gating_wires, Rows(2 * HIDDEN), gating, side, GATING_TIMES)
            for side in (0, 1)
        )

    def chip_rows(offset):
        start = pl.multiple_of(lax.rem(place.x + offset + 4, 4) * 256, 256)
        return pl.ds(start, 256)

    def grad_hidden_rows():
        for index in range(4):
            yield 60.5 + 1.3 * index
            at = pl.ds(index * 256, 256)
            grad_hidden[at, :] = contract_last(back[at, :], down[...])

    def forward(offset, when):
        at = chip_rows(offset)
        for tile in range(3):
            gate_at, up_at = pl.ds(tile * 256, 256), pl.ds(HIDDEN + tile * 256, 256)
            rows = tokens[at, :]
            gate = product(rows, gating[:, :, :, gate_at].reshape(MODEL_WIDTH, 256))
            up = product(rows, gating[:, :, :, up_at].reshape(MODEL_WIDTH, 256))
            grad = grad_hidden[at, gate_at]
            sigmoid = jax.nn.sigmoid(gate)
            silu = gate * sigmoid
            hidden[at, gate_at] = (silu * up).astype(BF16)
            grad_gated[at, gate_at] = (grad * up * sigmoid * (1.0 + gate * (1.0 - sigmoid))).astype(
                BF16
            )
            grad_gated[at, up_at] = (grad * silu).astype(BF16)
            yield when + 0.6 * (tile + 1)
        for row in range(4):
            part[at, pl.ds(row * 512, 512)] = contract_last(
                grad_gated[at, :], gating[row].reshape(512, 2 * HIDDEN)
            ).astype(BF16)
            if row % 2:
                yield when + 2.0 + 0.6 * row

    def main():
        yield 0.1
        yield from line_gather(
            place, token_wires, input_own, tokens, tile_block, tile_half, (0.1, 14.9, 23.6, 24.6)
        )
        input_rows[...] = token_block(tokens, place.line(0, 0))[...]
        yield 24.65
        normed = branch
        first = LineScatter(place, first_wires, part, line_scratch)
        yield from projections(
            tokens, gains, heads, cosine, sine, normed, query, pair,
        )
        normed_copy = wires.keep(normed, normed_out)
        token_wires.drain()
        yield 30.2
        for row in range(4):
            for slot in range(16):
                y, z = divmod(slot, 4)
                for half in range(2):
                    merge[pl.ds(z * 64 + y * 16, 16), pl.ds(row * 512 + half * 256, 256)] = (
                        merge_all[row, slot, pl.ds(16 * half, 16), :]
                    )
        then = [None, first.far, lambda: first.near(1), lambda: first.near(3)]
        for order, offset in enumerate((2, 1, -1, 0)):
            at = chip_rows(offset)
            when = 30.8 + 3.8 * order
            for _ in attention(
                at, lax.rem(place.x + offset + 4, 4), query, pair, sums, attended
            ):
                yield when + 1.5
                if order:
                    then[order]()
            part[at, :] = product(attended[at, :], merge[...]).astype(BF16)
            first.pair(offset % 4)
            yield when + 3.8
        hand(
            (query, query_out), (pair, pair_out), (sums, sums_out), (cosine, cosine_out),
            (sine, sine_out), (attended, attended_out), (merge, merge_out), (heads, heads_out),
            (gains, gains_out), (input_rows, input_rows_out),
        )
        yield 46.2
        first.join()
        yield 58.0
        first.finish()

        def chunk(index, carry):
            at = pl.ds(pl.multiple_of(index * 16, 16), 16)
            total = first.total_of(at) + input_rows[at, :].astype(F32)
            middle[at, :] = total
            scale = lax.rsqrt(
                jnp.sum(total * total, axis=1, keepdims=True) / MODEL_WIDTH + EPS_NORM
            )
            rows_own[at, :] = (total * scale * gains[1:2, :]).astype(BF16)
            return carry

        lax.fori_loop(0, OWN // 16, chunk, 0)
        first_wires.drain()
        normed_copy.wait()
        hand((middle, middle_out))
        me, block, half = place.line(0, 0), token_block, token_half
        mine = wires.keep(rows_own, block(tokens, me))
        near = token_wires.batch(
            [(rows_own, block(tokens, me), place.near(x=step)) for step in (1, -1)],
            tokens.at[pl.ds(0, 2 * OWN)],
        )
        beside = token_wires.push(rows_own, block(tokens, me), place.near(core=1))

        def pass_beside(offset):
            came = block(tokens, place.line(offset, 0))
            return token_wires.push(came, came, place.near(core=1))

        second = LineScatter(place, wires, part, line_scratch)
        yield 70.0
        mine.wait()
        beside()
        yield from forward(0, 70.0)
        second.pair(0)
        yield 78.5
        near()
        pieces = [half(tokens, place.line(-1, 0), 0), half(tokens, place.line(1, 0), 1)]
        far = token_wires.batch(
            [(piece, piece, place.near(x=step)) for piece, step in zip(pieces, (1, -1))],
            tokens.at[pl.ds(0, OWN)],
        )
        beside_left, beside_right = pass_beside(-1), pass_beside(1)
        yield 80.5
        beside_left()
        beside_right()
        yield from forward(1, 80.5)
        second.pair(1)
        yield 84.1
        yield from forward(-1, 84.1)
        second.pair(3)
        second.near(1)
        yield 87.8
        far()
        beside_far = pass_beside(2)
        yield 89.5
        beside_far()
        yield from forward(2, 89.5)
        second.pair(2)
        second.near(3)
        yield 94.5
        second.far()
        yield from second.rest(94.0, 11.4)
        gain_part[...] = jnp.zeros_like(gain_part)
        back_own_rows = token_block(back, place.line(0, 0))

        def chunk_back(index, carry):
            at = pl.ds(pl.multiple_of(index * 16, 16), 16)
            through, gain = norm_back(middle[at, :], gains[1:2, :], second.total_of(at))
            total = back_own_rows[at, :].astype(F32) + through
            grad_middle[at, :] = total
            rows_own[at, :] = total.astype(BF16)
            gain_part[...] += gain.reshape(2, 8, MODEL_WIDTH).sum(axis=0)
            return carry

        token_wires.drain()
        lax.fori_loop(0, OWN // 16, chunk_back, 0)

        def ready(offsets):
            hand(*[(branch.at[chip_rows(o)], branch_out.at[chip_rows(o)]) for o in offsets])

        yield from line_gather(
            place, wires, rows_own, branch, token_block, token_half, (117.2, 131.0, 138.8, 141.0), ready
        )
        hand((grad_middle, grad_middle_out), (gain_part, gain_part_out))

    computed = []

    def gradients():
        yield 94.6
        gating_wires.drain()
        for row in range(4):
            for piece in range(2):
                columns = pl.ds(row * 512 + piece * 256, 256)
                gating[row, pl.ds(8 * piece, 8)] = (
                    token_product(tokens[:, columns], grad_gated[...])
                    .astype(BF16)
                    .reshape(8, 32, 2 * HIDDEN)
                )
                computed.append(row)
                yield 96.0 + 1.05 * (2 * row + piece + 1)

    def gradient_side(side):
        yield 100.3 + 4.2 * side
        assert len(computed) >= 4 + 4 * side
        yield from ring_scatter(
            place, wires, Rows(2 * HIDDEN), gating, side, ring_scratch,
            gating_sum.at[pl.ds(2 * side, 2)], 100.3 + 4.2 * side, 4.3,
        )
        hand((gating_sum.at[pl.ds(2 * side, 2)], gating_sum_out.at[pl.ds(2 * side, 2)]))

    def down_products():
        yield 106.9
        token_wires.drain()
        for index in range(4):
            at = pl.ds(index * 256, 256)
            tokens[at, :] = product(hidden[at, :], down[...]).astype(BF16)
            hand((tokens.at[at], down_out.at[at]))
            yield 107.9 + 1.0 * index
        down_wires.drain()
        for tile in range(3):
            columns = pl.ds(tile * 256, 256)
            down[columns, :] = token_product(hidden[:, columns], back[...]).astype(BF16)
            hand((down.at[columns], down_part_out.at[columns]))
            yield 112.3 + 1.2 * tile

    interleave(
        main(),
        exchange(),
        gating_exchange(),
        merge_rows(),
        tables(),
        down_rows(),
        gating_rows(),
        line_gather(
            place, wires, back_own, back, tile_block, tile_half, (25.3, 38.0, 50.5, 52.0)
        ),
        grad_hidden_rows(),
        gradients(),
        gradient_side(0),
        gradient_side(1),
        down_products(),
        sweep([wires, gating_wires, down_wires], 66.0, 76.5),
        sweep([wires, token_wires], 117.5, 126.0),
    )
    wires.drain()
    for copy in handed:
        copy.wait()


def norm_back(values, gain_row, gradient):
    scale = lax.rsqrt(jnp.sum(values * values, axis=1, keepdims=True) / MODEL_WIDTH + EPS_NORM)
    weighted = gain_row * gradient
    inner = jnp.sum(weighted * values, axis=1, keepdims=True)
    through = scale * weighted - values * (scale * scale * scale * inner / MODEL_WIDTH)
    return through, gradient * values * scale


def turn(tile, cosine, sine):
    lane = lax.broadcasted_iota(jnp.int32, tile.shape, 1)
    first = lax.rem(lane, HEAD_SIZE) < HEAD_SIZE // 2
    swapped = jnp.where(first, pltpu.roll(tile, 96, axis=1), pltpu.roll(tile, 32, axis=1))
    return tile * cosine + swapped * sine


def rope_tables(cosine, sine):
    half_width = HEAD_SIZE // 2

    def chunk(index, carry):
        at = pl.ds(pl.multiple_of(index * 128, 128), 128)
        lane = lax.broadcasted_iota(jnp.int32, (128, 128), 1)
        row = lax.broadcasted_iota(jnp.int32, (128, 128), 0) + index * 128
        frequency = jnp.exp(
            lax.rem(lane, half_width).astype(F32) * (-2.0 / HEAD_SIZE * math.log(ROPE_BASE))
        )
        angles = row.astype(F32) * frequency
        cosine[at, :] = jnp.cos(angles)
        first = lax.rem(lane, HEAD_SIZE) < half_width
        sine[at, :] = jnp.where(first, -jnp.sin(angles), jnp.sin(angles))
        return carry

    lax.fori_loop(0, SEQ // 128, chunk, 0)


def keys_only(cosine, sine):
    key = lax.broadcasted_iota(jnp.int32, cosine.shape, 1) < HEAD_SIZE
    return jnp.where(key, cosine, 1.0), jnp.where(key, sine, 0.0)


def heads_weight_of(heads):
    return heads[...].reshape(MODEL_WIDTH, HEADS_COLS)


QUERY_BLOCK = 256


def projections(
    inputs, gains, heads, cosine, sine,
    normed, query, pair,
):
    for index in range(4):
        at = pl.ds(index * 256, 256)
        wide = inputs[at, :].astype(F32)
        scale = lax.rsqrt(jnp.sum(wide * wide, axis=1, keepdims=True) / MODEL_WIDTH + EPS_NORM)
        low = (wide * scale * gains[0:1, :]).astype(BF16)
        normed[at, :] = low
        mixed = product(low, heads_weight_of(heads))
        cos, sin = cosine[at, :], sine[at, :]
        query[at, pl.ds(0, 128)] = turn(mixed[:, :128], cos, sin).astype(BF16)
        query[at, pl.ds(128, 128)] = turn(mixed[:, 128:256], cos, sin).astype(BF16)
        pair[at, :] = turn(mixed[:, 256:], *keys_only(cos, sin)).astype(BF16)
        yield 24.7 + 1.3 * (index + 1)


def attention(at, block, query, pair, sums, attended):
    scale = HEAD_SIZE ** (-0.5)
    rows_at = lax.broadcasted_iota(jnp.int32, (QUERY_BLOCK, QUERY_BLOCK), 0)
    keys_at = lax.broadcasted_iota(jnp.int32, (QUERY_BLOCK, QUERY_BLOCK), 1)
    out, logs = [], []
    for two in range(2):
        if two:
            yield
        queries = [
            query[at, pl.ds(head * HEAD_SIZE, HEAD_SIZE)] for head in (2 * two, 2 * two + 1)
        ]

        def weigh(rows, keys):
            return contract_last(rows, pair[keys, pl.ds(0, HEAD_SIZE)]) * scale

        def values(keys):
            return pair[keys, pl.ds(HEAD_SIZE, HEAD_SIZE)]

        state = []
        for rows in queries:
            scores = jnp.where(rows_at >= keys_at, weigh(rows, at), MASK_FILL)
            top = jnp.max(scores, axis=1, keepdims=True)
            powers = jnp.exp(scores - top)
            total = jnp.sum(powers, axis=1, keepdims=True)
            state.append((top, total, product(powers.astype(BF16), values(at))))

        def step(index, state):
            keys = pl.ds(pl.multiple_of(index * QUERY_BLOCK, QUERY_BLOCK), QUERY_BLOCK)
            result = []
            for rows, (top, total, mean) in zip(queries, state):
                scores = weigh(rows, keys)
                higher = jnp.maximum(top, jnp.max(scores, axis=1, keepdims=True))
                shrink = jnp.exp(top - higher)
                powers = jnp.exp(scores - higher)
                total = total * shrink + jnp.sum(powers, axis=1, keepdims=True)
                mean = mean * shrink + product(powers.astype(BF16), values(keys))
                result.append((higher, total, mean))
            return tuple(result)

        for top, total, mean in lax.fori_loop(0, block, step, tuple(state)):
            out.append((mean * (1.0 / total)).astype(BF16))
            logs.append(top + jnp.log(total))
    logs.append(jnp.zeros((QUERY_BLOCK, 124), F32))
    sums[:, at] = jnp.transpose(jnp.concatenate(logs, axis=1))[:8]
    attended[at, :] = jnp.concatenate(out, axis=1)


def backward_kernel(*refs):
    given, refs = refs[:18], refs[18:]
    (
        output, input_grad, gains_grad, heads_pieces, merge_pieces, gating_pieces, down_pieces,
    ) = refs[:7]
    out_scratch, scratch = refs[7:10], refs[10:]
    line_scratch, scratch = scratch[:3], scratch[3:]
    down_scratch, scratch = scratch[:8], scratch[8:]
    heads_scratch, scratch = scratch[:8], scratch[8:]
    held, scratch = scratch[:18], scratch[18:]
    (
        branch, merge, query, pair, sums, cosine, sine, down_out, down_part, gating_sum,
        middle, heads, attended, normed, grad_middle, input_rows, gains, gain_part,
    ) = held
    (
        part, grad_mixed, grad_attended, grad_key, grad_value, key_columns, rows_own,
        down_sum, heads_all, heads_sum, input_grad_own, gain_rows, gain_came, gain_all,
        send, recv, local,
    ) = scratch
    place = Place()
    wires = Wires(send, recv, local)
    loads = [wires.keep(source, target) for source, target in zip(given, held)]

    def need(*names):
        for index in names:
            if loads[index] is not None:
                loads[index].wait()
                loads[index] = None

    users, homes = merge_devices(place)
    peers = [place.peer(step) for step in (1, 2, 3)]
    same = place.row == place.y
    barrier = pltpu.get_barrier_semaphore()
    devices = ring_neighbours(place) + line_neighbours(place) + [p for _, p in peers]
    signal_others(place, devices + users)

    def far(step):
        index = lax.rem(place.col * 16 + place.dp + step, 32)
        return {"dp": lax.rem(index, 16), "row": place.row, "col": lax.div(index, 16)}

    def greet(step, carry):
        pl.semaphore_signal(barrier, inc=1, device_id=far(step), device_id_type=MESH)
        return carry

    lax.fori_loop(1, 32, greet, 0)
    need(0, 1)
    attend = attention_back(
        branch, merge, query, pair, sums, cosine, sine, grad_mixed,
        grad_attended, grad_key, grad_value, key_columns,
    )
    next(attend)
    next(attend)
    pl.semaphore_wait(barrier, len(devices) + 31 + 4 - same.astype(jnp.int32))

    def outputs():
        yield 0.1
        need(7)
        scatter = LineScatter(place, wires, down_out, out_scratch)
        yield from scatter.run(0.1, 11.4)
        yield 21.2
        need(10)

        def chunk(index, carry):
            at = pl.ds(pl.multiple_of(index * 16, 16), 16)
            rows_own[at, :] = (scatter.total_of(at) + middle[at, :]).astype(BF16)
            return carry

        lax.fori_loop(0, OWN // 16, chunk, 0)
        yield 27.9
        yield from recut(place, wires, rows_own, output, 46.0)

    def down_rows():
        yield 0.3
        need(8)
        yield from nested(
            ring_scatter(
                place, wires, Flat(), down_part, side, down_scratch,
                down_sum.at[:, pl.ds(side * 1024, 1024)], 0.3, 2.1,
            )
            for side in (0, 1)
        )
        yield from back_pieces(
            place, wires, lambda row: column_block(down_sum, row), down_pieces, 46.0
        )

    def gating():
        yield 0.4
        need(9)
        yield from back_pieces(
            place, wires, lambda row: gating_sum.at[row], gating_pieces, 36.0
        )

    def compute():
        yield 0.2
        need(2, 3, 4, 5, 6)
        yield from attend
        need(11)
        scatter = LineScatter(place, wires, part, line_scratch)
        then = [None, scatter.far, lambda: scatter.near(1), None]
        for order, offset in enumerate((2, 1, -1, 0)):
            start = pl.multiple_of(lax.rem(place.x + offset + 4, 4) * 256, 256)
            at = pl.ds(start, 256)
            for row in range(4):
                part[at, pl.ds(row * 512, 512)] = contract_last(
                    grad_mixed[at, :],
                    heads[row].reshape(512, HEADS_COLS),
                ).astype(BF16)
            scatter.pair(offset % 4)
            if then[order]:
                then[order]()
        yield 19.6
        yield from gradient(scatter)

    computed = []

    def weights():
        yield 21.5
        need(12, 13, 16, 17)
        gain_rows[...] = jnp.zeros_like(gain_rows)
        gain_rows[1:2, :] = jnp.sum(gain_part[...], axis=0, keepdims=True)
        ones = jnp.ones((8, HEADS_COLS), BF16)
        for row in range(4):
            columns = pl.ds(row * 512, 512)
            merge_part = token_product(attended[...], branch[:, columns]).astype(BF16)
            for slot in range(16):
                y, z = divmod(slot, 4)
                for half in range(2):
                    heads_all[row, slot, pl.ds(16 * half, 16), pl.ds(HEADS_COLS, 256)] = (
                        merge_part[
                            z * 64 + y * 16 : z * 64 + y * 16 + 16,
                            half * 256 : half * 256 + 256,
                        ]
                    )
            for piece in range(2):
                columns = pl.ds(row * 512 + piece * 256, 256)
                grad = token_product(normed[:, columns], grad_mixed[...])
                slots = pl.ds(8 * piece, 8)
                heads_all[row, slots, :, pl.ds(0, HEADS_COLS)] = grad.astype(BF16).reshape(
                    8, 32, HEADS_COLS
                )
                weight = heads[row, slots].reshape(256, HEADS_COLS)
                terms = grad * weight.astype(F32)
                high = terms.astype(BF16)
                low = (terms - high.astype(F32)).astype(BF16)
                sums_ = contract_last(ones, high) + contract_last(ones, low)
                gain_rows[0:1, columns] = sums_[0:1] / gains[0:1, columns]
            computed.append(row)
            yield 21.5 + 1.55 * (row + 1)
        yield from gain_sums()

    def heads_side(side):
        yield 24.7 + 3.1 * side
        assert len(computed) >= 2 + 2 * side
        yield from ring_scatter(
            place, wires, Rows(HEADS_COLS + 256), heads_all, side, heads_scratch,
            heads_sum.at[pl.ds(2 * side, 2)], 24.7 + 3.1 * side, 1.8,
        )
        computed.append("side")

    def heads_back():
        yield 49.4
        assert computed.count("side") == 2
        merge_wait = merge_exchange(
            place, wires, homes,
            lambda row: heads_sum.at[row, :, pl.ds(HEADS_COLS, 256)],
            lambda row: merge_pieces.at[place.y],
            place.y,
        )
        yield from back_pieces(
            place, wires,
            lambda row: heads_sum.at[row, :, pl.ds(0, HEADS_COLS)], heads_pieces, 55.0,
        )
        merge_wait()

    def gain_sums():
        moved = wires.batch(
            [
                (column_block(gain_rows, other), gain_came.at[place.row], device)
                for other, device in peers
            ],
            gain_came.at[pl.ds(0, 3)],
        )
        kept = wires.keep(column_block(gain_rows, place.row), gain_came.at[place.row])
        yield 35.95
        kept.wait()
        moved()
        local_sum = gain_came[0] + gain_came[1] + gain_came[2] + gain_came[3]
        me = place.col * 16 + place.dp
        for kind in range(2):
            for tile in range(4):
                gain_all[me, pl.ds(4 * kind + tile, 1), :] = local_sum[
                    kind : kind + 1, tile * 128 : tile * 128 + 128
                ]
        send, recv = wires.reserve("send"), wires.reserve("recv")

        def start(step, carry):
            wires.start(gain_all.at[me], gain_all.at[me], far(step), send, recv)
            return carry

        lax.fori_loop(1, 32, start, 0)
        wires.owe(send, gain_all.at[pl.ds(0, 31)])
        yield 50.0
        wires.take(wires.recv.at[recv], gain_all.at[pl.ds(0, 31)])
        gains_grad[...] = functools.reduce(lambda a, b: a + b, [gain_all[i] for i in range(32)])

    def gradient(scatter):
        scatter.near(3)
        yield 26.2
        scatter.join()
        yield 36.0
        scatter.finish()
        need(14, 15)

        def chunk(index, carry):
            at = pl.ds(pl.multiple_of(index * 16, 16), 16)
            grad = scatter.total_of(at)
            through, _ = norm_back(input_rows[at, :].astype(F32), gains[0:1, :], grad)
            input_grad_own[at, :] = (grad_middle[at, :] + through).astype(BF16)
            return carry

        lax.fori_loop(0, OWN // 16, chunk, 0)
        yield from recut(place, wires, input_grad_own, input_grad, 52.0)

    interleave(
        compute(),
        outputs(),
        down_rows(),
        gating(),
        weights(),
        heads_side(0),
        heads_side(1),
        heads_back(),
        sweep([wires], 30.0, 44.9),
    )
    wires.drain()


def attention_back(
    branch, merge, query, pair, sums, cosine, sine, grad_mixed,
    grad_attended, grad_key, grad_value, key_columns,
):
    yield 0.3
    def attended_rows(index, carry):
        at = pl.ds(pl.multiple_of(index * 512, 512), 512)
        grad_attended[at, :] = contract_last(branch[at, :], merge[...]).astype(BF16)
        return carry

    attended_rows(0, 0)
    yield 2.0
    attended_rows(1, 0)
    key_columns[...] = jnp.transpose(pair[...].astype(F32))[:HEAD_SIZE].astype(BF16)
    grad_key[...] = jnp.zeros_like(grad_key)
    grad_value[...] = jnp.zeros_like(grad_value)
    scale = HEAD_SIZE ** (-0.5)
    keys_at = lax.broadcasted_iota(jnp.int32, (QUERY_BLOCK, QUERY_BLOCK), 0)
    rows_at = lax.broadcasted_iota(jnp.int32, (QUERY_BLOCK, QUERY_BLOCK), 1)
    for block in range(SEQ // QUERY_BLOCK):
        at = pl.ds(block * QUERY_BLOCK, QUERY_BLOCK)
        before = block * QUERY_BLOCK
        for two in range(2):
            turned = []
            for head in (2 * two, 2 * two + 1):
                columns = pl.ds(head * HEAD_SIZE, HEAD_SIZE)
                rows, back = query[at, columns], grad_attended[at, columns]
                log_total = sums[pl.ds(head, 1), at]
                spans = [at] + ([pl.ds(0, before)] if before else [])
                softs, grads = [], []
                for span in spans:
                    scores = contract_last(pair[span, pl.ds(0, HEAD_SIZE)], rows) * scale
                    soft = jnp.exp(scores - log_total)
                    if span is at:
                        soft = jnp.where(rows_at >= keys_at, soft, 0.0)
                    softs.append(soft)
                    grads.append(contract_last(pair[span, pl.ds(HEAD_SIZE, HEAD_SIZE)], back))
                inner = functools.reduce(
                    lambda a, b: a + b,
                    [jnp.sum(s * g, axis=0, keepdims=True) for s, g in zip(softs, grads)],
                )
                result = 0.0
                for span, soft, grad in zip(spans, softs, grads):
                    low = (soft * (grad - inner)).astype(BF16)
                    grad_key[span, :] += product(low, rows)
                    grad_value[span, :] += product(soft.astype(BF16), back)
                    result += product(key_columns[:, span], low)
                turned.append(result)
                yield 1.9 + (2.1, 5.0, 8.7, 13.2)[block] - (0.52, 0.72, 0.92, 1.15)[block] * (3 - head)
            tile = jnp.transpose(jnp.concatenate(turned, axis=0)) * scale
            grad_mixed[at, pl.ds(two * 128, 128)] = turn(
                tile, cosine[at, :], -sine[at, :]
            ).astype(BF16)

    def finish_rows(index, carry):
        at = pl.ds(pl.multiple_of(index * 128, 128), 128)
        cos, sin = keys_only(cosine[at, :], sine[at, :])
        tile = jnp.concatenate([grad_key[at, :] * scale, grad_value[at, :]], axis=1)
        grad_mixed[at, pl.ds(256, 128)] = turn(tile, cos, -sin).astype(BF16)
        return carry

    lax.fori_loop(0, SEQ // 128, finish_rows, 0)


def product(left, right):
    return jnp.dot(left, right, preferred_element_type=F32)


def contract_last(left, right):
    return lax.dot_general(left, right, (((1,), (1,)), ((), ())), preferred_element_type=F32)


def token_product(left, right):
    return lax.dot_general(left, right, (((0,), (0,)), ((), ())), preferred_element_type=F32)


def adamw(current, gradient, first, second, step_rate, decay_rate):
    mean_new = BETA_ONE * first + (1.0 - BETA_ONE) * gradient
    square_new = BETA_TWO * second + (1.0 - BETA_TWO) * gradient * gradient
    mean_hat = mean_new / (1.0 - BETA_ONE**STEP)
    square_hat = square_new / (1.0 - BETA_TWO**STEP)
    updated = current - step_rate * (
        mean_hat / (jnp.sqrt(square_hat) + EPS_ADAM) + decay_rate * current
    )
    return (updated, mean_new, square_new)


def update_kernel(*refs):
    output_given, input_grad_given, gains, heads, merge, gating, down = refs[:7]
    states = [refs[7 + 3 * n : 10 + 3 * n] for n in range(5)]
    output, input_grad = refs[22:24]
    results = [refs[24 + 4 * n : 28 + 4 * n] for n in range(5)]
    output[...] = output_given[...]
    input_grad[...] = input_grad_given[...].astype(F32)
    gains_grad, heads_grad, merge_grad, gating_grad, down_grad = [r[0] for r in results]
    for kind in range(2):
        for tile in range(4):
            gains_grad[pl.ds(kind, 1), pl.ds(tile * 128, 128)] = gains[
                pl.ds(4 * kind + tile, 1), :
            ]
    for row in range(4):
        group, half = divmod(row, 2)
        heads_grad[:, pl.ds(group * 640 + half * 256, 256)] = heads[
            row, :, pl.ds(0, 256)
        ].astype(F32)
        for side in range(2):
            merge_grad[pl.ds(16 * row, 16), pl.ds(256 * side, 256)] = merge[
                row, pl.ds(16 * side, 16)
            ].astype(F32)
        down_grad[pl.ds(PIECE_USED * row, PIECE_USED), :] = down[row].astype(F32)[:PIECE_USED]
    for group in range(2):
        pair = pl.ds(256, 128)
        heads_grad[:, pl.ds(group * 640 + 512, 128)] = heads[2 * group, :, pair].astype(
            F32
        ) + heads[2 * group + 1, :, pair].astype(F32)
    for kind in range(2):
        rows = [gating[row, :, pl.ds(kind * HIDDEN, HIDDEN)].astype(F32) for row in range(4)]
        whole = jnp.concatenate(
            [
                rows[row][:, slot * PIECE : slot * PIECE + PIECE_USED]
                for slot in range(16)
                for row in range(4)
            ],
            axis=1,
        )
        gating_grad[:, kind, :] = whole
    rates = [RATE_GAIN, RATE_MATRIX, RATE_MERGE, RATE_MATRIX, RATE_MATRIX]
    decays = [0.0] + [WEIGHT_DECAY] * 4
    for state, result, rate, decay in zip(states, results, rates, decays):
        rows = state[0].shape[0]
        step = 16 if rows % 16 == 0 else rows

        def chunk(index, carry):
            at = pl.ds(pl.multiple_of(index * step, step), step)
            new = adamw(state[0][at], result[0][at], state[1][at], state[2][at], rate, decay)
            for ref, value in zip(result[1:], new):
                ref[at] = value
            return carry

        lax.fori_loop(0, rows // step, chunk, 0)


def update(given, states):
    ins = list(given) + [array for state in states for array in state]
    outs = [shape(512, 512), shape(512, 512, dtype=F32)]
    for state in states:
        outs += [shape(*state[0].shape, dtype=F32)] * 4
    return pl.pallas_call(
        update_kernel,
        out_shape=outs,
        in_specs=[pl.BlockSpec(memory_space=pltpu.VMEM)] * len(ins),
        out_specs=[pl.BlockSpec(memory_space=pltpu.VMEM)] * len(outs),
        compiler_params=pltpu.CompilerParams(vmem_limit_bytes=VMEM_BYTES),
        cost_estimate=pl.CostEstimate(flops=2**24, bytes_accessed=2**24, transcendentals=2**20),
    )(*ins)


def body(
    block_input,
    cotangent,
    norm_gains,
    gains_first,
    gains_second,
    heads_projection_weight,
    heads_first_moment,
    heads_second_moment,
    merge_weight,
    merge_first,
    merge_second,
    gating_weight,
    gating_first,
    gating_second,
    down_weight,
    down_first,
    down_second,
):
    ANY, VMEM = pl.ANY, pltpu.VMEM
    saved = [
        shape(SEQ, 256),
        shape(SEQ, 128),
        shape(8, SEQ, dtype=F32),
        shape(SEQ, 128, dtype=F32),
        shape(SEQ, 128, dtype=F32),
        shape(SEQ, 256),
        shape(256, MODEL_WIDTH),
        shape(4, 16, 32, HEADS_COLS),
        shape(OWN, MODEL_WIDTH, dtype=F32),
        shape(OWN, MODEL_WIDTH, dtype=F32),
        shape(SEQ, MODEL_WIDTH),
        shape(8, MODEL_WIDTH, dtype=F32),
        shape(4, 32, 2 * HIDDEN),
        shape(16 * PIECE, MODEL_WIDTH),
        shape(2, MODEL_WIDTH, dtype=F32),
        shape(OWN, MODEL_WIDTH),
    ]

    def held(array):
        return pltpu.VMEM(array.shape, array.dtype)

    (
        normed_one, query, pair, sums, cosine, sine, attended, w_merge, w_heads,
        middle, grad_middle, branch, gain_part, gating_sum, down_part, down_out, gains, input_rows,
    ) = call(
        opening_kernel,
        [(shape(SEQ, MODEL_WIDTH), ANY)]
        + [(array, ANY) for array in saved[:14]]
        + [(shape(SEQ, MODEL_WIDTH), ANY)]
        + [(array, ANY) for array in saved[14:]],
        [
            (heads_projection_weight, VMEM),
            (merge_weight, VMEM),
            (gating_weight, VMEM),
            (down_weight, VMEM),
            (block_input, VMEM),
            (cotangent, VMEM),
            (norm_gains, VMEM),
        ],
        LINE_SCATTER_SCRATCH
        + ring_scatter_scratch(Rows(2 * HIDDEN))
        + [
            pltpu.VMEM((SEQ, MODEL_WIDTH), BF16),
            pltpu.VMEM((SEQ, MODEL_WIDTH), BF16),
            pltpu.VMEM((SEQ, MODEL_WIDTH), BF16),
            pltpu.VMEM((4, 16, 32, 2 * HIDDEN), BF16),
            pltpu.VMEM((SEQ, HIDDEN), F32),
            pltpu.VMEM((SEQ, HIDDEN), BF16),
            pltpu.VMEM((SEQ, 2 * HIDDEN), BF16),
            pltpu.VMEM((OWN, MODEL_WIDTH), BF16),
            pltpu.VMEM((4, 32, HEADS_COLS), BF16),
            pltpu.VMEM((4, 32, 256), BF16),
            pltpu.VMEM((4, 32, 2 * HIDDEN), BF16),
            pltpu.VMEM((4, PIECE, 512), BF16),
        ]
        + [held(array) for array in saved]
        + [pltpu.VMEM((4, 16, 32, 256), BF16)],
        (29, 117, 35),
        0,
        2**25,
    )
    given = [
        branch, w_merge, query, pair, sums, cosine, sine, down_out, down_part, gating_sum,
        middle, w_heads, attended, normed_one, grad_middle, input_rows, gains, gain_part,
    ]
    (
        block_output, input_grad, gains_grad,
        heads_pieces, merge_pieces, gating_pieces, down_pieces,
    ) = call(
        backward_kernel,
        [
            (shape(512, 512), VMEM),
            (shape(512, 512), VMEM),
            (shape(8, 128, dtype=F32), VMEM),
            (shape(4, 32, HEADS_COLS), VMEM),
            (shape(4, 32, 256), VMEM),
            (shape(4, 32, 2 * HIDDEN), VMEM),
            (shape(4, PIECE, 512), VMEM),
        ],
        [(array, ANY) for array in given],
        LINE_SCATTER_SCRATCH
        + LINE_SCATTER_SCRATCH
        + ring_scatter_scratch(Flat())
        + ring_scatter_scratch(Rows(HEADS_COLS + 256))
        + [held(array) for array in given]
        + [
            pltpu.VMEM((SEQ, MODEL_WIDTH), BF16),
            pltpu.VMEM((SEQ, HEADS_COLS), BF16),
            pltpu.VMEM((SEQ, 256), BF16),
            pltpu.VMEM((SEQ, HEAD_SIZE), F32),
            pltpu.VMEM((SEQ, HEAD_SIZE), F32),
            pltpu.VMEM((HEAD_SIZE, SEQ), BF16),
            pltpu.VMEM((OWN, MODEL_WIDTH), BF16),
            pltpu.VMEM((PIECE, MODEL_WIDTH), BF16),
            pltpu.VMEM((4, 16, 32, HEADS_COLS + 256), BF16),
            pltpu.VMEM((4, 32, HEADS_COLS + 256), BF16),
            pltpu.VMEM((OWN, MODEL_WIDTH), BF16),
            pltpu.VMEM((8, MODEL_WIDTH), F32),
            pltpu.VMEM((4, 8, 512), F32),
            pltpu.VMEM((32, 8, 128), F32),
        ],
        (17, 63, 24),
        3,
        2**25,
    )
    (
        block_output, input_grad,
        gains_grad, gains_next, gains_mean, gains_square,
        heads_grad, heads_next, heads_mean, heads_square,
        merge_grad, merge_next, merge_mean, merge_square,
        gating_grad, gating_next, gating_mean, gating_square,
        down_grad, down_next, down_mean, down_square,
    ) = update(
        (
            block_output, input_grad, gains_grad,
            heads_pieces, merge_pieces, gating_pieces, down_pieces,
        ),
        (
            (norm_gains, gains_first, gains_second),
            (heads_projection_weight, heads_first_moment, heads_second_moment),
            (merge_weight, merge_first, merge_second),
            (gating_weight, gating_first, gating_second),
            (down_weight, down_first, down_second),
        ),
    )
    return (
        block_output,
        input_grad,
        gains_grad,
        gains_next,
        gains_mean,
        gains_square,
        heads_grad,
        heads_next,
        heads_mean,
        heads_square,
        merge_grad,
        merge_next,
        merge_mean,
        merge_square,
        gating_grad,
        gating_next,
        gating_mean,
        gating_square,
        down_grad,
        down_next,
        down_mean,
        down_square,
    )


def solution(mesh):
    in_specs = (
        P(("dp", "col"), "row"),
        P(("dp", "col"), "row"),
        P(None, "row"),
        P(None, "row"),
        P(None, "row"),
        P(("row", "dp"), "col"),
        P(("row", "dp"), "col"),
        P(("row", "dp"), "col"),
        P(("col", "dp"), "row"),
        P(("col", "dp"), "row"),
        P(("col", "dp"), "row"),
        P(("row", "dp"), None, "col"),
        P(("row", "dp"), None, "col"),
        P(("row", "dp"), None, "col"),
        P(("col", "dp"), "row"),
        P(("col", "dp"), "row"),
        P(("col", "dp"), "row"),
    )
    out_specs = (
        P(("dp", "col"), "row"),
        P(("dp", "col"), "row"),
        P(None, "row"),
        P(None, "row"),
        P(None, "row"),
        P(None, "row"),
        P(("row", "dp"), "col"),
        P(("row", "dp"), "col"),
        P(("row", "dp"), "col"),
        P(("row", "dp"), "col"),
        P(("col", "dp"), "row"),
        P(("col", "dp"), "row"),
        P(("col", "dp"), "row"),
        P(("col", "dp"), "row"),
        P(("row", "dp"), None, "col"),
        P(("row", "dp"), None, "col"),
        P(("row", "dp"), None, "col"),
        P(("row", "dp"), None, "col"),
        P(("col", "dp"), "row"),
        P(("col", "dp"), "row"),
        P(("col", "dp"), "row"),
        P(("col", "dp"), "row"),
    )
    return jax.shard_map(body, mesh=mesh, in_specs=in_specs, out_specs=out_specs, check_vma=False)
```

```python
import functools
import math

import jax
import jax.numpy as jnp
from jax import lax
from jax.experimental import pallas as pl
from jax.experimental.pallas import tpu as pltpu
from jax.sharding import PartitionSpec as P

MODEL_WIDTH = 2048
KEY_VALUE_HEADS = 4
HEAD_SIZE = 64
QUERY_PER_GROUP = 8
STEP = 10


EPS_NORM = 1e-05
BETA_ONE = 0.9
BETA_TWO = 0.95
EPS_ADAM = 1e-08
RATE_MATRIX = 0.05
RATE_MERGE = 0.5
RATE_GAIN = 1.0
WEIGHT_DECAY = 0.1
ROPE_BASE = 10000.0
MASK_FILL = -1e30

MESH = pl.DeviceIdType.MESH
VMEM_BYTES = 63 * 2**20
BF16 = jnp.bfloat16
F32 = jnp.float32

SEQ = 1024
OWN = 128
HEADS_COLS = 384
HIDDEN = 768
PIECE = 48
PIECE_USED = 44


class Place:
    def __init__(self):
        self.dp = lax.axis_index("dp")
        self.row = lax.axis_index("row")
        self.col = lax.axis_index("col")
        self.y = lax.div(self.dp, 4)
        self.z = lax.rem(self.dp, 4)
        self.core = lax.rem(self.row, 2)
        self.x = self.col * 2 + lax.div(self.row, 2)

    def near(self, x=0, core=0, y=0, z=0):
        new_x = lax.rem(self.x + x + 4, 4)
        new_core = lax.rem(self.core + core, 2)
        new_y = lax.rem(self.y + y + 4, 4)
        new_z = lax.rem(self.z + z + 4, 4)
        return {
            "dp": new_y * 4 + new_z,
            "row": lax.rem(new_x, 2) * 2 + new_core,
            "col": lax.div(new_x, 2),
        }

    def slot(self, first_axis, first, second):
        y, z = (first, second) if first_axis == "y" else (second, first)
        return lax.rem(self.y + y + 4, 4) * 4 + lax.rem(self.z + z + 4, 4)

    def line(self, x, core):
        return lax.rem(self.x + x + 4, 4) * 2 + lax.rem(self.core + core, 2)

    def peer(self, step):
        other = lax.rem(self.row + step, 4)
        return other, {"dp": self.dp, "row": other, "col": self.col}


class Wires:
    def __init__(self, send, recv, local, parent=None):
        self.send, self.recv, self.local = send, recv, local
        self.root = parent or self
        self.used = {"send": 0, "recv": 0, "local": 0}
        self.debts = []

    def part(self):
        return Wires(self.send, self.recv, self.local, self.root)

    def reserve(self, kind, count=1):
        first = self.root.used[kind]
        self.root.used[kind] += count
        return first

    def start(self, source, target, device, send, recv):
        pltpu.make_async_remote_copy(
            src_ref=source,
            dst_ref=target,
            send_sem=self.send.at[send],
            recv_sem=self.recv.at[recv],
            device_id=device,
            device_id_type=MESH,
        ).start()

    def batch(self, copies, size, send=None):
        recv = self.reserve("recv")
        if send is None:
            send = self.reserve("send")
            self.owe(send, size)
        for source, target, device in copies:
            self.start(source, target, device, send, recv)
        return lambda: self.take(self.recv.at[recv], size)

    def push(self, source, target, device, send=None):
        return self.batch([(source, target, device)], target, send)

    def take(self, semaphore, size):
        pltpu.make_async_copy(size, size, semaphore).wait()

    def owe(self, send, size):
        self.debts.append((send, size))

    def keep(self, source, target):
        copy = pltpu.make_async_copy(source, target, self.local.at[self.reserve("local")])
        copy.start()
        return copy

    def settle(self, debts):
        for send, size in debts:
            self.take(self.send.at[send], size)
        self.debts = [debt for debt in self.debts if all(debt is not other for other in debts)]

    def drain(self):
        self.settle(list(self.debts))


def meet(devices, more=0):
    barrier = pltpu.get_barrier_semaphore()
    for device in devices:
        pl.semaphore_signal(barrier, inc=1, device_id=device, device_id_type=MESH)
    pl.semaphore_wait(barrier, len(devices))


def interleave(*plans):
    waiting = [[next(plan), order, plan] for order, plan in enumerate(plans)]
    while waiting:
        waiting.sort(key=lambda entry: (entry[0], entry[1]))
        entry = waiting[0]
        try:
            entry[0] = max(entry[0], next(entry[2]))
        except StopIteration:
            waiting.pop(0)


def sweep(accounts, since, until):
    yield since
    debts = [(account, debt) for account in accounts for debt in account.debts]
    yield until
    for account, debt in debts:
        if any(debt is other for other in account.debts):
            account.settle([debt])


def ring_neighbours(place):
    return [place.near(y=1), place.near(y=-1), place.near(z=1), place.near(z=-1)]


def line_neighbours(place):
    return [place.near(x=1), place.near(x=-1), place.near(core=1)]


def line_gather(place, wires, own, out, block, half, times, ready=None):
    def size(blocks):
        return out.at[pl.ds(0, blocks * OWN)]

    me = place.line(0, 0)
    send = wires.reserve("send")
    yield times[0]
    kept = wires.keep(own, block(out, me))
    near = wires.batch(
        [(own, block(out, me), place.near(x=1)), (own, block(out, me), place.near(x=-1))],
        size(2),
        send,
    )
    beside = [wires.push(own, block(out, me), place.near(core=1), send)]
    yield times[1]
    near()
    left, right = place.line(-1, 0), place.line(1, 0)
    far = wires.batch(
        [
            (half(out, left, 0), half(out, left, 0), place.near(x=1)),
            (half(out, right, 1), half(out, right, 1), place.near(x=-1)),
        ],
        size(1),
        send,
    )
    beside.append(
        wires.batch(
            [(block(out, came), block(out, came), place.near(core=1)) for came in (left, right)],
            size(2),
            send,
        )
    )
    yield times[2]
    kept.wait()
    for wait in beside:
        wait()
    if ready:
        ready((0, 1, -1))
    far()
    came = block(out, place.line(2, 0))
    last = wires.push(came, came, place.near(core=1), send)
    wires.owe(send, size(7))
    yield times[3]
    last()
    if ready:
        ready((2,))


def token_block(ref, index):
    return ref.at[pl.ds(pl.multiple_of(index * OWN, OWN), OWN)]


def token_half(ref, index, side):
    return ref.at[pl.ds(pl.multiple_of(index * OWN + side * (OWN // 2), OWN // 2), OWN // 2)]


def tile_block(ref, index):
    x, core = lax.div(index, 2), lax.rem(index, 2)
    rows = pl.ds(pl.multiple_of(lax.div(x, 2) * 512, 512), 512)
    columns = pl.ds(pl.multiple_of((lax.rem(x, 2) * 2 + core) * 512, 512), 512)
    return ref.at[rows, columns]


def tile_half(ref, index, side):
    x, core = lax.div(index, 2), lax.rem(index, 2)
    rows = pl.ds(pl.multiple_of(lax.div(x, 2) * 512 + side * 256, 256), 256)
    columns = pl.ds(pl.multiple_of((lax.rem(x, 2) * 2 + core) * 512, 512), 512)
    return ref.at[rows, columns]


def add_rows(out, terms, rows, step=16):
    def chunk(index, carry):
        at = pl.ds(pl.multiple_of(index * step, step), step)
        out[at, :] = functools.reduce(
            lambda a, b: a + b, [term[at, :].astype(F32) for term in terms]
        ).astype(out.dtype)
        return carry

    lax.fori_loop(0, rows // step, chunk, 0)


LINE_SCATTER_SCRATCH = [
    pltpu.VMEM((4, OWN, MODEL_WIDTH), BF16),
    pltpu.VMEM((2, OWN // 2, MODEL_WIDTH), BF16),
    pltpu.VMEM((2, OWN, MODEL_WIDTH), BF16),
]


class LineScatter:
    def __init__(self, place, wires, part, scratch):
        self.place, self.wires, self.part = place, wires, part
        self.beside, self.halves, self.full = scratch
        self.out = wires.reserve("send")
        self.late = wires.reserve("recv")
        self.pairs = {}

    def pair(self, offset):
        self.pairs[offset] = self.wires.push(
            token_block(self.part, self.place.line(offset, 1)),
            self.beside.at[offset],
            self.place.near(core=1),
            self.out,
        )

    def own(self, offset):
        return token_block(self.part, self.place.line(offset, 0))

    def far(self):
        self.pairs[2]()
        total = self.beside.at[2]
        add_rows(total, [self.own(2), total], OWN)
        self.beyond = self.wires.batch(
            [
                (total.at[pl.ds(0, OWN // 2)], self.halves.at[0], self.place.near(x=1)),
                (total.at[pl.ds(OWN // 2, OWN // 2)], self.halves.at[1], self.place.near(x=-1)),
            ],
            self.halves,
            self.out,
        )

    def near(self, offset):
        self.pairs[offset]()
        total = self.beside.at[offset]
        add_rows(total, [self.own(offset), total], OWN)
        self.send(offset, OWN // 2 if offset == 1 else 0)

    def send(self, offset, first):
        rows = pl.ds(first, OWN // 2)
        self.wires.start(
            self.beside.at[offset, rows],
            self.full.at[0 if offset == 1 else 1, rows],
            self.place.near(x=1 if offset == 1 else -1),
            self.out,
            self.late,
        )

    def join(self):
        self.beyond()
        for way, offset, first in ((0, 1, 0), (1, 3, OWN // 2)):
            rows = self.beside.at[offset, pl.ds(first, OWN // 2)]
            add_rows(rows, [rows, self.halves.at[way]], OWN // 2)
            self.send(offset, first)
        self.wires.owe(self.out, self.part.at[pl.ds(0, 7 * OWN)])

    def finish(self):
        self.pairs[0]()
        self.wires.take(self.wires.recv.at[self.late], self.full)

    def terms(self):
        return [self.own(0), self.beside.at[0], self.full.at[0], self.full.at[1]]

    def total_of(self, at):
        return functools.reduce(lambda a, b: a + b, [t[at, :].astype(F32) for t in self.terms()])

    def run(self, start, cost):
        yield start
        for offset in (2, 1, 3, 0):
            self.pair(offset)
        yield start + 2
        self.far()
        yield start + 3
        self.near(1)
        self.near(3)
        yield from self.rest(start, cost)

    def rest(self, start, cost):
        yield start + 5 + 0.5 * cost
        self.join()
        yield start + 4.5 + 1.4 * cost
        self.finish()


class Rows:
    def __init__(self, columns):
        self.item_shape = (2, 32, columns)
        self.half_shape = (1, 32, columns)

    def item(self, ref, side, slot):
        return ref.at[pl.ds(2 * side, 2), slot]

    def half(self, ref, side, part, slot):
        return ref.at[pl.ds(2 * side + part, 1), slot]

    def cut(self, item, part):
        return item.at[pl.ds(part, 1)]

    def span(self, ref, side, items):
        return ref.at[pl.ds(2 * side, 2), pl.ds(0, items)]


class Flat:
    def __init__(self):
        self.item_shape = (PIECE, MODEL_WIDTH // 2)
        self.half_shape = (PIECE, MODEL_WIDTH // 4)

    def item(self, ref, side, slot):
        rows = pl.ds(pl.multiple_of(slot * PIECE, PIECE), PIECE)
        return ref.at[rows, pl.ds(side * (MODEL_WIDTH // 2), MODEL_WIDTH // 2)]

    def half(self, ref, side, part, slot):
        rows = pl.ds(pl.multiple_of(slot * PIECE, PIECE), PIECE)
        return ref.at[rows, pl.ds((2 * side + part) * (MODEL_WIDTH // 4), MODEL_WIDTH // 4)]

    def cut(self, item, part):
        return item.at[:, pl.ds(part * (MODEL_WIDTH // 4), MODEL_WIDTH // 4)]

    def span(self, ref, side, items):
        return ref.at[pl.ds(0, items * PIECE), pl.ds(side * (MODEL_WIDTH // 2), MODEL_WIDTH // 2)]


def ring_move(place, axis, step):
    return place.near(y=step) if axis == "y" else place.near(z=step)


def ring_gather(place, wires, kind, out, side, times):
    first, second = ("z", "y") if side == 0 else ("y", "z")
    slot = functools.partial(place.slot, first)
    size = functools.partial(kind.span, out, side)
    send = wires.reserve("send")
    spread = {}

    def both(axis, items, count):
        return wires.batch(
            [(item, item, ring_move(place, axis, step)) for item, step in zip(items, (1, -1))],
            size(count),
            send,
        )

    def halves(axis, before, after):
        return both(
            axis,
            [kind.half(out, side, 0, before), kind.half(out, side, 1, after)],
            1,
        )

    def send_on(offset):
        spread[offset] = both(second, [kind.item(out, side, slot(offset, 0))] * 2, 2)

    last = wires.reserve("recv")

    def pass_on(offset):
        spread[offset]()
        for part, way, step in ((0, -1, 1), (1, 1, -1)):
            piece = kind.half(out, side, part, slot(offset, way))
            wires.start(piece, piece, ring_move(place, second, step), send, last)

    yield times[0]
    near = both(first, [kind.item(out, side, slot(0, 0))] * 2, 2)
    send_on(0)
    yield times[1]
    near()
    far = halves(first, slot(-1, 0), slot(1, 0))
    send_on(-1)
    send_on(1)
    yield times[2]
    pass_on(0)
    yield times[3]
    far()
    send_on(2)
    yield times[4]
    pass_on(-1)
    yield times[5]
    pass_on(1)
    yield times[6]
    pass_on(2)
    wires.owe(send, size(15))
    yield times[7]
    wires.take(wires.recv.at[last], size(4))


RING_SCATTER_SCRATCH = 8


def ring_scatter_scratch(kind):
    def stack(count, shape):
        return pltpu.VMEM((count, *shape), BF16)

    one_side = [
        stack(8, kind.half_shape),
        stack(8, kind.item_shape),
        stack(2, kind.half_shape),
        stack(2, kind.item_shape),
    ]
    return one_side + one_side


def add_to(out, *terms):
    out[...] = functools.reduce(
        lambda a, b: a + b, [t[...].astype(F32) for t in (out, *terms)]
    ).astype(out.dtype)


def ring_scatter(place, wires, kind, part, side, scratch, result, start, cost, then=None):
    far, came, far_last, came_last = scratch[4 * side : 4 * side + 4]
    first, second = ("z", "y") if side == 0 else ("y", "z")
    slot = functools.partial(place.slot, first)
    size = functools.partial(kind.span, part, side)
    send = wires.reserve("send")
    order = (2, 1, -1, 0)

    def both(axis, sources, targets, count):
        return wires.batch(
            [
                (source, target, ring_move(place, axis, step))
                for source, target, step in zip(sources, targets, (1, -1))
            ],
            size(count),
            send,
        )

    def halves(axis, target, into):
        return both(axis, [kind.half(part, side, n, target) for n in (0, 1)], into, 1)

    def add_halves(came_halves, after, before):
        add_to(kind.half(part, side, 0, after), came_halves[0])
        add_to(kind.half(part, side, 1, before), came_halves[1])

    yield start
    start = start if then is None else then
    beyond = [
        halves(second, slot(offset, 2), [far.at[2 * n], far.at[2 * n + 1]])
        for n, offset in enumerate(order)
    ]
    moved = []
    for n, offset in enumerate(order):
        yield start + 2.5 + (0.5 + n) * cost
        beyond[n]()
        after, before = slot(offset, 1), slot(offset, -1)
        add_halves([far.at[2 * n], far.at[2 * n + 1]], after, before)
        items = [kind.item(part, side, after), kind.item(part, side, before)]
        moved.append(both(second, items, [came.at[2 * n], came.at[2 * n + 1]], 2))

    def finish(n, offset):
        moved[n]()
        add_to(kind.item(part, side, slot(offset, 0)), came.at[2 * n], came.at[2 * n + 1])

    yield start + 4 + 3 * cost
    finish(0, 2)
    beyond_last = halves(first, slot(2, 0), [far_last.at[0], far_last.at[1]])
    yield start + 4 + 4 * cost
    finish(1, 1)
    yield start + 4 + 5 * cost
    finish(2, -1)
    beyond_last()
    after, before = slot(1, 0), slot(-1, 0)
    add_halves([far_last.at[0], far_last.at[1]], after, before)
    items = [kind.item(part, side, after), kind.item(part, side, before)]
    last = both(first, items, [came_last.at[0], came_last.at[1]], 2)
    wires.owe(send, size(15))
    yield start + 5 + 6 * cost
    finish(3, 0)
    yield start + 8 + 7.5 * cost
    last()
    own = kind.item(part, side, slot(0, 0))
    add_to(own, came_last.at[0], came_last.at[1])
    result[...] = own[...]


def call(kernel, outs, ins, scratch, wires, name, cost):
    return pl.pallas_call(
        kernel,
        out_shape=[shape for shape, _ in outs],
        in_specs=[pl.BlockSpec(memory_space=space) for _, space in ins],
        out_specs=[pl.BlockSpec(memory_space=space) for _, space in outs],
        scratch_shapes=list(scratch)
        + [pltpu.SemaphoreType.DMA((count,)) for count in wires],
        compiler_params=pltpu.CompilerParams(
            collective_id=name, has_side_effects=True, vmem_limit_bytes=VMEM_BYTES
        ),
        cost_estimate=pl.CostEstimate(flops=0, bytes_accessed=cost, transcendentals=0),
    )(*[array for array, _ in ins])


def shape(*extent, dtype=BF16):
    return jax.ShapeDtypeStruct(extent, dtype)


def merge_devices(place):
    users = [{"dp": j * 4 + place.z, "row": place.y, "col": place.col} for j in range(4)]
    homes = [
        {"dp": place.row * 4 + place.z, "row": jnp.int32(row), "col": place.col} for row in range(4)
    ]
    return users, homes


def signal_others(place, devices):
    barrier = pltpu.get_barrier_semaphore()
    for device in devices:
        alone = (device["dp"] == place.dp) & (device["row"] == place.row)

        @pl.when(jnp.logical_not(alone))
        def _():
            pl.semaphore_signal(barrier, inc=1, device_id=device, device_id_type=MESH)


def merge_exchange(place, wires, devices, source, target, mine):
    send, recv = wires.reserve("send", 4), wires.reserve("recv", 4)
    copies = []
    for index, device in enumerate(devices):
        copy = pltpu.make_async_remote_copy(
            src_ref=source(index),
            dst_ref=target(index),
            send_sem=wires.send.at[send + index],
            recv_sem=wires.recv.at[recv + mine],
            device_id=device,
            device_id_type=MESH,
        )
        here = pltpu.make_async_copy(source(index), target(index), wires.recv.at[recv + mine])
        alone = (device["dp"] == place.dp) & (device["row"] == place.row)
        copies.append((copy, alone))
        pl.when(alone)(here.start)
        pl.when(jnp.logical_not(alone))(copy.start)

    def wait():
        for index in range(4):
            wires.take(wires.recv.at[recv + index], target(0))
        for copy, alone in copies:
            pl.when(jnp.logical_not(alone))(copy.wait_send)

    return wait


def nested(plans):
    pending = [[next(plan), order, plan] for order, plan in enumerate(plans)]
    while pending:
        pending.sort(key=lambda entry: entry[:2])
        entry = pending[0]
        yield entry[0]
        try:
            entry[0] = max(entry[0], next(entry[2]))
        except StopIteration:
            pending.pop(0)


def column_block(ref, row):
    return ref.at[:, pl.ds(pl.multiple_of(row * 512, 512), 512)]


def down_slot(ref, slot, row):
    rows = pl.ds(pl.multiple_of(slot * PIECE, PIECE), PIECE)
    return ref.at[rows, pl.ds(pl.multiple_of(row * 512, 512), 512)]


def own_token_rows(ref, row):
    return ref.at[pl.ds(pl.multiple_of(row * OWN, OWN), OWN)]


def recut(place, wires, own, out, when):
    peers = [place.peer(step) for step in (1, 2, 3)]
    kept = wires.keep(column_block(own, place.row), own_token_rows(out, place.row))
    moved = wires.batch(
        [
            (column_block(own, other), own_token_rows(out, place.row), device)
            for other, device in peers
        ],
        out.at[pl.ds(0, 3 * OWN)],
    )
    yield when
    kept.wait()
    moved()


def back_pieces(place, wires, part_of, out, when):
    peers = [place.peer(step) for step in (1, 2, 3)]
    kept = wires.keep(part_of(place.row), out.at[place.row])
    moved = wires.batch(
        [(part_of(other), out.at[place.row], device) for other, device in peers],
        out.at[pl.ds(0, 3)],
    )
    yield when
    kept.wait()
    moved()


HEADS_TIMES = (2.6, 9.4, 10.0, 15.0, 15.5, 16.0, 20.0, 23.5)
MERGE_TIMES = (3.2, 11.2, 12.0, 16.5, 18.0, 18.5, 24.7, 28.0)
DOWN_TIMES = (20.1, 26.1, 26.2, 31.0, 34.0, 34.5, 39.0, 49.0)
GATING_TIMES = (26.3, 38.0, 40.0, 49.5, 53.0, 55.0, 60.0, 66.0)


def opening_kernel(
    heads_weight, merge_weight, gating_weight, down_weight, input_own, back_own, gains_own,
    *refs,
):
    (
        normed_out, query_out, pair_out, sums_out, cosine_out, sine_out, attended_out, merge_out,
        heads_out, middle_out, grad_middle_out, branch_out, gain_part_out, gating_sum_out,
        down_part_out, down_out, gains_out, input_rows_out,
    ) = refs[:18]
    line_scratch, scratch = refs[18:21], refs[21:]
    ring_scratch, scratch = scratch[:RING_SCATTER_SCRATCH], scratch[RING_SCATTER_SCRATCH:]
    (
        tokens, part, back, gating, grad_hidden, hidden, grad_gated, rows_own,
        heads_cut, merge_cut, gating_cut, down_cut,
        query, pair, sums, cosine, sine, attended, merge, heads, middle, grad_middle, branch,
        gain_part, gating_sum, down, gains, input_rows, merge_all,
        send, recv, local,
    ) = scratch
    handed = []

    def hand(*pairs):
        handed.extend(wires.keep(source, target) for source, target in pairs)

    place = Place()
    wires = Wires(send, recv, local)
    first_wires, token_wires, gating_wires, down_wires = [wires.part() for _ in range(4)]
    users, homes = merge_devices(place)
    peers = [place.peer(step) for step in (1, 2, 3)]
    same = place.row == place.y
    devices = ring_neighbours(place) + line_neighbours(place) + [p for _, p in peers]
    signal_others(place, devices + homes)
    for row in range(4):
        group, half = divmod(row, 2)
        rows = heads_weight[:, pl.ds(group * 640 + half * 256, 256)]
        heads_cut[row, :, pl.ds(0, 256)] = rows.astype(BF16)
        rows = heads_weight[:, pl.ds(group * 640 + 512, 128)]
        heads_cut[row, :, pl.ds(256, 128)] = rows.astype(BF16)
        for side in range(2):
            piece = merge_weight[pl.ds(16 * row, 16), pl.ds(256 * side, 256)]
            merge_cut[row, pl.ds(16 * side, 16)] = piece.astype(BF16)
    pl.semaphore_wait(
        pltpu.get_barrier_semaphore(), len(devices) + 4 - same.astype(jnp.int32)
    )
    merge_came, down_came, gating_came = [], [], []

    def exchange():
        yield 0.0
        came = [wires.keep(heads_cut.at[place.row], heads.at[place.row, place.dp]).wait]
        came.append(wires.keep(gains_own, column_block(gains, place.row)).wait)
        came.append(
            wires.batch(
                [
                    (heads_cut.at[other], heads.at[place.row, place.dp], device)
                    for other, device in peers
                ],
                heads_cut.at[pl.ds(0, 3)],
            )
        )
        merge_came.append(
            merge_exchange(
                place, wires, users,
                lambda j: merge_cut.at[j],
                lambda j: merge_all.at[place.row, j * 4 + place.z],
                place.row,
            )
        )
        came.append(
            wires.batch(
                [(gains_own, column_block(gains, place.row), device) for _, device in peers],
                gains.at[:, pl.ds(0, 1536)],
            )
        )
        yield 2.6
        for wait in came:
            wait()
        yield from nested(
            ring_gather(place, wires, Rows(HEADS_COLS), heads, side, HEADS_TIMES)
            for side in (0, 1)
        )

    def gating_exchange():
        yield 3.0
        for row in range(4):
            piece = down_weight[pl.ds(PIECE_USED * row, PIECE_USED), :]
            down_cut[row] = jnp.concatenate(
                [piece, jnp.zeros((PIECE - PIECE_USED, 512), F32)], axis=0
            ).astype(BF16)
        target = down_slot(down, place.dp, place.row)
        down_came.append(wires.keep(down_cut.at[place.row], target).wait)
        down_came.append(
            wires.batch(
                [(down_cut.at[other], target, device) for other, device in peers],
                down_cut.at[pl.ds(0, 3)],
            )
        )
        zeros = jnp.zeros((32, PIECE - PIECE_USED), F32)
        for kind in range(2):
            for row in range(4):
                pieces = []
                for slot in range(16):
                    first = slot * 4 * PIECE_USED + row * PIECE_USED
                    pieces += [gating_weight[:, kind, pl.ds(first, PIECE_USED)], zeros]
                gating_cut[row, :, pl.ds(kind * HIDDEN, HIDDEN)] = jnp.concatenate(
                    pieces, axis=1
                ).astype(BF16)
        yield 17.6
        target = gating.at[place.row, place.dp]
        gating_came.append(wires.keep(gating_cut.at[place.row], target).wait)
        gating_came.append(
            wires.batch(
                [(gating_cut.at[other], target, device) for other, device in peers],
                gating_cut.at[pl.ds(0, 3)],
            )
        )

    def tables():
        yield 3.4
        rope_tables(cosine, sine)

    def merge_rows():
        yield 3.2
        for wait in merge_came:
            wait()
        yield from nested(
            ring_gather(place, wires, Rows(256), merge_all, side, MERGE_TIMES) for side in (0, 1)
        )

    def down_rows():
        yield 20.1
        for wait in down_came:
            wait()
        yield from nested(
            ring_gather(place, down_wires, Flat(), down, side, DOWN_TIMES) for side in (0, 1)
        )

    def gating_rows():
        yield 26.3
        for wait in gating_came:
            wait()
        yield from nested(
            ring_gather(place, gating_wires, Rows(2 * HIDDEN), gating, side, GATING_TIMES)
            for side in (0, 1)
        )

    def chip_rows(offset):
        start = pl.multiple_of(lax.rem(place.x + offset + 4, 4) * 256, 256)
        return pl.ds(start, 256)

    def grad_hidden_rows():
        for index in range(4):
            yield 60.5 + 1.3 * index
            at = pl.ds(index * 256, 256)
            grad_hidden[at, :] = contract_last(back[at, :], down[...])

    def forward(offset, when):
        at = chip_rows(offset)
        for tile in range(3):
            gate_at, up_at = pl.ds(tile * 256, 256), pl.ds(HIDDEN + tile * 256, 256)
            rows = tokens[at, :]
            gate = product(rows, gating[:, :, :, gate_at].reshape(MODEL_WIDTH, 256))
            up = product(rows, gating[:, :, :, up_at].reshape(MODEL_WIDTH, 256))
            grad = grad_hidden[at, gate_at]
            sigmoid = jax.nn.sigmoid(gate)
            silu = gate * sigmoid
            hidden[at, gate_at] = (silu * up).astype(BF16)
            grad_gated[at, gate_at] = (grad * up * sigmoid * (1.0 + gate * (1.0 - sigmoid))).astype(
                BF16
            )
            grad_gated[at, up_at] = (grad * silu).astype(BF16)
            yield when + 0.6 * (tile + 1)
        for row in range(4):
            part[at, pl.ds(row * 512, 512)] = contract_last(
                grad_gated[at, :], gating[row].reshape(512, 2 * HIDDEN)
            ).astype(BF16)
            if row % 2:
                yield when + 2.0 + 0.6 * row

    def main():
        yield 0.1
        yield from line_gather(
            place, token_wires, input_own, tokens, tile_block, tile_half, (0.1, 14.9, 23.6, 24.6)
        )
        input_rows[...] = token_block(tokens, place.line(0, 0))[...]
        yield 24.65
        normed = branch
        first = LineScatter(place, first_wires, part, line_scratch)
        yield from projections(
            tokens, gains, heads, cosine, sine, normed, query, pair,
        )
        normed_copy = wires.keep(normed, normed_out)
        token_wires.drain()
        yield 30.2
        for row in range(4):
            for slot in range(16):
                y, z = divmod(slot, 4)
                for half in range(2):
                    merge[pl.ds(z * 64 + y * 16, 16), pl.ds(row * 512 + half * 256, 256)] = (
                        merge_all[row, slot, pl.ds(16 * half, 16), :]
                    )
        then = [None, first.far, lambda: first.near(1), lambda: first.near(3)]
        for order, offset in enumerate((2, 1, -1, 0)):
            at = chip_rows(offset)
            when = 30.8 + 3.8 * order
            for _ in attention(
                at, lax.rem(place.x + offset + 4, 4), query, pair, sums, attended
            ):
                yield when + 1.5
                if order:
                    then[order]()
            part[at, :] = product(attended[at, :], merge[...]).astype(BF16)
            first.pair(offset % 4)
            yield when + 3.8
        hand(
            (query, query_out), (pair, pair_out), (sums, sums_out), (cosine, cosine_out),
            (sine, sine_out), (attended, attended_out), (merge, merge_out), (heads, heads_out),
            (gains, gains_out), (input_rows, input_rows_out),
        )
        yield 46.2
        first.join()
        yield 58.0
        first.finish()

        def chunk(index, carry):
            at = pl.ds(pl.multiple_of(index * 16, 16), 16)
            total = first.total_of(at) + input_rows[at, :].astype(F32)
            middle[at, :] = total
            scale = lax.rsqrt(
                jnp.sum(total * total, axis=1, keepdims=True) / MODEL_WIDTH + EPS_NORM
            )
            rows_own[at, :] = (total * scale * gains[1:2, :]).astype(BF16)
            return carry

        lax.fori_loop(0, OWN // 16, chunk, 0)
        first_wires.drain()
        normed_copy.wait()
        hand((middle, middle_out))
        me, block, half = place.line(0, 0), token_block, token_half
        mine = wires.keep(rows_own, block(tokens, me))
        near = token_wires.batch(
            [(rows_own, block(tokens, me), place.near(x=step)) for step in (1, -1)],
            tokens.at[pl.ds(0, 2 * OWN)],
        )
        beside = token_wires.push(rows_own, block(tokens, me), place.near(core=1))

        def pass_beside(offset):
            came = block(tokens, place.line(offset, 0))
            return token_wires.push(came, came, place.near(core=1))

        second = LineScatter(place, wires, part, line_scratch)
        yield 70.0
        mine.wait()
        beside()
        yield from forward(0, 70.0)
        second.pair(0)
        yield 78.5
        near()
        pieces = [half(tokens, place.line(-1, 0), 0), half(tokens, place.line(1, 0), 1)]
        far = token_wires.batch(
            [(piece, piece, place.near(x=step)) for piece, step in zip(pieces, (1, -1))],
            tokens.at[pl.ds(0, OWN)],
        )
        beside_right, beside_left = pass_beside(1), pass_beside(-1)
        yield 80.5
        beside_right()
        yield from forward(1, 80.5)
        second.pair(1)
        yield 84.1
        beside_left()
        for step, when in enumerate(forward(-1, 84.1)):
            yield when
            if step == 3:
                far()
                beside_far = pass_beside(2)
        second.pair(3)
        second.near(1)
        yield 88.0
        beside_far()
        for step, when in enumerate(forward(2, 89.5)):
            yield when
            if step == 1:
                second.near(3)
        second.pair(2)
        yield 94.5
        second.far()
        yield from second.rest(94.0, 11.4)
        gain_part[...] = jnp.zeros_like(gain_part)
        back_own_rows = token_block(back, place.line(0, 0))

        def chunk_back(index, carry):
            at = pl.ds(pl.multiple_of(index * 16, 16), 16)
            through, gain = norm_back(middle[at, :], gains[1:2, :], second.total_of(at))
            total = back_own_rows[at, :].astype(F32) + through
            grad_middle[at, :] = total
            rows_own[at, :] = total.astype(BF16)
            gain_part[...] += gain.reshape(2, 8, MODEL_WIDTH).sum(axis=0)
            return carry

        token_wires.drain()
        lax.fori_loop(0, OWN // 16, chunk_back, 0)

        def ready(offsets):
            hand(*[(branch.at[chip_rows(o)], branch_out.at[chip_rows(o)]) for o in offsets])

        yield from line_gather(
            place, wires, rows_own, branch, token_block, token_half, (117.2, 131.0, 138.8, 141.0), ready
        )
        hand((grad_middle, grad_middle_out), (gain_part, gain_part_out))

    computed = []

    def gradients():
        yield 94.6
        gating_wires.drain()
        for row in range(4):
            for piece in range(2):
                columns = pl.ds(row * 512 + piece * 256, 256)
                gating[row, pl.ds(8 * piece, 8)] = (
                    token_product(tokens[:, columns], grad_gated[...])
                    .astype(BF16)
                    .reshape(8, 32, 2 * HIDDEN)
                )
                computed.append(row)
                yield 96.0 + 1.05 * (2 * row + piece + 1)

    def gradient_side(side):
        yield 100.3 + 4.2 * side
        assert len(computed) >= 4 + 4 * side
        yield from ring_scatter(
            place, wires, Rows(2 * HIDDEN), gating, side, ring_scratch,
            gating_sum.at[pl.ds(2 * side, 2)], 100.3 + 4.2 * side, 4.3,
        )
        hand((gating_sum.at[pl.ds(2 * side, 2)], gating_sum_out.at[pl.ds(2 * side, 2)]))

    def down_products():
        yield 106.9
        token_wires.drain()
        for index in range(4):
            at = pl.ds(index * 256, 256)
            tokens[at, :] = product(hidden[at, :], down[...]).astype(BF16)
            hand((tokens.at[at], down_out.at[at]))
            yield 107.9 + 1.0 * index
        down_wires.drain()
        for tile in range(3):
            columns = pl.ds(tile * 256, 256)
            down[columns, :] = token_product(hidden[:, columns], back[...]).astype(BF16)
            hand((down.at[columns], down_part_out.at[columns]))
            yield 112.3 + 1.2 * tile

    interleave(
        main(),
        exchange(),
        gating_exchange(),
        merge_rows(),
        tables(),
        down_rows(),
        gating_rows(),
        line_gather(
            place, wires, back_own, back, tile_block, tile_half, (25.3, 38.0, 50.5, 52.0)
        ),
        grad_hidden_rows(),
        gradients(),
        gradient_side(0),
        gradient_side(1),
        down_products(),
        sweep([wires, gating_wires, down_wires], 66.0, 76.5),
        sweep([wires, token_wires], 117.5, 126.0),
    )
    wires.drain()
    for copy in handed:
        copy.wait()


def norm_back(values, gain_row, gradient):
    scale = lax.rsqrt(jnp.sum(values * values, axis=1, keepdims=True) / MODEL_WIDTH + EPS_NORM)
    weighted = gain_row * gradient
    inner = jnp.sum(weighted * values, axis=1, keepdims=True)
    through = scale * weighted - values * (scale * scale * scale * inner / MODEL_WIDTH)
    return through, gradient * values * scale


def turn(tile, cosine, sine):
    lane = lax.broadcasted_iota(jnp.int32, tile.shape, 1)
    first = lax.rem(lane, HEAD_SIZE) < HEAD_SIZE // 2
    swapped = jnp.where(first, pltpu.roll(tile, 96, axis=1), pltpu.roll(tile, 32, axis=1))
    return tile * cosine + swapped * sine


def rope_tables(cosine, sine):
    half_width = HEAD_SIZE // 2

    def chunk(index, carry):
        at = pl.ds(pl.multiple_of(index * 128, 128), 128)
        lane = lax.broadcasted_iota(jnp.int32, (128, 128), 1)
        row = lax.broadcasted_iota(jnp.int32, (128, 128), 0) + index * 128
        frequency = jnp.exp(
            lax.rem(lane, half_width).astype(F32) * (-2.0 / HEAD_SIZE * math.log(ROPE_BASE))
        )
        angles = row.astype(F32) * frequency
        cosine[at, :] = jnp.cos(angles)
        first = lax.rem(lane, HEAD_SIZE) < half_width
        sine[at, :] = jnp.where(first, -jnp.sin(angles), jnp.sin(angles))
        return carry

    lax.fori_loop(0, SEQ // 128, chunk, 0)


def keys_only(cosine, sine):
    key = lax.broadcasted_iota(jnp.int32, cosine.shape, 1) < HEAD_SIZE
    return jnp.where(key, cosine, 1.0), jnp.where(key, sine, 0.0)


def heads_weight_of(heads):
    return heads[...].reshape(MODEL_WIDTH, HEADS_COLS)


QUERY_BLOCK = 256


def projections(
    inputs, gains, heads, cosine, sine,
    normed, query, pair,
):
    for index in range(4):
        at = pl.ds(index * 256, 256)
        wide = inputs[at, :].astype(F32)
        scale = lax.rsqrt(jnp.sum(wide * wide, axis=1, keepdims=True) / MODEL_WIDTH + EPS_NORM)
        low = (wide * scale * gains[0:1, :]).astype(BF16)
        normed[at, :] = low
        mixed = product(low, heads_weight_of(heads))
        cos, sin = cosine[at, :], sine[at, :]
        query[at, pl.ds(0, 128)] = turn(mixed[:, :128], cos, sin).astype(BF16)
        query[at, pl.ds(128, 128)] = turn(mixed[:, 128:256], cos, sin).astype(BF16)
        pair[at, :] = turn(mixed[:, 256:], *keys_only(cos, sin)).astype(BF16)
        yield 24.7 + 1.3 * (index + 1)


def attention(at, block, query, pair, sums, attended):
    scale = HEAD_SIZE ** (-0.5)
    rows_at = lax.broadcasted_iota(jnp.int32, (QUERY_BLOCK, QUERY_BLOCK), 0)
    keys_at = lax.broadcasted_iota(jnp.int32, (QUERY_BLOCK, QUERY_BLOCK), 1)
    out, logs = [], []
    for two in range(2):
        if two:
            yield
        queries = [
            query[at, pl.ds(head * HEAD_SIZE, HEAD_SIZE)] for head in (2 * two, 2 * two + 1)
        ]

        def weigh(rows, keys):
            return contract_last(rows, pair[keys, pl.ds(0, HEAD_SIZE)]) * scale

        def values(keys):
            return pair[keys, pl.ds(HEAD_SIZE, HEAD_SIZE)]

        state = []
        for rows in queries:
            scores = jnp.where(rows_at >= keys_at, weigh(rows, at), MASK_FILL)
            top = jnp.max(scores, axis=1, keepdims=True)
            powers = jnp.exp(scores - top)
            total = jnp.sum(powers, axis=1, keepdims=True)
            state.append((top, total, product(powers.astype(BF16), values(at))))

        def step(index, state):
            keys = pl.ds(pl.multiple_of(index * QUERY_BLOCK, QUERY_BLOCK), QUERY_BLOCK)
            result = []
            for rows, (top, total, mean) in zip(queries, state):
                scores = weigh(rows, keys)
                higher = jnp.maximum(top, jnp.max(scores, axis=1, keepdims=True))
                shrink = jnp.exp(top - higher)
                powers = jnp.exp(scores - higher)
                total = total * shrink + jnp.sum(powers, axis=1, keepdims=True)
                mean = mean * shrink + product(powers.astype(BF16), values(keys))
                result.append((higher, total, mean))
            return tuple(result)

        for top, total, mean in lax.fori_loop(0, block, step, tuple(state)):
            out.append((mean * (1.0 / total)).astype(BF16))
            logs.append(top + jnp.log(total))
    logs.append(jnp.zeros((QUERY_BLOCK, 124), F32))
    sums[:, at] = jnp.transpose(jnp.concatenate(logs, axis=1))[:8]
    attended[at, :] = jnp.concatenate(out, axis=1)


def backward_kernel(*refs):
    given, refs = refs[:18], refs[18:]
    (
        output, input_grad, gains_grad, heads_pieces, merge_pieces, gating_pieces, down_pieces,
    ) = refs[:7]
    out_scratch, scratch = refs[7:10], refs[10:]
    line_scratch, scratch = scratch[:3], scratch[3:]
    down_scratch, scratch = scratch[:8], scratch[8:]
    heads_scratch, scratch = scratch[:8], scratch[8:]
    held, scratch = scratch[:18], scratch[18:]
    (
        branch, merge, query, pair, sums, cosine, sine, down_out, down_part, gating_sum,
        middle, heads, attended, normed, grad_middle, input_rows, gains, gain_part,
    ) = held
    (
        part, grad_mixed, grad_attended, grad_key, grad_value, key_columns, rows_own,
        down_sum, heads_all, heads_sum, input_grad_own, gain_rows, gain_came, gain_all,
        send, recv, local,
    ) = scratch
    place = Place()
    wires = Wires(send, recv, local)
    loads = [wires.keep(source, target) for source, target in zip(given, held)]

    def need(*names):
        for index in names:
            if loads[index] is not None:
                loads[index].wait()
                loads[index] = None

    users, homes = merge_devices(place)
    peers = [place.peer(step) for step in (1, 2, 3)]
    same = place.row == place.y
    barrier = pltpu.get_barrier_semaphore()
    devices = ring_neighbours(place) + line_neighbours(place) + [p for _, p in peers]
    signal_others(place, devices + users)

    def far(step):
        index = lax.rem(place.col * 16 + place.dp + step, 32)
        return {"dp": lax.rem(index, 16), "row": place.row, "col": lax.div(index, 16)}

    def greet(step, carry):
        pl.semaphore_signal(barrier, inc=1, device_id=far(step), device_id_type=MESH)
        return carry

    lax.fori_loop(1, 32, greet, 0)
    need(0, 1)
    attend = attention_back(
        branch, merge, query, pair, sums, cosine, sine, grad_mixed,
        grad_attended, grad_key, grad_value, key_columns,
    )
    next(attend)
    next(attend)
    pl.semaphore_wait(barrier, len(devices) + 31 + 4 - same.astype(jnp.int32))

    def outputs():
        yield 0.1
        need(7)
        scatter = LineScatter(place, wires, down_out, out_scratch)
        yield from scatter.run(0.1, 11.4)
        yield 21.2
        need(10)

        def chunk(index, carry):
            at = pl.ds(pl.multiple_of(index * 16, 16), 16)
            rows_own[at, :] = (scatter.total_of(at) + middle[at, :]).astype(BF16)
            return carry

        lax.fori_loop(0, OWN // 16, chunk, 0)
        yield 27.9
        yield from recut(place, wires, rows_own, output, 46.0)

    def down_rows():
        yield 0.3
        need(8)
        yield from nested(
            ring_scatter(
                place, wires, Flat(), down_part, side, down_scratch,
                down_sum.at[:, pl.ds(side * 1024, 1024)], 0.3, 2.1,
            )
            for side in (0, 1)
        )
        yield from back_pieces(
            place, wires, lambda row: column_block(down_sum, row), down_pieces, 46.0
        )

    def gating():
        yield 0.4
        need(9)
        yield from back_pieces(
            place, wires, lambda row: gating_sum.at[row], gating_pieces, 36.0
        )

    def compute():
        yield 0.2
        need(2, 3, 4, 5, 6)
        yield from attend
        need(11)
        scatter = LineScatter(place, wires, part, line_scratch)
        then = [None, scatter.far, lambda: scatter.near(1), None]
        for order, offset in enumerate((2, 1, -1, 0)):
            start = pl.multiple_of(lax.rem(place.x + offset + 4, 4) * 256, 256)
            at = pl.ds(start, 256)
            for row in range(4):
                part[at, pl.ds(row * 512, 512)] = contract_last(
                    grad_mixed[at, :],
                    heads[row].reshape(512, HEADS_COLS),
                ).astype(BF16)
            scatter.pair(offset % 4)
            if then[order]:
                then[order]()
        yield 19.6
        yield from gradient(scatter)

    computed = []

    def weights():
        yield 21.5
        need(12, 13, 16, 17)
        gain_rows[...] = jnp.zeros_like(gain_rows)
        gain_rows[1:2, :] = jnp.sum(gain_part[...], axis=0, keepdims=True)
        ones = jnp.ones((8, HEADS_COLS), BF16)
        for row in range(4):
            columns = pl.ds(row * 512, 512)
            merge_part = token_product(attended[...], branch[:, columns]).astype(BF16)
            for slot in range(16):
                y, z = divmod(slot, 4)
                for half in range(2):
                    heads_all[row, slot, pl.ds(16 * half, 16), pl.ds(HEADS_COLS, 256)] = (
                        merge_part[
                            z * 64 + y * 16 : z * 64 + y * 16 + 16,
                            half * 256 : half * 256 + 256,
                        ]
                    )
            for piece in range(2):
                columns = pl.ds(row * 512 + piece * 256, 256)
                grad = token_product(normed[:, columns], grad_mixed[...])
                slots = pl.ds(8 * piece, 8)
                heads_all[row, slots, :, pl.ds(0, HEADS_COLS)] = grad.astype(BF16).reshape(
                    8, 32, HEADS_COLS
                )
                weight = heads[row, slots].reshape(256, HEADS_COLS)
                terms = grad * weight.astype(F32)
                high = terms.astype(BF16)
                low = (terms - high.astype(F32)).astype(BF16)
                sums_ = contract_last(ones, high) + contract_last(ones, low)
                gain_rows[0:1, columns] = sums_[0:1] / gains[0:1, columns]
            computed.append(row)
            yield 21.5 + 1.55 * (row + 1)
        yield from gain_sums()

    def heads_side(side):
        yield 24.7 + 3.1 * side
        assert len(computed) >= 2 + 2 * side
        yield from ring_scatter(
            place, wires, Rows(HEADS_COLS + 256), heads_all, side, heads_scratch,
            heads_sum.at[pl.ds(2 * side, 2)], 24.7 + 3.1 * side, 1.8,
        )
        computed.append("side")

    def heads_back():
        yield 49.4
        assert computed.count("side") == 2
        merge_wait = merge_exchange(
            place, wires, homes,
            lambda row: heads_sum.at[row, :, pl.ds(HEADS_COLS, 256)],
            lambda row: merge_pieces.at[place.y],
            place.y,
        )
        yield from back_pieces(
            place, wires,
            lambda row: heads_sum.at[row, :, pl.ds(0, HEADS_COLS)], heads_pieces, 55.0,
        )
        merge_wait()

    def gain_sums():
        moved = wires.batch(
            [
                (column_block(gain_rows, other), gain_came.at[place.row], device)
                for other, device in peers
            ],
            gain_came.at[pl.ds(0, 3)],
        )
        kept = wires.keep(column_block(gain_rows, place.row), gain_came.at[place.row])
        yield 35.95
        kept.wait()
        moved()
        local_sum = gain_came[0] + gain_came[1] + gain_came[2] + gain_came[3]
        me = place.col * 16 + place.dp
        for kind in range(2):
            for tile in range(4):
                gain_all[me, pl.ds(4 * kind + tile, 1), :] = local_sum[
                    kind : kind + 1, tile * 128 : tile * 128 + 128
                ]
        send, recv = wires.reserve("send"), wires.reserve("recv")

        def start(step, carry):
            wires.start(gain_all.at[me], gain_all.at[me], far(step), send, recv)
            return carry

        lax.fori_loop(1, 32, start, 0)
        wires.owe(send, gain_all.at[pl.ds(0, 31)])
        yield 50.0
        wires.take(wires.recv.at[recv], gain_all.at[pl.ds(0, 31)])
        gains_grad[...] = functools.reduce(lambda a, b: a + b, [gain_all[i] for i in range(32)])

    def gradient(scatter):
        scatter.near(3)
        yield 26.2
        scatter.join()
        yield 36.0
        scatter.finish()
        need(14, 15)

        def chunk(index, carry):
            at = pl.ds(pl.multiple_of(index * 16, 16), 16)
            grad = scatter.total_of(at)
            through, _ = norm_back(input_rows[at, :].astype(F32), gains[0:1, :], grad)
            input_grad_own[at, :] = (grad_middle[at, :] + through).astype(BF16)
            return carry

        lax.fori_loop(0, OWN // 16, chunk, 0)
        yield from recut(place, wires, input_grad_own, input_grad, 52.0)

    interleave(
        compute(),
        outputs(),
        down_rows(),
        gating(),
        weights(),
        heads_side(0),
        heads_side(1),
        heads_back(),
        sweep([wires], 30.0, 44.9),
    )
    wires.drain()


def attention_back(
    branch, merge, query, pair, sums, cosine, sine, grad_mixed,
    grad_attended, grad_key, grad_value, key_columns,
):
    yield 0.3
    def attended_rows(index, carry):
        at = pl.ds(pl.multiple_of(index * 512, 512), 512)
        grad_attended[at, :] = contract_last(branch[at, :], merge[...]).astype(BF16)
        return carry

    attended_rows(0, 0)
    yield 2.0
    attended_rows(1, 0)
    key_columns[...] = jnp.transpose(pair[...].astype(F32))[:HEAD_SIZE].astype(BF16)
    grad_key[...] = jnp.zeros_like(grad_key)
    grad_value[...] = jnp.zeros_like(grad_value)
    scale = HEAD_SIZE ** (-0.5)
    keys_at = lax.broadcasted_iota(jnp.int32, (QUERY_BLOCK, QUERY_BLOCK), 0)
    rows_at = lax.broadcasted_iota(jnp.int32, (QUERY_BLOCK, QUERY_BLOCK), 1)
    for block in range(SEQ // QUERY_BLOCK):
        at = pl.ds(block * QUERY_BLOCK, QUERY_BLOCK)
        before = block * QUERY_BLOCK
        for two in range(2):
            turned = []
            for head in (2 * two, 2 * two + 1):
                columns = pl.ds(head * HEAD_SIZE, HEAD_SIZE)
                rows, back = query[at, columns], grad_attended[at, columns]
                log_total = sums[pl.ds(head, 1), at]
                spans = [at] + ([pl.ds(0, before)] if before else [])
                softs, grads = [], []
                for span in spans:
                    scores = contract_last(pair[span, pl.ds(0, HEAD_SIZE)], rows) * scale
                    soft = jnp.exp(scores - log_total)
                    if span is at:
                        soft = jnp.where(rows_at >= keys_at, soft, 0.0)
                    softs.append(soft)
                    grads.append(contract_last(pair[span, pl.ds(HEAD_SIZE, HEAD_SIZE)], back))
                inner = functools.reduce(
                    lambda a, b: a + b,
                    [jnp.sum(s * g, axis=0, keepdims=True) for s, g in zip(softs, grads)],
                )
                result = 0.0
                for span, soft, grad in zip(spans, softs, grads):
                    low = (soft * (grad - inner)).astype(BF16)
                    grad_key[span, :] += product(low, rows)
                    grad_value[span, :] += product(soft.astype(BF16), back)
                    result += product(key_columns[:, span], low)
                turned.append(result)
                yield 1.9 + (2.1, 5.0, 8.7, 13.2)[block] - (0.52, 0.72, 0.92, 1.15)[block] * (3 - head)
            tile = jnp.transpose(jnp.concatenate(turned, axis=0)) * scale
            grad_mixed[at, pl.ds(two * 128, 128)] = turn(
                tile, cosine[at, :], -sine[at, :]
            ).astype(BF16)

    def finish_rows(index, carry):
        at = pl.ds(pl.multiple_of(index * 128, 128), 128)
        cos, sin = keys_only(cosine[at, :], sine[at, :])
        tile = jnp.concatenate([grad_key[at, :] * scale, grad_value[at, :]], axis=1)
        grad_mixed[at, pl.ds(256, 128)] = turn(tile, cos, -sin).astype(BF16)
        return carry

    lax.fori_loop(0, SEQ // 128, finish_rows, 0)


def product(left, right):
    return jnp.dot(left, right, preferred_element_type=F32)


def contract_last(left, right):
    return lax.dot_general(left, right, (((1,), (1,)), ((), ())), preferred_element_type=F32)


def token_product(left, right):
    return lax.dot_general(left, right, (((0,), (0,)), ((), ())), preferred_element_type=F32)


def adamw(current, gradient, first, second, step_rate, decay_rate):
    mean_new = BETA_ONE * first + (1.0 - BETA_ONE) * gradient
    square_new = BETA_TWO * second + (1.0 - BETA_TWO) * gradient * gradient
    mean_hat = mean_new / (1.0 - BETA_ONE**STEP)
    square_hat = square_new / (1.0 - BETA_TWO**STEP)
    updated = current - step_rate * (
        mean_hat / (jnp.sqrt(square_hat) + EPS_ADAM) + decay_rate * current
    )
    return (updated, mean_new, square_new)


def update_kernel(*refs):
    given, results = refs[:22], refs[22:44]
    held, made = refs[44:66], refs[66:87]
    load_sem, store_sem = refs[87:]
    loads, stores = {}, []

    def load(*indices):
        for index in indices:
            loads[index] = pltpu.make_async_copy(
                given[index], held[index], load_sem.at[index]
            )
            loads[index].start()

    def need(*indices):
        for index in indices:
            loads[index].wait()
        return [held[index] for index in indices]

    def store(source, target):
        copy = pltpu.make_async_copy(source, target, store_sem.at[len(stores)])
        copy.start()
        stores.append(copy)

    groups = {kind: [7 + 3 * kind + n for n in range(3)] for kind in range(5)}
    load(2, *groups[0], 4, *groups[2], 3, *groups[1], 6, *groups[4], 5, *groups[3], 1, 0)

    def advance(kind, gradient, rate, decay, rows):
        state = need(*groups[kind])
        outs = [made[1 + 4 * kind + n] for n in range(4)]
        targets = [results[2 + 4 * kind + n] for n in range(4)]
        gradient(outs[0])
        for first in range(0, outs[0].shape[0], rows):
            at = pl.ds(first, rows)
            new = adamw(
                state[0][at], outs[0][at], state[1][at], state[2][at], rate, decay
            )
            for ref, value in zip(outs[1:], new):
                ref[at] = value
            for ref, target in zip(outs, targets):
                store(ref.at[at], target.at[at])

    def gains_gradient(out):
        (gains,) = need(2)
        for kind in range(2):
            for tile in range(4):
                out[pl.ds(kind, 1), pl.ds(tile * 128, 128)] = gains[pl.ds(4 * kind + tile, 1), :]

    def merge_gradient(out):
        (merge,) = need(4)
        for row in range(4):
            for side in range(2):
                out[pl.ds(16 * row, 16), pl.ds(256 * side, 256)] = merge[
                    row, pl.ds(16 * side, 16)
                ].astype(F32)

    def heads_gradient(out):
        (heads,) = need(3)
        for row in range(4):
            group, half = divmod(row, 2)
            out[:, pl.ds(group * 640 + half * 256, 256)] = heads[row, :, pl.ds(0, 256)].astype(F32)
        for group in range(2):
            pair = pl.ds(256, 128)
            out[:, pl.ds(group * 640 + 512, 128)] = heads[2 * group, :, pair].astype(F32) + heads[
                2 * group + 1, :, pair
            ].astype(F32)

    def down_gradient(out):
        (down,) = need(6)
        for row in range(4):
            out[pl.ds(PIECE_USED * row, PIECE_USED), :] = down[row].astype(F32)[:PIECE_USED]

    def gating_gradient(out):
        (gating,) = need(5)
        for kind in range(2):
            rows = [gating[row, :, pl.ds(kind * HIDDEN, HIDDEN)].astype(F32) for row in range(4)]
            out[:, kind, :] = jnp.concatenate(
                [
                    rows[row][:, slot * PIECE : slot * PIECE + PIECE_USED]
                    for slot in range(16)
                    for row in range(4)
                ],
                axis=1,
            )

    advance(0, gains_gradient, RATE_GAIN, 0.0, 2)
    advance(2, merge_gradient, RATE_MERGE, WEIGHT_DECAY, 64)
    advance(1, heads_gradient, RATE_MATRIX, WEIGHT_DECAY, 32)
    advance(4, down_gradient, RATE_MATRIX, WEIGHT_DECAY, 88)
    advance(3, gating_gradient, RATE_MATRIX, WEIGHT_DECAY, 16)
    input_grad, output = need(1, 0)
    store(output, results[0])
    made[0][...] = input_grad[...].astype(F32)
    store(made[0], results[1])
    for copy in stores:
        copy.wait()


def update(given, states):
    ins = list(given) + [array for state in states for array in state]
    outs = [shape(512, 512), shape(512, 512, dtype=F32)]
    for state in states:
        outs += [shape(*state[0].shape, dtype=F32)] * 4
    return pl.pallas_call(
        update_kernel,
        out_shape=outs,
        in_specs=[pl.BlockSpec(memory_space=pl.ANY)] * len(ins),
        out_specs=[pl.BlockSpec(memory_space=pl.ANY)] * len(outs),
        scratch_shapes=[pltpu.VMEM(array.shape, array.dtype) for array in ins + outs[1:]]
        + [pltpu.SemaphoreType.DMA((22,)), pltpu.SemaphoreType.DMA((30,))],
        compiler_params=pltpu.CompilerParams(vmem_limit_bytes=VMEM_BYTES),
        cost_estimate=pl.CostEstimate(flops=2**24, bytes_accessed=2**24, transcendentals=2**20),
    )(*ins)


def body(
    block_input,
    cotangent,
    norm_gains,
    gains_first,
    gains_second,
    heads_projection_weight,
    heads_first_moment,
    heads_second_moment,
    merge_weight,
    merge_first,
    merge_second,
    gating_weight,
    gating_first,
    gating_second,
    down_weight,
    down_first,
    down_second,
):
    ANY, VMEM = pl.ANY, pltpu.VMEM
    saved = [
        shape(SEQ, 256),
        shape(SEQ, 128),
        shape(8, SEQ, dtype=F32),
        shape(SEQ, 128, dtype=F32),
        shape(SEQ, 128, dtype=F32),
        shape(SEQ, 256),
        shape(256, MODEL_WIDTH),
        shape(4, 16, 32, HEADS_COLS),
        shape(OWN, MODEL_WIDTH, dtype=F32),
        shape(OWN, MODEL_WIDTH, dtype=F32),
        shape(SEQ, MODEL_WIDTH),
        shape(8, MODEL_WIDTH, dtype=F32),
        shape(4, 32, 2 * HIDDEN),
        shape(16 * PIECE, MODEL_WIDTH),
        shape(2, MODEL_WIDTH, dtype=F32),
        shape(OWN, MODEL_WIDTH),
    ]

    def held(array):
        return pltpu.VMEM(array.shape, array.dtype)

    (
        normed_one, query, pair, sums, cosine, sine, attended, w_merge, w_heads,
        middle, grad_middle, branch, gain_part, gating_sum, down_part, down_out, gains, input_rows,
    ) = call(
        opening_kernel,
        [(shape(SEQ, MODEL_WIDTH), ANY)]
        + [(array, ANY) for array in saved[:14]]
        + [(shape(SEQ, MODEL_WIDTH), ANY)]
        + [(array, ANY) for array in saved[14:]],
        [
            (heads_projection_weight, VMEM),
            (merge_weight, VMEM),
            (gating_weight, VMEM),
            (down_weight, VMEM),
            (block_input, VMEM),
            (cotangent, VMEM),
            (norm_gains, VMEM),
        ],
        LINE_SCATTER_SCRATCH
        + ring_scatter_scratch(Rows(2 * HIDDEN))
        + [
            pltpu.VMEM((SEQ, MODEL_WIDTH), BF16),
            pltpu.VMEM((SEQ, MODEL_WIDTH), BF16),
            pltpu.VMEM((SEQ, MODEL_WIDTH), BF16),
            pltpu.VMEM((4, 16, 32, 2 * HIDDEN), BF16),
            pltpu.VMEM((SEQ, HIDDEN), F32),
            pltpu.VMEM((SEQ, HIDDEN), BF16),
            pltpu.VMEM((SEQ, 2 * HIDDEN), BF16),
            pltpu.VMEM((OWN, MODEL_WIDTH), BF16),
            pltpu.VMEM((4, 32, HEADS_COLS), BF16),
            pltpu.VMEM((4, 32, 256), BF16),
            pltpu.VMEM((4, 32, 2 * HIDDEN), BF16),
            pltpu.VMEM((4, PIECE, 512), BF16),
        ]
        + [held(array) for array in saved]
        + [pltpu.VMEM((4, 16, 32, 256), BF16)],
        (29, 117, 35),
        0,
        2**25,
    )
    given = [
        branch, w_merge, query, pair, sums, cosine, sine, down_out, down_part, gating_sum,
        middle, w_heads, attended, normed_one, grad_middle, input_rows, gains, gain_part,
    ]
    (
        block_output, input_grad, gains_grad,
        heads_pieces, merge_pieces, gating_pieces, down_pieces,
    ) = call(
        backward_kernel,
        [
            (shape(512, 512), VMEM),
            (shape(512, 512), VMEM),
            (shape(8, 128, dtype=F32), VMEM),
            (shape(4, 32, HEADS_COLS), VMEM),
            (shape(4, 32, 256), VMEM),
            (shape(4, 32, 2 * HIDDEN), VMEM),
            (shape(4, PIECE, 512), VMEM),
        ],
        [(array, ANY) for array in given],
        LINE_SCATTER_SCRATCH
        + LINE_SCATTER_SCRATCH
        + ring_scatter_scratch(Flat())
        + ring_scatter_scratch(Rows(HEADS_COLS + 256))
        + [held(array) for array in given]
        + [
            pltpu.VMEM((SEQ, MODEL_WIDTH), BF16),
            pltpu.VMEM((SEQ, HEADS_COLS), BF16),
            pltpu.VMEM((SEQ, 256), BF16),
            pltpu.VMEM((SEQ, HEAD_SIZE), F32),
            pltpu.VMEM((SEQ, HEAD_SIZE), F32),
            pltpu.VMEM((HEAD_SIZE, SEQ), BF16),
            pltpu.VMEM((OWN, MODEL_WIDTH), BF16),
            pltpu.VMEM((PIECE, MODEL_WIDTH), BF16),
            pltpu.VMEM((4, 16, 32, HEADS_COLS + 256), BF16),
            pltpu.VMEM((4, 32, HEADS_COLS + 256), BF16),
            pltpu.VMEM((OWN, MODEL_WIDTH), BF16),
            pltpu.VMEM((8, MODEL_WIDTH), F32),
            pltpu.VMEM((4, 8, 512), F32),
            pltpu.VMEM((32, 8, 128), F32),
        ],
        (17, 63, 24),
        3,
        2**25,
    )
    (
        block_output, input_grad,
        gains_grad, gains_next, gains_mean, gains_square,
        heads_grad, heads_next, heads_mean, heads_square,
        merge_grad, merge_next, merge_mean, merge_square,
        gating_grad, gating_next, gating_mean, gating_square,
        down_grad, down_next, down_mean, down_square,
    ) = update(
        (
            block_output, input_grad, gains_grad,
            heads_pieces, merge_pieces, gating_pieces, down_pieces,
        ),
        (
            (norm_gains, gains_first, gains_second),
            (heads_projection_weight, heads_first_moment, heads_second_moment),
            (merge_weight, merge_first, merge_second),
            (gating_weight, gating_first, gating_second),
            (down_weight, down_first, down_second),
        ),
    )
    return (
        block_output,
        input_grad,
        gains_grad,
        gains_next,
        gains_mean,
        gains_square,
        heads_grad,
        heads_next,
        heads_mean,
        heads_square,
        merge_grad,
        merge_next,
        merge_mean,
        merge_square,
        gating_grad,
        gating_next,
        gating_mean,
        gating_square,
        down_grad,
        down_next,
        down_mean,
        down_square,
    )


def solution(mesh):
    in_specs = (
        P(("dp", "col"), "row"),
        P(("dp", "col"), "row"),
        P(None, "row"),
        P(None, "row"),
        P(None, "row"),
        P(("row", "dp"), "col"),
        P(("row", "dp"), "col"),
        P(("row", "dp"), "col"),
        P(("col", "dp"), "row"),
        P(("col", "dp"), "row"),
        P(("col", "dp"), "row"),
        P(("row", "dp"), None, "col"),
        P(("row", "dp"), None, "col"),
        P(("row", "dp"), None, "col"),
        P(("col", "dp"), "row"),
        P(("col", "dp"), "row"),
        P(("col", "dp"), "row"),
    )
    out_specs = (
        P(("dp", "col"), "row"),
        P(("dp", "col"), "row"),
        P(None, "row"),
        P(None, "row"),
        P(None, "row"),
        P(None, "row"),
        P(("row", "dp"), "col"),
        P(("row", "dp"), "col"),
        P(("row", "dp"), "col"),
        P(("row", "dp"), "col"),
        P(("col", "dp"), "row"),
        P(("col", "dp"), "row"),
        P(("col", "dp"), "row"),
        P(("col", "dp"), "row"),
        P(("row", "dp"), None, "col"),
        P(("row", "dp"), None, "col"),
        P(("row", "dp"), None, "col"),
        P(("row", "dp"), None, "col"),
        P(("col", "dp"), "row"),
        P(("col", "dp"), "row"),
        P(("col", "dp"), "row"),
        P(("col", "dp"), "row"),
    )
    return jax.shard_map(body, mesh=mesh, in_specs=in_specs, out_specs=out_specs, check_vma=False)
```
